32 devices in a mesh: groups: 2 (over y), seq: 4 (over z), head: 2 (over x), rep: 2 (over core).
Axes of the slice: x: 2, y: 2, z: 4, core: 2. Of those that a mesh axis runs over, the one named last changes fastest.
Arguments:
- prefill_kv: bfloat16 [8, 8, 512, 256], P('groups', ('head', 'rep'), 'seq'), parts along dimension 0, may hold values from -6 to 6
- kept_blocks: int32 [8, 8, 2], P('groups'), parts along dimension 0, may hold values from 0 to 3, as said below
- kept_counts: int32 [8, 8], P('groups'), parts along dimension 0, may hold values from 1 to 2, as said below
- queries: bfloat16 [2, 8, 64, 128], P(None, ('groups', 'seq'), 'head'), parts along dimension 1, may hold values from -6 to 6
- new_kv: bfloat16 [2, 8, 8, 256], P(None, ('groups', 'seq'), 'head'), parts along dimension 1, may hold values from -6 to 6
- out_weight: bfloat16 [8192, 8192], P('head', ('seq', 'rep')), may hold values from -0.0625 to 0.0625
- prefill_state: float32 [8, 16, 16384], P('groups', None, ('head', 'seq')), parts along dimension 0, may hold values from -6 to 6
- a_log: float32 [16, 16384], P(None, 'head'), may hold values from 0 to 2.77
- step_input: bfloat16 [2, 8, 16384], P(None, ('groups', 'seq'), 'head'), parts along dimension 1, may hold values from -6 to 6
- step_dt: float32 [2, 8, 16384], P(None, ('groups', 'seq'), 'head'), parts along dimension 1, may hold values from 0.01 to 0.3
- step_bc: float32 [2, 8, 2, 16], P(None, ('groups', 'seq')), parts along dimension 1, may hold values from -3 to 3
- skip_gain: float32 [16384], P('head'), may hold values from 0.5 to 1.5
Outputs:
- handoff: bfloat16 [8, 8, 2, 128, 256], P(('groups', 'seq'), 'head', 'rep'), parts along dimension 0
- proj_out: bfloat16 [2, 8, 8192], P(None, ('groups', 'head'), ('seq', 'rep')), parts along dimension 1
- mamba_out: float32 [2, 8, 16384], P(None, ('groups', 'seq'), 'head'), parts along dimension 1
The draws below stay inside these ranges and needn't reach their ends.
There are 2 independent parts, one for each index of `groups`. The reference program is written for one: setup_inputs(seed, part) draws one part's arguments, and reference() takes and returns one part's arrays. A program takes and returns all parts, laid end to end along the dimension named above; an argument that names none is the same for every part. Nothing has to cross between parts.
Inputs may be any that keep to these rules, and one draw needn't show every extreme that they name: `kept_blocks`: for each request and kv head, 2 distinct block indices; only the first kept_counts of them are used. `kept_counts`: every request has a kv head with exactly 2 kept blocks.
All inputs are finite; a program needn't handle non-finite values.
Results may differ from the reference program's by a relative error of at most 0.01.
Values may be sent and summed in bfloat16 or wider, within the bound.
No kernel may reach another device: no remote copies, remote signals or barrier semaphores. Data moves between devices by JAX's collectives and lax.ppermute only.
A program may use at most 64 MiB of HBM per device.

```python
import math
import jax
import jax.numpy as jnp
from jax import lax

D = 8192
QH = 64
KVH = 8
HD = 128
DI = 16384
NS = 16
BLOCK = 128
STEPS = 2
GROUP = 8
REQ = 4
NBLK = 4
KEEP = 2


def draw_prefill_kv(key, part):
    key = jax.random.fold_in(key, 11)
    shape = (REQ, KVH, NBLK * BLOCK, 2 * HD)
    base = jnp.clip(jax.random.normal(key, shape, jnp.float32), -6.0, 6.0)
    return base.astype(jnp.bfloat16)


def draw_queries(key, part):
    key = jax.random.fold_in(key, 12)
    shape = (STEPS, REQ, QH, HD)
    base = jnp.clip(jax.random.normal(key, shape, jnp.float32), -6.0, 6.0)
    return base.astype(jnp.bfloat16)


def draw_kept_blocks(key, part):
    key = jax.random.fold_in(key, 13)
    row_keys = jax.random.split(key, REQ * KVH)
    chosen = jax.vmap(lambda row_key: jax.random.permutation(row_key, NBLK)[:KEEP])(row_keys)
    return chosen.reshape(REQ, KVH, KEEP).astype(jnp.int32)


def draw_kept_counts(key, part):
    key = jax.random.fold_in(key, 14)
    first_key, second_key = jax.random.split(key)
    counts = jax.random.randint(first_key, (REQ, KVH), max(1, KEEP // 2), KEEP + 1)
    fullest = jax.random.randint(second_key, (REQ, 1), 0, KVH)
    counts = jnp.where(jnp.arange(KVH)[None, :] == fullest, KEEP, counts)
    return counts.astype(jnp.int32)


def steps_of(key, extent, cuts, low, top_value):
    level, own = 1.0, jax.random.fold_in(key, 6)
    for position, parts in cuts:
        heights = jnp.exp(jax.random.uniform(jax.random.fold_in(own, position), (parts,), jnp.float32, low / len(cuts), top_value / len(cuts)))
        level = level * jnp.repeat(heights, extent[position] // parts).reshape([-1 if axis == position else 1 for axis in range(len(extent))])
    return level


def scatter_about(rng, extent, width, limit, cuts=(), kind=jnp.bfloat16):
    entries = width * jax.random.normal(rng, extent, jnp.float32)
    if cuts:
        entries = entries * steps_of(rng, extent, cuts, -0.22, 0.18)
    return jnp.clip(entries, -limit, limit).astype(kind)


def setup_inputs(seed: int = 0, part: int = 0) -> dict:
    keys = jax.random.split(jax.random.key(seed), 13)
    own_keys = jax.random.split(jax.random.fold_in(keys[12], part), 13)
    prefill_kv = draw_prefill_kv(jax.random.fold_in(jax.random.fold_in(keys[12], part), 71), part)
    kept_blocks = draw_kept_blocks(jax.random.fold_in(jax.random.fold_in(keys[12], part), 71), part)
    kept_counts = draw_kept_counts(jax.random.fold_in(jax.random.fold_in(keys[12], part), 71), part)
    queries = draw_queries(jax.random.fold_in(jax.random.fold_in(keys[12], part), 71), part)
    new_kv = scatter_about(own_keys[4], (STEPS, REQ, KVH, 2 * HD), 1.0, 6.0, ((1, 4), (2, 2)))
    out_weight = scatter_about(keys[5], (QH * HD, D), (QH * HD) ** -0.5, 0.0625, ((0, 2), (1, 8)))
    prefill_state = scatter_about(own_keys[6], (REQ, NS, DI), 1.0, 6.0, ((2, 8),), jnp.float32)
    a_log = jnp.clip(2.77 * jax.random.uniform(keys[7], (NS, DI), jnp.float32) ** steps_of(keys[7], (NS, DI), ((1, 2),), -0.2, 0.2), 0.0, 2.77)
    step_input = scatter_about(own_keys[8], (STEPS, REQ, DI), 1.0, 6.0, ((1, 4), (2, 2)))
    step_dt = jnp.clip(jnp.exp(math.log(0.3) - 3.4011974 * jax.random.uniform(own_keys[9], (STEPS, REQ, DI), jnp.float32) ** steps_of(own_keys[9], (STEPS, REQ, DI), ((1, 4), (2, 2)), -0.2, 0.2)), 0.01, 0.3)
    step_bc = scatter_about(own_keys[10], (STEPS, REQ, 2, NS), 0.5, 3.0, ((1, 4),), jnp.float32)
    skip_gain = jnp.clip(0.5 + 1.0 * jax.random.uniform(keys[11], (DI,), jnp.float32) ** steps_of(keys[11], (DI,), ((0, 2),), -0.2, 0.2), 0.5, 1.5)
    return dict(prefill_kv=prefill_kv, kept_blocks=kept_blocks, kept_counts=kept_counts, queries=queries, new_kv=new_kv, out_weight=out_weight, prefill_state=prefill_state, a_log=a_log, step_input=step_input, step_dt=step_dt, step_bc=step_bc, skip_gain=skip_gain)


def reference(prefill_kv, kept_blocks, kept_counts, queries, new_kv, out_weight, prefill_state, a_log, step_input, step_dt, step_bc, skip_gain):
    block_view = prefill_kv.reshape(REQ, KVH, NBLK, BLOCK, 2 * HD)
    picked = jnp.take_along_axis(block_view, kept_blocks[:, :, :, None, None].astype(jnp.int32), axis=2)
    slot_live = jnp.arange(KEEP, dtype=jnp.int32)[None, None, :] < kept_counts[:, :, None]
    handoff = jnp.where(slot_live[:, :, :, None, None], picked, jnp.zeros((), jnp.bfloat16))
    cache_keys = handoff[..., :HD].reshape(REQ, KVH, KEEP * BLOCK, HD).astype(jnp.float32)
    cache_values = handoff[..., HD:].reshape(REQ, KVH, KEEP * BLOCK, HD).astype(jnp.float32)
    token_live = jnp.repeat(slot_live, BLOCK, axis=2)[:, :, None, :]
    grouped = queries.reshape(STEPS, REQ, KVH, GROUP, HD).astype(jnp.float32)
    new_keys = new_kv[..., :HD].astype(jnp.float32)
    new_values = new_kv[..., HD:].astype(jnp.float32)
    score_scale = HD ** -0.5
    attn_steps = []
    for step_index in range(STEPS):
        query_step = grouped[step_index]
        cache_scores = jnp.einsum("rhgd,rhkd->rhgk", query_step, cache_keys) * score_scale
        cache_scores = jnp.where(token_live, cache_scores, -1e30)
        fresh_scores = jnp.einsum("rhgd,srhd->rhgs", query_step, new_keys[: step_index + 1]) * score_scale
        score_top = jnp.maximum(jnp.max(cache_scores, axis=-1), jnp.max(fresh_scores, axis=-1))[..., None]
        cache_weights = jnp.where(token_live, jnp.exp(cache_scores - score_top), 0.0)
        fresh_weights = jnp.exp(fresh_scores - score_top)
        softmax_total = jnp.sum(cache_weights, axis=-1) + jnp.sum(fresh_weights, axis=-1)
        cache_rounded = lax.optimization_barrier(cache_weights.astype(jnp.bfloat16)).astype(jnp.float32)
        fresh_rounded = lax.optimization_barrier(fresh_weights.astype(jnp.bfloat16)).astype(jnp.float32)
        weighted = jnp.einsum("rhgk,rhkd->rhgd", cache_rounded, cache_values)
        weighted = weighted + jnp.einsum("rhgs,srhd->rhgd", fresh_rounded, new_values[: step_index + 1])
        attn_steps.append((weighted / softmax_total[..., None]).astype(jnp.bfloat16).reshape(REQ, QH * HD))
    attention = jnp.stack(attn_steps)
    proj_out = jnp.einsum("trk,kd->trd", attention.astype(jnp.float32), out_weight.astype(jnp.float32)).astype(jnp.bfloat16)
    mamba_state = lax.optimization_barrier(prefill_state.astype(jnp.bfloat16)).astype(jnp.float32)
    decay_rate = -jnp.exp(a_log)
    mamba_steps = []
    for step_index in range(STEPS):
        step_rate = step_dt[step_index]
        inputs = step_input[step_index].astype(jnp.float32)
        drive_b = step_bc[step_index, :, 0, :]
        read_c = step_bc[step_index, :, 1, :]
        mamba_state = jnp.exp(step_rate[:, None, :] * decay_rate[None]) * mamba_state + step_rate[:, None, :] * drive_b[:, :, None] * inputs[:, None, :]
        mamba_steps.append(jnp.sum(read_c[:, :, None] * mamba_state, axis=1) + skip_gain[None, :] * inputs)
    mamba_out = jnp.stack(mamba_steps)
    return handoff, proj_out, mamba_out
```

```python
import functools

import jax
import jax.numpy as jnp
from jax import lax
from jax.experimental import pallas as pl
from jax.experimental.pallas import tpu as pltpu
from jax.sharding import PartitionSpec as P

BLOCK = 128
NEG = -1e30
BF = jnp.bfloat16
F32 = jnp.float32
VM = pl.BlockSpec(memory_space=pltpu.VMEM)
SM = pl.BlockSpec(memory_space=pltpu.SMEM)
ANY = pl.BlockSpec(memory_space=pl.ANY)


def shift(x, axis, c):
    count = lax.axis_size(axis)
    return lax.ppermute(x, axis, [(i, i ^ c) for i in range(count)])


def call(body, out_shape, in_specs, out_specs, scratch=(), cost=(0, 0)):
    return pl.pallas_call(
        body,
        out_shape=out_shape,
        in_specs=in_specs,
        out_specs=out_specs,
        scratch_shapes=list(scratch),
        cost_estimate=pl.CostEstimate(flops=cost[0], bytes_accessed=cost[1], transcendentals=0),
        compiler_params=pltpu.CompilerParams(vmem_limit_bytes=32 * 1024 * 1024),
    )


def stage_kv(count, kv_ref, *rest):
    outs, sems = rest[:count], rest[count]
    me = lax.axis_index("seq")
    copies = [
        pltpu.make_async_copy(kv_ref.at[me ^ c], outs[c], sems.at[c]) for c in range(count)
    ]
    for copy in copies:
        copy.start()
    for copy in copies:
        copy.wait()


def stage_state(count, split, state_ref, *outs):
    me = lax.axis_index("seq")
    rep = lax.axis_index("rep")
    part = outs[0].shape[-1]
    for c in range(count):
        if split:
            piece = state_ref[me ^ c, :, pl.ds(pl.multiple_of(rep * part, 128), part)]
        else:
            piece = state_ref[me ^ c]
        outs[c][...] = piece.astype(BF)


def attend(count, blocks_ref, counts_ref, kv_ref, new_ref, *rest):
    q_refs, out_ref = rest[:count], rest[count]
    me = lax.axis_index("seq")
    head_first = lax.axis_index("head") * new_ref.shape[2]
    rep = lax.axis_index("rep")
    heads = kv_ref.shape[1]
    hd = kv_ref.shape[3] // 2
    steps, _, q_heads, _ = q_refs[0].shape
    keep = blocks_ref.shape[2]
    own_q = q_heads // 2
    group = own_q // heads
    rows = steps * group
    scale = hd ** (-0.5)
    fresh = []
    for step in range(steps):
        both = new_ref[step, 0].astype(F32)
        fresh.append(jnp.where(rep == 0, both[:heads], both[heads:]))
    pieces, lses = [], []
    for c in range(count):
        request = me ^ c
        q_all = [q_refs[c][step, 0].astype(F32) for step in range(steps)]
        q_all = [jnp.where(rep == 0, q[:own_q], q[own_q:]) for q in q_all]
        for j in range(heads):
            head = head_first + rep * heads + j
            live_count = counts_ref[request, head]
            live = jnp.int32(0)
            for slot in range(keep):
                hit = (blocks_ref[request, head, slot] == me) & (slot < live_count)
                live = live | hit.astype(jnp.int32)
            dead = jnp.where(live > 0, 0.0, NEG).astype(F32)
            q = jnp.concatenate([x[j * group : (j + 1) * group] for x in q_all], axis=0)
            keys = kv_ref[request, j, :, :hd]
            values = kv_ref[request, j, :, hd:]
            scores = lax.dot_general(
                q.astype(BF), keys, (((1,), (1,)), ((), ())), preferred_element_type=F32
            )
            scores = jnp.where(live > 0, scores * scale, dead)
            top = jnp.max(scores, axis=1, keepdims=True)
            fresh_scores = []
            if c == 0:
                row_step = lax.broadcasted_iota(jnp.int32, (rows, 1), 0) // group
                for step in range(steps):
                    dots = jnp.sum(q * fresh[step][j : j + 1, :hd], axis=1, keepdims=True)
                    dots = jnp.where(row_step >= step, dots * scale, NEG)
                    fresh_scores.append(dots)
                    top = jnp.maximum(top, dots)
            weights = jnp.where(live > 0, jnp.exp(scores - top), 0.0)
            total = jnp.sum(weights, axis=1, keepdims=True)
            summed = jnp.dot(weights.astype(BF), values, preferred_element_type=F32)
            for step, dots in enumerate(fresh_scores):
                weight = jnp.where(row_step >= step, jnp.exp(dots - top), 0.0)
                total = total + weight
                summed = summed + weight.astype(BF).astype(F32) * fresh[step][j : j + 1, hd:]
            safe = jnp.where(total > 0.0, total, 1.0)
            pieces.append(summed / safe)
            lses.append(jnp.where(total > 0.0, top + jnp.log(safe), NEG))
    all_rows = jnp.concatenate(pieces, axis=0)
    all_lse = jnp.concatenate(lses, axis=0)
    chunks = out_ref.shape[0]
    line = lax.broadcasted_iota(jnp.int32, (16, 128), 0)
    for k in range(chunks):
        out_ref[k, :128, :] = all_rows[k * 128 : (k + 1) * 128].astype(BF)
        flat = jnp.transpose(jnp.broadcast_to(all_lse[k * 128 : (k + 1) * 128], (128, 128)))[:16]
        high = flat.astype(BF).astype(F32)
        middle = (flat - high).astype(BF).astype(F32)
        low = flat - high - middle
        stats = jnp.where(line == 0, high, jnp.where(line == 1, middle, jnp.where(line == 2, low, 0.0)))
        out_ref[k, 128:, :] = stats.astype(BF)


def merge(count, heads, steps, group, *rest):
    parts, out_ref, scratch = rest[:count], rest[count], rest[count + 1]
    me = lax.axis_index("seq")
    rows = steps * group
    chunks = parts[0].shape[0]
    lse = []
    for c in range(count):
        columns = []
        for k in range(chunks):
            stats = parts[c][k, 128:, :].astype(F32)
            line = jnp.sum(stats[:8], axis=0, keepdims=True)
            columns.append(jnp.transpose(jnp.broadcast_to(line, (128, 128))))
        lse.append(columns)
    for e in range(count):
        for j in range(heads):
            tops, values = [], []
            for c in range(count):
                base = ((e ^ c) * heads + j) * rows
                k, at = base // 128, base % 128
                tops.append(lse[c][k][at : at + rows])
                values.append(parts[c][k, at : at + rows, :].astype(F32))
            top = functools.reduce(jnp.maximum, tops)
            total = jnp.zeros_like(top)
            summed = jnp.zeros_like(top)
            for c in range(count):
                weight = jnp.exp(tops[c] - top)
                total = total + weight
                summed = summed + weight * values[c]
            result = summed / total
            for step in range(steps):
                at = pl.multiple_of((step * count + (me ^ e)) * group, group)
                scratch[j, pl.ds(at, group), :] = result[step * group : (step + 1) * group]
    for j in range(heads):
        for g in range(group):
            at = (j * group + g) * 128
            tile = scratch[j, pl.ds(g, steps * count, stride=group), :]
            out_ref[:, at : at + 128] = tile.astype(BF)


def load_weight(weight_ref, out_ref, sem):
    copy = pltpu.make_async_copy(weight_ref, out_ref, sem)
    copy.start()
    copy.wait()


def project_own(attn_ref, weight_ref, out_ref):
    half = attn_ref.shape[1]
    first = pl.multiple_of(lax.axis_index("rep") * half, half)
    out_ref[...] = jnp.dot(
        attn_ref[...], weight_ref[pl.ds(first, half), :], preferred_element_type=F32
    )


def pick(options, index):
    chosen = options[0]
    for i in range(1, len(options)):
        chosen = jnp.where(index == i, options[i], chosen)
    return chosen


def project_other(heads_count, count, acc_ref, attn_ref, weight_ref, *outs):
    half = attn_ref.shape[1]
    first = pl.multiple_of((1 - lax.axis_index("rep")) * half, half)
    total = acc_ref[...] + jnp.dot(
        attn_ref[...], weight_ref[pl.ds(first, half), :], preferred_element_type=F32
    )
    head = lax.axis_index("head")
    steps = total.shape[0] // count
    share = count // heads_count
    for step in range(steps):
        slices = [
            total[step * count + x * share : step * count + (x + 1) * share]
            for x in range(heads_count)
        ]
        for c in range(heads_count):
            outs[c][step] = pick(slices, head ^ c)


def add_up(*refs):
    total = refs[0][...]
    for ref in refs[1:-1]:
        total = total + ref[...]
    refs[-1][...] = total.astype(BF)


def scan_steps(count, split, dt_ref, x_ref, bc_ref, gain_ref, log_ref, *rest):
    states, out_ref = rest[:count], rest[count]
    me = lax.axis_index("seq")
    rep = lax.axis_index("rep")
    ns, part = states[0].shape
    block = part * 2 if split else part
    steps = dt_ref.shape[0]
    diagonal = lax.broadcasted_iota(jnp.int32, (ns, ns), 0) == lax.broadcasted_iota(
        jnp.int32, (ns, ns), 1
    )

    def column(row):
        return jnp.sum(jnp.where(diagonal, row, 0.0), axis=1, keepdims=True)

    drive = [column(bc_ref[step, 0, 0:1, :]) for step in range(steps)]
    read = [column(bc_ref[step, 0, 1:2, :]) for step in range(steps)]
    for c in range(count):
        place = me ^ c
        first = place * block + (rep * part if split else 0)
        lanes = pl.ds(pl.multiple_of(first, 128), part)
        state = states[c][...].astype(F32)
        rate = -jnp.exp(log_ref[:, lanes])
        gain = gain_ref[:, lanes]
        for step in range(steps):
            dt = dt_ref[step, :, lanes]
            inputs = x_ref[step, :, lanes].astype(F32)
            state = jnp.exp(dt * rate) * state + drive[step] * (dt * inputs)
            out_ref[step, pl.ds(place, 1), :] = (
                jnp.sum(read[step] * state, axis=0, keepdims=True) + gain * inputs
            )


def join_halves(own_ref, other_ref, out_ref):
    rep = lax.axis_index("rep")
    steps, count, part = own_ref.shape
    for step in range(steps):
        for b in range(count):
            own, other = own_ref[step, b : b + 1, :], other_ref[step, b : b + 1, :]
            at = b * 2 * part
            out_ref[step, :, at : at + part] = jnp.where(rep == 0, own, other)
            out_ref[step, :, at + part : at + 2 * part] = jnp.where(rep == 0, other, own)


def assemble(count, blocks_ref, counts_ref, *rest):
    own, other = rest[:count], rest[count : 2 * count]
    out_ref, zeros, sems = rest[2 * count :]
    me = lax.axis_index("seq")
    rep = lax.axis_index("rep")
    heads = own[0].shape[0]
    _, dec_heads, keep_rep, _, _ = out_ref.shape
    head_first = lax.axis_index("head") * dec_heads
    zeros[...] = jnp.zeros_like(zeros)
    for side in range(2):
        pieces = own if side == 0 else other
        owner = rep if side == 0 else 1 - rep
        for j in range(heads):
            local = owner * heads + j
            head = head_first + local
            live_count = counts_ref[me, head]
            for k in range(keep_rep):
                slot = rep * keep_rep + k
                source = blocks_ref[me, head, slot] ^ me
                live = slot < live_count
                sem = sems.at[side, j, k]
                for c in range(count):

                    @pl.when(live & (source == c))
                    def _():
                        pltpu.make_async_copy(pieces[c].at[j], out_ref.at[0, local, k], sem).start()

                @pl.when(jnp.logical_not(live))
                def _():
                    pltpu.make_async_copy(zeros, out_ref.at[0, local, k], sem).start()

    for side in range(2):
        owner = rep if side == 0 else 1 - rep
        for j in range(heads):
            for k in range(keep_rep):
                pltpu.make_async_copy(
                    zeros, out_ref.at[0, owner * heads + j, k], sems.at[side, j, k]
                ).wait()


def per_device(
    prefill_kv,
    kept_blocks,
    kept_counts,
    queries,
    new_kv,
    out_weight,
    prefill_state,
    a_log,
    step_input,
    step_dt,
    step_bc,
    skip_gain,
):
    count = lax.axis_size("seq")
    reps = lax.axis_size("rep")
    heads_count = lax.axis_size("head")
    requests, heads, tokens, width = prefill_kv.shape
    assert requests == count and tokens == BLOCK and reps == 2 and width == 256
    assert count & (count - 1) == 0 and heads_count & (heads_count - 1) == 0
    keep = kept_blocks.shape[2]
    steps, _, q_heads, hd = queries.shape
    dec_heads = new_kv.shape[2]
    group = q_heads // dec_heads
    _, ns, block = prefill_state.shape
    split = block % (reps * 128) == 0
    part = block // reps if split else block
    all_rows = count * heads * steps * group
    chunks = all_rows // 128
    shape = jax.ShapeDtypeStruct

    asked = [queries] + [shift(queries, "seq", c) for c in range(1, count)]

    kv = call(
        functools.partial(stage_kv, count),
        [shape((heads, BLOCK, width), BF)] * count,
        [ANY],
        [ANY] * count,
        [pltpu.SemaphoreType.DMA((count,))],
    )(prefill_kv)
    state = call(
        functools.partial(stage_state, count, split),
        [shape((ns, part), BF)] * count,
        [VM],
        [VM] * count,
    )(prefill_state)
    kv_own = [kv[0]] + [shift(kv[c], "seq", c) for c in range(1, count)]
    kv_other = [shift(piece, "rep", 1) for piece in kv_own]
    state = [state[0]] + [shift(state[c], "seq", c) for c in range(1, count)]

    weight = call(
        load_weight, pltpu.VMEM(out_weight.shape, BF), [ANY], VM, [pltpu.SemaphoreType.DMA]
    )(out_weight)

    partial_sums = call(
        functools.partial(attend, count),
        shape((chunks, 144, 128), BF),
        [SM, SM, VM, VM] + [VM] * count,
        VM,
    )(kept_blocks, kept_counts, prefill_kv, new_kv, *asked)
    gathered = [partial_sums] + [shift(partial_sums, "seq", c) for c in range(1, count)]
    half = heads * group * hd
    attn = call(
        functools.partial(merge, count, heads, steps, group),
        shape((steps * count, half), BF),
        [VM] * count,
        VM,
        [pltpu.VMEM((heads, steps * count * group, hd), F32)],
    )(*gathered)
    attn_other = shift(attn, "rep", 1)
    columns = out_weight.shape[1]
    own_sum = call(project_own, shape((steps * count, columns), F32), [VM, VM], VM)(attn, weight)
    share = count // heads_count
    sums = call(
        functools.partial(project_other, heads_count, count),
        [shape((steps, share, columns), F32)] * heads_count,
        [VM, VM, VM],
        [VM] * heads_count,
    )(own_sum, attn_other, weight)
    sums = [sums[0]] + [shift(sums[c], "head", c) for c in range(1, heads_count)]
    proj_out = call(
        add_up, shape((steps, share, columns), BF), [VM] * heads_count, VM
    )(*sums)

    mamba = call(
        functools.partial(scan_steps, count, split),
        shape((steps, count, part), F32),
        [VM] * 5 + [VM] * count,
        VM,
    )(step_dt, step_input, step_bc, skip_gain.reshape(1, -1), a_log, *state)
    if split:
        mamba_out = call(
            join_halves, shape((steps, 1, count * block), F32), [VM, VM], VM
        )(mamba, shift(mamba, "rep", 1))
    else:
        mamba_out = mamba.reshape(steps, 1, count * block)

    keep_rep = keep // reps
    handoff = call(
        functools.partial(assemble, count),
        shape((1, dec_heads, keep_rep, BLOCK, width), BF),
        [SM, SM] + [ANY] * (2 * count),
        ANY,
        [pltpu.VMEM((BLOCK, width), BF), pltpu.SemaphoreType.DMA((2, heads, keep_rep))],
    )(kept_blocks, kept_counts, *kv_own, *kv_other)
    return handoff, proj_out, mamba_out


def solution(mesh):
    return jax.shard_map(
        per_device,
        mesh=mesh,
        in_specs=(
            P("groups", ("head", "rep"), "seq", None),
            P("groups", None, None),
            P("groups", None),
            P(None, ("groups", "seq"), "head", None),
            P(None, ("groups", "seq"), "head", None),
            P("head", ("seq", "rep")),
            P("groups", None, ("head", "seq")),
            P(None, "head"),
            P(None, ("groups", "seq"), "head"),
            P(None, ("groups", "seq"), "head"),
            P(None, ("groups", "seq"), None, None),
            P("head"),
        ),
        out_specs=(
            P(("groups", "seq"), "head", "rep", None, None),
            P(None, ("groups", "head"), ("seq", "rep")),
            P(None, ("groups", "seq"), "head"),
        ),
        check_vma=False,
    )
```

```python
import functools

import jax
import jax.numpy as jnp
from jax import lax
from jax.experimental import pallas as pl
from jax.experimental.pallas import tpu as pltpu
from jax.sharding import PartitionSpec as P

BLOCK = 128
NEG = -1e30
BF = jnp.bfloat16
F32 = jnp.float32
VM = pl.BlockSpec(memory_space=pltpu.VMEM)
HB = pl.BlockSpec(memory_space=pltpu.HBM)
DMA = pltpu.SemaphoreType.DMA


def shift(x, axis, c):
    size = lax.axis_size(axis)
    return lax.ppermute(x, axis, [(i, i ^ c) for i in range(size)])


def call(body, out_shape, in_specs, out_specs, scratch=(), us=1.0):
    return pl.pallas_call(
        body,
        out_shape=out_shape,
        in_specs=in_specs,
        out_specs=out_specs,
        scratch_shapes=list(scratch),
        cost_estimate=pl.CostEstimate(
            flops=0, bytes_accessed=int(us * 3.6e6), transcendentals=0
        ),
        compiler_params=pltpu.CompilerParams(vmem_limit_bytes=32 * 1024 * 1024),
    )


def in_hbm(x):
    return pltpu.with_memory_space_constraint(x, pltpu.HBM)


def after(arrays, *earlier):
    return lax.optimization_barrier((*arrays, *earlier))[: len(arrays)]


def run_all(copies):
    for copy in copies:
        copy.start()
    for copy in copies:
        copy.wait()


def copier(sems):
    position = iter(range(sems.shape[0]))
    return lambda src, dst: pltpu.make_async_copy(src, dst, sems.at[next(position)])


def state_rows(part):
    return 16 * pl.cdiv(part, 256)


def pack_state(piece, out_ref, first):
    ns, part = piece.shape
    for i in range(pl.cdiv(part, 256)):
        cut = piece[:, i * 256 : (i + 1) * 256]
        if cut.shape[1] < 256:
            cut = jnp.concatenate([cut, jnp.zeros((ns, 256 - cut.shape[1]), F32)], axis=1)
        out_ref[first + i * 16 : first + (i + 1) * 16, :] = cut.astype(BF)


def stage(count, split, kv_ref, state_ref, q_ref, new_ref, blocks_ref, counts_ref, *rest):
    sends = rest[: count - 1]
    own_state, kv_out, q_out, new_out, bias_out = rest[count - 1 : count + 4]
    loaded, blocks, counts, sems, early = rest[count + 4 :]
    me, rep = lax.axis_index("seq"), lax.axis_index("rep")
    heads = kv_ref.shape[1]
    part = loaded.shape[2]
    copy = copier(early)
    first = [copy(blocks_ref, blocks), copy(counts_ref, counts)]
    for c in range(count):
        if split:
            src = state_ref.at[me ^ c, :, pl.ds(pl.multiple_of(rep * part, 128), part)]
        else:
            src = state_ref.at[me ^ c]
        first.append(copy(src, loaded.at[c]))
    copy = copier(sems)
    moves = []
    for c in range(1, count):
        for j in range(heads):
            rows = pl.ds(j * BLOCK, BLOCK)
            moves.append(copy(kv_ref.at[me ^ c, j], sends[c - 1].at[rows]))
    moves += [copy(kv_ref, kv_out), copy(q_ref, q_out), copy(new_ref, new_out)]
    for move in first + moves:
        move.start()
    for move in first:
        move.wait()
    pack_state(loaded[0], own_state, 0)
    for c in range(1, count):
        pack_state(loaded[c], sends[c - 1], heads * BLOCK)
    head_first = lax.axis_index("head") * new_ref.shape[2] + rep * heads
    rows = bias_out.shape[0] // (count * heads)
    for c in range(count):
        for j in range(heads):
            live = jnp.int32(0)
            for slot in range(blocks.shape[1]):
                hit = blocks[me ^ c, slot, head_first + j] == me
                live = live | (hit & (slot < counts[me ^ c, head_first + j])).astype(jnp.int32)
            at = (c * heads + j) * rows
            dead = jnp.where(live > 0, 0.0, NEG).astype(F32)
            bias_out[at : at + rows, :] = jnp.full((rows, 128), dead, F32)
    for move in moves:
        move.wait()


def dot_f32(a, b, contract):
    return lax.dot_general(a, b, (contract, ((), ())), preferred_element_type=F32)


def attend(count, kv_ref, new_ref, bias_ref, *rest):
    q_refs, out_ref = rest[:count], rest[count]
    me, rep = lax.axis_index("seq"), lax.axis_index("rep")
    heads = kv_ref.shape[1]
    hd = kv_ref.shape[3] // 2
    steps, _, q_heads, _ = q_refs[0].shape
    own_q = q_heads // 2
    group = own_q // heads
    rows = steps * group
    scale = hd ** (-0.5)
    fresh = []
    for step in range(steps):
        both = new_ref[step, 0].astype(F32)
        fresh.append(jnp.where(rep == 0, both[:heads], both[heads:]))
    queries = []
    for c in range(count):
        q_all = [q_refs[c][step, 0].astype(F32) for step in range(steps)]
        q_all = [jnp.where(rep == 0, q[:own_q], q[own_q:]) for q in q_all]
        for j in range(heads):
            queries.append(
                jnp.concatenate([x[j * group : (j + 1) * group] for x in q_all], axis=0)
            )
    scores = []
    for c in range(count):
        for j in range(heads):
            keys = kv_ref[me ^ c, j, :, :hd]
            scores.append(dot_f32(queries[c * heads + j].astype(BF), keys, ((1,), (1,))))
    scores = jnp.concatenate(scores, axis=0)
    alive = bias_ref[...] == 0.0
    scores = jnp.where(alive, scores * scale, NEG)
    top = jnp.max(scores, axis=1, keepdims=True)
    own_rows = heads * rows
    own_q_rows = jnp.concatenate(queries[:heads], axis=0)
    row_step = (lax.broadcasted_iota(jnp.int32, (own_rows, 1), 0) // group) % steps
    own_top = top[:own_rows]
    dots = []
    for step in range(steps):
        wide = jnp.concatenate(
            [jnp.broadcast_to(fresh[step][j : j + 1, :hd], (rows, hd)) for j in range(heads)],
            axis=0,
        )
        dot = jnp.sum(own_q_rows * wide, axis=1, keepdims=True)
        dots.append(jnp.where(row_step >= step, dot * scale, NEG))
        own_top = jnp.maximum(own_top, dots[-1])
    top = jnp.concatenate([own_top, top[own_rows:]], axis=0)
    weights = jnp.where(alive, jnp.exp(scores - top), 0.0)
    total = jnp.sum(weights, axis=1, keepdims=True)
    weights = weights.astype(BF)
    summed = []
    for c in range(count):
        for j in range(heads):
            at = (c * heads + j) * rows
            values = kv_ref[me ^ c, j, :, hd:]
            summed.append(dot_f32(weights[at : at + rows], values, ((1,), (0,))))
    own_sum = jnp.concatenate(summed[:heads], axis=0)
    own_total = total[:own_rows]
    for step in range(steps):
        weight = jnp.where(row_step >= step, jnp.exp(dots[step] - own_top), 0.0)
        own_total = own_total + weight
        wide = jnp.concatenate(
            [jnp.broadcast_to(fresh[step][j : j + 1, hd:], (rows, hd)) for j in range(heads)],
            axis=0,
        )
        own_sum = own_sum + weight.astype(BF).astype(F32) * wide
    total = jnp.concatenate([own_total, total[own_rows:]], axis=0)
    summed = jnp.concatenate([own_sum] + summed[heads:], axis=0)
    chunks = out_ref.shape[0]
    line = lax.broadcasted_iota(jnp.int32, (16, 128), 0)
    for k in range(chunks):
        cut = slice(k * 128, (k + 1) * 128)
        out_ref[k, :128, :] = summed[cut].astype(BF)
        stats = jnp.zeros((16, 128), F32)
        for kind, column in ((0, top[cut]), (3, total[cut])):
            flat = jnp.transpose(jnp.broadcast_to(column, (128, 128)))[:16]
            high = flat.astype(BF).astype(F32)
            middle = (flat - high).astype(BF).astype(F32)
            low = flat - high - middle
            for at, piece in ((kind, high), (kind + 1, middle), (kind + 2, low)):
                stats = jnp.where(line == at, piece, stats)
        out_ref[k, 128:, :] = stats.astype(BF)


def merge(count, heads, steps, group, *rest):
    parts, out_ref, scratch = rest[:count], rest[count], rest[count + 1]
    me = lax.axis_index("seq")
    rows = steps * group
    chunks = parts[0].shape[0]
    line = lax.broadcasted_iota(jnp.int32, (16, 128), 0)
    top_all, total_all = [], []
    for c in range(count):
        tops, totals = [], []
        for k in range(chunks):
            stats = parts[c][k, 128:, :].astype(F32)
            for kind, out in ((0, tops), (3, totals)):
                mine = (line >= kind) & (line < kind + 3)
                row = jnp.sum(jnp.where(mine, stats, 0.0), axis=0, keepdims=True)
                out.append(jnp.transpose(jnp.broadcast_to(row, (128, 128))))
        top_all.append(tops)
        total_all.append(totals)
    for e in range(count):
        for j in range(heads):
            places = [divmod(((e ^ c) * heads + j) * rows, 128) for c in range(count)]
            tops = [top_all[c][k][at : at + rows] for c, (k, at) in enumerate(places)]
            top = functools.reduce(jnp.maximum, tops)
            total = jnp.zeros_like(top)
            summed = jnp.zeros_like(top)
            for c, (k, at) in enumerate(places):
                weight = jnp.exp(tops[c] - top)
                total = total + weight * total_all[c][k][at : at + rows]
                summed = summed + weight * parts[c][k, at : at + rows, :].astype(F32)
            result = summed / total
            for step in range(steps):
                at = pl.multiple_of((step * count + (me ^ e)) * group, group)
                scratch[j, pl.ds(at, group), :] = result[step * group : (step + 1) * group]
    for j in range(heads):
        for g in range(group):
            at = (j * group + g) * 128
            tile = scratch[j, pl.ds(g, steps * count, stride=group), :]
            out_ref[:, at : at + 128] = tile.astype(BF)


def load_weight(weight_ref, out_ref, sems):
    pieces = sems.shape[0]
    rows = weight_ref.shape[0] // pieces
    copy = copier(sems)
    cuts = [pl.ds(i * rows, rows) for i in range(pieces)]
    run_all([copy(weight_ref.at[cut], out_ref.at[cut]) for cut in cuts])


def project_own(attn_ref, weight_ref, out_ref):
    half = attn_ref.shape[1]
    first = pl.multiple_of(lax.axis_index("rep") * half, half)
    out_ref[...] = dot_f32(attn_ref[...], weight_ref[pl.ds(first, half), :], ((1,), (0,)))


def pick(options, index):
    chosen = options[0]
    for i in range(1, len(options)):
        chosen = jnp.where(index == i, options[i], chosen)
    return chosen


def project_other(heads_count, count, acc_ref, attn_ref, weight_ref, *outs):
    half = attn_ref.shape[1]
    first = pl.multiple_of((1 - lax.axis_index("rep")) * half, half)
    total = acc_ref[...] + dot_f32(
        attn_ref[...], weight_ref[pl.ds(first, half), :], ((1,), (0,))
    )
    head = lax.axis_index("head")
    steps = total.shape[0] // count
    share = count // heads_count
    for step in range(steps):
        slices = [
            total[step * count + x * share : step * count + (x + 1) * share]
            for x in range(heads_count)
        ]
        for c in range(heads_count):
            outs[c][step] = pick(slices, head ^ c)


def add_up(*refs):
    total = refs[0][...]
    for ref in refs[1:-1]:
        total = total + ref[...]
    refs[-1][...] = total.astype(BF)


def coefficients(count, split, dt_hbm, x_hbm, bc_hbm, gain_hbm, log_hbm, slope_ref, base_ref,
                 dt_ref, x_ref, bc_ref, gain_ref, log_ref, sems):
    copy = copier(sems)
    run_all(
        [
            copy(dt_hbm, dt_ref),
            copy(x_hbm, x_ref),
            copy(bc_hbm, bc_ref),
            copy(gain_hbm, gain_ref),
            copy(log_hbm, log_ref),
        ]
    )
    me, rep = lax.axis_index("seq"), lax.axis_index("rep")
    _, steps, ns, part = slope_ref.shape
    block = part * 2 if split else part
    diagonal = lax.broadcasted_iota(jnp.int32, (ns, ns), 0) == lax.broadcasted_iota(
        jnp.int32, (ns, ns), 1
    )

    def column(row):
        return jnp.sum(jnp.where(diagonal, row, 0.0), axis=1, keepdims=True)

    drive = [column(bc_ref[step, 0, 0:1, :]) for step in range(steps)]
    read = [column(bc_ref[step, 0, 1:2, :]) for step in range(steps)]
    for c in range(count):
        first = (me ^ c) * block + (rep * part if split else 0)
        lanes = pl.ds(pl.multiple_of(first, 128), part)
        rate = -jnp.exp(log_ref[:, lanes])
        gain = gain_ref[:, lanes]
        kept = jnp.ones((ns, part), F32)
        added = jnp.zeros((ns, part), F32)
        for step in range(steps):
            dt = dt_ref[step, :, lanes]
            inputs = x_ref[step : step + 1, lanes].astype(F32)
            decay = jnp.exp(dt * rate)
            kept = kept * decay
            added = added * decay + drive[step] * (dt * inputs)
            slope_ref[c, step] = read[step] * kept
            base_ref[c, step] = (
                jnp.sum(read[step] * added, axis=0, keepdims=True) + gain * inputs
            )


def select(count, blocks_ref, counts_ref, kv_ref, state_ref, slope_ref, base_ref, *rest):
    received = rest[: count - 1]
    kept_ref, sent_ref, mamba_ref, blocks, counts, zeros, sems, early = rest[count - 1 :]
    me, rep = lax.axis_index("seq"), lax.axis_index("rep")
    heads, keep_rep = kept_ref.shape[:2]
    copy = copier(early)
    scalars = [copy(blocks_ref, blocks), copy(counts_ref, counts)]
    for move in scalars:
        move.start()
    zeros[...] = jnp.zeros_like(zeros)
    _, steps, ns, part = slope_ref.shape
    for c in range(count):
        source, first = (state_ref, 0) if c == 0 else (received[c - 1], heads * BLOCK)
        rows = [
            source[first + 16 * i : first + 16 * (i + 1), :].astype(F32)
            for i in range(pl.cdiv(part, 256))
        ]
        state = jnp.concatenate(rows, axis=1)[:, :part]
        for step in range(steps):
            mamba_ref[step, me ^ c] = base_ref[c, step] + jnp.sum(
                slope_ref[c, step] * state, axis=0, keepdims=True
            )
    for move in scalars:
        move.wait()
    head_first = lax.axis_index("head") * (2 * heads) + rep * heads
    for side, out in ((0, kept_ref), (1, sent_ref)):
        owner = rep if side == 0 else 1 - rep
        for j in range(heads):
            live_count = counts[me, head_first + j]
            for k in range(keep_rep):
                slot = owner * keep_rep + k
                source = blocks[me, slot, head_first + j] ^ me
                live = slot < live_count
                sem = sems.at[side, j, k]
                for c in range(count):
                    piece = kv_ref.at[me, j] if c == 0 else received[c - 1].at[pl.ds(j * BLOCK, BLOCK)]

                    @pl.when(live & (source == c))
                    def _():
                        pltpu.make_async_copy(piece, out.at[j, k], sem).start()

                @pl.when(jnp.logical_not(live))
                def _():
                    pltpu.make_async_copy(zeros, out.at[j, k], sem).start()

    for side, out in ((0, kept_ref), (1, sent_ref)):
        for j in range(heads):
            for k in range(keep_rep):
                pltpu.make_async_copy(zeros, out.at[j, k], sems.at[side, j, k]).wait()


def assemble(split, kept_ref, got_ref, mamba_ref, *rest):
    rep = lax.axis_index("rep")
    if split:
        other_ref, handoff_ref, out_ref, sems = rest
    else:
        handoff_ref, out_ref, sems = rest
    heads = kept_ref.shape[0]
    copy = copier(sems)
    moves = [
        copy(kept_ref, handoff_ref.at[0, pl.ds(rep * heads, heads)]),
        copy(got_ref, handoff_ref.at[0, pl.ds((1 - rep) * heads, heads)]),
    ]
    steps, count, _, part = mamba_ref.shape
    for step in range(steps):
        for b in range(count):
            if split:
                for ref, side in ((mamba_ref, rep), (other_ref, 1 - rep)):
                    lanes = pl.ds(pl.multiple_of((2 * b + side) * part, 128), part)
                    moves.append(copy(ref.at[step, b], out_ref.at[step, :, lanes]))
            else:
                moves.append(copy(mamba_ref.at[step, b], out_ref.at[step, :, pl.ds(b * part, part)]))
    run_all(moves)


def per_device(
    prefill_kv,
    kept_blocks,
    kept_counts,
    queries,
    new_kv,
    out_weight,
    prefill_state,
    a_log,
    step_input,
    step_dt,
    step_bc,
    skip_gain,
):
    count = lax.axis_size("seq")
    reps = lax.axis_size("rep")
    heads_count = lax.axis_size("head")
    requests, heads, tokens, width = prefill_kv.shape
    assert requests == count and tokens == BLOCK and reps == 2 and width == 256
    assert count & (count - 1) == 0 and heads_count & (heads_count - 1) == 0
    keep = kept_blocks.shape[2]
    keep_rep = keep // reps
    steps, _, q_heads, hd = queries.shape
    dec_heads = new_kv.shape[2]
    group = q_heads // dec_heads
    _, ns, block = prefill_state.shape
    split = block % (reps * 128) == 0
    part = block // reps if split else block
    all_rows = count * heads * steps * group
    chunks = all_rows // 128
    channels = count * block
    shape = jax.ShapeDtypeStruct
    smem = pltpu.SMEM
    blocks = jnp.swapaxes(kept_blocks, 1, 2)

    asked = [shift(queries, "seq", c) for c in range(1, count)]
    prefill_kv, prefill_state, queries, new_kv = map(in_hbm, (prefill_kv, prefill_state, queries, new_kv))
    step_dt, step_bc, a_log, out_weight = map(in_hbm, (step_dt, step_bc, a_log, out_weight))
    step_input = in_hbm(step_input.reshape(steps, channels))
    skip_gain = in_hbm(skip_gain.reshape(1, -1))
    blocks, kept_counts = in_hbm(blocks), in_hbm(kept_counts)

    packed = heads * BLOCK + state_rows(part)
    staged = call(
        functools.partial(stage, count, split),
        [shape((packed, width), BF)] * (count - 1)
        + [
            shape((state_rows(part), width), BF),
            shape(prefill_kv.shape, BF),
            shape(queries.shape, BF),
            shape(new_kv.shape, BF),
            shape((all_rows, 128), F32),
        ],
        [HB] * 6,
        [VM] * (count + 4),
        [
            pltpu.VMEM((count, ns, part), F32),
            smem(blocks.shape, jnp.int32),
            smem(kept_counts.shape, jnp.int32),
            DMA(((count - 1) * heads + 3,)),
            DMA((count + 2,)),
        ],
        us=1.5,
    )(prefill_kv, prefill_state, queries, new_kv, blocks, kept_counts)
    sends = staged[: count - 1]
    own_state, kv_near, q_near, new_near, bias = staged[count - 1 :]
    far = after(sends[1:], *asked)
    received = [shift(far[c - 2], "seq", c) for c in range(2, count)]

    slope, base = call(
        functools.partial(coefficients, count, split),
        [shape((count, steps, ns, part), F32), shape((count, steps, 1, part), F32)],
        [HB] * 5,
        [VM] * 2,
        [
            pltpu.VMEM((steps, 1, channels), F32),
            pltpu.VMEM((steps, channels), BF),
            pltpu.VMEM(step_bc.shape, F32),
            pltpu.VMEM((1, channels), F32),
            pltpu.VMEM(a_log.shape, F32),
            DMA((5,)),
        ],
        us=2.0,
    )(step_dt, step_input, step_bc, skip_gain, a_log)

    partial_sums = call(
        functools.partial(attend, count),
        shape((chunks, 144, 128), BF),
        [VM] * (3 + count),
        VM,
        us=1.5,
    )(kv_near, new_near, bias, q_near, *asked)
    weight = call(load_weight, pltpu.VMEM(out_weight.shape, BF), [HB], VM, [DMA((8,))], us=3.4)(
        *after([out_weight], partial_sums)
    )
    gathered = [partial_sums] + [shift(partial_sums, "seq", c) for c in range(1, count)]
    half = heads * group * hd
    attn = call(
        functools.partial(merge, count, heads, steps, group),
        shape((steps * count, half), BF),
        [VM] * count,
        VM,
        [pltpu.VMEM((heads, steps * count * group, hd), F32)],
        us=0.3,
    )(*gathered)
    attn_other = shift(attn, "rep", 1)
    received = [shift(after(sends[:1], attn)[0], "seq", 1)] + received
    columns = out_weight.shape[1]
    own_sum = call(
        project_own, shape((steps * count, columns), F32), [VM, VM], VM, us=0.7
    )(attn, weight)
    share = count // heads_count
    sums = call(
        functools.partial(project_other, heads_count, count),
        [shape((steps, share, columns), F32)] * heads_count,
        [VM, VM, VM],
        [VM] * heads_count,
        us=0.7,
    )(own_sum, attn_other, weight)
    sums = [sums[0]] + [shift(sums[c], "head", c) for c in range(1, heads_count)]
    proj_out = call(
        add_up, shape((steps, share, columns), BF), [VM] * heads_count, VM, us=0.6
    )(*sums)

    received = after(received, proj_out)
    half_shape = (heads, keep_rep, BLOCK, width)
    kept, sent, mamba = call(
        functools.partial(select, count),
        [shape(half_shape, BF), shape(half_shape, BF), shape((steps, count, 1, part), F32)],
        [HB] * 3 + [VM] * (3 + count - 1),
        [VM] * 3,
        [
            smem(blocks.shape, jnp.int32),
            smem(kept_counts.shape, jnp.int32),
            pltpu.VMEM((BLOCK, width), BF),
            DMA((2, heads, keep_rep)),
            DMA((2,)),
        ],
        us=1.0,
    )(blocks, kept_counts, prefill_kv, own_state, slope, base, *received)
    got = shift(sent, "rep", 1)
    operands = [kept, got, mamba] + ([shift(mamba, "rep", 1)] if split else [])
    handoff, mamba_out = call(
        functools.partial(assemble, split),
        [
            shape((1, dec_heads, keep_rep, BLOCK, width), BF),
            shape((steps, 1, channels), F32),
        ],
        [VM] * len(operands),
        [HB] * 2,
        [DMA((2 + steps * count * (2 if split else 1),))],
        us=1.0,
    )(*operands)
    return handoff, proj_out, mamba_out


def solution(mesh):
    return jax.shard_map(
        per_device,
        mesh=mesh,
        in_specs=(
            P("groups", ("head", "rep"), "seq", None),
            P("groups", None, None),
            P("groups", None),
            P(None, ("groups", "seq"), "head", None),
            P(None, ("groups", "seq"), "head", None),
            P("head", ("seq", "rep")),
            P("groups", None, ("head", "seq")),
            P(None, "head"),
            P(None, ("groups", "seq"), "head"),
            P(None, ("groups", "seq"), "head"),
            P(None, ("groups", "seq"), None, None),
            P("head"),
        ),
        out_specs=(
            P(("groups", "seq"), "head", "rep", None, None),
            P(None, ("groups", "head"), ("seq", "rep")),
            P(None, ("groups", "seq"), "head"),
        ),
        check_vma=False,
    )
```

```python
import functools

import jax
import jax.numpy as jnp
from jax import lax
from jax.experimental import pallas as pl
from jax.experimental.pallas import tpu as pltpu
from jax.sharding import PartitionSpec as P

BLOCK = 128
PIECES = 4
NEG = -1e30
BF = jnp.bfloat16
F32 = jnp.float32
VM = pl.BlockSpec(memory_space=pltpu.VMEM)
HB = pl.BlockSpec(memory_space=pltpu.HBM)
DMA = pltpu.SemaphoreType.DMA


def shift(x, axis, c):
    size = lax.axis_size(axis)
    return lax.ppermute(x, axis, [(i, i ^ c) for i in range(size)])


def call(body, out_shape, in_specs, out_specs, scratch=(), us=1.0):
    return pl.pallas_call(
        body,
        out_shape=out_shape,
        in_specs=in_specs,
        out_specs=out_specs,
        scratch_shapes=list(scratch),
        cost_estimate=pl.CostEstimate(
            flops=0, bytes_accessed=int(us * 3.6e4), transcendentals=0
        ),
        compiler_params=pltpu.CompilerParams(vmem_limit_bytes=32 * 1024 * 1024),
    )


def in_hbm(x):
    return pltpu.with_memory_space_constraint(x, pltpu.HBM)


def after(arrays, *earlier):
    return lax.optimization_barrier((*arrays, *earlier))[: len(arrays)]


def run_all(copies):
    for copy in copies:
        copy.start()
    for copy in copies:
        copy.wait()


def copier(sems):
    position = iter(range(sems.shape[0]))
    return lambda src, dst: pltpu.make_async_copy(src, dst, sems.at[next(position)])


def state_rows(part):
    return 16 * pl.cdiv(part, 256)


def pack_state(piece, out_ref, first):
    ns, part = piece.shape
    for i in range(pl.cdiv(part, 256)):
        cut = piece[:, i * 256 : (i + 1) * 256]
        if cut.shape[1] < 256:
            cut = jnp.concatenate([cut, jnp.zeros((ns, 256 - cut.shape[1]), F32)], axis=1)
        out_ref[first + i * 16 : first + (i + 1) * 16, :] = cut.astype(BF)


def stage(count, split, kv_ref, state_ref, q_ref, new_ref, blocks_ref, counts_ref, weight_ref, *rest):
    sends = rest[: count - 1]
    own_state, kv_out, q_out, new_out, bias_out, weight_out = rest[count - 1 : count + 5]
    loaded, blocks, counts, sems, early = rest[count + 5 :]
    me, rep = lax.axis_index("seq"), lax.axis_index("rep")
    heads = kv_ref.shape[1]
    part = loaded.shape[2]
    copy = copier(early)
    first = [copy(blocks_ref, blocks), copy(counts_ref, counts)]
    for c in range(count):
        if split:
            src = state_ref.at[me ^ c, :, pl.ds(pl.multiple_of(rep * part, 128), part)]
        else:
            src = state_ref.at[me ^ c]
        first.append(copy(src, loaded.at[c]))
    copy = copier(sems)
    moves = []
    for c in range(1, count):
        for j in range(heads):
            rows = pl.ds(j * BLOCK, BLOCK)
            moves.append(copy(kv_ref.at[me ^ c, j], sends[c - 1].at[rows]))
    moves += [copy(kv_ref, kv_out), copy(q_ref, q_out), copy(new_ref, new_out)]
    moves += weight_half(weight_ref, weight_out, rep, copy)
    for move in first + moves:
        move.start()
    for move in first:
        move.wait()
    pack_state(loaded[0], own_state, 0)
    for c in range(1, count):
        pack_state(loaded[c], sends[c - 1], heads * BLOCK)
    head_first = lax.axis_index("head") * new_ref.shape[2] + rep * heads
    rows = bias_out.shape[0] // (count * heads)
    for c in range(count):
        for j in range(heads):
            live = jnp.int32(0)
            for slot in range(blocks.shape[1]):
                hit = blocks[me ^ c, slot, head_first + j] == me
                live = live | (hit & (slot < counts[me ^ c, head_first + j])).astype(jnp.int32)
            at = (c * heads + j) * rows
            dead = jnp.where(live > 0, 0.0, NEG).astype(F32)
            bias_out[at : at + rows, :] = jnp.full((rows, 128), dead, F32)
    for move in moves:
        move.wait()


def dot_f32(a, b, contract):
    return lax.dot_general(a, b, (contract, ((), ())), preferred_element_type=F32)


def attend(count, kv_ref, new_ref, bias_ref, *rest):
    q_refs, out_ref = rest[:1] + rest[1:count][::-1], rest[count]
    me, rep = lax.axis_index("seq"), lax.axis_index("rep")
    heads = kv_ref.shape[1]
    hd = kv_ref.shape[3] // 2
    steps, _, q_heads, _ = q_refs[0].shape
    own_q = q_heads // 2
    group = own_q // heads
    rows = steps * group
    scale = hd ** (-0.5)
    fresh = []
    for step in range(steps):
        both = new_ref[step, 0].astype(F32)
        fresh.append(jnp.where(rep == 0, both[:heads], both[heads:]))
    queries = []
    for c in range(count):
        q_all = [q_refs[c][step, 0].astype(F32) for step in range(steps)]
        q_all = [jnp.where(rep == 0, q[:own_q], q[own_q:]) for q in q_all]
        for j in range(heads):
            queries.append(
                jnp.concatenate([x[j * group : (j + 1) * group] for x in q_all], axis=0)
            )
    scores = []
    for c in range(count):
        for j in range(heads):
            keys = kv_ref[me ^ c, j, :, :hd]
            scores.append(dot_f32(queries[c * heads + j].astype(BF), keys, ((1,), (1,))))
    scores = jnp.concatenate(scores, axis=0)
    alive = bias_ref[...] == 0.0
    scores = jnp.where(alive, scores * scale, NEG)
    top = jnp.max(scores, axis=1, keepdims=True)
    own_rows = heads * rows
    own_q_rows = jnp.concatenate(queries[:heads], axis=0)
    row_step = (lax.broadcasted_iota(jnp.int32, (own_rows, 1), 0) // group) % steps
    own_top = top[:own_rows]
    dots = []
    for step in range(steps):
        wide = jnp.concatenate(
            [jnp.broadcast_to(fresh[step][j : j + 1, :hd], (rows, hd)) for j in range(heads)],
            axis=0,
        )
        dot = jnp.sum(own_q_rows * wide, axis=1, keepdims=True)
        dots.append(jnp.where(row_step >= step, dot * scale, NEG))
        own_top = jnp.maximum(own_top, dots[-1])
    top = jnp.concatenate([own_top, top[own_rows:]], axis=0)
    weights = jnp.where(alive, jnp.exp(scores - top), 0.0)
    total = jnp.sum(weights, axis=1, keepdims=True)
    weights = weights.astype(BF)
    summed = []
    for c in range(count):
        for j in range(heads):
            at = (c * heads + j) * rows
            values = kv_ref[me ^ c, j, :, hd:]
            summed.append(dot_f32(weights[at : at + rows], values, ((1,), (0,))))
    own_sum = jnp.concatenate(summed[:heads], axis=0)
    own_total = total[:own_rows]
    for step in range(steps):
        weight = jnp.where(row_step >= step, jnp.exp(dots[step] - own_top), 0.0)
        own_total = own_total + weight
        wide = jnp.concatenate(
            [jnp.broadcast_to(fresh[step][j : j + 1, hd:], (rows, hd)) for j in range(heads)],
            axis=0,
        )
        own_sum = own_sum + weight.astype(BF).astype(F32) * wide
    total = jnp.concatenate([own_total, total[own_rows:]], axis=0)
    summed = jnp.concatenate([own_sum] + summed[heads:], axis=0)
    chunks = out_ref.shape[0]
    line = lax.broadcasted_iota(jnp.int32, (16, 128), 0)
    for k in range(chunks):
        cut = slice(k * 128, (k + 1) * 128)
        out_ref[k, :128, :] = summed[cut].astype(BF)
        stats = jnp.zeros((16, 128), F32)
        for kind, column in ((0, top[cut]), (3, total[cut])):
            flat = jnp.transpose(jnp.broadcast_to(column, (128, 128)))[:16]
            high = flat.astype(BF).astype(F32)
            middle = (flat - high).astype(BF).astype(F32)
            low = flat - high - middle
            for at, piece in ((kind, high), (kind + 1, middle), (kind + 2, low)):
                stats = jnp.where(line == at, piece, stats)
        out_ref[k, 128:, :] = stats.astype(BF)


def merge(count, heads, steps, group, *rest):
    parts = rest[:1] + rest[1:count][::-1]
    out_ref, scratch = rest[count:]
    me = lax.axis_index("seq")
    rows = steps * group
    chunks = parts[0].shape[0]
    line = lax.broadcasted_iota(jnp.int32, (16, 128), 0)
    top_all, total_all = [], []
    for c in range(count):
        tops, totals = [], []
        for k in range(chunks):
            stats = parts[c][k, 128:, :].astype(F32)
            for kind, out in ((0, tops), (3, totals)):
                mine = (line >= kind) & (line < kind + 3)
                row = jnp.sum(jnp.where(mine, stats, 0.0), axis=0, keepdims=True)
                out.append(jnp.transpose(jnp.broadcast_to(row, (128, 128))))
        top_all.append(tops)
        total_all.append(totals)
    for e in range(count):
        for j in range(heads):
            places = [divmod(((e ^ c) * heads + j) * rows, 128) for c in range(count)]
            tops = [top_all[c][k][at : at + rows] for c, (k, at) in enumerate(places)]
            top = functools.reduce(jnp.maximum, tops)
            total = jnp.zeros_like(top)
            summed = jnp.zeros_like(top)
            for c, (k, at) in enumerate(places):
                weight = jnp.exp(tops[c] - top)
                total = total + weight * total_all[c][k][at : at + rows]
                summed = summed + weight * parts[c][k, at : at + rows, :].astype(F32)
            result = summed / total
            for step in range(steps):
                at = pl.multiple_of((step * count + (me ^ e)) * group, group)
                scratch[j, pl.ds(at, group), :] = result[step * group : (step + 1) * group]
    for j in range(heads):
        for g in range(group):
            at = (j * group + g) * 128
            tile = scratch[j, pl.ds(g, steps * count, stride=group), :]
            out_ref[:, at : at + 128] = tile.astype(BF)


def weight_half(weight_ref, out_ref, which, copy):
    half = out_ref.shape[0]
    rows = half // PIECES
    cuts = [(pl.ds(which * half + i * rows, rows), pl.ds(i * rows, rows)) for i in range(PIECES)]
    return [copy(weight_ref.at[src], out_ref.at[dst]) for src, dst in cuts]


def load_weight(weight_ref, out_ref, sems):
    run_all(weight_half(weight_ref, out_ref, 1 - lax.axis_index("rep"), copier(sems)))


def project_own(attn_ref, weight_ref, out_ref):
    out_ref[...] = dot_f32(attn_ref[...], weight_ref[...], ((1,), (0,)))


def pick(options, index):
    chosen = options[0]
    for i in range(1, len(options)):
        chosen = jnp.where(index == i, options[i], chosen)
    return chosen


def project_other(heads_count, count, acc_ref, attn_ref, weight_ref, *outs):
    total = acc_ref[...] + dot_f32(attn_ref[...], weight_ref[...], ((1,), (0,)))
    head = lax.axis_index("head")
    steps = total.shape[0] // count
    share = count // heads_count
    for step in range(steps):
        slices = [
            total[step * count + x * share : step * count + (x + 1) * share]
            for x in range(heads_count)
        ]
        for c in range(heads_count):
            outs[c][step] = pick(slices, head ^ c)


def add_up(*refs):
    total = refs[0][...]
    for ref in refs[1:-1]:
        total = total + ref[...]
    refs[-1][...] = total.astype(BF)


def coefficients(count, split, dt_hbm, x_hbm, bc_hbm, gain_hbm, log_hbm, slope_ref, base_ref,
                 dt_ref, x_ref, bc_ref, gain_ref, log_ref, sems):
    copy = copier(sems)
    run_all(
        [
            copy(dt_hbm, dt_ref),
            copy(x_hbm, x_ref),
            copy(bc_hbm, bc_ref),
            copy(gain_hbm, gain_ref),
            copy(log_hbm, log_ref),
        ]
    )
    me, rep = lax.axis_index("seq"), lax.axis_index("rep")
    _, steps, ns, part = slope_ref.shape
    block = part * 2 if split else part
    diagonal = lax.broadcasted_iota(jnp.int32, (ns, ns), 0) == lax.broadcasted_iota(
        jnp.int32, (ns, ns), 1
    )

    def column(row):
        return jnp.sum(jnp.where(diagonal, row, 0.0), axis=1, keepdims=True)

    drive = [column(bc_ref[step, 0, 0:1, :]) for step in range(steps)]
    read = [column(bc_ref[step, 0, 1:2, :]) for step in range(steps)]
    for c in range(count):
        first = (me ^ c) * block + (rep * part if split else 0)
        lanes = pl.ds(pl.multiple_of(first, 128), part)
        rate = -jnp.exp(log_ref[:, lanes])
        gain = gain_ref[:, lanes]
        kept = jnp.ones((ns, part), F32)
        added = jnp.zeros((ns, part), F32)
        for step in range(steps):
            dt = dt_ref[step, :, lanes]
            inputs = x_ref[step : step + 1, lanes].astype(F32)
            decay = jnp.exp(dt * rate)
            kept = kept * decay
            added = added * decay + drive[step] * (dt * inputs)
            slope_ref[c, step] = read[step] * kept
            base_ref[c, step] = (
                jnp.sum(read[step] * added, axis=0, keepdims=True) + gain * inputs
            )


def select(count, blocks_ref, counts_ref, kv_ref, state_ref, slope_ref, base_ref, *rest):
    received = rest[: count - 1]
    kept_ref, sent_ref, mamba_ref, blocks, counts, zeros, sems, early = rest[count - 1 :]
    me, rep = lax.axis_index("seq"), lax.axis_index("rep")
    heads, keep_rep = kept_ref.shape[:2]
    copy = copier(early)
    scalars = [copy(blocks_ref, blocks), copy(counts_ref, counts)]
    for move in scalars:
        move.start()
    zeros[...] = jnp.zeros_like(zeros)
    _, steps, ns, part = slope_ref.shape
    for c in range(count):
        source, first = (state_ref, 0) if c == 0 else (received[c - 1], heads * BLOCK)
        rows = [
            source[first + 16 * i : first + 16 * (i + 1), :].astype(F32)
            for i in range(pl.cdiv(part, 256))
        ]
        state = jnp.concatenate(rows, axis=1)[:, :part]
        for step in range(steps):
            mamba_ref[step, me ^ c] = base_ref[c, step] + jnp.sum(
                slope_ref[c, step] * state, axis=0, keepdims=True
            )
    for move in scalars:
        move.wait()
    head_first = lax.axis_index("head") * (2 * heads) + rep * heads
    for side, out in ((0, kept_ref), (1, sent_ref)):
        owner = rep if side == 0 else 1 - rep
        for j in range(heads):
            live_count = counts[me, head_first + j]
            for k in range(keep_rep):
                slot = owner * keep_rep + k
                source = blocks[me, slot, head_first + j] ^ me
                live = slot < live_count
                sem = sems.at[side, j, k]
                for c in range(count):
                    piece = kv_ref.at[me, j] if c == 0 else received[c - 1].at[pl.ds(j * BLOCK, BLOCK)]

                    @pl.when(live & (source == c))
                    def _():
                        pltpu.make_async_copy(piece, out.at[j, k], sem).start()

                @pl.when(jnp.logical_not(live))
                def _():
                    pltpu.make_async_copy(zeros, out.at[j, k], sem).start()

    for side, out in ((0, kept_ref), (1, sent_ref)):
        for j in range(heads):
            for k in range(keep_rep):
                pltpu.make_async_copy(zeros, out.at[j, k], sems.at[side, j, k]).wait()


def assemble(split, kept_ref, got_ref, mamba_ref, *rest):
    rep = lax.axis_index("rep")
    if split:
        other_ref, handoff_ref, out_ref, sems = rest
    else:
        handoff_ref, out_ref, sems = rest
    heads = kept_ref.shape[0]
    copy = copier(sems)
    moves = [
        copy(kept_ref, handoff_ref.at[0, pl.ds(rep * heads, heads)]),
        copy(got_ref, handoff_ref.at[0, pl.ds((1 - rep) * heads, heads)]),
    ]
    steps, count, _, part = mamba_ref.shape
    for step in range(steps):
        for b in range(count):
            if split:
                for ref, side in ((mamba_ref, rep), (other_ref, 1 - rep)):
                    lanes = pl.ds(pl.multiple_of((2 * b + side) * part, 128), part)
                    moves.append(copy(ref.at[step, b], out_ref.at[step, :, lanes]))
            else:
                moves.append(copy(mamba_ref.at[step, b], out_ref.at[step, :, pl.ds(b * part, part)]))
    run_all(moves)


def per_device(
    prefill_kv,
    kept_blocks,
    kept_counts,
    queries,
    new_kv,
    out_weight,
    prefill_state,
    a_log,
    step_input,
    step_dt,
    step_bc,
    skip_gain,
):
    count = lax.axis_size("seq")
    reps = lax.axis_size("rep")
    heads_count = lax.axis_size("head")
    requests, heads, tokens, width = prefill_kv.shape
    assert requests == count and tokens == BLOCK and reps == 2 and width == 256
    assert count & (count - 1) == 0 and heads_count & (heads_count - 1) == 0
    keep = kept_blocks.shape[2]
    keep_rep = keep // reps
    steps, _, q_heads, hd = queries.shape
    dec_heads = new_kv.shape[2]
    group = q_heads // dec_heads
    _, ns, block = prefill_state.shape
    split = block % (reps * 128) == 0
    part = block // reps if split else block
    all_rows = count * heads * steps * group
    chunks = all_rows // 128
    channels = count * block
    shape = jax.ShapeDtypeStruct
    smem = pltpu.SMEM
    blocks = jnp.swapaxes(kept_blocks, 1, 2)

    asked = [shift(queries, "seq", c) for c in range(count - 1, 0, -1)][::-1]
    prefill_kv, prefill_state, queries, new_kv = map(in_hbm, (prefill_kv, prefill_state, queries, new_kv))
    step_dt, step_bc, a_log, out_weight = map(in_hbm, (step_dt, step_bc, a_log, out_weight))
    step_input = in_hbm(step_input.reshape(steps, channels))
    skip_gain = in_hbm(skip_gain.reshape(1, -1))
    blocks, kept_counts = in_hbm(blocks), in_hbm(kept_counts)

    columns = out_weight.shape[1]
    half = heads * group * hd
    half_weight = pltpu.VMEM((half, columns), BF)
    packed = heads * BLOCK + state_rows(part)
    staged = call(
        functools.partial(stage, count, split),
        [shape((packed, width), BF)] * (count - 1)
        + [
            shape((state_rows(part), width), BF),
            shape(prefill_kv.shape, BF),
            shape(queries.shape, BF),
            shape(new_kv.shape, BF),
            shape((all_rows, 128), F32),
            half_weight,
        ],
        [HB] * 7,
        [VM] * (count + 5),
        [
            pltpu.VMEM((count, ns, part), F32),
            smem(blocks.shape, jnp.int32),
            smem(kept_counts.shape, jnp.int32),
            DMA(((count - 1) * heads + 3 + PIECES,)),
            DMA((count + 2,)),
        ],
        us=1.5,
    )(prefill_kv, prefill_state, queries, new_kv, blocks, kept_counts, out_weight)
    sends = staged[: count - 1]
    own_state, kv_near, q_near, new_near, bias, own_weight = staged[count - 1 :]
    early = shift(after(sends[-1:], *asked)[0], "seq", count - 1)

    slope, base = call(
        functools.partial(coefficients, count, split),
        [shape((count, steps, ns, part), F32), shape((count, steps, 1, part), F32)],
        [HB] * 5,
        [VM] * 2,
        [
            pltpu.VMEM((steps, 1, channels), F32),
            pltpu.VMEM((steps, channels), BF),
            pltpu.VMEM(step_bc.shape, F32),
            pltpu.VMEM((1, channels), F32),
            pltpu.VMEM(a_log.shape, F32),
            DMA((5,)),
        ],
        us=2.0,
    )(step_dt, step_input, step_bc, skip_gain, a_log)

    partial_sums = call(
        functools.partial(attend, count),
        shape((chunks, 144, 128), BF),
        [VM] * (3 + count),
        VM,
        us=1.5,
    )(kv_near, new_near, bias, q_near, *asked[::-1])
    other_weight = call(load_weight, half_weight, [HB], VM, [DMA((PIECES,))], us=1.7)(
        *after([out_weight], partial_sums)
    )
    middle = after(sends[1:-1], partial_sums)
    middle = [shift(middle[c - 2], "seq", c) for c in range(count - 2, 1, -1)][::-1]
    gathered = [partial_sums] + [shift(partial_sums, "seq", c) for c in range(count - 1, 0, -1)][::-1]
    *gathered, early, other_weight = after([*gathered[::-1], early, other_weight])
    gathered = gathered[::-1]
    attn = call(
        functools.partial(merge, count, heads, steps, group),
        shape((steps * count, half), BF),
        [VM] * count,
        VM,
        [pltpu.VMEM((heads, steps * count * group, hd), F32)],
        us=0.3,
    )(*gathered[:1], *gathered[:0:-1])
    attn_other = shift(attn, "rep", 1)
    received = [shift(after(sends[:1], attn)[0], "seq", 1), *middle, early]
    own_sum = call(
        project_own, shape((steps * count, columns), F32), [VM, VM], VM, us=0.7
    )(attn, own_weight)
    share = count // heads_count
    sums = call(
        functools.partial(project_other, heads_count, count),
        [shape((steps, share, columns), F32)] * heads_count,
        [VM, VM, VM],
        [VM] * heads_count,
        us=0.7,
    )(own_sum, attn_other, other_weight)
    sums = [sums[0]] + [shift(sums[c], "head", c) for c in range(1, heads_count)]
    proj_out = call(
        add_up, shape((steps, share, columns), BF), [VM] * heads_count, VM, us=0.6
    )(*sums)

    received = after(received, proj_out)
    half_shape = (heads, keep_rep, BLOCK, width)
    kept, sent, mamba = call(
        functools.partial(select, count),
        [shape(half_shape, BF), shape(half_shape, BF), shape((steps, count, 1, part), F32)],
        [HB] * 3 + [VM] * (3 + count - 1),
        [VM] * 3,
        [
            smem(blocks.shape, jnp.int32),
            smem(kept_counts.shape, jnp.int32),
            pltpu.VMEM((BLOCK, width), BF),
            DMA((2, heads, keep_rep)),
            DMA((2,)),
        ],
        us=1.0,
    )(blocks, kept_counts, prefill_kv, own_state, slope, base, *received)
    got = shift(sent, "rep", 1)
    operands = [kept, got, mamba] + ([shift(mamba, "rep", 1)] if split else [])
    handoff, mamba_out = call(
        functools.partial(assemble, split),
        [
            shape((1, dec_heads, keep_rep, BLOCK, width), BF),
            shape((steps, 1, channels), F32),
        ],
        [VM] * len(operands),
        [HB] * 2,
        [DMA((2 + steps * count * (2 if split else 1),))],
        us=1.0,
    )(*operands)
    return handoff, proj_out, mamba_out


def solution(mesh):
    return jax.shard_map(
        per_device,
        mesh=mesh,
        in_specs=(
            P("groups", ("head", "rep"), "seq", None),
            P("groups", None, None),
            P("groups", None),
            P(None, ("groups", "seq"), "head", None),
            P(None, ("groups", "seq"), "head", None),
            P("head", ("seq", "rep")),
            P("groups", None, ("head", "seq")),
            P(None, "head"),
            P(None, ("groups", "seq"), "head"),
            P(None, ("groups", "seq"), "head"),
            P(None, ("groups", "seq"), None, None),
            P("head"),
        ),
        out_specs=(
            P(("groups", "seq"), "head", "rep", None, None),
            P(None, ("groups", "head"), ("seq", "rep")),
            P(None, ("groups", "seq"), "head"),
        ),
        check_vma=False,
    )
```

```python
import functools

import jax
import jax.numpy as jnp
from jax import lax
from jax.experimental import pallas as pl
from jax.experimental.pallas import tpu as pltpu
from jax.sharding import PartitionSpec as P

BLOCK = 128
PIECES = 4
NEG = -1e30
BF = jnp.bfloat16
F32 = jnp.float32
VM = pl.BlockSpec(memory_space=pltpu.VMEM)
HB = pl.BlockSpec(memory_space=pltpu.HBM)
DMA = pltpu.SemaphoreType.DMA


def shift(x, axis, c):
    size = lax.axis_size(axis)
    return lax.ppermute(x, axis, [(i, i ^ c) for i in range(size)])


def call(body, out_shape, in_specs, out_specs, scratch=(), us=1.0):
    return pl.pallas_call(
        body,
        out_shape=out_shape,
        in_specs=in_specs,
        out_specs=out_specs,
        scratch_shapes=list(scratch),
        cost_estimate=pl.CostEstimate(
            flops=0, bytes_accessed=int(us * 3.6e4), transcendentals=0
        ),
        compiler_params=pltpu.CompilerParams(vmem_limit_bytes=32 * 1024 * 1024),
    )


def in_hbm(x):
    return pltpu.with_memory_space_constraint(x, pltpu.HBM)


def after(arrays, *earlier):
    return lax.optimization_barrier((*arrays, *earlier))[: len(arrays)]


def run_all(copies):
    for copy in copies:
        copy.start()
    for copy in copies:
        copy.wait()


def copier(sems):
    position = iter(range(sems.shape[0]))
    return lambda src, dst: pltpu.make_async_copy(src, dst, sems.at[next(position)])


def state_rows(part):
    return 16 * pl.cdiv(part, 256)


def pack_state(piece, out_ref, first):
    ns, part = piece.shape
    for i in range(pl.cdiv(part, 256)):
        cut = piece[:, i * 256 : (i + 1) * 256]
        if cut.shape[1] < 256:
            cut = jnp.concatenate([cut, jnp.zeros((ns, 256 - cut.shape[1]), F32)], axis=1)
        out_ref[first + i * 16 : first + (i + 1) * 16, :] = cut.astype(BF)


def stage(count, split, kv_ref, state_ref, q_ref, new_ref, blocks_ref, counts_ref, *rest):
    sends = rest[: count - 1]
    own_state, kv_out, q_out, new_out, bias_out = rest[count - 1 : count + 4]
    loaded, blocks, counts, sems, early = rest[count + 4 :]
    me, rep = lax.axis_index("seq"), lax.axis_index("rep")
    heads = kv_ref.shape[1]
    part = loaded.shape[2]
    copy = copier(early)
    first = [copy(blocks_ref, blocks), copy(counts_ref, counts)]
    for c in range(count):
        if split:
            src = state_ref.at[me ^ c, :, pl.ds(pl.multiple_of(rep * part, 128), part)]
        else:
            src = state_ref.at[me ^ c]
        first.append(copy(src, loaded.at[c]))
    copy = copier(sems)
    moves = []
    for c in range(1, count):
        for j in range(heads):
            rows = pl.ds(j * BLOCK, BLOCK)
            moves.append(copy(kv_ref.at[me ^ c, j], sends[c - 1].at[rows]))
    moves += [copy(kv_ref, kv_out), copy(q_ref, q_out), copy(new_ref, new_out)]
    for move in first + moves:
        move.start()
    for move in first:
        move.wait()
    pack_state(loaded[0], own_state, 0)
    for c in range(1, count):
        pack_state(loaded[c], sends[c - 1], heads * BLOCK)
    head_first = lax.axis_index("head") * new_ref.shape[2] + rep * heads
    rows = bias_out.shape[0] // (count * heads)
    for c in range(count):
        for j in range(heads):
            live = jnp.int32(0)
            for slot in range(blocks.shape[1]):
                hit = blocks[me ^ c, slot, head_first + j] == me
                live = live | (hit & (slot < counts[me ^ c, head_first + j])).astype(jnp.int32)
            at = (c * heads + j) * rows
            dead = jnp.where(live > 0, 0.0, NEG).astype(F32)
            bias_out[at : at + rows, :] = jnp.full((rows, 128), dead, F32)
    for move in moves:
        move.wait()


def dot_f32(a, b, contract):
    return lax.dot_general(a, b, (contract, ((), ())), preferred_element_type=F32)


def attend(count, kv_ref, new_ref, bias_ref, *rest):
    q_refs, out_ref = rest[:1] + rest[1:count][::-1], rest[count]
    me, rep = lax.axis_index("seq"), lax.axis_index("rep")
    heads = kv_ref.shape[1]
    hd = kv_ref.shape[3] // 2
    steps, _, q_heads, _ = q_refs[0].shape
    own_q = q_heads // 2
    group = own_q // heads
    rows = steps * group
    scale = hd ** (-0.5)
    fresh = []
    for step in range(steps):
        both = new_ref[step, 0].astype(F32)
        fresh.append(jnp.where(rep == 0, both[:heads], both[heads:]))
    queries = []
    for c in range(count):
        q_all = [q_refs[c][step, 0].astype(F32) for step in range(steps)]
        q_all = [jnp.where(rep == 0, q[:own_q], q[own_q:]) for q in q_all]
        for j in range(heads):
            queries.append(
                jnp.concatenate([x[j * group : (j + 1) * group] for x in q_all], axis=0)
            )
    scores = []
    for c in range(count):
        for j in range(heads):
            keys = kv_ref[me ^ c, j, :, :hd]
            scores.append(dot_f32(queries[c * heads + j].astype(BF), keys, ((1,), (1,))))
    scores = jnp.concatenate(scores, axis=0)
    alive = bias_ref[...] == 0.0
    scores = jnp.where(alive, scores * scale, NEG)
    top = jnp.max(scores, axis=1, keepdims=True)
    own_rows = heads * rows
    own_q_rows = jnp.concatenate(queries[:heads], axis=0)
    row_step = (lax.broadcasted_iota(jnp.int32, (own_rows, 1), 0) // group) % steps
    own_top = top[:own_rows]
    dots = []
    for step in range(steps):
        wide = jnp.concatenate(
            [jnp.broadcast_to(fresh[step][j : j + 1, :hd], (rows, hd)) for j in range(heads)],
            axis=0,
        )
        dot = jnp.sum(own_q_rows * wide, axis=1, keepdims=True)
        dots.append(jnp.where(row_step >= step, dot * scale, NEG))
        own_top = jnp.maximum(own_top, dots[-1])
    top = jnp.concatenate([own_top, top[own_rows:]], axis=0)
    weights = jnp.where(alive, jnp.exp(scores - top), 0.0)
    total = jnp.sum(weights, axis=1, keepdims=True)
    weights = weights.astype(BF)
    summed = []
    for c in range(count):
        for j in range(heads):
            at = (c * heads + j) * rows
            values = kv_ref[me ^ c, j, :, hd:]
            summed.append(dot_f32(weights[at : at + rows], values, ((1,), (0,))))
    own_sum = jnp.concatenate(summed[:heads], axis=0)
    own_total = total[:own_rows]
    for step in range(steps):
        weight = jnp.where(row_step >= step, jnp.exp(dots[step] - own_top), 0.0)
        own_total = own_total + weight
        wide = jnp.concatenate(
            [jnp.broadcast_to(fresh[step][j : j + 1, hd:], (rows, hd)) for j in range(heads)],
            axis=0,
        )
        own_sum = own_sum + weight.astype(BF).astype(F32) * wide
    total = jnp.concatenate([own_total, total[own_rows:]], axis=0)
    summed = jnp.concatenate([own_sum] + summed[heads:], axis=0)
    chunks = out_ref.shape[0]
    line = lax.broadcasted_iota(jnp.int32, (16, 128), 0)
    for k in range(chunks):
        cut = slice(k * 128, (k + 1) * 128)
        out_ref[k, :128, :] = summed[cut].astype(BF)
        stats = jnp.zeros((16, 128), F32)
        for kind, column in ((0, top[cut]), (3, total[cut])):
            flat = jnp.transpose(jnp.broadcast_to(column, (128, 128)))[:16]
            high = flat.astype(BF).astype(F32)
            middle = (flat - high).astype(BF).astype(F32)
            low = flat - high - middle
            for at, piece in ((kind, high), (kind + 1, middle), (kind + 2, low)):
                stats = jnp.where(line == at, piece, stats)
        out_ref[k, 128:, :] = stats.astype(BF)


def merge(count, heads, steps, group, *rest):
    parts = rest[:1] + rest[1:count][::-1]
    out_ref, scratch = rest[count:]
    me = lax.axis_index("seq")
    rows = steps * group
    chunks = parts[0].shape[0]
    line = lax.broadcasted_iota(jnp.int32, (16, 128), 0)
    top_all, total_all = [], []
    for c in range(count):
        tops, totals = [], []
        for k in range(chunks):
            stats = parts[c][k, 128:, :].astype(F32)
            for kind, out in ((0, tops), (3, totals)):
                mine = (line >= kind) & (line < kind + 3)
                row = jnp.sum(jnp.where(mine, stats, 0.0), axis=0, keepdims=True)
                out.append(jnp.transpose(jnp.broadcast_to(row, (128, 128))))
        top_all.append(tops)
        total_all.append(totals)
    for e in range(count):
        for j in range(heads):
            places = [divmod(((e ^ c) * heads + j) * rows, 128) for c in range(count)]
            tops = [top_all[c][k][at : at + rows] for c, (k, at) in enumerate(places)]
            top = functools.reduce(jnp.maximum, tops)
            total = jnp.zeros_like(top)
            summed = jnp.zeros_like(top)
            for c, (k, at) in enumerate(places):
                weight = jnp.exp(tops[c] - top)
                total = total + weight * total_all[c][k][at : at + rows]
                summed = summed + weight * parts[c][k, at : at + rows, :].astype(F32)
            result = summed / total
            for step in range(steps):
                at = pl.multiple_of((step * count + (me ^ e)) * group, group)
                scratch[j, pl.ds(at, group), :] = result[step * group : (step + 1) * group]
    for j in range(heads):
        for g in range(group):
            at = (j * group + g) * 128
            tile = scratch[j, pl.ds(g, steps * count, stride=group), :]
            out_ref[:, at : at + 128] = tile.astype(BF)


def weight_half(weight_ref, out_ref, which, copy):
    half = out_ref.shape[0]
    rows = half // PIECES
    cuts = [(pl.ds(which * half + i * rows, rows), pl.ds(i * rows, rows)) for i in range(PIECES)]
    return [copy(weight_ref.at[src], out_ref.at[dst]) for src, dst in cuts]


def project_own(attn_ref, weight_ref, out_ref):
    out_ref[...] = dot_f32(attn_ref[...], weight_ref[...], ((1,), (0,)))


def pick(options, index):
    chosen = options[0]
    for i in range(1, len(options)):
        chosen = jnp.where(index == i, options[i], chosen)
    return chosen


def project_other(heads_count, count, acc_ref, attn_ref, weight_ref, *outs):
    total = acc_ref[...] + dot_f32(attn_ref[...], weight_ref[...], ((1,), (0,)))
    head = lax.axis_index("head")
    steps = total.shape[0] // count
    share = count // heads_count
    for step in range(steps):
        slices = [
            total[step * count + x * share : step * count + (x + 1) * share]
            for x in range(heads_count)
        ]
        for c in range(heads_count):
            outs[c][step] = pick(slices, head ^ c)


def add_up(*refs):
    total = refs[0][...]
    for ref in refs[1:-1]:
        total = total + ref[...]
    refs[-1][...] = total.astype(BF)


def prepare(count, split, weight_hbm, dt_hbm, x_hbm, bc_hbm, gain_hbm, log_hbm, own_ref, other_ref,
            slope_ref, base_ref, dt_ref, x_ref, bc_ref, gain_ref, log_ref, sems, weight_sems):
    copy = copier(sems)
    first = [
        copy(dt_hbm, dt_ref),
        copy(x_hbm, x_ref),
        copy(bc_hbm, bc_ref),
        copy(gain_hbm, gain_ref),
        copy(log_hbm, log_ref),
    ]
    copy = copier(weight_sems)
    which = lax.axis_index("rep")
    weights = weight_half(weight_hbm, own_ref, which, copy)
    weights += weight_half(weight_hbm, other_ref, 1 - which, copy)
    for move in first + weights:
        move.start()
    for move in first:
        move.wait()
    me, rep = lax.axis_index("seq"), lax.axis_index("rep")
    _, steps, ns, part = slope_ref.shape
    block = part * 2 if split else part
    diagonal = lax.broadcasted_iota(jnp.int32, (ns, ns), 0) == lax.broadcasted_iota(
        jnp.int32, (ns, ns), 1
    )

    def column(row):
        return jnp.sum(jnp.where(diagonal, row, 0.0), axis=1, keepdims=True)

    drive = [column(bc_ref[step, 0, 0:1, :]) for step in range(steps)]
    read = [column(bc_ref[step, 0, 1:2, :]) for step in range(steps)]
    for c in range(count):
        first = (me ^ c) * block + (rep * part if split else 0)
        lanes = pl.ds(pl.multiple_of(first, 128), part)
        rate = -jnp.exp(log_ref[:, lanes])
        gain = gain_ref[:, lanes]
        kept = jnp.ones((ns, part), F32)
        added = jnp.zeros((ns, part), F32)
        for step in range(steps):
            dt = dt_ref[step, :, lanes]
            inputs = x_ref[step : step + 1, lanes].astype(F32)
            decay = jnp.exp(dt * rate)
            kept = kept * decay
            added = added * decay + drive[step] * (dt * inputs)
            slope_ref[c, step] = read[step] * kept
            base_ref[c, step] = (
                jnp.sum(read[step] * added, axis=0, keepdims=True) + gain * inputs
            )
    for move in weights:
        move.wait()


def select(count, blocks_ref, counts_ref, kv_ref, state_ref, slope_ref, base_ref, *rest):
    received = rest[: count - 1]
    kept_ref, sent_ref, mamba_ref, blocks, counts, zeros, sems, early = rest[count - 1 :]
    me, rep = lax.axis_index("seq"), lax.axis_index("rep")
    heads, keep_rep = kept_ref.shape[:2]
    copy = copier(early)
    scalars = [copy(blocks_ref, blocks), copy(counts_ref, counts)]
    for move in scalars:
        move.start()
    zeros[...] = jnp.zeros_like(zeros)
    _, steps, ns, part = slope_ref.shape
    for c in range(count):
        source, first = (state_ref, 0) if c == 0 else (received[c - 1], heads * BLOCK)
        rows = [
            source[first + 16 * i : first + 16 * (i + 1), :].astype(F32)
            for i in range(pl.cdiv(part, 256))
        ]
        state = jnp.concatenate(rows, axis=1)[:, :part]
        for step in range(steps):
            mamba_ref[step, me ^ c] = base_ref[c, step] + jnp.sum(
                slope_ref[c, step] * state, axis=0, keepdims=True
            )
    for move in scalars:
        move.wait()
    head_first = lax.axis_index("head") * (2 * heads) + rep * heads
    for side, out in ((0, kept_ref), (1, sent_ref)):
        owner = rep if side == 0 else 1 - rep
        for j in range(heads):
            live_count = counts[me, head_first + j]
            for k in range(keep_rep):
                slot = owner * keep_rep + k
                source = blocks[me, slot, head_first + j] ^ me
                live = slot < live_count
                sem = sems.at[side, j, k]
                for c in range(count):
                    piece = kv_ref.at[me, j] if c == 0 else received[c - 1].at[pl.ds(j * BLOCK, BLOCK)]

                    @pl.when(live & (source == c))
                    def _():
                        pltpu.make_async_copy(piece, out.at[j, k], sem).start()

                @pl.when(jnp.logical_not(live))
                def _():
                    pltpu.make_async_copy(zeros, out.at[j, k], sem).start()

    for side, out in ((0, kept_ref), (1, sent_ref)):
        for j in range(heads):
            for k in range(keep_rep):
                pltpu.make_async_copy(zeros, out.at[j, k], sems.at[side, j, k]).wait()


def assemble(split, kept_ref, got_ref, mamba_ref, *rest):
    rep = lax.axis_index("rep")
    if split:
        other_ref, handoff_ref, out_ref, sems = rest
    else:
        handoff_ref, out_ref, sems = rest
    heads = kept_ref.shape[0]
    copy = copier(sems)
    moves = [
        copy(kept_ref, handoff_ref.at[0, pl.ds(rep * heads, heads)]),
        copy(got_ref, handoff_ref.at[0, pl.ds((1 - rep) * heads, heads)]),
    ]
    steps, count, _, part = mamba_ref.shape
    for step in range(steps):
        for b in range(count):
            if split:
                for ref, side in ((mamba_ref, rep), (other_ref, 1 - rep)):
                    lanes = pl.ds(pl.multiple_of((2 * b + side) * part, 128), part)
                    moves.append(copy(ref.at[step, b], out_ref.at[step, :, lanes]))
            else:
                moves.append(copy(mamba_ref.at[step, b], out_ref.at[step, :, pl.ds(b * part, part)]))
    run_all(moves)


def per_device(
    prefill_kv,
    kept_blocks,
    kept_counts,
    queries,
    new_kv,
    out_weight,
    prefill_state,
    a_log,
    step_input,
    step_dt,
    step_bc,
    skip_gain,
):
    count = lax.axis_size("seq")
    reps = lax.axis_size("rep")
    heads_count = lax.axis_size("head")
    requests, heads, tokens, width = prefill_kv.shape
    assert requests == count and tokens == BLOCK and reps == 2 and width == 256
    assert count & (count - 1) == 0 and heads_count & (heads_count - 1) == 0
    keep = kept_blocks.shape[2]
    keep_rep = keep // reps
    steps, _, q_heads, hd = queries.shape
    dec_heads = new_kv.shape[2]
    group = q_heads // dec_heads
    _, ns, block = prefill_state.shape
    split = block % (reps * 128) == 0
    part = block // reps if split else block
    all_rows = count * heads * steps * group
    chunks = all_rows // 128
    channels = count * block
    shape = jax.ShapeDtypeStruct
    smem = pltpu.SMEM
    blocks = jnp.swapaxes(kept_blocks, 1, 2)

    asked = [shift(queries, "seq", c) for c in range(count - 1, 0, -1)][::-1]
    prefill_kv, prefill_state, queries, new_kv = map(in_hbm, (prefill_kv, prefill_state, queries, new_kv))
    step_dt, step_bc, a_log, out_weight = map(in_hbm, (step_dt, step_bc, a_log, out_weight))
    step_input = in_hbm(step_input.reshape(steps, channels))
    skip_gain = in_hbm(skip_gain.reshape(1, -1))
    blocks, kept_counts = in_hbm(blocks), in_hbm(kept_counts)

    columns = out_weight.shape[1]
    half = heads * group * hd
    half_weight = pltpu.VMEM((half, columns), BF)
    packed = heads * BLOCK + state_rows(part)
    staged = call(
        functools.partial(stage, count, split),
        [shape((packed, width), BF)] * (count - 1)
        + [
            shape((state_rows(part), width), BF),
            shape(prefill_kv.shape, BF),
            shape(queries.shape, BF),
            shape(new_kv.shape, BF),
            shape((all_rows, 128), F32),
        ],
        [HB] * 6,
        [VM] * (count + 4),
        [
            pltpu.VMEM((count, ns, part), F32),
            smem(blocks.shape, jnp.int32),
            smem(kept_counts.shape, jnp.int32),
            DMA(((count - 1) * heads + 3,)),
            DMA((count + 2,)),
        ],
        us=1.5,
    )(prefill_kv, prefill_state, queries, new_kv, blocks, kept_counts)
    sends = staged[: count - 1]
    own_state, kv_near, q_near, new_near, bias = staged[count - 1 :]
    far = after(sends[1:], *asked)
    far = [shift(far[c - 2], "seq", c) for c in range(count - 1, 1, -1)][::-1]

    partial_sums = call(
        functools.partial(attend, count),
        shape((chunks, 144, 128), BF),
        [VM] * (3 + count),
        VM,
        us=1.5,
    )(kv_near, new_near, bias, q_near, *asked[::-1])
    own_weight, other_weight, slope, base = call(
        functools.partial(prepare, count, split),
        [
            half_weight,
            half_weight,
            shape((count, steps, ns, part), F32),
            shape((count, steps, 1, part), F32),
        ],
        [HB] * 6,
        [VM] * 4,
        [
            pltpu.VMEM((steps, 1, channels), F32),
            pltpu.VMEM((steps, channels), BF),
            pltpu.VMEM(step_bc.shape, F32),
            pltpu.VMEM((1, channels), F32),
            pltpu.VMEM(a_log.shape, F32),
            DMA((5,)),
            DMA((2 * PIECES,)),
        ],
        us=3.6,
    )(*after([out_weight], partial_sums), step_dt, step_input, step_bc, skip_gain, a_log)
    gathered = [partial_sums] + [shift(partial_sums, "seq", c) for c in range(count - 1, 0, -1)][::-1]
    joint = after([*gathered, *far, other_weight])
    gathered, far, other_weight = joint[:count], joint[count:-1], joint[-1]
    attn = call(
        functools.partial(merge, count, heads, steps, group),
        shape((steps * count, half), BF),
        [VM] * count,
        VM,
        [pltpu.VMEM((heads, steps * count * group, hd), F32)],
        us=0.3,
    )(*gathered[:1], *gathered[:0:-1])
    attn_other = shift(attn, "rep", 1)
    received = [shift(after(sends[:1], attn)[0], "seq", 1), *far]
    own_sum = call(
        project_own, shape((steps * count, columns), F32), [VM, VM], VM, us=0.7
    )(attn, own_weight)
    share = count // heads_count
    sums = call(
        functools.partial(project_other, heads_count, count),
        [shape((steps, share, columns), F32)] * heads_count,
        [VM, VM, VM],
        [VM] * heads_count,
        us=0.7,
    )(own_sum, attn_other, other_weight)
    sums = [sums[0]] + [shift(sums[c], "head", c) for c in range(1, heads_count)]
    received = after(received, sums[0])
    half_shape = (heads, keep_rep, BLOCK, width)
    kept, sent, mamba = call(
        functools.partial(select, count),
        [shape(half_shape, BF), shape(half_shape, BF), shape((steps, count, 1, part), F32)],
        [HB] * 3 + [VM] * (3 + count - 1),
        [VM] * 3,
        [
            smem(blocks.shape, jnp.int32),
            smem(kept_counts.shape, jnp.int32),
            pltpu.VMEM((BLOCK, width), BF),
            DMA((2, heads, keep_rep)),
            DMA((2,)),
        ],
        us=1.0,
    )(blocks, kept_counts, prefill_kv, own_state, slope, base, *received)
    got = shift(sent, "rep", 1)
    sums[1:] = after(sums[1:], kept)
    proj_out = call(
        add_up, shape((steps, share, columns), BF), [VM] * heads_count, VM, us=0.6
    )(*sums)

    operands = [kept, got, mamba] + ([shift(mamba, "rep", 1)] if split else [])
    handoff, mamba_out = call(
        functools.partial(assemble, split),
        [
            shape((1, dec_heads, keep_rep, BLOCK, width), BF),
            shape((steps, 1, channels), F32),
        ],
        [VM] * len(operands),
        [HB] * 2,
        [DMA((2 + steps * count * (2 if split else 1),))],
        us=1.0,
    )(*operands)
    return handoff, proj_out, mamba_out


def solution(mesh):
    return jax.shard_map(
        per_device,
        mesh=mesh,
        in_specs=(
            P("groups", ("head", "rep"), "seq", None),
            P("groups", None, None),
            P("groups", None),
            P(None, ("groups", "seq"), "head", None),
            P(None, ("groups", "seq"), "head", None),
            P("head", ("seq", "rep")),
            P("groups", None, ("head", "seq")),
            P(None, "head"),
            P(None, ("groups", "seq"), "head"),
            P(None, ("groups", "seq"), "head"),
            P(None, ("groups", "seq"), None, None),
            P("head"),
        ),
        out_specs=(
            P(("groups", "seq"), "head", "rep", None, None),
            P(None, ("groups", "head"), ("seq", "rep")),
            P(None, ("groups", "seq"), "head"),
        ),
        check_vma=False,
    )
```

```python
import functools

import jax
import jax.numpy as jnp
from jax import lax
from jax.experimental import pallas as pl
from jax.experimental.pallas import tpu as pltpu
from jax.sharding import PartitionSpec as P

BLOCK = 128
PIECES = 4
NEG = -1e30
BF = jnp.bfloat16
F32 = jnp.float32
VM = pl.BlockSpec(memory_space=pltpu.VMEM)
HB = pl.BlockSpec(memory_space=pltpu.HBM)
DMA = pltpu.SemaphoreType.DMA


def shift(x, axis, c):
    size = lax.axis_size(axis)
    return lax.ppermute(x, axis, [(i, i ^ c) for i in range(size)])


def call(body, out_shape, in_specs, out_specs, scratch=(), us=1.0):
    return pl.pallas_call(
        body,
        out_shape=out_shape,
        in_specs=in_specs,
        out_specs=out_specs,
        scratch_shapes=list(scratch),
        cost_estimate=pl.CostEstimate(
            flops=0, bytes_accessed=int(us * 3.6e4), transcendentals=0
        ),
        compiler_params=pltpu.CompilerParams(vmem_limit_bytes=32 * 1024 * 1024),
    )


def in_hbm(x):
    return pltpu.with_memory_space_constraint(x, pltpu.HBM)


def after(arrays, *earlier):
    return lax.optimization_barrier((*arrays, *earlier))[: len(arrays)]


def run_all(copies):
    for copy in copies:
        copy.start()
    for copy in copies:
        copy.wait()


def copier(sems):
    position = iter(range(sems.shape[0]))
    return lambda src, dst: pltpu.make_async_copy(src, dst, sems.at[next(position)])


def state_rows(part):
    return 16 * pl.cdiv(part, 256)


def pack_state(piece, out_ref, first):
    ns, part = piece.shape
    for i in range(pl.cdiv(part, 256)):
        cut = piece[:, i * 256 : (i + 1) * 256]
        if cut.shape[1] < 256:
            cut = jnp.concatenate([cut, jnp.zeros((ns, 256 - cut.shape[1]), F32)], axis=1)
        out_ref[first + i * 16 : first + (i + 1) * 16, :] = cut.astype(BF)


def stage(count, kv_ref, q_ref, new_ref, blocks_ref, counts_ref, *rest):
    pieces = rest[:count]
    q_out, new_out, bias_out, blocks, counts, sems, early = rest[count:]
    me, rep = lax.axis_index("seq"), lax.axis_index("rep")
    heads = kv_ref.shape[1]
    copy = copier(sems)
    moves = []
    for c in range(count - 1, -1, -1):
        for j in range(heads):
            moves.append(copy(kv_ref.at[me ^ c, j], pieces[c].at[pl.ds(j * BLOCK, BLOCK)]))
    moves += [copy(q_ref, q_out), copy(new_ref, new_out)]
    copy = copier(early)
    first = [copy(blocks_ref, blocks), copy(counts_ref, counts)]
    for move in moves + first:
        move.start()
    for move in first:
        move.wait()
    head_first = lax.axis_index("head") * new_ref.shape[2] + rep * heads
    rows = bias_out.shape[0] // heads
    for j in range(heads):
        for c in range(count):
            live = jnp.int32(0)
            for slot in range(blocks.shape[1]):
                hit = blocks[me, slot, head_first + j] == (me ^ c)
                live = live | (hit & (slot < counts[me, head_first + j])).astype(jnp.int32)
            dead = jnp.where(live > 0, 0.0, NEG).astype(F32)
            bias_out[j * rows : (j + 1) * rows, c * BLOCK : (c + 1) * BLOCK] = jnp.full(
                (rows, BLOCK), dead, F32
            )
    for move in moves:
        move.wait()


def stage_state(count, split, state_ref, *rest):
    outs, loaded, sems = rest[:count], rest[count], rest[count + 1]
    me, rep = lax.axis_index("seq"), lax.axis_index("rep")
    part = loaded.shape[2]
    copy = copier(sems)
    moves = []
    for c in range(count):
        if split:
            src = state_ref.at[me ^ c, :, pl.ds(pl.multiple_of(rep * part, 128), part)]
        else:
            src = state_ref.at[me ^ c]
        moves.append(copy(src, loaded.at[c]))
    run_all(moves)
    for c in range(count):
        pack_state(loaded[c], outs[c], 0)


def dot_f32(a, b, contract):
    return lax.dot_general(a, b, (contract, ((), ())), preferred_element_type=F32)


def query_rows(q_ref, heads):
    rep = lax.axis_index("rep")
    steps, _, q_heads, _ = q_ref.shape
    own_q = q_heads // 2
    group = own_q // heads
    q_all = [q_ref[step, 0].astype(F32) for step in range(steps)]
    q_all = [jnp.where(rep == 0, q[:own_q], q[own_q:]) for q in q_all]
    return [
        jnp.concatenate([x[j * group : (j + 1) * group] for x in q_all], axis=0)
        for j in range(heads)
    ]


def block_scores(q, piece_ref, j):
    hd = piece_ref.shape[1] // 2
    keys = piece_ref[j * BLOCK : (j + 1) * BLOCK, :hd]
    return dot_f32(q.astype(BF), keys, ((1,), (1,))) * hd ** (-0.5)


def block_sums(weights, piece_ref, j):
    values = piece_ref[j * BLOCK : (j + 1) * BLOCK, piece_ref.shape[1] // 2 :]
    return dot_f32(weights, values, ((1,), (0,)))


def choose(count, pieces, blocks, counts, zeros, sems, kept_ref, sent_ref):
    me, rep = lax.axis_index("seq"), lax.axis_index("rep")
    heads, keep_rep = kept_ref.shape[:2]
    head_first = lax.axis_index("head") * (2 * heads) + rep * heads
    waits = []
    for side, out in ((1, sent_ref), (0, kept_ref)):
        owner = rep if side == 0 else 1 - rep
        for j in range(heads):
            live_count = counts[me, head_first + j]
            for k in range(keep_rep):
                slot = owner * keep_rep + k
                source = blocks[me, slot, head_first + j] ^ me
                live = slot < live_count
                sem = sems.at[side, j, k]
                for c in range(count):
                    piece = pieces[c].at[pl.ds(j * BLOCK, BLOCK)]

                    @pl.when(live & (source == c))
                    def _():
                        pltpu.make_async_copy(piece, out.at[j, k], sem).start()

                @pl.when(jnp.logical_not(live))
                def _():
                    pltpu.make_async_copy(zeros, out.at[j, k], sem).start()

                waits.append(pltpu.make_async_copy(zeros, out.at[j, k], sem))
    return waits


def attend(count, heads, blocks_ref, counts_ref, q_ref, new_ref, bias_ref, *rest):
    pieces, states = rest[:count], rest[count : 2 * count - 1]
    outs, rest = rest[2 * count - 1 : 3 * count - 1], rest[3 * count - 1 :]
    kept_ref, sent_ref, blocks, counts, zeros, sems, early = rest
    copy = copier(early)
    scalars = [copy(blocks_ref, blocks), copy(counts_ref, counts)]
    for move in scalars:
        move.start()
    zeros[...] = jnp.zeros_like(zeros)
    rep = lax.axis_index("rep")
    queries = query_rows(q_ref, heads)
    rows, hd = queries[0].shape
    steps = q_ref.shape[0]
    group = rows // steps
    all_rows = heads * rows
    scale = hd ** (-0.5)
    scores = [
        jnp.concatenate([block_scores(q, piece, j) for piece in pieces], axis=1)
        for j, q in enumerate(queries)
    ]
    scores = jnp.concatenate(scores, axis=0)
    alive = bias_ref[...] == 0.0
    scores = jnp.where(alive, scores, NEG)
    row_step = (lax.broadcasted_iota(jnp.int32, (all_rows, 1), 0) // group) % steps
    wide_q = jnp.concatenate(queries, axis=0)
    dots, fresh_values = [], []
    top = jnp.max(scores, axis=1, keepdims=True)
    for step in range(steps):
        both = new_ref[step, 0].astype(F32)
        fresh = jnp.where(rep == 0, both[:heads], both[heads:])
        wide = jnp.concatenate(
            [jnp.broadcast_to(fresh[j : j + 1], (rows, 2 * hd)) for j in range(heads)], axis=0
        )
        dot = jnp.sum(wide_q * wide[:, :hd], axis=1, keepdims=True) * scale
        dots.append(jnp.where(row_step >= step, dot, NEG))
        fresh_values.append(wide[:, hd:])
        top = jnp.maximum(top, dots[-1])
    weights = jnp.where(alive, jnp.exp(scores - top), 0.0)
    total = jnp.sum(weights, axis=1, keepdims=True)
    weights = weights.astype(BF)
    for move in scalars:
        move.wait()
    waits = choose(count, pieces, blocks, counts, zeros, sems, kept_ref, sent_ref)
    summed = []
    for j in range(heads):
        parts = [
            block_sums(weights[j * rows : (j + 1) * rows, c * BLOCK : (c + 1) * BLOCK], piece, j)
            for c, piece in enumerate(pieces)
        ]
        summed.append(functools.reduce(jnp.add, parts))
    summed = jnp.concatenate(summed, axis=0)
    for step in range(steps):
        weight = jnp.where(row_step >= step, jnp.exp(dots[step] - top), 0.0)
        total = total + weight
        summed = summed + weight.astype(BF).astype(F32) * fresh_values[step]
    result = (summed / total).astype(BF)
    for c in range(count):
        for j in range(2):
            half = result[j * rows : (j + 1) * rows] if j < heads else jnp.zeros((rows, hd), BF)
            outs[c][:rows, j * hd : (j + 1) * hd] = half
        if c:
            outs[c][rows:, :] = states[c - 1][...]
    for move in waits:
        move.wait()


def collect(count, heads, steps, group, *rest):
    parts = rest[:1] + rest[1:count][::-1]
    out_ref, scratch = rest[count:]
    me = lax.axis_index("seq")
    for c in range(count):
        rows = parts[c][: steps * group, :].astype(F32)
        for j in range(heads):
            for step in range(steps):
                at = pl.multiple_of((step * count + (me ^ c)) * group, group)
                cut = rows[step * group : (step + 1) * group, j * 128 : (j + 1) * 128]
                scratch[j, pl.ds(at, group), :] = cut
    for j in range(heads):
        for g in range(group):
            at = (j * group + g) * 128
            tile = scratch[j, pl.ds(g, steps * count, stride=group), :]
            out_ref[:, at : at + 128] = tile.astype(BF)


def weight_half(weight_ref, out_ref, which, copy):
    half = out_ref.shape[0]
    rows = half // PIECES
    cuts = [(pl.ds(which * half + i * rows, rows), pl.ds(i * rows, rows)) for i in range(PIECES)]
    return [copy(weight_ref.at[src], out_ref.at[dst]) for src, dst in cuts]


def project_own(attn_ref, weight_ref, out_ref):
    out_ref[...] = dot_f32(attn_ref[...], weight_ref[...], ((1,), (0,)))


def pick(options, index):
    chosen = options[0]
    for i in range(1, len(options)):
        chosen = jnp.where(index == i, options[i], chosen)
    return chosen


def project_other(heads_count, count, acc_ref, attn_ref, weight_ref, *outs):
    total = acc_ref[...] + dot_f32(attn_ref[...], weight_ref[...], ((1,), (0,)))
    head = lax.axis_index("head")
    steps = total.shape[0] // count
    share = count // heads_count
    for step in range(steps):
        slices = [
            total[step * count + x * share : step * count + (x + 1) * share]
            for x in range(heads_count)
        ]
        for c in range(heads_count):
            outs[c][step] = pick(slices, head ^ c)


def add_up(*refs):
    total = refs[0][...]
    for ref in refs[1:-1]:
        total = total + ref[...]
    refs[-1][...] = total.astype(BF)


def prepare(count, split, weight_hbm, dt_hbm, x_hbm, bc_hbm, gain_hbm, log_hbm, own_ref, other_ref,
            slope_ref, base_ref, dt_ref, x_ref, bc_ref, gain_ref, log_ref, sems, weight_sems):
    copy = copier(sems)
    first = [
        copy(dt_hbm, dt_ref),
        copy(x_hbm, x_ref),
        copy(bc_hbm, bc_ref),
        copy(gain_hbm, gain_ref),
        copy(log_hbm, log_ref),
    ]
    copy, which = copier(weight_sems), lax.axis_index("rep")
    weights = weight_half(weight_hbm, own_ref, which, copy)
    weights += weight_half(weight_hbm, other_ref, 1 - which, copy)
    for move in first + weights:
        move.start()
    for move in first:
        move.wait()
    me, rep = lax.axis_index("seq"), lax.axis_index("rep")
    _, steps, ns, part = slope_ref.shape
    block = part * 2 if split else part
    diagonal = lax.broadcasted_iota(jnp.int32, (ns, ns), 0) == lax.broadcasted_iota(
        jnp.int32, (ns, ns), 1
    )

    def column(row):
        return jnp.sum(jnp.where(diagonal, row, 0.0), axis=1, keepdims=True)

    drive = [column(bc_ref[step, 0, 0:1, :]) for step in range(steps)]
    read = [column(bc_ref[step, 0, 1:2, :]) for step in range(steps)]
    for c in range(count):
        first = (me ^ c) * block + (rep * part if split else 0)
        lanes = pl.ds(pl.multiple_of(first, 128), part)
        rate = -jnp.exp(log_ref[:, lanes])
        gain = gain_ref[:, lanes]
        kept = jnp.ones((ns, part), F32)
        added = jnp.zeros((ns, part), F32)
        for step in range(steps):
            dt = dt_ref[step, :, lanes]
            inputs = x_ref[step : step + 1, lanes].astype(F32)
            decay = jnp.exp(dt * rate)
            kept = kept * decay
            added = added * decay + drive[step] * (dt * inputs)
            slope_ref[c, step] = read[step] * kept
            base_ref[c, step] = (
                jnp.sum(read[step] * added, axis=0, keepdims=True) + gain * inputs
            )
    for move in weights:
        move.wait()


def mamba_steps(count, slope_ref, base_ref, own_ref, *rest):
    parts, out_ref = rest[:-1][::-1], rest[-1]
    me = lax.axis_index("seq")
    _, steps, ns, part = slope_ref.shape
    for c in range(count):
        source = own_ref if c == 0 else parts[c - 1]
        first = source.shape[0] - state_rows(part)
        rows = [
            source[first + 16 * i : first + 16 * (i + 1), :].astype(F32)
            for i in range(pl.cdiv(part, 256))
        ]
        state = jnp.concatenate(rows, axis=1)[:, :part]
        for step in range(steps):
            out_ref[step, me ^ c] = base_ref[c, step] + jnp.sum(
                slope_ref[c, step] * state, axis=0, keepdims=True
            )


def assemble(split, kept_ref, got_ref, mamba_ref, *rest):
    rep = lax.axis_index("rep")
    if split:
        other_ref, handoff_ref, out_ref, sems = rest
    else:
        handoff_ref, out_ref, sems = rest
    heads = kept_ref.shape[0]
    copy = copier(sems)
    moves = [
        copy(kept_ref, handoff_ref.at[0, pl.ds(rep * heads, heads)]),
        copy(got_ref, handoff_ref.at[0, pl.ds((1 - rep) * heads, heads)]),
    ]
    steps, count, _, part = mamba_ref.shape
    for step in range(steps):
        for b in range(count):
            if split:
                for ref, side in ((mamba_ref, rep), (other_ref, 1 - rep)):
                    lanes = pl.ds(pl.multiple_of((2 * b + side) * part, 128), part)
                    moves.append(copy(ref.at[step, b], out_ref.at[step, :, lanes]))
            else:
                moves.append(copy(mamba_ref.at[step, b], out_ref.at[step, :, pl.ds(b * part, part)]))
    run_all(moves)


def per_device(
    prefill_kv,
    kept_blocks,
    kept_counts,
    queries,
    new_kv,
    out_weight,
    prefill_state,
    a_log,
    step_input,
    step_dt,
    step_bc,
    skip_gain,
):
    count = lax.axis_size("seq")
    reps = lax.axis_size("rep")
    heads_count = lax.axis_size("head")
    requests, heads, tokens, width = prefill_kv.shape
    assert requests == count and tokens == BLOCK and reps == 2 and width == 256
    assert count & (count - 1) == 0 and heads_count & (heads_count - 1) == 0
    keep = kept_blocks.shape[2]
    keep_rep = keep // reps
    steps, _, q_heads, hd = queries.shape
    dec_heads = new_kv.shape[2]
    group = q_heads // dec_heads
    _, ns, block = prefill_state.shape
    split = block % (reps * 128) == 0
    part = block // reps if split else block
    all_rows = heads * steps * group
    assert all_rows <= 128
    channels = count * block
    shape = jax.ShapeDtypeStruct
    smem = pltpu.SMEM
    blocks = jnp.swapaxes(kept_blocks, 1, 2)

    prefill_kv, prefill_state, queries, new_kv = map(in_hbm, (prefill_kv, prefill_state, queries, new_kv))
    step_dt, step_bc, a_log, out_weight = map(in_hbm, (step_dt, step_bc, a_log, out_weight))
    step_input = in_hbm(step_input.reshape(steps, channels))
    skip_gain = in_hbm(skip_gain.reshape(1, -1))
    blocks, kept_counts = in_hbm(blocks), in_hbm(kept_counts)

    columns = out_weight.shape[1]
    half = heads * group * hd
    half_weight = pltpu.VMEM((half, columns), BF)
    *pieces, q_near, new_near, bias = call(
        functools.partial(stage, count),
        [shape((heads * BLOCK, width), BF)] * count
        + [
            shape(queries.shape, BF),
            shape(new_kv.shape, BF),
            shape((all_rows, count * BLOCK), F32),
        ],
        [HB] * 5,
        [VM] * (count + 3),
        [
            smem(blocks.shape, jnp.int32),
            smem(kept_counts.shape, jnp.int32),
            DMA((count * heads + 2,)),
            DMA((2,)),
        ],
    )(prefill_kv, queries, new_kv, blocks, kept_counts)
    moved = [shift(pieces[c], "seq", c) for c in range(count - 1, 0, -1)][::-1]
    states = call(
        functools.partial(stage_state, count, split),
        [shape((state_rows(part), width), BF)] * count,
        [HB],
        [VM] * count,
        [pltpu.VMEM((count, ns, part), F32), DMA((count,))],
    )(*after([prefill_state], pieces[0]))
    own_weight, other_weight, slope, base = call(
        functools.partial(prepare, count, split),
        [
            half_weight,
            half_weight,
            shape((count, steps, ns, part), F32),
            shape((count, steps, 1, part), F32),
        ],
        [HB] * 6,
        [VM] * 4,
        [
            pltpu.VMEM((steps, 1, channels), F32),
            pltpu.VMEM((steps, channels), BF),
            pltpu.VMEM(step_bc.shape, F32),
            pltpu.VMEM((1, channels), F32),
            pltpu.VMEM(a_log.shape, F32),
            DMA((5,)),
            DMA((2 * PIECES,)),
        ],
    )(*after([out_weight], pieces[0]), step_dt, step_input, step_bc, skip_gain, a_log)

    *moved, own_weight = after([*moved[::-1], own_weight])
    kv = [pieces[0], *moved[::-1]]
    rows = steps * group
    half_shape = (heads, keep_rep, BLOCK, width)
    *sends, kept, sent = call(
        functools.partial(attend, count, heads),
        [shape((rows, width), BF)]
        + [shape((rows + state_rows(part), width), BF)] * (count - 1)
        + [shape(half_shape, BF)] * 2,
        [HB] * 2 + [VM] * (2 + 2 * count),
        [VM] * (count + 2),
        [
            smem(blocks.shape, jnp.int32),
            smem(kept_counts.shape, jnp.int32),
            pltpu.VMEM((BLOCK, width), BF),
            DMA((2, heads, keep_rep)),
            DMA((2,)),
        ],
    )(blocks, kept_counts, q_near, new_near, bias, *kv, *states[1:])
    gathered = [shift(sends[c], "seq", c) for c in range(count - 1, 0, -1)][::-1]
    attn = call(
        functools.partial(collect, count, heads, steps, group),
        shape((steps * count, half), BF),
        [VM] * count,
        VM,
        [pltpu.VMEM((heads, steps * count * group, hd), F32)],
    )(sends[0], *gathered[::-1])
    attn_other = shift(attn, "rep", 1)
    own_sum = call(
        project_own, shape((steps * count, columns), F32), [VM, VM], VM, us=0.7
    )(attn, own_weight)
    share = count // heads_count
    sums = call(
        functools.partial(project_other, heads_count, count),
        [shape((steps, share, columns), F32)] * heads_count,
        [VM, VM, VM],
        [VM] * heads_count,
        us=0.7,
    )(own_sum, attn_other, other_weight)
    sums = [sums[0]] + [shift(sums[c], "head", c) for c in range(1, heads_count)]
    mamba = call(
        functools.partial(mamba_steps, count),
        shape((steps, count, 1, part), F32),
        [VM] * (2 + count),
        VM,
    )(slope, base, *after(states[:1], attn), *gathered[::-1])
    got = shift(after([sent], mamba)[0], "rep", 1)
    kept = after([kept], sums[0])[0]
    operands = [kept, got, mamba] + ([shift(mamba, "rep", 1)] if split else [])
    handoff, mamba_out = call(
        functools.partial(assemble, split),
        [
            shape((1, dec_heads, keep_rep, BLOCK, width), BF),
            shape((steps, 1, channels), F32),
        ],
        [VM] * len(operands),
        [HB] * 2,
        [DMA((2 + steps * count * (2 if split else 1),))],
    )(*operands)
    sums[1:] = after(sums[1:], handoff)
    proj_out = call(
        add_up, shape((steps, share, columns), BF), [VM] * heads_count, VM, us=0.6
    )(*sums)
    return handoff, proj_out, mamba_out


def solution(mesh):
    return jax.shard_map(
        per_device,
        mesh=mesh,
        in_specs=(
            P("groups", ("head", "rep"), "seq", None),
            P("groups", None, None),
            P("groups", None),
            P(None, ("groups", "seq"), "head", None),
            P(None, ("groups", "seq"), "head", None),
            P("head", ("seq", "rep")),
            P("groups", None, ("head", "seq")),
            P(None, "head"),
            P(None, ("groups", "seq"), "head"),
            P(None, ("groups", "seq"), "head"),
            P(None, ("groups", "seq"), None, None),
            P("head"),
        ),
        out_specs=(
            P(("groups", "seq"), "head", "rep", None, None),
            P(None, ("groups", "head"), ("seq", "rep")),
            P(None, ("groups", "seq"), "head"),
        ),
        check_vma=False,
    )
```

```python
import functools

import jax
import jax.numpy as jnp
from jax import lax
from jax.experimental import pallas as pl
from jax.experimental.pallas import tpu as pltpu
from jax.sharding import PartitionSpec as P

BLOCK = 128
PIECES = 4
NEG = -1e30
BF = jnp.bfloat16
F32 = jnp.float32
VM = pl.BlockSpec(memory_space=pltpu.VMEM)
HB = pl.BlockSpec(memory_space=pltpu.HBM)
DMA = pltpu.SemaphoreType.DMA


def shift(x, axis, c):
    size = lax.axis_size(axis)
    return lax.ppermute(x, axis, [(i, i ^ c) for i in range(size)])


def call(body, out_shape, in_specs, out_specs, scratch=(), us=1.0):
    return pl.pallas_call(
        body,
        out_shape=out_shape,
        in_specs=in_specs,
        out_specs=out_specs,
        scratch_shapes=list(scratch),
        cost_estimate=pl.CostEstimate(
            flops=0, bytes_accessed=int(us * 3.6e4), transcendentals=0
        ),
        compiler_params=pltpu.CompilerParams(vmem_limit_bytes=32 * 1024 * 1024),
    )


def in_hbm(x):
    return pltpu.with_memory_space_constraint(x, pltpu.HBM)


def after(arrays, *earlier):
    return lax.optimization_barrier((*arrays, *earlier))[: len(arrays)]


def run_all(copies):
    for copy in copies:
        copy.start()
    for copy in copies:
        copy.wait()


def copier(sems):
    position = iter(range(sems.shape[0]))
    return lambda src, dst: pltpu.make_async_copy(src, dst, sems.at[next(position)])


def state_rows(part):
    return 16 * pl.cdiv(part, 256)


def pack_state(piece, out_ref, first):
    ns, part = piece.shape
    for i in range(pl.cdiv(part, 256)):
        cut = piece[:, i * 256 : (i + 1) * 256]
        if cut.shape[1] < 256:
            cut = jnp.concatenate([cut, jnp.zeros((ns, 256 - cut.shape[1]), F32)], axis=1)
        out_ref[first + i * 16 : first + (i + 1) * 16, :] = cut.astype(BF)


def own_state(state_ref, c, split, part):
    me, rep = lax.axis_index("seq"), lax.axis_index("rep")
    if split:
        return state_ref.at[me ^ c, :, pl.ds(pl.multiple_of(rep * part, 128), part)]
    return state_ref.at[me ^ c]


def stage(count, split, kv_ref, q_ref, new_ref, state_ref, blocks_ref, counts_ref, *rest):
    pieces = rest[:count]
    q_out, new_out, bias_out, pick_out, loaded, blocks, counts, sems, early = rest[count:]
    me, rep = lax.axis_index("seq"), lax.axis_index("rep")
    heads = kv_ref.shape[1]
    copy = copier(sems)
    moves = []
    for c in range(count - 1, -1, -1):
        for j in range(heads):
            moves.append(copy(kv_ref.at[me ^ c, j], pieces[c].at[pl.ds(j * BLOCK, BLOCK)]))
    moves += [copy(q_ref, q_out), copy(new_ref, new_out)]
    copy = copier(early)
    first = [copy(blocks_ref, blocks), copy(counts_ref, counts)]
    first.append(copy(own_state(state_ref, 1, split, loaded.shape[1]), loaded))
    for move in moves + first:
        move.start()
    for move in first:
        move.wait()
    pack_state(loaded[...], pieces[1], heads * BLOCK)
    head_first = lax.axis_index("head") * new_ref.shape[2] + rep * heads
    rows = bias_out.shape[0] // heads
    keep_rep = pick_out.shape[2]
    for j in range(heads):
        live_count = counts[me, head_first + j]
        for c in range(count):
            live = jnp.int32(0)
            for side in range(2):
                for k in range(keep_rep):
                    slot = (rep if side == 0 else 1 - rep) * keep_rep + k
                    hit = (blocks[me, slot, head_first + j] == (me ^ c)) & (slot < live_count)
                    one = jnp.where(hit, 1.0, 0.0).astype(F32)
                    pick_out[side, j, k, c] = jnp.full(pick_out.shape[4:], one, F32).astype(BF)
                    live = live | hit.astype(jnp.int32)
            dead = jnp.where(live > 0, 0.0, NEG).astype(F32)
            bias_out[j * rows : (j + 1) * rows, c * BLOCK : (c + 1) * BLOCK] = jnp.full(
                (rows, BLOCK), dead, F32
            )
    for move in moves:
        move.wait()


def stage_state(count, split, state_ref, *rest):
    outs, loaded, sems = rest[: count - 1], rest[count - 1], rest[count]
    copy = copier(sems)
    steps_away = [0, *range(2, count)]
    run_all(
        [
            copy(own_state(state_ref, c, split, loaded.shape[2]), loaded.at[i])
            for i, c in enumerate(steps_away)
        ]
    )
    for i in range(count - 1):
        pack_state(loaded[i], outs[i], 0)


def dot_f32(a, b, contract):
    return lax.dot_general(a, b, (contract, ((), ())), preferred_element_type=F32)


def query_rows(q_ref, heads):
    rep = lax.axis_index("rep")
    steps, _, q_heads, _ = q_ref.shape
    own_q = q_heads // 2
    group = own_q // heads
    q_all = [q_ref[step, 0].astype(F32) for step in range(steps)]
    q_all = [jnp.where(rep == 0, q[:own_q], q[own_q:]) for q in q_all]
    return [
        jnp.concatenate([x[j * group : (j + 1) * group] for x in q_all], axis=0)
        for j in range(heads)
    ]


def block_scores(q, piece_ref, j):
    hd = piece_ref.shape[1] // 2
    keys = piece_ref[j * BLOCK : (j + 1) * BLOCK, :hd]
    return dot_f32(q.astype(BF), keys, ((1,), (1,))) * hd ** (-0.5)


def block_sums(weights, piece_ref, j):
    values = piece_ref[j * BLOCK : (j + 1) * BLOCK, piece_ref.shape[1] // 2 :]
    return dot_f32(weights, values, ((1,), (0,)))


def attend(count, heads, q_ref, new_ref, bias_ref, pick_ref, *rest):
    pieces, (out_ref, kept_ref, sent_ref) = rest[:count], rest[count:]
    rep = lax.axis_index("rep")
    queries = query_rows(q_ref, heads)
    rows, hd = queries[0].shape
    steps = q_ref.shape[0]
    group = rows // steps
    all_rows = heads * rows
    scale = hd ** (-0.5)
    scores = [
        jnp.concatenate([block_scores(q, piece, j) for piece in pieces], axis=1)
        for j, q in enumerate(queries)
    ]
    scores = jnp.concatenate(scores, axis=0)
    alive = bias_ref[...] == 0.0
    scores = jnp.where(alive, scores, NEG)
    row_step = (lax.broadcasted_iota(jnp.int32, (all_rows, 1), 0) // group) % steps
    wide_q = jnp.concatenate(queries, axis=0)
    dots, fresh_values = [], []
    top = jnp.max(scores, axis=1, keepdims=True)
    for step in range(steps):
        both = new_ref[step, 0].astype(F32)
        fresh = jnp.where(rep == 0, both[:heads], both[heads:])
        wide = jnp.concatenate(
            [jnp.broadcast_to(fresh[j : j + 1], (rows, 2 * hd)) for j in range(heads)], axis=0
        )
        dot = jnp.sum(wide_q * wide[:, :hd], axis=1, keepdims=True) * scale
        dots.append(jnp.where(row_step >= step, dot, NEG))
        fresh_values.append(wide[:, hd:])
        top = jnp.maximum(top, dots[-1])
    weights = jnp.where(alive, jnp.exp(scores - top), 0.0)
    total = jnp.sum(weights, axis=1, keepdims=True)
    weights = weights.astype(BF)
    summed = []
    for j in range(heads):
        parts = [
            block_sums(weights[j * rows : (j + 1) * rows, c * BLOCK : (c + 1) * BLOCK], piece, j)
            for c, piece in enumerate(pieces)
        ]
        summed.append(functools.reduce(jnp.add, parts))
    summed = jnp.concatenate(summed, axis=0)
    for step in range(steps):
        weight = jnp.where(row_step >= step, jnp.exp(dots[step] - top), 0.0)
        total = total + weight
        summed = summed + weight.astype(BF).astype(F32) * fresh_values[step]
    result = (summed / total).astype(BF)
    for j in range(2):
        half = result[j * rows : (j + 1) * rows] if j < heads else jnp.zeros((rows, hd), BF)
        out_ref[:, j * hd : (j + 1) * hd] = half
    tile = pick_ref.shape[4]
    for side, ref in ((1, sent_ref), (0, kept_ref)):
        for j in range(heads):
            for k in range(ref.shape[1]):
                total = None
                for c in range(count):
                    piece = pieces[c][j * BLOCK : (j + 1) * BLOCK, :].reshape(-1, tile, 2 * hd)
                    term = piece * pick_ref[side, j, k, c][None]
                    total = term if total is None else total + term
                ref[j, k] = total.reshape(BLOCK, 2 * hd)


def collect(count, heads, steps, group, slope_ref, base_ref, *rest):
    parts = rest[:1] + rest[1:count][::-1]
    states = rest[count : 2 * count]
    out_ref, mamba_ref, scratch = rest[2 * count :]
    me = lax.axis_index("seq")
    ns, part = slope_ref.shape[2:]
    for c in range(count):
        first = states[c].shape[0] - state_rows(part)
        rows = [
            states[c][first + 16 * i : first + 16 * (i + 1), :].astype(F32)
            for i in range(pl.cdiv(part, 256))
        ]
        state = jnp.concatenate(rows, axis=1)[:, :part]
        for step in range(steps):
            mamba_ref[step, me ^ c] = base_ref[c, step] + jnp.sum(
                slope_ref[c, step] * state, axis=0, keepdims=True
            )
    for c in range(count):
        rows = parts[c][: steps * group, :].astype(F32)
        for j in range(heads):
            for step in range(steps):
                at = pl.multiple_of((step * count + (me ^ c)) * group, group)
                cut = rows[step * group : (step + 1) * group, j * 128 : (j + 1) * 128]
                scratch[j, pl.ds(at, group), :] = cut
    for j in range(heads):
        for g in range(group):
            at = (j * group + g) * 128
            tile = scratch[j, pl.ds(g, steps * count, stride=group), :]
            out_ref[:, at : at + 128] = tile.astype(BF)


def weight_half(weight_ref, out_ref, which, copy):
    half = out_ref.shape[0]
    rows = half // PIECES
    cuts = [(pl.ds(which * half + i * rows, rows), pl.ds(i * rows, rows)) for i in range(PIECES)]
    return [copy(weight_ref.at[src], out_ref.at[dst]) for src, dst in cuts]


def project_own(attn_ref, weight_ref, out_ref):
    out_ref[...] = dot_f32(attn_ref[...], weight_ref[...], ((1,), (0,)))


def pick(options, index):
    chosen = options[0]
    for i in range(1, len(options)):
        chosen = jnp.where(index == i, options[i], chosen)
    return chosen


def project_other(heads_count, count, acc_ref, attn_ref, weight_ref, *outs):
    total = acc_ref[...] + dot_f32(attn_ref[...], weight_ref[...], ((1,), (0,)))
    head = lax.axis_index("head")
    steps = total.shape[0] // count
    share = count // heads_count
    for step in range(steps):
        slices = [
            total[step * count + x * share : step * count + (x + 1) * share]
            for x in range(heads_count)
        ]
        for c in range(heads_count):
            outs[c][step] = pick(slices, head ^ c)


def add_up(*refs):
    total = refs[0][...]
    for ref in refs[1:-1]:
        total = total + ref[...]
    refs[-1][...] = total.astype(BF)


def prepare(count, split, weight_hbm, dt_hbm, x_hbm, bc_hbm, gain_hbm, log_hbm, own_ref, other_ref,
            slope_ref, base_ref, dt_ref, x_ref, bc_ref, gain_ref, log_ref, sems, weight_sems):
    copy = copier(sems)
    first = [
        copy(dt_hbm, dt_ref),
        copy(x_hbm, x_ref),
        copy(bc_hbm, bc_ref),
        copy(gain_hbm, gain_ref),
        copy(log_hbm, log_ref),
    ]
    copy, which = copier(weight_sems), lax.axis_index("rep")
    weights = weight_half(weight_hbm, own_ref, which, copy)
    weights += weight_half(weight_hbm, other_ref, 1 - which, copy)
    for move in first + weights:
        move.start()
    for move in first:
        move.wait()
    me, rep = lax.axis_index("seq"), lax.axis_index("rep")
    _, steps, ns, part = slope_ref.shape
    block = part * 2 if split else part
    diagonal = lax.broadcasted_iota(jnp.int32, (ns, ns), 0) == lax.broadcasted_iota(
        jnp.int32, (ns, ns), 1
    )

    def column(row):
        return jnp.sum(jnp.where(diagonal, row, 0.0), axis=1, keepdims=True)

    drive = [column(bc_ref[step, 0, 0:1, :]) for step in range(steps)]
    read = [column(bc_ref[step, 0, 1:2, :]) for step in range(steps)]
    for c in range(count):
        first = (me ^ c) * block + (rep * part if split else 0)
        lanes = pl.ds(pl.multiple_of(first, 128), part)
        rate = -jnp.exp(log_ref[:, lanes])
        gain = gain_ref[:, lanes]
        kept = jnp.ones((ns, part), F32)
        added = jnp.zeros((ns, part), F32)
        for step in range(steps):
            dt = dt_ref[step, :, lanes]
            inputs = x_ref[step : step + 1, lanes].astype(F32)
            decay = jnp.exp(dt * rate)
            kept = kept * decay
            added = added * decay + drive[step] * (dt * inputs)
            slope_ref[c, step] = read[step] * kept
            base_ref[c, step] = (
                jnp.sum(read[step] * added, axis=0, keepdims=True) + gain * inputs
            )
    for move in weights:
        move.wait()


def assemble(split, kept_ref, got_ref, mamba_ref, *rest):
    rep = lax.axis_index("rep")
    if split:
        other_ref, handoff_ref, out_ref, sems = rest
    else:
        handoff_ref, out_ref, sems = rest
    heads = kept_ref.shape[0]
    copy = copier(sems)
    moves = [
        copy(kept_ref, handoff_ref.at[0, pl.ds(rep * heads, heads)]),
        copy(got_ref, handoff_ref.at[0, pl.ds((1 - rep) * heads, heads)]),
    ]
    steps, count, _, part = mamba_ref.shape
    for step in range(steps):
        for b in range(count):
            if split:
                for ref, side in ((mamba_ref, rep), (other_ref, 1 - rep)):
                    lanes = pl.ds(pl.multiple_of((2 * b + side) * part, 128), part)
                    moves.append(copy(ref.at[step, b], out_ref.at[step, :, lanes]))
            else:
                moves.append(copy(mamba_ref.at[step, b], out_ref.at[step, :, pl.ds(b * part, part)]))
    run_all(moves)


def per_device(
    prefill_kv,
    kept_blocks,
    kept_counts,
    queries,
    new_kv,
    out_weight,
    prefill_state,
    a_log,
    step_input,
    step_dt,
    step_bc,
    skip_gain,
):
    count = lax.axis_size("seq")
    reps = lax.axis_size("rep")
    heads_count = lax.axis_size("head")
    requests, heads, tokens, width = prefill_kv.shape
    assert requests == count and tokens == BLOCK and reps == 2 and width == 256
    assert count & (count - 1) == 0 and heads_count & (heads_count - 1) == 0
    keep = kept_blocks.shape[2]
    keep_rep = keep // reps
    steps, _, q_heads, hd = queries.shape
    dec_heads = new_kv.shape[2]
    group = q_heads // dec_heads
    _, ns, block = prefill_state.shape
    split = block % (reps * 128) == 0
    part = block // reps if split else block
    all_rows = heads * steps * group
    assert all_rows <= 128
    channels = count * block
    shape = jax.ShapeDtypeStruct
    smem = pltpu.SMEM
    blocks = jnp.swapaxes(kept_blocks, 1, 2)

    prefill_kv, prefill_state, queries, new_kv = map(in_hbm, (prefill_kv, prefill_state, queries, new_kv))
    step_dt, step_bc, a_log, out_weight = map(in_hbm, (step_dt, step_bc, a_log, out_weight))
    step_input = in_hbm(step_input.reshape(steps, channels))
    skip_gain = in_hbm(skip_gain.reshape(1, -1))
    blocks, kept_counts = in_hbm(blocks), in_hbm(kept_counts)

    columns = out_weight.shape[1]
    half = heads * group * hd
    half_weight = pltpu.VMEM((half, columns), BF)
    tall = heads * BLOCK
    *pieces, q_near, new_near, bias, picks = call(
        functools.partial(stage, count, split),
        [
            shape((tall + (state_rows(part) if c == 1 else 0), width), BF)
            for c in range(count)
        ]
        + [
            shape(queries.shape, BF),
            shape(new_kv.shape, BF),
            shape((all_rows, count * BLOCK), F32),
            shape((reps, heads, keep_rep, count, 16, width), BF),
        ],
        [HB] * 6,
        [VM] * (count + 4),
        [
            pltpu.VMEM((ns, part), F32),
            smem(blocks.shape, jnp.int32),
            smem(kept_counts.shape, jnp.int32),
            DMA((count * heads + 2,)),
            DMA((3,)),
        ],
    )(prefill_kv, queries, new_kv, prefill_state, blocks, kept_counts)
    moved = [shift(pieces[c], "seq", c) for c in range(count - 1, 0, -1)][::-1]
    home_state, *states = call(
        functools.partial(stage_state, count, split),
        [shape((state_rows(part), width), BF)] * (count - 1),
        [HB],
        [VM] * (count - 1),
        [pltpu.VMEM((count - 1, ns, part), F32), DMA((count - 1,))],
    )(*after([prefill_state], pieces[0]))
    own_weight, other_weight, slope, base = call(
        functools.partial(prepare, count, split),
        [
            half_weight,
            half_weight,
            shape((count, steps, ns, part), F32),
            shape((count, steps, 1, part), F32),
        ],
        [HB] * 6,
        [VM] * 4,
        [
            pltpu.VMEM((steps, 1, channels), F32),
            pltpu.VMEM((steps, channels), BF),
            pltpu.VMEM(step_bc.shape, F32),
            pltpu.VMEM((1, channels), F32),
            pltpu.VMEM(a_log.shape, F32),
            DMA((5,)),
            DMA((2 * PIECES,)),
        ],
    )(*after([out_weight], pieces[0]), step_dt, step_input, step_bc, skip_gain, a_log)

    states = after(states, own_weight)
    states = [shift(states[c - 2], "seq", c) for c in range(count - 1, 1, -1)][::-1]
    *moved, own_weight = after([*moved[::-1], own_weight])
    kv = [pieces[0], *moved[::-1]]
    half_shape = (heads, keep_rep, BLOCK, width)
    rows, kept, sent = call(
        functools.partial(attend, count, heads),
        [shape((steps * group, width), BF)] + [shape(half_shape, BF)] * 2,
        [VM] * (4 + count),
        [VM] * 3,
    )(q_near, new_near, bias, picks, *kv)
    gathered = [shift(rows, "seq", c) for c in range(count - 1, 0, -1)]
    attn, mamba = call(
        functools.partial(collect, count, heads, steps, group),
        [shape((steps * count, half), BF), shape((steps, count, 1, part), F32)],
        [VM] * (2 + 2 * count),
        [VM] * 2,
        [pltpu.VMEM((heads, steps * count * group, hd), F32)],
    )(slope, base, rows, *gathered, home_state, kv[1], *states)
    attn_other = shift(attn, "rep", 1)
    own_sum = call(
        project_own, shape((steps * count, columns), F32), [VM, VM], VM, us=0.7
    )(attn, own_weight)
    share = count // heads_count
    sums = call(
        functools.partial(project_other, heads_count, count),
        [shape((steps, share, columns), F32)] * heads_count,
        [VM, VM, VM],
        [VM] * heads_count,
        us=0.7,
    )(own_sum, attn_other, other_weight)
    sums = [sums[0]] + [shift(sums[c], "head", c) for c in range(1, heads_count)]
    got = shift(after([sent], mamba)[0], "rep", 1)
    kept = after([kept], sums[0])[0]
    operands = [kept, got, mamba] + ([shift(mamba, "rep", 1)] if split else [])
    handoff, mamba_out = call(
        functools.partial(assemble, split),
        [
            shape((1, dec_heads, keep_rep, BLOCK, width), BF),
            shape((steps, 1, channels), F32),
        ],
        [VM] * len(operands),
        [HB] * 2,
        [DMA((2 + steps * count * (2 if split else 1),))],
    )(*operands)
    sums[1:] = after(sums[1:], handoff)
    proj_out = call(
        add_up, shape((steps, share, columns), BF), [VM] * heads_count, VM, us=0.6
    )(*sums)
    return handoff, proj_out, mamba_out


def solution(mesh):
    return jax.shard_map(
        per_device,
        mesh=mesh,
        in_specs=(
            P("groups", ("head", "rep"), "seq", None),
            P("groups", None, None),
            P("groups", None),
            P(None, ("groups", "seq"), "head", None),
            P(None, ("groups", "seq"), "head", None),
            P("head", ("seq", "rep")),
            P("groups", None, ("head", "seq")),
            P(None, "head"),
            P(None, ("groups", "seq"), "head"),
            P(None, ("groups", "seq"), "head"),
            P(None, ("groups", "seq"), None, None),
            P("head"),
        ),
        out_specs=(
            P(("groups", "seq"), "head", "rep", None, None),
            P(None, ("groups", "head"), ("seq", "rep")),
            P(None, ("groups", "seq"), "head"),
        ),
        check_vma=False,
    )
```

```python
import functools

import jax
import jax.numpy as jnp
from jax import lax
from jax.experimental import pallas as pl
from jax.experimental.pallas import tpu as pltpu
from jax.sharding import PartitionSpec as P

BLOCK = 128
PIECES = 4
NEG = -1e30
BF = jnp.bfloat16
F32 = jnp.float32
VM = pl.BlockSpec(memory_space=pltpu.VMEM)
HB = pl.BlockSpec(memory_space=pltpu.HBM)
DMA = pltpu.SemaphoreType.DMA


def shift(x, axis, c):
    size = lax.axis_size(axis)
    return lax.ppermute(x, axis, [(i, i ^ c) for i in range(size)])


def call(body, out_shape, in_specs, out_specs, scratch=(), us=1.0):
    return pl.pallas_call(
        body,
        out_shape=out_shape,
        in_specs=in_specs,
        out_specs=out_specs,
        scratch_shapes=list(scratch),
        cost_estimate=pl.CostEstimate(
            flops=0, bytes_accessed=int(us * 3.6e4), transcendentals=0
        ),
        compiler_params=pltpu.CompilerParams(vmem_limit_bytes=32 * 1024 * 1024),
    )


def in_hbm(x):
    return pltpu.with_memory_space_constraint(x, pltpu.HBM)


def after(arrays, *earlier):
    return lax.optimization_barrier((*arrays, *earlier))[: len(arrays)]


def run_all(copies):
    for copy in copies:
        copy.start()
    for copy in copies:
        copy.wait()


def copier(sems):
    position = iter(range(sems.shape[0]))
    return lambda src, dst: pltpu.make_async_copy(src, dst, sems.at[next(position)])


def state_rows(part):
    return 16 * pl.cdiv(part, 256)


def pack_state(piece, out_ref, first):
    ns, part = piece.shape
    for i in range(pl.cdiv(part, 256)):
        cut = piece[:, i * 256 : (i + 1) * 256]
        if cut.shape[1] < 256:
            cut = jnp.concatenate([cut, jnp.zeros((ns, 256 - cut.shape[1]), F32)], axis=1)
        out_ref[first + i * 16 : first + (i + 1) * 16, :] = cut.astype(BF)


def own_state(state_ref, c, split, part):
    me, rep = lax.axis_index("seq"), lax.axis_index("rep")
    if split:
        return state_ref.at[me ^ c, :, pl.ds(pl.multiple_of(rep * part, 128), part)]
    return state_ref.at[me ^ c]


def stage(count, kv_ref, q_ref, new_ref, blocks_ref, counts_ref, *rest):
    pieces = rest[:count]
    q_out, new_out, bias_out, pick_out, blocks, counts, sems, early = rest[count:]
    me, rep = lax.axis_index("seq"), lax.axis_index("rep")
    heads = kv_ref.shape[1]
    copy = copier(sems)
    moves = []
    for c in range(count - 1, -1, -1):
        for j in range(heads):
            moves.append(copy(kv_ref.at[me ^ c, j], pieces[c].at[pl.ds(j * BLOCK, BLOCK)]))
    moves += [copy(q_ref, q_out), copy(new_ref, new_out)]
    copy = copier(early)
    first = [copy(blocks_ref, blocks), copy(counts_ref, counts)]
    for move in moves + first:
        move.start()
    for move in first:
        move.wait()
    head_first = lax.axis_index("head") * new_ref.shape[2] + rep * heads
    rows = bias_out.shape[0] // heads
    keep_rep = pick_out.shape[2]
    for j in range(heads):
        live_count = counts[me, head_first + j]
        for c in range(count):
            live = jnp.int32(0)
            for side in range(2):
                for k in range(keep_rep):
                    slot = (rep if side == 0 else 1 - rep) * keep_rep + k
                    hit = (blocks[me, slot, head_first + j] == (me ^ c)) & (slot < live_count)
                    one = jnp.where(hit, 1.0, 0.0).astype(F32)
                    pick_out[side, j, k, c] = jnp.full(pick_out.shape[4:], one, F32).astype(BF)
                    live = live | hit.astype(jnp.int32)
            dead = jnp.where(live > 0, 0.0, NEG).astype(F32)
            bias_out[j * rows : (j + 1) * rows, c * BLOCK : (c + 1) * BLOCK] = jnp.full(
                (rows, BLOCK), dead, F32
            )
    for move in moves:
        move.wait()


def stage_state(count, split, state_ref, *rest):
    outs, loaded, sems = rest[:count], rest[count], rest[count + 1]
    copy = copier(sems)
    run_all(
        [copy(own_state(state_ref, c, split, loaded.shape[2]), loaded.at[c]) for c in range(count)]
    )
    for c in range(count):
        pack_state(loaded[c], outs[c], 0)


def dot_f32(a, b, contract):
    return lax.dot_general(a, b, (contract, ((), ())), preferred_element_type=F32)


def query_rows(q_ref, heads):
    rep = lax.axis_index("rep")
    steps, _, q_heads, _ = q_ref.shape
    own_q = q_heads // 2
    group = own_q // heads
    q_all = [q_ref[step, 0].astype(F32) for step in range(steps)]
    q_all = [jnp.where(rep == 0, q[:own_q], q[own_q:]) for q in q_all]
    return [
        jnp.concatenate([x[j * group : (j + 1) * group] for x in q_all], axis=0)
        for j in range(heads)
    ]


def block_scores(q, piece_ref, j):
    hd = piece_ref.shape[1] // 2
    keys = piece_ref[j * BLOCK : (j + 1) * BLOCK, :hd]
    return dot_f32(q.astype(BF), keys, ((1,), (1,))) * hd ** (-0.5)


def block_sums(weights, piece_ref, j):
    values = piece_ref[j * BLOCK : (j + 1) * BLOCK, piece_ref.shape[1] // 2 :]
    return dot_f32(weights, values, ((1,), (0,)))


def attend(count, heads, q_ref, new_ref, bias_ref, pick_ref, *rest):
    pieces, states = rest[:count], rest[count : 2 * count - 1]
    outs, (kept_ref, sent_ref) = rest[2 * count - 1 : 3 * count - 1], rest[3 * count - 1 :]
    rep = lax.axis_index("rep")
    queries = query_rows(q_ref, heads)
    rows, hd = queries[0].shape
    steps = q_ref.shape[0]
    group = rows // steps
    all_rows = heads * rows
    scale = hd ** (-0.5)
    scores = [
        jnp.concatenate([block_scores(q, piece, j) for piece in pieces], axis=1)
        for j, q in enumerate(queries)
    ]
    scores = jnp.concatenate(scores, axis=0)
    alive = bias_ref[...] == 0.0
    scores = jnp.where(alive, scores, NEG)
    row_step = (lax.broadcasted_iota(jnp.int32, (all_rows, 1), 0) // group) % steps
    wide_q = jnp.concatenate(queries, axis=0)
    dots, fresh_values = [], []
    top = jnp.max(scores, axis=1, keepdims=True)
    for step in range(steps):
        both = new_ref[step, 0].astype(F32)
        fresh = jnp.where(rep == 0, both[:heads], both[heads:])
        wide = jnp.concatenate(
            [jnp.broadcast_to(fresh[j : j + 1], (rows, 2 * hd)) for j in range(heads)], axis=0
        )
        dot = jnp.sum(wide_q * wide[:, :hd], axis=1, keepdims=True) * scale
        dots.append(jnp.where(row_step >= step, dot, NEG))
        fresh_values.append(wide[:, hd:])
        top = jnp.maximum(top, dots[-1])
    weights = jnp.where(alive, jnp.exp(scores - top), 0.0)
    total = jnp.sum(weights, axis=1, keepdims=True)
    weights = weights.astype(BF)
    summed = []
    for j in range(heads):
        parts = [
            block_sums(weights[j * rows : (j + 1) * rows, c * BLOCK : (c + 1) * BLOCK], piece, j)
            for c, piece in enumerate(pieces)
        ]
        summed.append(functools.reduce(jnp.add, parts))
    summed = jnp.concatenate(summed, axis=0)
    for step in range(steps):
        weight = jnp.where(row_step >= step, jnp.exp(dots[step] - top), 0.0)
        total = total + weight
        summed = summed + weight.astype(BF).astype(F32) * fresh_values[step]
    result = (summed / total).astype(BF)
    for c in range(count):
        for j in range(2):
            half = result[j * rows : (j + 1) * rows] if j < heads else jnp.zeros((rows, hd), BF)
            outs[c][:rows, j * hd : (j + 1) * hd] = half
        if c:
            outs[c][rows:, :] = states[c - 1][...]
    tile = pick_ref.shape[4]
    for side, ref in ((1, sent_ref), (0, kept_ref)):
        for j in range(heads):
            for k in range(ref.shape[1]):
                total = None
                for c in range(count):
                    piece = pieces[c][j * BLOCK : (j + 1) * BLOCK, :].reshape(-1, tile, 2 * hd)
                    term = piece * pick_ref[side, j, k, c][None]
                    total = term if total is None else total + term
                ref[j, k] = total.reshape(BLOCK, 2 * hd)


def collect(count, heads, steps, group, slope_ref, base_ref, home_ref, *rest):
    parts = rest[:1] + rest[1:count][::-1]
    states = [home_ref, *parts[1:]]
    out_ref, mamba_ref, scratch = rest[count:]
    me = lax.axis_index("seq")
    ns, part = slope_ref.shape[2:]
    for c in range(count):
        first = states[c].shape[0] - state_rows(part)
        rows = [
            states[c][first + 16 * i : first + 16 * (i + 1), :].astype(F32)
            for i in range(pl.cdiv(part, 256))
        ]
        state = jnp.concatenate(rows, axis=1)[:, :part]
        for step in range(steps):
            mamba_ref[step, me ^ c] = base_ref[c, step] + jnp.sum(
                slope_ref[c, step] * state, axis=0, keepdims=True
            )
    for c in range(count):
        rows = parts[c][: steps * group, :].astype(F32)
        for j in range(heads):
            for step in range(steps):
                at = pl.multiple_of((step * count + (me ^ c)) * group, group)
                cut = rows[step * group : (step + 1) * group, j * 128 : (j + 1) * 128]
                scratch[j, pl.ds(at, group), :] = cut
    for j in range(heads):
        for g in range(group):
            at = (j * group + g) * 128
            tile = scratch[j, pl.ds(g, steps * count, stride=group), :]
            out_ref[:, at : at + 128] = tile.astype(BF)


def weight_half(weight_ref, out_ref, which, copy):
    half = out_ref.shape[0]
    rows = half // PIECES
    cuts = [(pl.ds(which * half + i * rows, rows), pl.ds(i * rows, rows)) for i in range(PIECES)]
    return [copy(weight_ref.at[src], out_ref.at[dst]) for src, dst in cuts]


def project_own(attn_ref, weight_ref, out_ref):
    out_ref[...] = dot_f32(attn_ref[...], weight_ref[...], ((1,), (0,)))


def pick(options, index):
    chosen = options[0]
    for i in range(1, len(options)):
        chosen = jnp.where(index == i, options[i], chosen)
    return chosen


def project_other(heads_count, count, acc_ref, attn_ref, weight_ref, *outs):
    total = acc_ref[...] + dot_f32(attn_ref[...], weight_ref[...], ((1,), (0,)))
    head = lax.axis_index("head")
    steps = total.shape[0] // count
    share = count // heads_count
    for step in range(steps):
        slices = [
            total[step * count + x * share : step * count + (x + 1) * share]
            for x in range(heads_count)
        ]
        for c in range(heads_count):
            outs[c][step] = pick(slices, head ^ c)


def add_up(*refs):
    total = refs[0][...]
    for ref in refs[1:-1]:
        total = total + ref[...]
    refs[-1][...] = total.astype(BF)


def prepare(count, split, weight_hbm, dt_hbm, x_hbm, bc_hbm, gain_hbm, log_hbm, own_ref, other_ref,
            slope_ref, base_ref, dt_ref, x_ref, bc_ref, gain_ref, log_ref, sems, weight_sems):
    copy = copier(sems)
    first = [
        copy(dt_hbm, dt_ref),
        copy(x_hbm, x_ref),
        copy(bc_hbm, bc_ref),
        copy(gain_hbm, gain_ref),
        copy(log_hbm, log_ref),
    ]
    copy, which = copier(weight_sems), lax.axis_index("rep")
    weights = weight_half(weight_hbm, own_ref, which, copy)
    weights += weight_half(weight_hbm, other_ref, 1 - which, copy)
    for move in first + weights:
        move.start()
    for move in first:
        move.wait()
    me, rep = lax.axis_index("seq"), lax.axis_index("rep")
    _, steps, ns, part = slope_ref.shape
    block = part * 2 if split else part
    diagonal = lax.broadcasted_iota(jnp.int32, (ns, ns), 0) == lax.broadcasted_iota(
        jnp.int32, (ns, ns), 1
    )

    def column(row):
        return jnp.sum(jnp.where(diagonal, row, 0.0), axis=1, keepdims=True)

    drive = [column(bc_ref[step, 0, 0:1, :]) for step in range(steps)]
    read = [column(bc_ref[step, 0, 1:2, :]) for step in range(steps)]
    for c in range(count):
        first = (me ^ c) * block + (rep * part if split else 0)
        lanes = pl.ds(pl.multiple_of(first, 128), part)
        rate = -jnp.exp(log_ref[:, lanes])
        gain = gain_ref[:, lanes]
        kept = jnp.ones((ns, part), F32)
        added = jnp.zeros((ns, part), F32)
        for step in range(steps):
            dt = dt_ref[step, :, lanes]
            inputs = x_ref[step : step + 1, lanes].astype(F32)
            decay = jnp.exp(dt * rate)
            kept = kept * decay
            added = added * decay + drive[step] * (dt * inputs)
            slope_ref[c, step] = read[step] * kept
            base_ref[c, step] = (
                jnp.sum(read[step] * added, axis=0, keepdims=True) + gain * inputs
            )
    for move in weights:
        move.wait()


def assemble(split, kept_ref, got_ref, mamba_ref, *rest):
    rep = lax.axis_index("rep")
    if split:
        other_ref, handoff_ref, out_ref, sems = rest
    else:
        handoff_ref, out_ref, sems = rest
    heads = kept_ref.shape[0]
    copy = copier(sems)
    moves = [
        copy(kept_ref, handoff_ref.at[0, pl.ds(rep * heads, heads)]),
        copy(got_ref, handoff_ref.at[0, pl.ds((1 - rep) * heads, heads)]),
    ]
    steps, count, _, part = mamba_ref.shape
    for step in range(steps):
        for b in range(count):
            if split:
                for ref, side in ((mamba_ref, rep), (other_ref, 1 - rep)):
                    lanes = pl.ds(pl.multiple_of((2 * b + side) * part, 128), part)
                    moves.append(copy(ref.at[step, b], out_ref.at[step, :, lanes]))
            else:
                moves.append(copy(mamba_ref.at[step, b], out_ref.at[step, :, pl.ds(b * part, part)]))
    run_all(moves)


def per_device(
    prefill_kv,
    kept_blocks,
    kept_counts,
    queries,
    new_kv,
    out_weight,
    prefill_state,
    a_log,
    step_input,
    step_dt,
    step_bc,
    skip_gain,
):
    count = lax.axis_size("seq")
    reps = lax.axis_size("rep")
    heads_count = lax.axis_size("head")
    requests, heads, tokens, width = prefill_kv.shape
    assert requests == count and tokens == BLOCK and reps == 2 and width == 256
    assert count & (count - 1) == 0 and heads_count & (heads_count - 1) == 0
    keep = kept_blocks.shape[2]
    keep_rep = keep // reps
    steps, _, q_heads, hd = queries.shape
    dec_heads = new_kv.shape[2]
    group = q_heads // dec_heads
    _, ns, block = prefill_state.shape
    split = block % (reps * 128) == 0
    part = block // reps if split else block
    all_rows = heads * steps * group
    assert all_rows <= 128
    channels = count * block
    shape = jax.ShapeDtypeStruct
    smem = pltpu.SMEM
    blocks = jnp.swapaxes(kept_blocks, 1, 2)

    prefill_kv, prefill_state, queries, new_kv = map(in_hbm, (prefill_kv, prefill_state, queries, new_kv))
    step_dt, step_bc, a_log, out_weight = map(in_hbm, (step_dt, step_bc, a_log, out_weight))
    step_input = in_hbm(step_input.reshape(steps, channels))
    skip_gain = in_hbm(skip_gain.reshape(1, -1))
    blocks, kept_counts = in_hbm(blocks), in_hbm(kept_counts)

    columns = out_weight.shape[1]
    half = heads * group * hd
    half_weight = pltpu.VMEM((half, columns), BF)
    *pieces, q_near, new_near, bias, picks = call(
        functools.partial(stage, count),
        [shape((heads * BLOCK, width), BF)] * count
        + [
            shape(queries.shape, BF),
            shape(new_kv.shape, BF),
            shape((all_rows, count * BLOCK), F32),
            shape((reps, heads, keep_rep, count, 16, width), BF),
        ],
        [HB] * 5,
        [VM] * (count + 4),
        [
            smem(blocks.shape, jnp.int32),
            smem(kept_counts.shape, jnp.int32),
            DMA((count * heads + 2,)),
            DMA((2,)),
        ],
    )(prefill_kv, queries, new_kv, blocks, kept_counts)
    moved = [shift(pieces[c], "seq", c) for c in range(count - 1, 0, -1)][::-1]
    states = call(
        functools.partial(stage_state, count, split),
        [shape((state_rows(part), width), BF)] * count,
        [HB],
        [VM] * count,
        [pltpu.VMEM((count, ns, part), F32), DMA((count,))],
    )(*after([prefill_state], pieces[0]))
    own_weight, other_weight, slope, base = call(
        functools.partial(prepare, count, split),
        [
            half_weight,
            half_weight,
            shape((count, steps, ns, part), F32),
            shape((count, steps, 1, part), F32),
        ],
        [HB] * 6,
        [VM] * 4,
        [
            pltpu.VMEM((steps, 1, channels), F32),
            pltpu.VMEM((steps, channels), BF),
            pltpu.VMEM(step_bc.shape, F32),
            pltpu.VMEM((1, channels), F32),
            pltpu.VMEM(a_log.shape, F32),
            DMA((5,)),
            DMA((2 * PIECES,)),
        ],
    )(*after([out_weight], pieces[0]), step_dt, step_input, step_bc, skip_gain, a_log)

    *moved, own_weight = after([*moved[::-1], own_weight])
    kv = [pieces[0], *moved[::-1]]
    half_shape = (heads, keep_rep, BLOCK, width)
    rows = steps * group
    *sends, kept, sent = call(
        functools.partial(attend, count, heads),
        [shape((rows, width), BF)]
        + [shape((rows + state_rows(part), width), BF)] * (count - 1)
        + [shape(half_shape, BF)] * 2,
        [VM] * (3 + 2 * count),
        [VM] * (count + 2),
    )(q_near, new_near, bias, picks, *kv, *states[1:])
    gathered = [shift(sends[c], "seq", c) for c in range(count - 1, 0, -1)]
    attn, mamba = call(
        functools.partial(collect, count, heads, steps, group),
        [shape((steps * count, half), BF), shape((steps, count, 1, part), F32)],
        [VM] * (3 + count),
        [VM] * 2,
        [pltpu.VMEM((heads, steps * count * group, hd), F32)],
    )(slope, base, states[0], sends[0], *gathered)
    attn_other = shift(attn, "rep", 1)
    own_sum = call(
        project_own, shape((steps * count, columns), F32), [VM, VM], VM, us=0.7
    )(attn, own_weight)
    share = count // heads_count
    sums = call(
        functools.partial(project_other, heads_count, count),
        [shape((steps, share, columns), F32)] * heads_count,
        [VM, VM, VM],
        [VM] * heads_count,
        us=0.7,
    )(own_sum, attn_other, other_weight)
    sums = [sums[0]] + [shift(sums[c], "head", c) for c in range(1, heads_count)]
    got = shift(after([sent], mamba)[0], "rep", 1)
    kept = after([kept], sums[0])[0]
    operands = [kept, got, mamba] + ([shift(mamba, "rep", 1)] if split else [])
    handoff, mamba_out = call(
        functools.partial(assemble, split),
        [
            shape((1, dec_heads, keep_rep, BLOCK, width), BF),
            shape((steps, 1, channels), F32),
        ],
        [VM] * len(operands),
        [HB] * 2,
        [DMA((2 + steps * count * (2 if split else 1),))],
    )(*operands)
    sums[1:] = after(sums[1:], handoff)
    proj_out = call(
        add_up, shape((steps, share, columns), BF), [VM] * heads_count, VM, us=0.6
    )(*sums)
    return handoff, proj_out, mamba_out


def solution(mesh):
    return jax.shard_map(
        per_device,
        mesh=mesh,
        in_specs=(
            P("groups", ("head", "rep"), "seq", None),
            P("groups", None, None),
            P("groups", None),
            P(None, ("groups", "seq"), "head", None),
            P(None, ("groups", "seq"), "head", None),
            P("head", ("seq", "rep")),
            P("groups", None, ("head", "seq")),
            P(None, "head"),
            P(None, ("groups", "seq"), "head"),
            P(None, ("groups", "seq"), "head"),
            P(None, ("groups", "seq"), None, None),
            P("head"),
        ),
        out_specs=(
            P(("groups", "seq"), "head", "rep", None, None),
            P(None, ("groups", "head"), ("seq", "rep")),
            P(None, ("groups", "seq"), "head"),
        ),
        check_vma=False,
    )
```

```python
import functools

import jax
import jax.numpy as jnp
from jax import lax
from jax.experimental import pallas as pl
from jax.experimental.pallas import tpu as pltpu
from jax.sharding import PartitionSpec as P

BLOCK = 128
PIECES = 4
NEG = -1e30
BF = jnp.bfloat16
F32 = jnp.float32
VM = pl.BlockSpec(memory_space=pltpu.VMEM)
HB = pl.BlockSpec(memory_space=pltpu.HBM)
DMA = pltpu.SemaphoreType.DMA


def shift(x, axis, c):
    size = lax.axis_size(axis)
    return lax.ppermute(x, axis, [(i, i ^ c) for i in range(size)])


def call(body, out_shape, in_specs, out_specs, scratch=(), us=1.0):
    return pl.pallas_call(
        body,
        out_shape=out_shape,
        in_specs=in_specs,
        out_specs=out_specs,
        scratch_shapes=list(scratch),
        cost_estimate=pl.CostEstimate(
            flops=0, bytes_accessed=int(us * 3.6e4), transcendentals=0
        ),
        compiler_params=pltpu.CompilerParams(vmem_limit_bytes=32 * 1024 * 1024),
    )


def in_hbm(x):
    return pltpu.with_memory_space_constraint(x, pltpu.HBM)


def after(arrays, *earlier):
    return lax.optimization_barrier((*arrays, *earlier))[: len(arrays)]


def run_all(copies):
    for copy in copies:
        copy.start()
    for copy in copies:
        copy.wait()


def copier(sems):
    position = iter(range(sems.shape[0]))
    return lambda src, dst: pltpu.make_async_copy(src, dst, sems.at[next(position)])


def state_rows(part):
    return 16 * pl.cdiv(part, 256)


def pack_state(piece, out_ref, first):
    ns, part = piece.shape
    for i in range(pl.cdiv(part, 256)):
        cut = piece[:, i * 256 : (i + 1) * 256]
        if cut.shape[1] < 256:
            cut = jnp.concatenate([cut, jnp.zeros((ns, 256 - cut.shape[1]), F32)], axis=1)
        out_ref[first + i * 16 : first + (i + 1) * 16, :] = cut.astype(BF)


def own_state(state_ref, c, split, part):
    me, rep = lax.axis_index("seq"), lax.axis_index("rep")
    if split:
        return state_ref.at[me ^ c, :, pl.ds(pl.multiple_of(rep * part, 128), part)]
    return state_ref.at[me ^ c]


def stage(count, kv_ref, q_ref, new_ref, blocks_ref, counts_ref, *rest):
    pieces = rest[:count]
    q_out, new_out, bias_out, pick_out, blocks, counts, sems, early = rest[count:]
    me, rep = lax.axis_index("seq"), lax.axis_index("rep")
    heads = kv_ref.shape[1]
    copy = copier(sems)
    moves = []
    for c in range(count - 1, -1, -1):
        for j in range(heads):
            moves.append(copy(kv_ref.at[me ^ c, j], pieces[c].at[pl.ds(j * BLOCK, BLOCK)]))
    moves += [copy(q_ref, q_out), copy(new_ref, new_out)]
    copy = copier(early)
    first = [copy(blocks_ref, blocks), copy(counts_ref, counts)]
    for move in moves + first:
        move.start()
    for move in first:
        move.wait()
    head_first = lax.axis_index("head") * new_ref.shape[2] + rep * heads
    rows = bias_out.shape[0] // heads
    keep_rep = pick_out.shape[2]
    for j in range(heads):
        live_count = counts[me, head_first + j]
        for c in range(count):
            live = jnp.int32(0)
            for side in range(2):
                for k in range(keep_rep):
                    slot = (rep if side == 0 else 1 - rep) * keep_rep + k
                    hit = (blocks[me, slot, head_first + j] == (me ^ c)) & (slot < live_count)
                    one = jnp.where(hit, 1.0, 0.0).astype(F32)
                    pick_out[side, j, k, c] = jnp.full(pick_out.shape[4:], one, F32).astype(BF)
                    live = live | hit.astype(jnp.int32)
            dead = jnp.where(live > 0, 0.0, NEG).astype(F32)
            bias_out[j * rows : (j + 1) * rows, c * BLOCK : (c + 1) * BLOCK] = jnp.full(
                (rows, BLOCK), dead, F32
            )
    for move in moves:
        move.wait()


def stage_state(count, split, state_ref, *rest):
    outs, loaded, sems = rest[:count], rest[count], rest[count + 1]
    copy = copier(sems)
    run_all(
        [copy(own_state(state_ref, c, split, loaded.shape[2]), loaded.at[c]) for c in range(count)]
    )
    for c in range(count):
        pack_state(loaded[c], outs[c], 0)


def dot_f32(a, b, contract):
    return lax.dot_general(a, b, (contract, ((), ())), preferred_element_type=F32)


def query_rows(q_ref, heads):
    rep = lax.axis_index("rep")
    steps, _, q_heads, _ = q_ref.shape
    own_q = q_heads // 2
    group = own_q // heads
    q_all = [q_ref[step, 0].astype(F32) for step in range(steps)]
    q_all = [jnp.where(rep == 0, q[:own_q], q[own_q:]) for q in q_all]
    return [
        jnp.concatenate([x[j * group : (j + 1) * group] for x in q_all], axis=0)
        for j in range(heads)
    ]


def block_scores(q, piece_ref, j):
    hd = piece_ref.shape[1] // 2
    keys = piece_ref[j * BLOCK : (j + 1) * BLOCK, :hd]
    return dot_f32(q.astype(BF), keys, ((1,), (1,))) * hd ** (-0.5)


def block_sums(weights, piece_ref, j):
    values = piece_ref[j * BLOCK : (j + 1) * BLOCK, piece_ref.shape[1] // 2 :]
    return dot_f32(weights, values, ((1,), (0,)))


def attend(count, heads, q_ref, new_ref, bias_ref, pick_ref, *rest):
    pieces, states = rest[:count], rest[count : 2 * count]
    out_ref, kept_ref, sent_ref = rest[2 * count :]
    rep = lax.axis_index("rep")
    queries = query_rows(q_ref, heads)
    rows, hd = queries[0].shape
    steps = q_ref.shape[0]
    group = rows // steps
    all_rows = heads * rows
    scale = hd ** (-0.5)
    scores = [
        jnp.concatenate([block_scores(q, piece, j) for piece in pieces], axis=1)
        for j, q in enumerate(queries)
    ]
    scores = jnp.concatenate(scores, axis=0)
    alive = bias_ref[...] == 0.0
    scores = jnp.where(alive, scores, NEG)
    row_step = (lax.broadcasted_iota(jnp.int32, (all_rows, 1), 0) // group) % steps
    wide_q = jnp.concatenate(queries, axis=0)
    dots, fresh_values = [], []
    top = jnp.max(scores, axis=1, keepdims=True)
    for step in range(steps):
        both = new_ref[step, 0].astype(F32)
        fresh = jnp.where(rep == 0, both[:heads], both[heads:])
        wide = jnp.concatenate(
            [jnp.broadcast_to(fresh[j : j + 1], (rows, 2 * hd)) for j in range(heads)], axis=0
        )
        dot = jnp.sum(wide_q * wide[:, :hd], axis=1, keepdims=True) * scale
        dots.append(jnp.where(row_step >= step, dot, NEG))
        fresh_values.append(wide[:, hd:])
        top = jnp.maximum(top, dots[-1])
    weights = jnp.where(alive, jnp.exp(scores - top), 0.0)
    total = jnp.sum(weights, axis=1, keepdims=True)
    weights = weights.astype(BF)
    summed = []
    for j in range(heads):
        parts = [
            block_sums(weights[j * rows : (j + 1) * rows, c * BLOCK : (c + 1) * BLOCK], piece, j)
            for c, piece in enumerate(pieces)
        ]
        summed.append(functools.reduce(jnp.add, parts))
    summed = jnp.concatenate(summed, axis=0)
    for step in range(steps):
        weight = jnp.where(row_step >= step, jnp.exp(dots[step] - top), 0.0)
        total = total + weight
        summed = summed + weight.astype(BF).astype(F32) * fresh_values[step]
    result = (summed / total).astype(BF)
    me = lax.axis_index("seq")
    for c in range(count):
        for j in range(2):
            half = result[j * rows : (j + 1) * rows] if j < heads else jnp.zeros((rows, hd), BF)
            out_ref[me ^ c, :rows, j * hd : (j + 1) * hd] = half
        out_ref[me ^ c, rows:, :] = states[c][...]
    tile = pick_ref.shape[4]
    for side, ref in ((1, sent_ref), (0, kept_ref)):
        for j in range(heads):
            for k in range(ref.shape[1]):
                total = None
                for c in range(count):
                    piece = pieces[c][j * BLOCK : (j + 1) * BLOCK, :].reshape(-1, tile, 2 * hd)
                    term = piece * pick_ref[side, j, k, c][None]
                    total = term if total is None else total + term
                ref[j, k] = total.reshape(BLOCK, 2 * hd)


def collect(count, heads, steps, group, slope_ref, base_ref, got_ref, out_ref, mamba_ref, scratch):
    me = lax.axis_index("seq")
    parts = [got_ref.at[me ^ c] for c in range(count)]
    states = parts
    ns, part = slope_ref.shape[2:]
    for c in range(count):
        first = states[c].shape[0] - state_rows(part)
        rows = [
            states[c][first + 16 * i : first + 16 * (i + 1), :].astype(F32)
            for i in range(pl.cdiv(part, 256))
        ]
        state = jnp.concatenate(rows, axis=1)[:, :part]
        for step in range(steps):
            mamba_ref[step, me ^ c] = base_ref[c, step] + jnp.sum(
                slope_ref[c, step] * state, axis=0, keepdims=True
            )
    for c in range(count):
        rows = parts[c][: steps * group, :].astype(F32)
        for j in range(heads):
            for step in range(steps):
                at = pl.multiple_of((step * count + (me ^ c)) * group, group)
                cut = rows[step * group : (step + 1) * group, j * 128 : (j + 1) * 128]
                scratch[j, pl.ds(at, group), :] = cut
    for j in range(heads):
        for g in range(group):
            at = (j * group + g) * 128
            tile = scratch[j, pl.ds(g, steps * count, stride=group), :]
            out_ref[:, at : at + 128] = tile.astype(BF)


def weight_half(weight_ref, out_ref, which, copy):
    half = out_ref.shape[0]
    rows = half // PIECES
    cuts = [(pl.ds(which * half + i * rows, rows), pl.ds(i * rows, rows)) for i in range(PIECES)]
    return [copy(weight_ref.at[src], out_ref.at[dst]) for src, dst in cuts]


def project_own(attn_ref, weight_ref, out_ref):
    out_ref[...] = dot_f32(attn_ref[...], weight_ref[...], ((1,), (0,)))


def pick(options, index):
    chosen = options[0]
    for i in range(1, len(options)):
        chosen = jnp.where(index == i, options[i], chosen)
    return chosen


def project_other(heads_count, count, acc_ref, attn_ref, weight_ref, *outs):
    total = acc_ref[...] + dot_f32(attn_ref[...], weight_ref[...], ((1,), (0,)))
    head = lax.axis_index("head")
    steps = total.shape[0] // count
    share = count // heads_count
    for step in range(steps):
        slices = [
            total[step * count + x * share : step * count + (x + 1) * share]
            for x in range(heads_count)
        ]
        for c in range(heads_count):
            outs[c][step] = pick(slices, head ^ c)


def add_up(*refs):
    total = refs[0][...]
    for ref in refs[1:-1]:
        total = total + ref[...]
    refs[-1][...] = total.astype(BF)


def prepare(count, split, weight_hbm, dt_hbm, x_hbm, bc_hbm, gain_hbm, log_hbm, own_ref, other_ref,
            slope_ref, base_ref, dt_ref, x_ref, bc_ref, gain_ref, log_ref, sems, weight_sems):
    copy = copier(sems)
    first = [
        copy(dt_hbm, dt_ref),
        copy(x_hbm, x_ref),
        copy(bc_hbm, bc_ref),
        copy(gain_hbm, gain_ref),
        copy(log_hbm, log_ref),
    ]
    copy, which = copier(weight_sems), lax.axis_index("rep")
    weights = weight_half(weight_hbm, own_ref, which, copy)
    weights += weight_half(weight_hbm, other_ref, 1 - which, copy)
    for move in first + weights:
        move.start()
    for move in first:
        move.wait()
    me, rep = lax.axis_index("seq"), lax.axis_index("rep")
    _, steps, ns, part = slope_ref.shape
    block = part * 2 if split else part
    diagonal = lax.broadcasted_iota(jnp.int32, (ns, ns), 0) == lax.broadcasted_iota(
        jnp.int32, (ns, ns), 1
    )

    def column(row):
        return jnp.sum(jnp.where(diagonal, row, 0.0), axis=1, keepdims=True)

    drive = [column(bc_ref[step, 0, 0:1, :]) for step in range(steps)]
    read = [column(bc_ref[step, 0, 1:2, :]) for step in range(steps)]
    for c in range(count):
        first = (me ^ c) * block + (rep * part if split else 0)
        lanes = pl.ds(pl.multiple_of(first, 128), part)
        rate = -jnp.exp(log_ref[:, lanes])
        gain = gain_ref[:, lanes]
        kept = jnp.ones((ns, part), F32)
        added = jnp.zeros((ns, part), F32)
        for step in range(steps):
            dt = dt_ref[step, :, lanes]
            inputs = x_ref[step : step + 1, lanes].astype(F32)
            decay = jnp.exp(dt * rate)
            kept = kept * decay
            added = added * decay + drive[step] * (dt * inputs)
            slope_ref[c, step] = read[step] * kept
            base_ref[c, step] = (
                jnp.sum(read[step] * added, axis=0, keepdims=True) + gain * inputs
            )
    for move in weights:
        move.wait()


def assemble(split, kept_ref, got_ref, mamba_ref, *rest):
    rep = lax.axis_index("rep")
    if split:
        other_ref, handoff_ref, out_ref, sems = rest
    else:
        handoff_ref, out_ref, sems = rest
    heads = kept_ref.shape[0]
    copy = copier(sems)
    moves = [
        copy(kept_ref, handoff_ref.at[0, pl.ds(rep * heads, heads)]),
        copy(got_ref, handoff_ref.at[0, pl.ds((1 - rep) * heads, heads)]),
    ]
    steps, count, _, part = mamba_ref.shape
    for step in range(steps):
        for b in range(count):
            if split:
                for ref, side in ((mamba_ref, rep), (other_ref, 1 - rep)):
                    lanes = pl.ds(pl.multiple_of((2 * b + side) * part, 128), part)
                    moves.append(copy(ref.at[step, b], out_ref.at[step, :, lanes]))
            else:
                moves.append(copy(mamba_ref.at[step, b], out_ref.at[step, :, pl.ds(b * part, part)]))
    run_all(moves)


def per_device(
    prefill_kv,
    kept_blocks,
    kept_counts,
    queries,
    new_kv,
    out_weight,
    prefill_state,
    a_log,
    step_input,
    step_dt,
    step_bc,
    skip_gain,
):
    count = lax.axis_size("seq")
    reps = lax.axis_size("rep")
    heads_count = lax.axis_size("head")
    requests, heads, tokens, width = prefill_kv.shape
    assert requests == count and tokens == BLOCK and reps == 2 and width == 256
    assert count & (count - 1) == 0 and heads_count & (heads_count - 1) == 0
    keep = kept_blocks.shape[2]
    keep_rep = keep // reps
    steps, _, q_heads, hd = queries.shape
    dec_heads = new_kv.shape[2]
    group = q_heads // dec_heads
    _, ns, block = prefill_state.shape
    split = block % (reps * 128) == 0
    part = block // reps if split else block
    all_rows = heads * steps * group
    assert all_rows <= 128
    channels = count * block
    shape = jax.ShapeDtypeStruct
    smem = pltpu.SMEM
    blocks = jnp.swapaxes(kept_blocks, 1, 2)

    prefill_kv, prefill_state, queries, new_kv = map(in_hbm, (prefill_kv, prefill_state, queries, new_kv))
    step_dt, step_bc, a_log, out_weight = map(in_hbm, (step_dt, step_bc, a_log, out_weight))
    step_input = in_hbm(step_input.reshape(steps, channels))
    skip_gain = in_hbm(skip_gain.reshape(1, -1))
    blocks, kept_counts = in_hbm(blocks), in_hbm(kept_counts)

    columns = out_weight.shape[1]
    half = heads * group * hd
    half_weight = pltpu.VMEM((half, columns), BF)
    *pieces, q_near, new_near, bias, picks = call(
        functools.partial(stage, count),
        [shape((heads * BLOCK, width), BF)] * count
        + [
            shape(queries.shape, BF),
            shape(new_kv.shape, BF),
            shape((all_rows, count * BLOCK), F32),
            shape((reps, heads, keep_rep, count, 16, width), BF),
        ],
        [HB] * 5,
        [VM] * (count + 4),
        [
            smem(blocks.shape, jnp.int32),
            smem(kept_counts.shape, jnp.int32),
            DMA((count * heads + 2,)),
            DMA((2,)),
        ],
    )(prefill_kv, queries, new_kv, blocks, kept_counts)
    moved = [shift(pieces[c], "seq", c) for c in range(count - 1, 0, -1)][::-1]
    states = call(
        functools.partial(stage_state, count, split),
        [shape((state_rows(part), width), BF)] * count,
        [HB],
        [VM] * count,
        [pltpu.VMEM((count, ns, part), F32), DMA((count,))],
    )(*after([prefill_state], pieces[0]))
    own_weight, other_weight, slope, base = call(
        functools.partial(prepare, count, split),
        [
            half_weight,
            half_weight,
            shape((count, steps, ns, part), F32),
            shape((count, steps, 1, part), F32),
        ],
        [HB] * 6,
        [VM] * 4,
        [
            pltpu.VMEM((steps, 1, channels), F32),
            pltpu.VMEM((steps, channels), BF),
            pltpu.VMEM(step_bc.shape, F32),
            pltpu.VMEM((1, channels), F32),
            pltpu.VMEM(a_log.shape, F32),
            DMA((5,)),
            DMA((2 * PIECES,)),
        ],
    )(*after([out_weight], pieces[0]), step_dt, step_input, step_bc, skip_gain, a_log)

    *moved, own_weight = after([*moved[::-1], own_weight])
    kv = [pieces[0], *moved[::-1]]
    half_shape = (heads, keep_rep, BLOCK, width)
    rows = steps * group
    sends, kept, sent = call(
        functools.partial(attend, count, heads),
        [shape((count, rows + state_rows(part), width), BF)] + [shape(half_shape, BF)] * 2,
        [VM] * (4 + 2 * count),
        [VM] * 3,
    )(q_near, new_near, bias, picks, *kv, *states)
    gathered = lax.all_to_all(sends, "seq", split_axis=0, concat_axis=0, tiled=True)
    attn, mamba = call(
        functools.partial(collect, count, heads, steps, group),
        [shape((steps * count, half), BF), shape((steps, count, 1, part), F32)],
        [VM] * 3,
        [VM] * 2,
        [pltpu.VMEM((heads, steps * count * group, hd), F32)],
    )(slope, base, gathered)
    attn_other = shift(attn, "rep", 1)
    own_sum = call(
        project_own, shape((steps * count, columns), F32), [VM, VM], VM, us=0.7
    )(attn, own_weight)
    share = count // heads_count
    sums = call(
        functools.partial(project_other, heads_count, count),
        [shape((steps, share, columns), F32)] * heads_count,
        [VM, VM, VM],
        [VM] * heads_count,
        us=0.7,
    )(own_sum, attn_other, other_weight)
    sums = [sums[0]] + [shift(sums[c], "head", c) for c in range(1, heads_count)]
    got = shift(after([sent], mamba)[0], "rep", 1)
    kept = after([kept], sums[0])[0]
    operands = [kept, got, mamba] + ([shift(mamba, "rep", 1)] if split else [])
    handoff, mamba_out = call(
        functools.partial(assemble, split),
        [
            shape((1, dec_heads, keep_rep, BLOCK, width), BF),
            shape((steps, 1, channels), F32),
        ],
        [VM] * len(operands),
        [HB] * 2,
        [DMA((2 + steps * count * (2 if split else 1),))],
    )(*operands)
    sums[1:] = after(sums[1:], handoff)
    proj_out = call(
        add_up, shape((steps, share, columns), BF), [VM] * heads_count, VM, us=0.6
    )(*sums)
    return handoff, proj_out, mamba_out


def solution(mesh):
    return jax.shard_map(
        per_device,
        mesh=mesh,
        in_specs=(
            P("groups", ("head", "rep"), "seq", None),
            P("groups", None, None),
            P("groups", None),
            P(None, ("groups", "seq"), "head", None),
            P(None, ("groups", "seq"), "head", None),
            P("head", ("seq", "rep")),
            P("groups", None, ("head", "seq")),
            P(None, "head"),
            P(None, ("groups", "seq"), "head"),
            P(None, ("groups", "seq"), "head"),
            P(None, ("groups", "seq"), None, None),
            P("head"),
        ),
        out_specs=(
            P(("groups", "seq"), "head", "rep", None, None),
            P(None, ("groups", "head"), ("seq", "rep")),
            P(None, ("groups", "seq"), "head"),
        ),
        check_vma=False,
    )
```

```python
import functools

import jax
import jax.numpy as jnp
from jax import lax
from jax.experimental import pallas as pl
from jax.experimental.pallas import tpu as pltpu
from jax.sharding import PartitionSpec as P

BLOCK = 128
PIECES = 4
NEG = -1e30
BF = jnp.bfloat16
F32 = jnp.float32
VM = pl.BlockSpec(memory_space=pltpu.VMEM)
HB = pl.BlockSpec(memory_space=pltpu.HBM)
DMA = pltpu.SemaphoreType.DMA


def shift(x, axis, c):
    size = lax.axis_size(axis)
    return lax.ppermute(x, axis, [(i, i ^ c) for i in range(size)])


def call(body, out_shape, in_specs, out_specs, scratch=(), us=1.0):
    return pl.pallas_call(
        body,
        out_shape=out_shape,
        in_specs=in_specs,
        out_specs=out_specs,
        scratch_shapes=list(scratch),
        cost_estimate=pl.CostEstimate(
            flops=0, bytes_accessed=int(us * 3.6e4), transcendentals=0
        ),
        compiler_params=pltpu.CompilerParams(vmem_limit_bytes=32 * 1024 * 1024),
    )


def in_hbm(x):
    return pltpu.with_memory_space_constraint(x, pltpu.HBM)


def after(arrays, *earlier):
    return lax.optimization_barrier((*arrays, *earlier))[: len(arrays)]


def run_all(copies):
    for copy in copies:
        copy.start()
    for copy in copies:
        copy.wait()


def copier(sems):
    position = iter(range(sems.shape[0]))
    return lambda src, dst: pltpu.make_async_copy(src, dst, sems.at[next(position)])


def state_rows(part):
    return 16 * pl.cdiv(part, 256)


def pack_state(piece, out_ref, first):
    ns, part = piece.shape
    for i in range(pl.cdiv(part, 256)):
        cut = piece[:, i * 256 : (i + 1) * 256]
        if cut.shape[1] < 256:
            cut = jnp.concatenate([cut, jnp.zeros((ns, 256 - cut.shape[1]), F32)], axis=1)
        out_ref[first + i * 16 : first + (i + 1) * 16, :] = cut.astype(BF)


def own_state(state_ref, c, split, part):
    me, rep = lax.axis_index("seq"), lax.axis_index("rep")
    if split:
        return state_ref.at[me ^ c, :, pl.ds(pl.multiple_of(rep * part, 128), part)]
    return state_ref.at[me ^ c]


def stage_blocks(count, kv_ref, *rest):
    outs, sems = rest[:-1], rest[-1]
    me = lax.axis_index("seq")
    copy = copier(sems)
    run_all(
        [
            copy(kv_ref.at[me ^ c, j], outs[c - 1].at[pl.ds(j * BLOCK, BLOCK)])
            for c in range(count - 1, 0, -1)
            for j in range(kv_ref.shape[1])
        ]
    )


def stage_rest(count, split, kv_ref, q_ref, new_ref, state_ref, blocks_ref, counts_ref, *rest):
    own_out, q_out, new_out, bias_out, pick_out = rest[:5]
    states = rest[5 : 5 + count]
    loaded, blocks, counts, sems, early = rest[5 + count :]
    me, rep = lax.axis_index("seq"), lax.axis_index("rep")
    heads = kv_ref.shape[1]
    copy = copier(sems)
    moves = [copy(kv_ref.at[me, j], own_out.at[pl.ds(j * BLOCK, BLOCK)]) for j in range(heads)]
    moves += [copy(q_ref, q_out), copy(new_ref, new_out)]
    copy = copier(early)
    first = [copy(blocks_ref, blocks), copy(counts_ref, counts)]
    part = loaded.shape[2]
    for c in range(count):
        if split:
            src = state_ref.at[me ^ c, :, pl.ds(pl.multiple_of(rep * part, 128), part)]
        else:
            src = state_ref.at[me ^ c]
        first.append(copy(src, loaded.at[c]))
    for move in first + moves:
        move.start()
    for move in first:
        move.wait()
    for c in range(count):
        pack_state(loaded[c], states[c], 0)
    head_first = lax.axis_index("head") * new_ref.shape[2] + rep * heads
    rows = bias_out.shape[0] // heads
    keep_rep = pick_out.shape[2]
    for j in range(heads):
        live_count = counts[me, head_first + j]
        for c in range(count):
            live = jnp.int32(0)
            for side in range(2):
                for k in range(keep_rep):
                    slot = (rep if side == 0 else 1 - rep) * keep_rep + k
                    hit = (blocks[me, slot, head_first + j] == (me ^ c)) & (slot < live_count)
                    one = jnp.where(hit, 1.0, 0.0).astype(F32)
                    pick_out[side, j, k, c] = jnp.full(pick_out.shape[4:], one, F32).astype(BF)
                    live = live | hit.astype(jnp.int32)
            dead = jnp.where(live > 0, 0.0, NEG).astype(F32)
            bias_out[j * rows : (j + 1) * rows, c * BLOCK : (c + 1) * BLOCK] = jnp.full(
                (rows, BLOCK), dead, F32
            )
    for move in moves:
        move.wait()


def dot_f32(a, b, contract):
    return lax.dot_general(a, b, (contract, ((), ())), preferred_element_type=F32)


def query_rows(q_ref, heads):
    rep = lax.axis_index("rep")
    steps, _, q_heads, _ = q_ref.shape
    own_q = q_heads // 2
    group = own_q // heads
    q_all = [q_ref[step, 0].astype(F32) for step in range(steps)]
    q_all = [jnp.where(rep == 0, q[:own_q], q[own_q:]) for q in q_all]
    return [
        jnp.concatenate([x[j * group : (j + 1) * group] for x in q_all], axis=0)
        for j in range(heads)
    ]


def block_scores(q, piece_ref, j):
    hd = piece_ref.shape[1] // 2
    keys = piece_ref[j * BLOCK : (j + 1) * BLOCK, :hd]
    return dot_f32(q.astype(BF), keys, ((1,), (1,))) * hd ** (-0.5)


def block_sums(weights, piece_ref, j):
    values = piece_ref[j * BLOCK : (j + 1) * BLOCK, piece_ref.shape[1] // 2 :]
    return dot_f32(weights, values, ((1,), (0,)))


def attend(count, heads, q_ref, new_ref, bias_ref, pick_ref, *rest):
    pieces, states = rest[:count], rest[count : 2 * count - 1]
    outs, (kept_ref, sent_ref) = rest[2 * count - 1 : 3 * count - 1], rest[3 * count - 1 :]
    rep = lax.axis_index("rep")
    queries = query_rows(q_ref, heads)
    rows, hd = queries[0].shape
    steps = q_ref.shape[0]
    group = rows // steps
    all_rows = heads * rows
    scale = hd ** (-0.5)
    scores = [
        jnp.concatenate([block_scores(q, piece, j) for piece in pieces], axis=1)
        for j, q in enumerate(queries)
    ]
    scores = jnp.concatenate(scores, axis=0)
    alive = bias_ref[...] == 0.0
    scores = jnp.where(alive, scores, NEG)
    row_step = (lax.broadcasted_iota(jnp.int32, (all_rows, 1), 0) // group) % steps
    wide_q = jnp.concatenate(queries, axis=0)
    dots, fresh_values = [], []
    top = jnp.max(scores, axis=1, keepdims=True)
    for step in range(steps):
        both = new_ref[step, 0].astype(F32)
        fresh = jnp.where(rep == 0, both[:heads], both[heads:])
        wide = jnp.concatenate(
            [jnp.broadcast_to(fresh[j : j + 1], (rows, 2 * hd)) for j in range(heads)], axis=0
        )
        dot = jnp.sum(wide_q * wide[:, :hd], axis=1, keepdims=True) * scale
        dots.append(jnp.where(row_step >= step, dot, NEG))
        fresh_values.append(wide[:, hd:])
        top = jnp.maximum(top, dots[-1])
    weights = jnp.where(alive, jnp.exp(scores - top), 0.0)
    total = jnp.sum(weights, axis=1, keepdims=True)
    weights = weights.astype(BF)
    summed = []
    for j in range(heads):
        parts = [
            block_sums(weights[j * rows : (j + 1) * rows, c * BLOCK : (c + 1) * BLOCK], piece, j)
            for c, piece in enumerate(pieces)
        ]
        summed.append(functools.reduce(jnp.add, parts))
    summed = jnp.concatenate(summed, axis=0)
    for step in range(steps):
        weight = jnp.where(row_step >= step, jnp.exp(dots[step] - top), 0.0)
        total = total + weight
        summed = summed + weight.astype(BF).astype(F32) * fresh_values[step]
    result = (summed / total).astype(BF)
    for c in range(count):
        for j in range(2):
            half = result[j * rows : (j + 1) * rows] if j < heads else jnp.zeros((rows, hd), BF)
            outs[c][:rows, j * hd : (j + 1) * hd] = half
        if c:
            outs[c][rows:, :] = states[c - 1][...]
    tile = pick_ref.shape[4]
    for side, ref in ((1, sent_ref), (0, kept_ref)):
        for j in range(heads):
            for k in range(ref.shape[1]):
                total = None
                for c in range(count):
                    piece = pieces[c][j * BLOCK : (j + 1) * BLOCK, :].reshape(-1, tile, 2 * hd)
                    term = piece * pick_ref[side, j, k, c][None]
                    total = term if total is None else total + term
                ref[j, k] = total.reshape(BLOCK, 2 * hd)


def collect(count, heads, steps, group, slope_ref, base_ref, home_ref, *rest):
    parts = [rest[0], rest[count - 1], *rest[1 : count - 1]]
    states = [home_ref, *parts[1:]]
    out_ref, mamba_ref, scratch = rest[count:]
    me = lax.axis_index("seq")
    ns, part = slope_ref.shape[2:]
    for c in range(count):
        first = states[c].shape[0] - state_rows(part)
        rows = [
            states[c][first + 16 * i : first + 16 * (i + 1), :].astype(F32)
            for i in range(pl.cdiv(part, 256))
        ]
        state = jnp.concatenate(rows, axis=1)[:, :part]
        for step in range(steps):
            mamba_ref[step, me ^ c] = base_ref[c, step] + jnp.sum(
                slope_ref[c, step] * state, axis=0, keepdims=True
            )
    for c in range(count):
        rows = parts[c][: steps * group, :].astype(F32)
        for j in range(heads):
            for step in range(steps):
                at = pl.multiple_of((step * count + (me ^ c)) * group, group)
                cut = rows[step * group : (step + 1) * group, j * 128 : (j + 1) * 128]
                scratch[j, pl.ds(at, group), :] = cut
    for j in range(heads):
        for g in range(group):
            at = (j * group + g) * 128
            tile = scratch[j, pl.ds(g, steps * count, stride=group), :]
            out_ref[:, at : at + 128] = tile.astype(BF)


def weight_half(weight_ref, out_ref, which, copy):
    half = out_ref.shape[0]
    rows = half // PIECES
    cuts = [(pl.ds(which * half + i * rows, rows), pl.ds(i * rows, rows)) for i in range(PIECES)]
    return [copy(weight_ref.at[src], out_ref.at[dst]) for src, dst in cuts]


def project_own(attn_ref, weight_ref, out_ref):
    out_ref[...] = dot_f32(attn_ref[...], weight_ref[...], ((1,), (0,)))


def pick(options, index):
    chosen = options[0]
    for i in range(1, len(options)):
        chosen = jnp.where(index == i, options[i], chosen)
    return chosen


def project_other(heads_count, count, acc_ref, attn_ref, weight_ref, *outs):
    total = acc_ref[...] + dot_f32(attn_ref[...], weight_ref[...], ((1,), (0,)))
    head = lax.axis_index("head")
    steps = total.shape[0] // count
    share = count // heads_count
    for step in range(steps):
        slices = [
            total[step * count + x * share : step * count + (x + 1) * share]
            for x in range(heads_count)
        ]
        for c in range(heads_count):
            outs[c][step] = pick(slices, head ^ c)


def add_up(*refs):
    total = refs[0][...]
    for ref in refs[1:-1]:
        total = total + ref[...]
    refs[-1][...] = total.astype(BF)


def prepare(count, split, weight_hbm, dt_hbm, x_hbm, bc_hbm, gain_hbm, log_hbm, own_ref, other_ref,
            slope_ref, base_ref, dt_ref, x_ref, bc_ref, gain_ref, log_ref, sems, weight_sems):
    copy = copier(sems)
    first = [
        copy(dt_hbm, dt_ref),
        copy(x_hbm, x_ref),
        copy(bc_hbm, bc_ref),
        copy(gain_hbm, gain_ref),
        copy(log_hbm, log_ref),
    ]
    copy, which = copier(weight_sems), lax.axis_index("rep")
    weights = weight_half(weight_hbm, own_ref, which, copy)
    weights += weight_half(weight_hbm, other_ref, 1 - which, copy)
    for move in first + weights:
        move.start()
    for move in first:
        move.wait()
    me, rep = lax.axis_index("seq"), lax.axis_index("rep")
    _, steps, ns, part = slope_ref.shape
    block = part * 2 if split else part
    diagonal = lax.broadcasted_iota(jnp.int32, (ns, ns), 0) == lax.broadcasted_iota(
        jnp.int32, (ns, ns), 1
    )

    def column(row):
        return jnp.sum(jnp.where(diagonal, row, 0.0), axis=1, keepdims=True)

    drive = [column(bc_ref[step, 0, 0:1, :]) for step in range(steps)]
    read = [column(bc_ref[step, 0, 1:2, :]) for step in range(steps)]
    for c in range(count):
        first = (me ^ c) * block + (rep * part if split else 0)
        lanes = pl.ds(pl.multiple_of(first, 128), part)
        rate = -jnp.exp(log_ref[:, lanes])
        gain = gain_ref[:, lanes]
        kept = jnp.ones((ns, part), F32)
        added = jnp.zeros((ns, part), F32)
        for step in range(steps):
            dt = dt_ref[step, :, lanes]
            inputs = x_ref[step : step + 1, lanes].astype(F32)
            decay = jnp.exp(dt * rate)
            kept = kept * decay
            added = added * decay + drive[step] * (dt * inputs)
            slope_ref[c, step] = read[step] * kept
            base_ref[c, step] = (
                jnp.sum(read[step] * added, axis=0, keepdims=True) + gain * inputs
            )
    for move in weights:
        move.wait()


def assemble(split, kept_ref, got_ref, mamba_ref, *rest):
    rep = lax.axis_index("rep")
    if split:
        other_ref, handoff_ref, out_ref, sems = rest
    else:
        handoff_ref, out_ref, sems = rest
    heads = kept_ref.shape[0]
    copy = copier(sems)
    moves = [
        copy(kept_ref, handoff_ref.at[0, pl.ds(rep * heads, heads)]),
        copy(got_ref, handoff_ref.at[0, pl.ds((1 - rep) * heads, heads)]),
    ]
    steps, count, _, part = mamba_ref.shape
    for step in range(steps):
        for b in range(count):
            if split:
                for ref, side in ((mamba_ref, rep), (other_ref, 1 - rep)):
                    lanes = pl.ds(pl.multiple_of((2 * b + side) * part, 128), part)
                    moves.append(copy(ref.at[step, b], out_ref.at[step, :, lanes]))
            else:
                moves.append(copy(mamba_ref.at[step, b], out_ref.at[step, :, pl.ds(b * part, part)]))
    run_all(moves)


def per_device(
    prefill_kv,
    kept_blocks,
    kept_counts,
    queries,
    new_kv,
    out_weight,
    prefill_state,
    a_log,
    step_input,
    step_dt,
    step_bc,
    skip_gain,
):
    count = lax.axis_size("seq")
    reps = lax.axis_size("rep")
    heads_count = lax.axis_size("head")
    requests, heads, tokens, width = prefill_kv.shape
    assert requests == count and tokens == BLOCK and reps == 2 and width == 256
    assert count & (count - 1) == 0 and heads_count & (heads_count - 1) == 0
    keep = kept_blocks.shape[2]
    keep_rep = keep // reps
    steps, _, q_heads, hd = queries.shape
    dec_heads = new_kv.shape[2]
    group = q_heads // dec_heads
    _, ns, block = prefill_state.shape
    split = block % (reps * 128) == 0
    part = block // reps if split else block
    all_rows = heads * steps * group
    assert all_rows <= 128
    channels = count * block
    shape = jax.ShapeDtypeStruct
    smem = pltpu.SMEM
    blocks = jnp.swapaxes(kept_blocks, 1, 2)

    prefill_kv, prefill_state, queries, new_kv = map(in_hbm, (prefill_kv, prefill_state, queries, new_kv))
    step_dt, step_bc, a_log, out_weight = map(in_hbm, (step_dt, step_bc, a_log, out_weight))
    step_input = in_hbm(step_input.reshape(steps, channels))
    skip_gain = in_hbm(skip_gain.reshape(1, -1))
    blocks, kept_counts = in_hbm(blocks), in_hbm(kept_counts)

    columns = out_weight.shape[1]
    half = heads * group * hd
    half_weight = pltpu.VMEM((half, columns), BF)
    block_shape = shape((heads * BLOCK, width), BF)
    pieces = call(
        functools.partial(stage_blocks, count),
        [block_shape] * (count - 1),
        [HB],
        [VM] * (count - 1),
        [DMA(((count - 1) * heads,))],
    )(prefill_kv)
    moved = [shift(pieces[c - 1], "seq", c) for c in range(count - 1, 0, -1)][::-1]
    own_piece, q_near, new_near, bias, picks, *states = call(
        functools.partial(stage_rest, count, split),
        [
            block_shape,
            shape(queries.shape, BF),
            shape(new_kv.shape, BF),
            shape((all_rows, count * BLOCK), F32),
            shape((reps, heads, keep_rep, count, 16, width), BF),
        ]
        + [shape((state_rows(part), width), BF)] * count,
        [HB] * 6,
        [VM] * (5 + count),
        [
            pltpu.VMEM((count, ns, part), F32),
            smem(blocks.shape, jnp.int32),
            smem(kept_counts.shape, jnp.int32),
            DMA((heads + 2,)),
            DMA((count + 2,)),
        ],
    )(*after([prefill_kv], pieces[0]), queries, new_kv, prefill_state, blocks, kept_counts)
    own_weight, other_weight, slope, base = call(
        functools.partial(prepare, count, split),
        [
            half_weight,
            half_weight,
            shape((count, steps, ns, part), F32),
            shape((count, steps, 1, part), F32),
        ],
        [HB] * 6,
        [VM] * 4,
        [
            pltpu.VMEM((steps, 1, channels), F32),
            pltpu.VMEM((steps, channels), BF),
            pltpu.VMEM(step_bc.shape, F32),
            pltpu.VMEM((1, channels), F32),
            pltpu.VMEM(a_log.shape, F32),
            DMA((5,)),
            DMA((2 * PIECES,)),
        ],
    )(*after([out_weight], pieces[0]), step_dt, step_input, step_bc, skip_gain, a_log)

    *moved, own_weight = after([*moved[::-1], own_weight])
    kv = [own_piece, *moved[::-1]]
    half_shape = (heads, keep_rep, BLOCK, width)
    rows = steps * group
    *sends, kept, sent = call(
        functools.partial(attend, count, heads),
        [shape((rows, width), BF)]
        + [shape((rows + state_rows(part), width), BF)] * (count - 1)
        + [shape(half_shape, BF)] * 2,
        [VM] * (3 + 2 * count),
        [VM] * (count + 2),
    )(q_near, new_near, bias, picks, *kv, *states[1:])
    order = [*range(2, count), 1]
    gathered = [shift(sends[c], "seq", c) for c in order]
    attn, mamba = call(
        functools.partial(collect, count, heads, steps, group),
        [shape((steps * count, half), BF), shape((steps, count, 1, part), F32)],
        [VM] * (3 + count),
        [VM] * 2,
        [pltpu.VMEM((heads, steps * count * group, hd), F32)],
    )(slope, base, states[0], sends[0], *gathered)
    attn_other = shift(attn, "rep", 1)
    own_sum = call(
        project_own, shape((steps * count, columns), F32), [VM, VM], VM, us=0.7
    )(attn, own_weight)
    share = count // heads_count
    sums = call(
        functools.partial(project_other, heads_count, count),
        [shape((steps, share, columns), F32)] * heads_count,
        [VM, VM, VM],
        [VM] * heads_count,
        us=0.7,
    )(own_sum, attn_other, other_weight)
    sums = [sums[0]] + [shift(sums[c], "head", c) for c in range(1, heads_count)]
    got = shift(after([sent], mamba)[0], "rep", 1)
    kept = after([kept], sums[0])[0]
    operands = [kept, got, mamba] + ([shift(mamba, "rep", 1)] if split else [])
    handoff, mamba_out = call(
        functools.partial(assemble, split),
        [
            shape((1, dec_heads, keep_rep, BLOCK, width), BF),
            shape((steps, 1, channels), F32),
        ],
        [VM] * len(operands),
        [HB] * 2,
        [DMA((2 + steps * count * (2 if split else 1),))],
    )(*operands)
    sums[1:] = after(sums[1:], handoff)
    proj_out = call(
        add_up, shape((steps, share, columns), BF), [VM] * heads_count, VM, us=0.6
    )(*sums)
    return handoff, proj_out, mamba_out


def solution(mesh):
    return jax.shard_map(
        per_device,
        mesh=mesh,
        in_specs=(
            P("groups", ("head", "rep"), "seq", None),
            P("groups", None, None),
            P("groups", None),
            P(None, ("groups", "seq"), "head", None),
            P(None, ("groups", "seq"), "head", None),
            P("head", ("seq", "rep")),
            P("groups", None, ("head", "seq")),
            P(None, "head"),
            P(None, ("groups", "seq"), "head"),
            P(None, ("groups", "seq"), "head"),
            P(None, ("groups", "seq"), None, None),
            P("head"),
        ),
        out_specs=(
            P(("groups", "seq"), "head", "rep", None, None),
            P(None, ("groups", "head"), ("seq", "rep")),
            P(None, ("groups", "seq"), "head"),
        ),
        check_vma=False,
    )
```

```python
import functools

import jax
import jax.numpy as jnp
from jax import lax
from jax.experimental import pallas as pl
from jax.experimental.pallas import tpu as pltpu
from jax.sharding import PartitionSpec as P

BLOCK = 128
PIECES = 4
CUTS = 4
NEG = -1e30
BF = jnp.bfloat16
F32 = jnp.float32
VM = pl.BlockSpec(memory_space=pltpu.VMEM)
HB = pl.BlockSpec(memory_space=pltpu.HBM)
DMA = pltpu.SemaphoreType.DMA


def shift(x, axis, c):
    size = lax.axis_size(axis)
    return lax.ppermute(x, axis, [(i, i ^ c) for i in range(size)])


def call(body, out_shape, in_specs, out_specs, scratch=(), us=1.0):
    return pl.pallas_call(
        body,
        out_shape=out_shape,
        in_specs=in_specs,
        out_specs=out_specs,
        scratch_shapes=list(scratch),
        cost_estimate=pl.CostEstimate(
            flops=0, bytes_accessed=int(us * 3.6e4), transcendentals=0
        ),
        compiler_params=pltpu.CompilerParams(vmem_limit_bytes=32 * 1024 * 1024),
    )


def in_hbm(x):
    return pltpu.with_memory_space_constraint(x, pltpu.HBM)


def after(arrays, *earlier):
    return lax.optimization_barrier((*arrays, *earlier))[: len(arrays)]


def run_all(copies):
    for copy in copies:
        copy.start()
    for copy in copies:
        copy.wait()


def copier(sems):
    position = iter(range(sems.shape[0]))
    return lambda src, dst: pltpu.make_async_copy(src, dst, sems.at[next(position)])


def state_rows(part):
    return 16 * pl.cdiv(part, 256)


def pack_state(piece, out_ref, first):
    ns, part = piece.shape
    for i in range(pl.cdiv(part, 256)):
        cut = piece[:, i * 256 : (i + 1) * 256]
        if cut.shape[1] < 256:
            cut = jnp.concatenate([cut, jnp.zeros((ns, 256 - cut.shape[1]), F32)], axis=1)
        out_ref[first + i * 16 : first + (i + 1) * 16, :] = cut.astype(BF)


def own_state(state_ref, c, split, part):
    me, rep = lax.axis_index("seq"), lax.axis_index("rep")
    if split:
        return state_ref.at[me ^ c, :, pl.ds(pl.multiple_of(rep * part, 128), part)]
    return state_ref.at[me ^ c]


def stage_blocks(count, kv_ref, *rest):
    outs, sems = rest[:-1], rest[-1]
    me = lax.axis_index("seq")
    copy = copier(sems)
    cut = BLOCK // CUTS
    run_all(
        [
            copy(
                kv_ref.at[me ^ c, j, pl.ds(i * cut, cut)],
                outs[c - 1].at[pl.ds(j * BLOCK + i * cut, cut)],
            )
            for c in range(count - 1, 0, -1)
            for j in range(kv_ref.shape[1])
            for i in range(CUTS)
        ]
    )


def stage_rest(count, split, kv_ref, q_ref, new_ref, state_ref, blocks_ref, counts_ref, *rest):
    own_out, q_out, new_out, bias_out, pick_out = rest[:5]
    states = rest[5 : 5 + count]
    loaded, blocks, counts, sems, early = rest[5 + count :]
    me, rep = lax.axis_index("seq"), lax.axis_index("rep")
    heads = kv_ref.shape[1]
    copy = copier(sems)
    moves = [copy(kv_ref.at[me, j], own_out.at[pl.ds(j * BLOCK, BLOCK)]) for j in range(heads)]
    moves += [copy(q_ref, q_out), copy(new_ref, new_out)]
    copy = copier(early)
    first = [copy(blocks_ref, blocks), copy(counts_ref, counts)]
    part = loaded.shape[2]
    for c in range(count):
        if split:
            src = state_ref.at[me ^ c, :, pl.ds(pl.multiple_of(rep * part, 128), part)]
        else:
            src = state_ref.at[me ^ c]
        first.append(copy(src, loaded.at[c]))
    for move in first + moves:
        move.start()
    for move in first:
        move.wait()
    for c in range(count):
        pack_state(loaded[c], states[c], 0)
    head_first = lax.axis_index("head") * new_ref.shape[2] + rep * heads
    rows = bias_out.shape[0] // heads
    keep_rep = pick_out.shape[2]
    for j in range(heads):
        live_count = counts[me, head_first + j]
        for c in range(count):
            live = jnp.int32(0)
            for side in range(2):
                for k in range(keep_rep):
                    slot = (rep if side == 0 else 1 - rep) * keep_rep + k
                    hit = (blocks[me, slot, head_first + j] == (me ^ c)) & (slot < live_count)
                    one = jnp.where(hit, 1.0, 0.0).astype(F32)
                    pick_out[side, j, k, c] = jnp.full(pick_out.shape[4:], one, F32).astype(BF)
                    live = live | hit.astype(jnp.int32)
            dead = jnp.where(live > 0, 0.0, NEG).astype(F32)
            bias_out[j * rows : (j + 1) * rows, c * BLOCK : (c + 1) * BLOCK] = jnp.full(
                (rows, BLOCK), dead, F32
            )
    for move in moves:
        move.wait()


def dot_f32(a, b, contract):
    return lax.dot_general(a, b, (contract, ((), ())), preferred_element_type=F32)


def query_rows(q_ref, heads):
    rep = lax.axis_index("rep")
    steps, _, q_heads, _ = q_ref.shape
    own_q = q_heads // 2
    group = own_q // heads
    q_all = [q_ref[step, 0].astype(F32) for step in range(steps)]
    q_all = [jnp.where(rep == 0, q[:own_q], q[own_q:]) for q in q_all]
    return [
        jnp.concatenate([x[j * group : (j + 1) * group] for x in q_all], axis=0)
        for j in range(heads)
    ]


def block_scores(q, piece_ref, j):
    hd = piece_ref.shape[1] // 2
    keys = piece_ref[j * BLOCK : (j + 1) * BLOCK, :hd]
    return dot_f32(q.astype(BF), keys, ((1,), (1,))) * hd ** (-0.5)


def block_sums(weights, piece_ref, j):
    values = piece_ref[j * BLOCK : (j + 1) * BLOCK, piece_ref.shape[1] // 2 :]
    return dot_f32(weights, values, ((1,), (0,)))


def attend(count, heads, q_ref, new_ref, bias_ref, pick_ref, *rest):
    pieces, states = rest[:count], rest[count : 2 * count - 1]
    outs, (kept_ref, sent_ref) = rest[2 * count - 1 : 3 * count - 1], rest[3 * count - 1 :]
    rep = lax.axis_index("rep")
    queries = query_rows(q_ref, heads)
    rows, hd = queries[0].shape
    steps = q_ref.shape[0]
    group = rows // steps
    all_rows = heads * rows
    scale = hd ** (-0.5)
    scores = [
        jnp.concatenate([block_scores(q, piece, j) for piece in pieces], axis=1)
        for j, q in enumerate(queries)
    ]
    scores = jnp.concatenate(scores, axis=0)
    alive = bias_ref[...] == 0.0
    scores = jnp.where(alive, scores, NEG)
    row_step = (lax.broadcasted_iota(jnp.int32, (all_rows, 1), 0) // group) % steps
    wide_q = jnp.concatenate(queries, axis=0)
    dots, fresh_values = [], []
    top = jnp.max(scores, axis=1, keepdims=True)
    for step in range(steps):
        both = new_ref[step, 0].astype(F32)
        fresh = jnp.where(rep == 0, both[:heads], both[heads:])
        wide = jnp.concatenate(
            [jnp.broadcast_to(fresh[j : j + 1], (rows, 2 * hd)) for j in range(heads)], axis=0
        )
        dot = jnp.sum(wide_q * wide[:, :hd], axis=1, keepdims=True) * scale
        dots.append(jnp.where(row_step >= step, dot, NEG))
        fresh_values.append(wide[:, hd:])
        top = jnp.maximum(top, dots[-1])
    weights = jnp.where(alive, jnp.exp(scores - top), 0.0)
    total = jnp.sum(weights, axis=1, keepdims=True)
    weights = weights.astype(BF)
    summed = []
    for j in range(heads):
        parts = [
            block_sums(weights[j * rows : (j + 1) * rows, c * BLOCK : (c + 1) * BLOCK], piece, j)
            for c, piece in enumerate(pieces)
        ]
        summed.append(functools.reduce(jnp.add, parts))
    summed = jnp.concatenate(summed, axis=0)
    for step in range(steps):
        weight = jnp.where(row_step >= step, jnp.exp(dots[step] - top), 0.0)
        total = total + weight
        summed = summed + weight.astype(BF).astype(F32) * fresh_values[step]
    result = (summed / total).astype(BF)
    for c in range(count):
        for j in range(2):
            half = result[j * rows : (j + 1) * rows] if j < heads else jnp.zeros((rows, hd), BF)
            outs[c][:rows, j * hd : (j + 1) * hd] = half
        if c:
            outs[c][rows:, :] = states[c - 1][...]
    tile = pick_ref.shape[4]
    for side, ref in ((1, sent_ref), (0, kept_ref)):
        for j in range(heads):
            for k in range(ref.shape[1]):
                total = None
                for c in range(count):
                    piece = pieces[c][j * BLOCK : (j + 1) * BLOCK, :].reshape(-1, tile, 2 * hd)
                    term = piece * pick_ref[side, j, k, c][None]
                    total = term if total is None else total + term
                ref[j, k] = total.reshape(BLOCK, 2 * hd)


def collect(count, heads, steps, group, slope_ref, base_ref, home_ref, *rest):
    parts = [rest[0], rest[count - 1], *rest[1 : count - 1]]
    states = [home_ref, *parts[1:]]
    out_ref, mamba_ref, scratch = rest[count:]
    me = lax.axis_index("seq")
    ns, part = slope_ref.shape[2:]
    for c in range(count):
        first = states[c].shape[0] - state_rows(part)
        rows = [
            states[c][first + 16 * i : first + 16 * (i + 1), :].astype(F32)
            for i in range(pl.cdiv(part, 256))
        ]
        state = jnp.concatenate(rows, axis=1)[:, :part]
        for step in range(steps):
            mamba_ref[step, me ^ c] = base_ref[c, step] + jnp.sum(
                slope_ref[c, step] * state, axis=0, keepdims=True
            )
    for c in range(count):
        rows = parts[c][: steps * group, :].astype(F32)
        for j in range(heads):
            for step in range(steps):
                at = pl.multiple_of((step * count + (me ^ c)) * group, group)
                cut = rows[step * group : (step + 1) * group, j * 128 : (j + 1) * 128]
                scratch[j, pl.ds(at, group), :] = cut
    for j in range(heads):
        for g in range(group):
            at = (j * group + g) * 128
            tile = scratch[j, pl.ds(g, steps * count, stride=group), :]
            out_ref[:, at : at + 128] = tile.astype(BF)


def weight_half(weight_ref, out_ref, which, copy):
    half = out_ref.shape[0]
    rows = half // PIECES
    cuts = [(pl.ds(which * half + i * rows, rows), pl.ds(i * rows, rows)) for i in range(PIECES)]
    return [copy(weight_ref.at[src], out_ref.at[dst]) for src, dst in cuts]


def project_own(attn_ref, weight_ref, out_ref):
    out_ref[...] = dot_f32(attn_ref[...], weight_ref[...], ((1,), (0,)))


def pick(options, index):
    chosen = options[0]
    for i in range(1, len(options)):
        chosen = jnp.where(index == i, options[i], chosen)
    return chosen


def project_other(heads_count, count, acc_ref, attn_ref, weight_ref, *outs):
    total = acc_ref[...] + dot_f32(attn_ref[...], weight_ref[...], ((1,), (0,)))
    head = lax.axis_index("head")
    steps = total.shape[0] // count
    share = count // heads_count
    for step in range(steps):
        slices = [
            total[step * count + x * share : step * count + (x + 1) * share]
            for x in range(heads_count)
        ]
        for c in range(heads_count):
            outs[c][step] = pick(slices, head ^ c)


def add_up(*refs):
    total = refs[0][...]
    for ref in refs[1:-1]:
        total = total + ref[...]
    refs[-1][...] = total.astype(BF)


def prepare(count, split, weight_hbm, dt_hbm, x_hbm, bc_hbm, gain_hbm, log_hbm, own_ref, other_ref,
            slope_ref, base_ref, dt_ref, x_ref, bc_ref, gain_ref, log_ref, sems, weight_sems):
    copy = copier(sems)
    first = [
        copy(dt_hbm, dt_ref),
        copy(x_hbm, x_ref),
        copy(bc_hbm, bc_ref),
        copy(gain_hbm, gain_ref),
        copy(log_hbm, log_ref),
    ]
    copy, which = copier(weight_sems), lax.axis_index("rep")
    weights = weight_half(weight_hbm, own_ref, which, copy)
    weights += weight_half(weight_hbm, other_ref, 1 - which, copy)
    for move in first + weights:
        move.start()
    for move in first:
        move.wait()
    me, rep = lax.axis_index("seq"), lax.axis_index("rep")
    _, steps, ns, part = slope_ref.shape
    block = part * 2 if split else part
    diagonal = lax.broadcasted_iota(jnp.int32, (ns, ns), 0) == lax.broadcasted_iota(
        jnp.int32, (ns, ns), 1
    )

    def column(row):
        return jnp.sum(jnp.where(diagonal, row, 0.0), axis=1, keepdims=True)

    drive = [column(bc_ref[step, 0, 0:1, :]) for step in range(steps)]
    read = [column(bc_ref[step, 0, 1:2, :]) for step in range(steps)]
    for c in range(count):
        first = (me ^ c) * block + (rep * part if split else 0)
        lanes = pl.ds(pl.multiple_of(first, 128), part)
        rate = -jnp.exp(log_ref[:, lanes])
        gain = gain_ref[:, lanes]
        kept = jnp.ones((ns, part), F32)
        added = jnp.zeros((ns, part), F32)
        for step in range(steps):
            dt = dt_ref[step, :, lanes]
            inputs = x_ref[step : step + 1, lanes].astype(F32)
            decay = jnp.exp(dt * rate)
            kept = kept * decay
            added = added * decay + drive[step] * (dt * inputs)
            slope_ref[c, step] = read[step] * kept
            base_ref[c, step] = (
                jnp.sum(read[step] * added, axis=0, keepdims=True) + gain * inputs
            )
    for move in weights:
        move.wait()


def assemble(split, kept_ref, got_ref, mamba_ref, *rest):
    rep = lax.axis_index("rep")
    if split:
        other_ref, handoff_ref, out_ref, sems = rest
    else:
        handoff_ref, out_ref, sems = rest
    heads = kept_ref.shape[0]
    copy = copier(sems)
    moves = [
        copy(kept_ref, handoff_ref.at[0, pl.ds(rep * heads, heads)]),
        copy(got_ref, handoff_ref.at[0, pl.ds((1 - rep) * heads, heads)]),
    ]
    steps, count, _, part = mamba_ref.shape
    for step in range(steps):
        for b in range(count):
            if split:
                for ref, side in ((mamba_ref, rep), (other_ref, 1 - rep)):
                    lanes = pl.ds(pl.multiple_of((2 * b + side) * part, 128), part)
                    moves.append(copy(ref.at[step, b], out_ref.at[step, :, lanes]))
            else:
                moves.append(copy(mamba_ref.at[step, b], out_ref.at[step, :, pl.ds(b * part, part)]))
    run_all(moves)


def per_device(
    prefill_kv,
    kept_blocks,
    kept_counts,
    queries,
    new_kv,
    out_weight,
    prefill_state,
    a_log,
    step_input,
    step_dt,
    step_bc,
    skip_gain,
):
    count = lax.axis_size("seq")
    reps = lax.axis_size("rep")
    heads_count = lax.axis_size("head")
    requests, heads, tokens, width = prefill_kv.shape
    assert requests == count and tokens == BLOCK and reps == 2 and width == 256
    assert count & (count - 1) == 0 and heads_count & (heads_count - 1) == 0
    keep = kept_blocks.shape[2]
    keep_rep = keep // reps
    steps, _, q_heads, hd = queries.shape
    dec_heads = new_kv.shape[2]
    group = q_heads // dec_heads
    _, ns, block = prefill_state.shape
    split = block % (reps * 128) == 0
    part = block // reps if split else block
    all_rows = heads * steps * group
    assert all_rows <= 128
    channels = count * block
    shape = jax.ShapeDtypeStruct
    smem = pltpu.SMEM
    blocks = jnp.swapaxes(kept_blocks, 1, 2)

    prefill_kv, prefill_state, queries, new_kv = map(in_hbm, (prefill_kv, prefill_state, queries, new_kv))
    step_dt, step_bc, a_log, out_weight = map(in_hbm, (step_dt, step_bc, a_log, out_weight))
    step_input = in_hbm(step_input.reshape(steps, channels))
    skip_gain = in_hbm(skip_gain.reshape(1, -1))
    blocks, kept_counts = in_hbm(blocks), in_hbm(kept_counts)

    columns = out_weight.shape[1]
    half = heads * group * hd
    half_weight = pltpu.VMEM((half, columns), BF)
    block_shape = shape((heads * BLOCK, width), BF)
    pieces = call(
        functools.partial(stage_blocks, count),
        [block_shape] * (count - 1),
        [HB],
        [VM] * (count - 1),
        [DMA(((count - 1) * heads * CUTS,))],
    )(prefill_kv)
    moved = [shift(pieces[c - 1], "seq", c) for c in range(count - 1, 0, -1)][::-1]
    own_piece, q_near, new_near, bias, picks, *states = call(
        functools.partial(stage_rest, count, split),
        [
            block_shape,
            shape(queries.shape, BF),
            shape(new_kv.shape, BF),
            shape((all_rows, count * BLOCK), F32),
            shape((reps, heads, keep_rep, count, 16, width), BF),
        ]
        + [shape((state_rows(part), width), BF)] * count,
        [HB] * 6,
        [VM] * (5 + count),
        [
            pltpu.VMEM((count, ns, part), F32),
            smem(blocks.shape, jnp.int32),
            smem(kept_counts.shape, jnp.int32),
            DMA((heads + 2,)),
            DMA((count + 2,)),
        ],
    )(*after([prefill_kv], pieces[0]), queries, new_kv, prefill_state, blocks, kept_counts)
    own_weight, other_weight, slope, base = call(
        functools.partial(prepare, count, split),
        [
            half_weight,
            half_weight,
            shape((count, steps, ns, part), F32),
            shape((count, steps, 1, part), F32),
        ],
        [HB] * 6,
        [VM] * 4,
        [
            pltpu.VMEM((steps, 1, channels), F32),
            pltpu.VMEM((steps, channels), BF),
            pltpu.VMEM(step_bc.shape, F32),
            pltpu.VMEM((1, channels), F32),
            pltpu.VMEM(a_log.shape, F32),
            DMA((5,)),
            DMA((2 * PIECES,)),
        ],
    )(*after([out_weight], pieces[0]), step_dt, step_input, step_bc, skip_gain, a_log)

    *moved, own_weight = after([*moved[::-1], own_weight])
    kv = [own_piece, *moved[::-1]]
    half_shape = (heads, keep_rep, BLOCK, width)
    rows = steps * group
    *sends, kept, sent = call(
        functools.partial(attend, count, heads),
        [shape((rows, width), BF)]
        + [shape((rows + state_rows(part), width), BF)] * (count - 1)
        + [shape(half_shape, BF)] * 2,
        [VM] * (3 + 2 * count),
        [VM] * (count + 2),
    )(q_near, new_near, bias, picks, *kv, *states[1:])
    order = [*range(2, count), 1]
    gathered = [shift(sends[c], "seq", c) for c in order]
    got = shift(sent, "rep", 1)
    *gathered, got = after([*gathered, got])
    attn, mamba = call(
        functools.partial(collect, count, heads, steps, group),
        [shape((steps * count, half), BF), shape((steps, count, 1, part), F32)],
        [VM] * (3 + count),
        [VM] * 2,
        [pltpu.VMEM((heads, steps * count * group, hd), F32)],
    )(slope, base, states[0], sends[0], *gathered)
    attn_other = shift(attn, "rep", 1)
    own_sum = call(
        project_own, shape((steps * count, columns), F32), [VM, VM], VM, us=0.7
    )(attn, own_weight)
    share = count // heads_count
    sums = call(
        functools.partial(project_other, heads_count, count),
        [shape((steps, share, columns), F32)] * heads_count,
        [VM, VM, VM],
        [VM] * heads_count,
        us=0.7,
    )(own_sum, attn_other, other_weight)
    sums = [sums[0]] + [shift(sums[c], "head", c) for c in range(1, heads_count)]
    mamba = after([mamba], own_sum)[0]
    kept = after([kept], sums[0])[0]
    operands = [kept, got, mamba] + ([shift(mamba, "rep", 1)] if split else [])
    handoff, mamba_out = call(
        functools.partial(assemble, split),
        [
            shape((1, dec_heads, keep_rep, BLOCK, width), BF),
            shape((steps, 1, channels), F32),
        ],
        [VM] * len(operands),
        [HB] * 2,
        [DMA((2 + steps * count * (2 if split else 1),))],
    )(*operands)
    sums[1:] = after(sums[1:], handoff)
    proj_out = call(
        add_up, shape((steps, share, columns), BF), [VM] * heads_count, VM, us=0.6
    )(*sums)
    return handoff, proj_out, mamba_out


def solution(mesh):
    return jax.shard_map(
        per_device,
        mesh=mesh,
        in_specs=(
            P("groups", ("head", "rep"), "seq", None),
            P("groups", None, None),
            P("groups", None),
            P(None, ("groups", "seq"), "head", None),
            P(None, ("groups", "seq"), "head", None),
            P("head", ("seq", "rep")),
            P("groups", None, ("head", "seq")),
            P(None, "head"),
            P(None, ("groups", "seq"), "head"),
            P(None, ("groups", "seq"), "head"),
            P(None, ("groups", "seq"), None, None),
            P("head"),
        ),
        out_specs=(
            P(("groups", "seq"), "head", "rep", None, None),
            P(None, ("groups", "head"), ("seq", "rep")),
            P(None, ("groups", "seq"), "head"),
        ),
        check_vma=False,
    )
```

```python
import functools

import jax
import jax.numpy as jnp
from jax import lax
from jax.experimental import pallas as pl
from jax.experimental.pallas import tpu as pltpu
from jax.sharding import PartitionSpec as P

BLOCK = 128
PIECES = 4
NEG = -1e30
BF = jnp.bfloat16
F32 = jnp.float32
VM = pl.BlockSpec(memory_space=pltpu.VMEM)
HB = pl.BlockSpec(memory_space=pltpu.HBM)
DMA = pltpu.SemaphoreType.DMA


def shift(x, axis, c):
    size = lax.axis_size(axis)
    return lax.ppermute(x, axis, [(i, i ^ c) for i in range(size)])


def call(body, out_shape, in_specs, out_specs, scratch=(), us=1.0, aliases=None):
    return pl.pallas_call(
        body,
        out_shape=out_shape,
        in_specs=in_specs,
        out_specs=out_specs,
        scratch_shapes=list(scratch),
        input_output_aliases=aliases or {},
        cost_estimate=pl.CostEstimate(
            flops=0, bytes_accessed=int(us * 3.6e4), transcendentals=0
        ),
        compiler_params=pltpu.CompilerParams(vmem_limit_bytes=32 * 1024 * 1024),
    )


def in_hbm(x):
    return pltpu.with_memory_space_constraint(x, pltpu.HBM)


def after(arrays, *earlier):
    return lax.optimization_barrier((*arrays, *earlier))[: len(arrays)]


def run_all(copies):
    for copy in copies:
        copy.start()
    for copy in copies:
        copy.wait()


def copier(sems):
    position = iter(range(sems.shape[0]))
    return lambda src, dst: pltpu.make_async_copy(src, dst, sems.at[next(position)])


def state_rows(part):
    return 16 * pl.cdiv(part, 256)


def pack_state(piece, out_ref, first):
    ns, part = piece.shape
    for i in range(pl.cdiv(part, 256)):
        cut = piece[:, i * 256 : (i + 1) * 256]
        if cut.shape[1] < 256:
            cut = jnp.concatenate([cut, jnp.zeros((ns, 256 - cut.shape[1]), F32)], axis=1)
        out_ref[first + i * 16 : first + (i + 1) * 16, :] = cut.astype(BF)


def own_state(state_ref, c, split, part):
    me, rep = lax.axis_index("seq"), lax.axis_index("rep")
    if split:
        return state_ref.at[me ^ c, :, pl.ds(pl.multiple_of(rep * part, 128), part)]
    return state_ref.at[me ^ c]


def stage_blocks(count, kv_ref, *rest):
    outs, sems = rest[:-1], rest[-1]
    me = lax.axis_index("seq")
    copy = copier(sems)
    run_all(
        [
            copy(kv_ref.at[me ^ c, j], outs[c - 1].at[pl.ds(j * BLOCK, BLOCK)])
            for c in range(count - 1, 0, -1)
            for j in range(kv_ref.shape[1])
        ]
    )


def stage_others(count, split, sources, outs, scratch):
    kv_ref, q_ref, new_ref, state_ref, blocks_ref, counts_ref = sources
    own_out, q_out, new_out, bias_out, pick_out, *states = outs
    loaded, blocks, counts, sems, early = scratch
    me, rep = lax.axis_index("seq"), lax.axis_index("rep")
    heads = kv_ref.shape[1]
    copy = copier(sems)
    moves = [copy(kv_ref.at[me, j], own_out.at[pl.ds(j * BLOCK, BLOCK)]) for j in range(heads)]
    moves += [copy(q_ref, q_out), copy(new_ref, new_out)]
    copy = copier(early)
    first = [copy(blocks_ref, blocks), copy(counts_ref, counts)]
    part = loaded.shape[2]
    for c in range(count):
        if split:
            src = state_ref.at[me ^ c, :, pl.ds(pl.multiple_of(rep * part, 128), part)]
        else:
            src = state_ref.at[me ^ c]
        first.append(copy(src, loaded.at[c]))
    for move in first + moves:
        move.start()
    for move in first:
        move.wait()
    for c in range(count):
        pack_state(loaded[c], states[c], 0)
    head_first = lax.axis_index("head") * new_ref.shape[2] + rep * heads
    rows = bias_out.shape[0] // heads
    keep_rep = pick_out.shape[2]
    for j in range(heads):
        live_count = counts[me, head_first + j]
        for c in range(count):
            live = jnp.int32(0)
            for side in range(2):
                for k in range(keep_rep):
                    slot = (rep if side == 0 else 1 - rep) * keep_rep + k
                    hit = (blocks[me, slot, head_first + j] == (me ^ c)) & (slot < live_count)
                    one = jnp.where(hit, 1.0, 0.0).astype(F32)
                    pick_out[side, j, k, c] = jnp.full(pick_out.shape[4:], one, F32).astype(BF)
                    live = live | hit.astype(jnp.int32)
            dead = jnp.where(live > 0, 0.0, NEG).astype(F32)
            bias_out[j * rows : (j + 1) * rows, c * BLOCK : (c + 1) * BLOCK] = jnp.full(
                (rows, BLOCK), dead, F32
            )
    for move in moves:
        move.wait()


def stage_first(count, split, *refs):
    sources, pieces, outs = refs[:6], refs[6 : 5 + count], refs[5 + count : 10 + 2 * count]
    block_sems, *scratch = refs[10 + 2 * count :]
    stage_blocks(count, sources[0], *pieces, block_sems)

    @pl.when(lax.axis_index("rep") == 1)
    def _():
        stage_others(count, split, sources, outs, scratch)


def stage_second(count, split, *refs):
    sources, outs, scratch = refs[:6], refs[11 + count : 16 + 2 * count], refs[16 + 2 * count :]

    @pl.when(lax.axis_index("rep") == 0)
    def _():
        stage_others(count, split, sources, outs, scratch)


def dot_f32(a, b, contract):
    return lax.dot_general(a, b, (contract, ((), ())), preferred_element_type=F32)


def query_rows(q_ref, heads):
    rep = lax.axis_index("rep")
    steps, _, q_heads, _ = q_ref.shape
    own_q = q_heads // 2
    group = own_q // heads
    q_all = [q_ref[step, 0].astype(F32) for step in range(steps)]
    q_all = [jnp.where(rep == 0, q[:own_q], q[own_q:]) for q in q_all]
    return [
        jnp.concatenate([x[j * group : (j + 1) * group] for x in q_all], axis=0)
        for j in range(heads)
    ]


def block_scores(q, piece_ref, j):
    hd = piece_ref.shape[1] // 2
    keys = piece_ref[j * BLOCK : (j + 1) * BLOCK, :hd]
    return dot_f32(q.astype(BF), keys, ((1,), (1,))) * hd ** (-0.5)


def block_sums(weights, piece_ref, j):
    values = piece_ref[j * BLOCK : (j + 1) * BLOCK, piece_ref.shape[1] // 2 :]
    return dot_f32(weights, values, ((1,), (0,)))


def attend(count, heads, q_ref, new_ref, bias_ref, pick_ref, *rest):
    pieces, states = rest[:count], rest[count : 2 * count - 1]
    outs, (kept_ref, sent_ref) = rest[2 * count - 1 : 3 * count - 1], rest[3 * count - 1 :]
    rep = lax.axis_index("rep")
    queries = query_rows(q_ref, heads)
    rows, hd = queries[0].shape
    steps = q_ref.shape[0]
    group = rows // steps
    all_rows = heads * rows
    scale = hd ** (-0.5)
    scores = [
        jnp.concatenate([block_scores(q, piece, j) for piece in pieces], axis=1)
        for j, q in enumerate(queries)
    ]
    scores = jnp.concatenate(scores, axis=0)
    alive = bias_ref[...] == 0.0
    scores = jnp.where(alive, scores, NEG)
    row_step = (lax.broadcasted_iota(jnp.int32, (all_rows, 1), 0) // group) % steps
    wide_q = jnp.concatenate(queries, axis=0)
    dots, fresh_values = [], []
    top = jnp.max(scores, axis=1, keepdims=True)
    for step in range(steps):
        both = new_ref[step, 0].astype(F32)
        fresh = jnp.where(rep == 0, both[:heads], both[heads:])
        wide = jnp.concatenate(
            [jnp.broadcast_to(fresh[j : j + 1], (rows, 2 * hd)) for j in range(heads)], axis=0
        )
        dot = jnp.sum(wide_q * wide[:, :hd], axis=1, keepdims=True) * scale
        dots.append(jnp.where(row_step >= step, dot, NEG))
        fresh_values.append(wide[:, hd:])
        top = jnp.maximum(top, dots[-1])
    weights = jnp.where(alive, jnp.exp(scores - top), 0.0)
    total = jnp.sum(weights, axis=1, keepdims=True)
    weights = weights.astype(BF)
    summed = []
    for j in range(heads):
        parts = [
            block_sums(weights[j * rows : (j + 1) * rows, c * BLOCK : (c + 1) * BLOCK], piece, j)
            for c, piece in enumerate(pieces)
        ]
        summed.append(functools.reduce(jnp.add, parts))
    summed = jnp.concatenate(summed, axis=0)
    for step in range(steps):
        weight = jnp.where(row_step >= step, jnp.exp(dots[step] - top), 0.0)
        total = total + weight
        summed = summed + weight.astype(BF).astype(F32) * fresh_values[step]
    result = (summed / total).astype(BF)
    for c in range(count):
        for j in range(2):
            half = result[j * rows : (j + 1) * rows] if j < heads else jnp.zeros((rows, hd), BF)
            outs[c][:rows, j * hd : (j + 1) * hd] = half
        if c:
            outs[c][rows:, :] = states[c - 1][...]
    tile = pick_ref.shape[4]
    for side, ref in ((1, sent_ref), (0, kept_ref)):
        for j in range(heads):
            for k in range(ref.shape[1]):
                total = None
                for c in range(count):
                    piece = pieces[c][j * BLOCK : (j + 1) * BLOCK, :].reshape(-1, tile, 2 * hd)
                    term = piece * pick_ref[side, j, k, c][None]
                    total = term if total is None else total + term
                ref[j, k] = total.reshape(BLOCK, 2 * hd)


def collect(count, heads, steps, group, slope_ref, base_ref, home_ref, *rest):
    parts = [rest[0], rest[count - 1], *rest[1 : count - 1]]
    states = [home_ref, *parts[1:]]
    out_ref, mamba_ref, scratch = rest[count:]
    me = lax.axis_index("seq")
    ns, part = slope_ref.shape[2:]
    for c in range(count):
        first = states[c].shape[0] - state_rows(part)
        rows = [
            states[c][first + 16 * i : first + 16 * (i + 1), :].astype(F32)
            for i in range(pl.cdiv(part, 256))
        ]
        state = jnp.concatenate(rows, axis=1)[:, :part]
        for step in range(steps):
            mamba_ref[step, me ^ c] = base_ref[c, step] + jnp.sum(
                slope_ref[c, step] * state, axis=0, keepdims=True
            )
    for c in range(count):
        rows = parts[c][: steps * group, :].astype(F32)
        for j in range(heads):
            for step in range(steps):
                at = pl.multiple_of((step * count + (me ^ c)) * group, group)
                cut = rows[step * group : (step + 1) * group, j * 128 : (j + 1) * 128]
                scratch[j, pl.ds(at, group), :] = cut
    for j in range(heads):
        for g in range(group):
            at = (j * group + g) * 128
            tile = scratch[j, pl.ds(g, steps * count, stride=group), :]
            out_ref[:, at : at + 128] = tile.astype(BF)


def weight_half(weight_ref, out_ref, which, copy):
    half = out_ref.shape[0]
    rows = half // PIECES
    cuts = [(pl.ds(which * half + i * rows, rows), pl.ds(i * rows, rows)) for i in range(PIECES)]
    return [copy(weight_ref.at[src], out_ref.at[dst]) for src, dst in cuts]


def project_own(attn_ref, weight_ref, out_ref):
    out_ref[...] = dot_f32(attn_ref[...], weight_ref[...], ((1,), (0,)))


def pick(options, index):
    chosen = options[0]
    for i in range(1, len(options)):
        chosen = jnp.where(index == i, options[i], chosen)
    return chosen


def project_other(heads_count, count, acc_ref, attn_ref, weight_ref, *outs):
    total = acc_ref[...] + dot_f32(attn_ref[...], weight_ref[...], ((1,), (0,)))
    head = lax.axis_index("head")
    steps = total.shape[0] // count
    share = count // heads_count
    for step in range(steps):
        slices = [
            total[step * count + x * share : step * count + (x + 1) * share]
            for x in range(heads_count)
        ]
        for c in range(heads_count):
            outs[c][step] = pick(slices, head ^ c)


def add_up(*refs):
    total = refs[0][...]
    for ref in refs[1:-1]:
        total = total + ref[...]
    refs[-1][...] = total.astype(BF)


def prepare(count, split, weight_hbm, dt_hbm, x_hbm, bc_hbm, gain_hbm, log_hbm, own_ref, other_ref,
            slope_ref, base_ref, dt_ref, x_ref, bc_ref, gain_ref, log_ref, sems, weight_sems):
    copy = copier(sems)
    first = [
        copy(dt_hbm, dt_ref),
        copy(x_hbm, x_ref),
        copy(bc_hbm, bc_ref),
        copy(gain_hbm, gain_ref),
        copy(log_hbm, log_ref),
    ]
    copy, which = copier(weight_sems), lax.axis_index("rep")
    weights = weight_half(weight_hbm, own_ref, which, copy)
    weights += weight_half(weight_hbm, other_ref, 1 - which, copy)
    for move in first + weights:
        move.start()
    for move in first:
        move.wait()
    me, rep = lax.axis_index("seq"), lax.axis_index("rep")
    _, steps, ns, part = slope_ref.shape
    block = part * 2 if split else part
    diagonal = lax.broadcasted_iota(jnp.int32, (ns, ns), 0) == lax.broadcasted_iota(
        jnp.int32, (ns, ns), 1
    )

    def column(row):
        return jnp.sum(jnp.where(diagonal, row, 0.0), axis=1, keepdims=True)

    drive = [column(bc_ref[step, 0, 0:1, :]) for step in range(steps)]
    read = [column(bc_ref[step, 0, 1:2, :]) for step in range(steps)]
    for c in range(count):
        first = (me ^ c) * block + (rep * part if split else 0)
        lanes = pl.ds(pl.multiple_of(first, 128), part)
        rate = -jnp.exp(log_ref[:, lanes])
        gain = gain_ref[:, lanes]
        kept = jnp.ones((ns, part), F32)
        added = jnp.zeros((ns, part), F32)
        for step in range(steps):
            dt = dt_ref[step, :, lanes]
            inputs = x_ref[step : step + 1, lanes].astype(F32)
            decay = jnp.exp(dt * rate)
            kept = kept * decay
            added = added * decay + drive[step] * (dt * inputs)
            slope_ref[c, step] = read[step] * kept
            base_ref[c, step] = (
                jnp.sum(read[step] * added, axis=0, keepdims=True) + gain * inputs
            )
    for move in weights:
        move.wait()


def assemble(split, kept_ref, got_ref, mamba_ref, *rest):
    rep = lax.axis_index("rep")
    if split:
        other_ref, handoff_ref, out_ref, sems = rest
    else:
        handoff_ref, out_ref, sems = rest
    heads = kept_ref.shape[0]
    copy = copier(sems)
    moves = [
        copy(kept_ref, handoff_ref.at[0, pl.ds(rep * heads, heads)]),
        copy(got_ref, handoff_ref.at[0, pl.ds((1 - rep) * heads, heads)]),
    ]
    steps, count, _, part = mamba_ref.shape
    for step in range(steps):
        for b in range(count):
            if split:
                for ref, side in ((mamba_ref, rep), (other_ref, 1 - rep)):
                    lanes = pl.ds(pl.multiple_of((2 * b + side) * part, 128), part)
                    moves.append(copy(ref.at[step, b], out_ref.at[step, :, lanes]))
            else:
                moves.append(copy(mamba_ref.at[step, b], out_ref.at[step, :, pl.ds(b * part, part)]))
    run_all(moves)


def per_device(
    prefill_kv,
    kept_blocks,
    kept_counts,
    queries,
    new_kv,
    out_weight,
    prefill_state,
    a_log,
    step_input,
    step_dt,
    step_bc,
    skip_gain,
):
    count = lax.axis_size("seq")
    reps = lax.axis_size("rep")
    heads_count = lax.axis_size("head")
    requests, heads, tokens, width = prefill_kv.shape
    assert requests == count and tokens == BLOCK and reps == 2 and width == 256
    assert count & (count - 1) == 0 and heads_count & (heads_count - 1) == 0
    keep = kept_blocks.shape[2]
    keep_rep = keep // reps
    steps, _, q_heads, hd = queries.shape
    dec_heads = new_kv.shape[2]
    group = q_heads // dec_heads
    _, ns, block = prefill_state.shape
    split = block % (reps * 128) == 0
    part = block // reps if split else block
    all_rows = heads * steps * group
    assert all_rows <= 128
    channels = count * block
    shape = jax.ShapeDtypeStruct
    smem = pltpu.SMEM
    blocks = jnp.swapaxes(kept_blocks, 1, 2)

    prefill_kv, prefill_state, queries, new_kv = map(in_hbm, (prefill_kv, prefill_state, queries, new_kv))
    step_dt, step_bc, a_log, out_weight = map(in_hbm, (step_dt, step_bc, a_log, out_weight))
    step_input = in_hbm(step_input.reshape(steps, channels))
    skip_gain = in_hbm(skip_gain.reshape(1, -1))
    blocks, kept_counts = in_hbm(blocks), in_hbm(kept_counts)

    columns = out_weight.shape[1]
    half = heads * group * hd
    half_weight = pltpu.VMEM((half, columns), BF)
    block_shape = shape((heads * BLOCK, width), BF)
    sources = (prefill_kv, queries, new_kv, prefill_state, blocks, kept_counts)
    other_shapes = [
        block_shape,
        shape(queries.shape, BF),
        shape(new_kv.shape, BF),
        shape((all_rows, count * BLOCK), F32),
        shape((reps, heads, keep_rep, count, 16, width), BF),
    ] + [shape((state_rows(part), width), BF)] * count
    other_scratch = [
        pltpu.VMEM((count, ns, part), F32),
        smem(blocks.shape, jnp.int32),
        smem(kept_counts.shape, jnp.int32),
        DMA((heads + 2,)),
        DMA((count + 2,)),
    ]
    staged = call(
        functools.partial(stage_first, count, split),
        [block_shape] * (count - 1) + other_shapes,
        [HB] * 6,
        [VM] * (2 * count + 4),
        [DMA(((count - 1) * heads,)), *other_scratch],
    )(*sources)
    pieces, others = staged[: count - 1], staged[count - 1 :]
    moved = [shift(pieces[c - 1], "seq", c) for c in range(count - 1, 0, -1)][::-1]
    own_piece, q_near, new_near, bias, picks, *states = call(
        functools.partial(stage_second, count, split),
        other_shapes,
        [HB] * 6 + [VM] * (5 + count),
        [VM] * (5 + count),
        other_scratch,
        aliases={6 + i: i for i in range(5 + count)},
    )(*sources, *others)
    own_weight, other_weight, slope, base = call(
        functools.partial(prepare, count, split),
        [
            half_weight,
            half_weight,
            shape((count, steps, ns, part), F32),
            shape((count, steps, 1, part), F32),
        ],
        [HB] * 6,
        [VM] * 4,
        [
            pltpu.VMEM((steps, 1, channels), F32),
            pltpu.VMEM((steps, channels), BF),
            pltpu.VMEM(step_bc.shape, F32),
            pltpu.VMEM((1, channels), F32),
            pltpu.VMEM(a_log.shape, F32),
            DMA((5,)),
            DMA((2 * PIECES,)),
        ],
    )(*after([out_weight], pieces[0]), step_dt, step_input, step_bc, skip_gain, a_log)

    *moved, own_weight = after([*moved[::-1], own_weight])
    kv = [own_piece, *moved[::-1]]
    half_shape = (heads, keep_rep, BLOCK, width)
    rows = steps * group
    *sends, kept, sent = call(
        functools.partial(attend, count, heads),
        [shape((rows, width), BF)]
        + [shape((rows + state_rows(part), width), BF)] * (count - 1)
        + [shape(half_shape, BF)] * 2,
        [VM] * (3 + 2 * count),
        [VM] * (count + 2),
    )(q_near, new_near, bias, picks, *kv, *states[1:])
    order = [*range(2, count), 1]
    gathered = [shift(sends[c], "seq", c) for c in order]
    attn, mamba = call(
        functools.partial(collect, count, heads, steps, group),
        [shape((steps * count, half), BF), shape((steps, count, 1, part), F32)],
        [VM] * (3 + count),
        [VM] * 2,
        [pltpu.VMEM((heads, steps * count * group, hd), F32)],
    )(slope, base, states[0], sends[0], *gathered)
    attn_other = shift(attn, "rep", 1)
    own_sum = call(
        project_own, shape((steps * count, columns), F32), [VM, VM], VM, us=0.7
    )(attn, own_weight)
    share = count // heads_count
    sums = call(
        functools.partial(project_other, heads_count, count),
        [shape((steps, share, columns), F32)] * heads_count,
        [VM, VM, VM],
        [VM] * heads_count,
        us=0.7,
    )(own_sum, attn_other, other_weight)
    sums = [sums[0]] + [shift(sums[c], "head", c) for c in range(1, heads_count)]
    got = shift(after([sent], mamba)[0], "rep", 1)
    kept = after([kept], sums[0])[0]
    operands = [kept, got, mamba] + ([shift(mamba, "rep", 1)] if split else [])
    handoff, mamba_out = call(
        functools.partial(assemble, split),
        [
            shape((1, dec_heads, keep_rep, BLOCK, width), BF),
            shape((steps, 1, channels), F32),
        ],
        [VM] * len(operands),
        [HB] * 2,
        [DMA((2 + steps * count * (2 if split else 1),))],
    )(*operands)
    sums[1:] = after(sums[1:], handoff)
    proj_out = call(
        add_up, shape((steps, share, columns), BF), [VM] * heads_count, VM, us=0.6
    )(*sums)
    return handoff, proj_out, mamba_out


def solution(mesh):
    return jax.shard_map(
        per_device,
        mesh=mesh,
        in_specs=(
            P("groups", ("head", "rep"), "seq", None),
            P("groups", None, None),
            P("groups", None),
            P(None, ("groups", "seq"), "head", None),
            P(None, ("groups", "seq"), "head", None),
            P("head", ("seq", "rep")),
            P("groups", None, ("head", "seq")),
            P(None, "head"),
            P(None, ("groups", "seq"), "head"),
            P(None, ("groups", "seq"), "head"),
            P(None, ("groups", "seq"), None, None),
            P("head"),
        ),
        out_specs=(
            P(("groups", "seq"), "head", "rep", None, None),
            P(None, ("groups", "head"), ("seq", "rep")),
            P(None, ("groups", "seq"), "head"),
        ),
        check_vma=False,
    )
```

```python
import functools

import jax
import jax.numpy as jnp
from jax import lax
from jax.experimental import pallas as pl
from jax.experimental.pallas import tpu as pltpu
from jax.sharding import PartitionSpec as P

BLOCK = 128
PIECES = 4
NEG = -1e30
BF = jnp.bfloat16
F32 = jnp.float32
VM = pl.BlockSpec(memory_space=pltpu.VMEM)
HB = pl.BlockSpec(memory_space=pltpu.HBM)
DMA = pltpu.SemaphoreType.DMA


def shift(x, axis, c):
    size = lax.axis_size(axis)
    return lax.ppermute(x, axis, [(i, i ^ c) for i in range(size)])


def call(body, out_shape, in_specs, out_specs, scratch=(), us=1.0):
    return pl.pallas_call(
        body,
        out_shape=out_shape,
        in_specs=in_specs,
        out_specs=out_specs,
        scratch_shapes=list(scratch),
        cost_estimate=pl.CostEstimate(
            flops=0, bytes_accessed=int(us * 3.6e4), transcendentals=0
        ),
        compiler_params=pltpu.CompilerParams(vmem_limit_bytes=32 * 1024 * 1024),
    )


def in_hbm(x):
    return pltpu.with_memory_space_constraint(x, pltpu.HBM)


def after(arrays, *earlier):
    return lax.optimization_barrier((*arrays, *earlier))[: len(arrays)]


def run_all(copies):
    for copy in copies:
        copy.start()
    for copy in copies:
        copy.wait()


def copier(sems):
    position = iter(range(sems.shape[0]))
    return lambda src, dst: pltpu.make_async_copy(src, dst, sems.at[next(position)])


def state_rows(part):
    return 16 * pl.cdiv(part, 256)


def pack_state(piece, out_ref, first):
    ns, part = piece.shape
    for i in range(pl.cdiv(part, 256)):
        cut = piece[:, i * 256 : (i + 1) * 256]
        if cut.shape[1] < 256:
            cut = jnp.concatenate([cut, jnp.zeros((ns, 256 - cut.shape[1]), F32)], axis=1)
        out_ref[first + i * 16 : first + (i + 1) * 16, :] = cut.astype(BF)


def own_state(state_ref, c, split, part):
    me, rep = lax.axis_index("seq"), lax.axis_index("rep")
    if split:
        return state_ref.at[me ^ c, :, pl.ds(pl.multiple_of(rep * part, 128), part)]
    return state_ref.at[me ^ c]


def stage_blocks(count, kv_ref, *rest):
    outs, sems = rest[:-1], rest[-1]
    me = lax.axis_index("seq")
    copy = copier(sems)
    run_all(
        [
            copy(kv_ref.at[me ^ c, j], outs[c - 1].at[pl.ds(j * BLOCK, BLOCK)])
            for c in range(count - 1, 0, -1)
            for j in range(kv_ref.shape[1])
        ]
    )


def stage_rest(count, split, kv_ref, q_ref, new_ref, state_ref, blocks_ref, counts_ref, *rest):
    own_out, q_out, new_out, bias_out, pick_out = rest[:5]
    states = rest[5 : 5 + count]
    loaded, blocks, counts, sems, early = rest[5 + count :]
    me, rep = lax.axis_index("seq"), lax.axis_index("rep")
    heads = kv_ref.shape[1]
    copy = copier(sems)
    moves = [copy(kv_ref.at[me, j], own_out.at[pl.ds(j * BLOCK, BLOCK)]) for j in range(heads)]
    moves += [copy(q_ref, q_out), copy(new_ref, new_out)]
    copy = copier(early)
    first = [copy(blocks_ref, blocks), copy(counts_ref, counts)]
    part = loaded.shape[2]
    for c in range(count):
        if split:
            src = state_ref.at[me ^ c, :, pl.ds(pl.multiple_of(rep * part, 128), part)]
        else:
            src = state_ref.at[me ^ c]
        first.append(copy(src, loaded.at[c]))
    for move in first + moves:
        move.start()
    for move in first:
        move.wait()
    for c in range(count):
        pack_state(loaded[c], states[c], 0)
    head_first = lax.axis_index("head") * new_ref.shape[2] + rep * heads
    rows = bias_out.shape[0] // heads
    keep_rep = pick_out.shape[2]
    for j in range(heads):
        live_count = counts[me, head_first + j]
        for c in range(count):
            live = jnp.int32(0)
            for side in range(2):
                for k in range(keep_rep):
                    slot = (rep if side == 0 else 1 - rep) * keep_rep + k
                    hit = (blocks[me, slot, head_first + j] == (me ^ c)) & (slot < live_count)
                    one = jnp.where(hit, 1.0, 0.0).astype(F32)
                    pick_out[side, j, k, c] = jnp.full(pick_out.shape[4:], one, F32).astype(BF)
                    live = live | hit.astype(jnp.int32)
            dead = jnp.where(live > 0, 0.0, NEG).astype(F32)
            bias_out[j * rows : (j + 1) * rows, c * BLOCK : (c + 1) * BLOCK] = jnp.full(
                (rows, BLOCK), dead, F32
            )
    for move in moves:
        move.wait()


def dot_f32(a, b, contract):
    return lax.dot_general(a, b, (contract, ((), ())), preferred_element_type=F32)


def query_rows(q_ref, heads):
    rep = lax.axis_index("rep")
    steps, _, q_heads, _ = q_ref.shape
    own_q = q_heads // 2
    group = own_q // heads
    q_all = [q_ref[step, 0].astype(F32) for step in range(steps)]
    q_all = [jnp.where(rep == 0, q[:own_q], q[own_q:]) for q in q_all]
    return [
        jnp.concatenate([x[j * group : (j + 1) * group] for x in q_all], axis=0)
        for j in range(heads)
    ]


def block_scores(q, piece_ref, j):
    hd = piece_ref.shape[1] // 2
    keys = piece_ref[j * BLOCK : (j + 1) * BLOCK, :hd]
    return dot_f32(q.astype(BF), keys, ((1,), (1,))) * hd ** (-0.5)


def block_sums(weights, piece_ref, j):
    values = piece_ref[j * BLOCK : (j + 1) * BLOCK, piece_ref.shape[1] // 2 :]
    return dot_f32(weights, values, ((1,), (0,)))


def attend(count, heads, q_ref, new_ref, bias_ref, pick_ref, *rest):
    pieces, states = rest[:count], rest[count : 2 * count - 2]
    outs, (kept_ref, sent_ref) = rest[2 * count - 2 : 3 * count - 2], rest[3 * count - 2 :]
    rep = lax.axis_index("rep")
    queries = query_rows(q_ref, heads)
    rows, hd = queries[0].shape
    steps = q_ref.shape[0]
    group = rows // steps
    all_rows = heads * rows
    scale = hd ** (-0.5)
    scores = [
        jnp.concatenate([block_scores(q, piece, j) for piece in pieces], axis=1)
        for j, q in enumerate(queries)
    ]
    scores = jnp.concatenate(scores, axis=0)
    alive = bias_ref[...] == 0.0
    scores = jnp.where(alive, scores, NEG)
    row_step = (lax.broadcasted_iota(jnp.int32, (all_rows, 1), 0) // group) % steps
    wide_q = jnp.concatenate(queries, axis=0)
    dots, fresh_values = [], []
    top = jnp.max(scores, axis=1, keepdims=True)
    for step in range(steps):
        both = new_ref[step, 0].astype(F32)
        fresh = jnp.where(rep == 0, both[:heads], both[heads:])
        wide = jnp.concatenate(
            [jnp.broadcast_to(fresh[j : j + 1], (rows, 2 * hd)) for j in range(heads)], axis=0
        )
        dot = jnp.sum(wide_q * wide[:, :hd], axis=1, keepdims=True) * scale
        dots.append(jnp.where(row_step >= step, dot, NEG))
        fresh_values.append(wide[:, hd:])
        top = jnp.maximum(top, dots[-1])
    weights = jnp.where(alive, jnp.exp(scores - top), 0.0)
    total = jnp.sum(weights, axis=1, keepdims=True)
    weights = weights.astype(BF)
    summed = []
    for j in range(heads):
        parts = [
            block_sums(weights[j * rows : (j + 1) * rows, c * BLOCK : (c + 1) * BLOCK], piece, j)
            for c, piece in enumerate(pieces)
        ]
        summed.append(functools.reduce(jnp.add, parts))
    summed = jnp.concatenate(summed, axis=0)
    for step in range(steps):
        weight = jnp.where(row_step >= step, jnp.exp(dots[step] - top), 0.0)
        total = total + weight
        summed = summed + weight.astype(BF).astype(F32) * fresh_values[step]
    result = (summed / total).astype(BF)
    for c in range(count):
        for j in range(2):
            half = result[j * rows : (j + 1) * rows] if j < heads else jnp.zeros((rows, hd), BF)
            outs[c][:rows, j * hd : (j + 1) * hd] = half
        if c > 1:
            outs[c][rows:, :] = states[c - 2][...]
    tile = pick_ref.shape[4]
    for side, ref in ((1, sent_ref), (0, kept_ref)):
        for j in range(heads):
            for k in range(ref.shape[1]):
                total = None
                for c in range(count):
                    piece = pieces[c][j * BLOCK : (j + 1) * BLOCK, :].reshape(-1, tile, 2 * hd)
                    term = piece * pick_ref[side, j, k, c][None]
                    total = term if total is None else total + term
                ref[j, k] = total.reshape(BLOCK, 2 * hd)


def collect(count, heads, steps, group, slope_ref, base_ref, home_ref, beside_ref, *rest):
    parts = [rest[0], rest[count - 1], *rest[1 : count - 1]]
    states = [home_ref, beside_ref, *parts[2:]]
    out_ref, mamba_ref, scratch = rest[count:]
    me = lax.axis_index("seq")
    ns, part = slope_ref.shape[2:]
    for c in range(count):
        first = states[c].shape[0] - state_rows(part)
        rows = [
            states[c][first + 16 * i : first + 16 * (i + 1), :].astype(F32)
            for i in range(pl.cdiv(part, 256))
        ]
        state = jnp.concatenate(rows, axis=1)[:, :part]
        for step in range(steps):
            mamba_ref[step, me ^ c] = base_ref[c, step] + jnp.sum(
                slope_ref[c, step] * state, axis=0, keepdims=True
            )
    for c in range(count):
        rows = parts[c][: steps * group, :].astype(F32)
        for j in range(heads):
            for step in range(steps):
                at = pl.multiple_of((step * count + (me ^ c)) * group, group)
                cut = rows[step * group : (step + 1) * group, j * 128 : (j + 1) * 128]
                scratch[j, pl.ds(at, group), :] = cut
    for j in range(heads):
        for g in range(group):
            at = (j * group + g) * 128
            tile = scratch[j, pl.ds(g, steps * count, stride=group), :]
            out_ref[:, at : at + 128] = tile.astype(BF)


def weight_half(weight_ref, out_ref, which, copy):
    half = out_ref.shape[0]
    rows = half // PIECES
    cuts = [(pl.ds(which * half + i * rows, rows), pl.ds(i * rows, rows)) for i in range(PIECES)]
    return [copy(weight_ref.at[src], out_ref.at[dst]) for src, dst in cuts]


def project_own(attn_ref, weight_ref, out_ref):
    out_ref[...] = dot_f32(attn_ref[...], weight_ref[...], ((1,), (0,)))


def pick(options, index):
    chosen = options[0]
    for i in range(1, len(options)):
        chosen = jnp.where(index == i, options[i], chosen)
    return chosen


def project_other(heads_count, count, acc_ref, attn_ref, weight_ref, *outs):
    total = acc_ref[...] + dot_f32(attn_ref[...], weight_ref[...], ((1,), (0,)))
    head = lax.axis_index("head")
    steps = total.shape[0] // count
    share = count // heads_count
    for step in range(steps):
        slices = [
            total[step * count + x * share : step * count + (x + 1) * share]
            for x in range(heads_count)
        ]
        for c in range(heads_count):
            outs[c][step] = pick(slices, head ^ c)


def add_up(*refs):
    total = refs[0][...]
    for ref in refs[1:-1]:
        total = total + ref[...]
    refs[-1][...] = total.astype(BF)


def prepare(count, split, weight_hbm, dt_hbm, x_hbm, bc_hbm, gain_hbm, log_hbm, own_ref, other_ref,
            slope_ref, base_ref, dt_ref, x_ref, bc_ref, gain_ref, log_ref, sems, weight_sems):
    copy = copier(sems)
    first = [
        copy(dt_hbm, dt_ref),
        copy(x_hbm, x_ref),
        copy(bc_hbm, bc_ref),
        copy(gain_hbm, gain_ref),
        copy(log_hbm, log_ref),
    ]
    copy, which = copier(weight_sems), lax.axis_index("rep")
    weights = weight_half(weight_hbm, own_ref, which, copy)
    weights += weight_half(weight_hbm, other_ref, 1 - which, copy)
    for move in first + weights:
        move.start()
    for move in first:
        move.wait()
    me, rep = lax.axis_index("seq"), lax.axis_index("rep")
    _, steps, ns, part = slope_ref.shape
    block = part * 2 if split else part
    diagonal = lax.broadcasted_iota(jnp.int32, (ns, ns), 0) == lax.broadcasted_iota(
        jnp.int32, (ns, ns), 1
    )

    def column(row):
        return jnp.sum(jnp.where(diagonal, row, 0.0), axis=1, keepdims=True)

    drive = [column(bc_ref[step, 0, 0:1, :]) for step in range(steps)]
    read = [column(bc_ref[step, 0, 1:2, :]) for step in range(steps)]
    for c in range(count):
        first = (me ^ c) * block + (rep * part if split else 0)
        lanes = pl.ds(pl.multiple_of(first, 128), part)
        rate = -jnp.exp(log_ref[:, lanes])
        gain = gain_ref[:, lanes]
        kept = jnp.ones((ns, part), F32)
        added = jnp.zeros((ns, part), F32)
        for step in range(steps):
            dt = dt_ref[step, :, lanes]
            inputs = x_ref[step : step + 1, lanes].astype(F32)
            decay = jnp.exp(dt * rate)
            kept = kept * decay
            added = added * decay + drive[step] * (dt * inputs)
            slope_ref[c, step] = read[step] * kept
            base_ref[c, step] = (
                jnp.sum(read[step] * added, axis=0, keepdims=True) + gain * inputs
            )
    for move in weights:
        move.wait()


def assemble(split, kept_ref, got_ref, mamba_ref, *rest):
    rep = lax.axis_index("rep")
    if split:
        other_ref, handoff_ref, out_ref, sems = rest
    else:
        handoff_ref, out_ref, sems = rest
    heads = kept_ref.shape[0]
    copy = copier(sems)
    moves = [
        copy(kept_ref, handoff_ref.at[0, pl.ds(rep * heads, heads)]),
        copy(got_ref, handoff_ref.at[0, pl.ds((1 - rep) * heads, heads)]),
    ]
    steps, count, _, part = mamba_ref.shape
    for step in range(steps):
        for b in range(count):
            if split:
                for ref, side in ((mamba_ref, rep), (other_ref, 1 - rep)):
                    lanes = pl.ds(pl.multiple_of((2 * b + side) * part, 128), part)
                    moves.append(copy(ref.at[step, b], out_ref.at[step, :, lanes]))
            else:
                moves.append(copy(mamba_ref.at[step, b], out_ref.at[step, :, pl.ds(b * part, part)]))
    run_all(moves)


def per_device(
    prefill_kv,
    kept_blocks,
    kept_counts,
    queries,
    new_kv,
    out_weight,
    prefill_state,
    a_log,
    step_input,
    step_dt,
    step_bc,
    skip_gain,
):
    count = lax.axis_size("seq")
    reps = lax.axis_size("rep")
    heads_count = lax.axis_size("head")
    requests, heads, tokens, width = prefill_kv.shape
    assert requests == count and tokens == BLOCK and reps == 2 and width == 256
    assert count & (count - 1) == 0 and heads_count & (heads_count - 1) == 0
    keep = kept_blocks.shape[2]
    keep_rep = keep // reps
    steps, _, q_heads, hd = queries.shape
    dec_heads = new_kv.shape[2]
    group = q_heads // dec_heads
    _, ns, block = prefill_state.shape
    split = block % (reps * 128) == 0
    part = block // reps if split else block
    all_rows = heads * steps * group
    assert all_rows <= 128
    channels = count * block
    shape = jax.ShapeDtypeStruct
    smem = pltpu.SMEM
    blocks = jnp.swapaxes(kept_blocks, 1, 2)

    prefill_kv, prefill_state, queries, new_kv = map(in_hbm, (prefill_kv, prefill_state, queries, new_kv))
    step_dt, step_bc, a_log, out_weight = map(in_hbm, (step_dt, step_bc, a_log, out_weight))
    step_input = in_hbm(step_input.reshape(steps, channels))
    skip_gain = in_hbm(skip_gain.reshape(1, -1))
    blocks, kept_counts = in_hbm(blocks), in_hbm(kept_counts)

    columns = out_weight.shape[1]
    half = heads * group * hd
    half_weight = pltpu.VMEM((half, columns), BF)
    block_shape = shape((heads * BLOCK, width), BF)
    pieces = call(
        functools.partial(stage_blocks, count),
        [block_shape] * (count - 1),
        [HB],
        [VM] * (count - 1),
        [DMA(((count - 1) * heads,))],
    )(prefill_kv)
    moved = [shift(pieces[c - 1], "seq", c) for c in range(count - 1, 0, -1)][::-1]
    own_piece, q_near, new_near, bias, picks, *states = call(
        functools.partial(stage_rest, count, split),
        [
            block_shape,
            shape(queries.shape, BF),
            shape(new_kv.shape, BF),
            shape((all_rows, count * BLOCK), F32),
            shape((reps, heads, keep_rep, count, 16, width), BF),
        ]
        + [shape((state_rows(part), width), BF)] * count,
        [HB] * 6,
        [VM] * (5 + count),
        [
            pltpu.VMEM((count, ns, part), F32),
            smem(blocks.shape, jnp.int32),
            smem(kept_counts.shape, jnp.int32),
            DMA((heads + 2,)),
            DMA((count + 2,)),
        ],
    )(*after([prefill_kv], pieces[0]), queries, new_kv, prefill_state, blocks, kept_counts)
    own_weight, other_weight, slope, base = call(
        functools.partial(prepare, count, split),
        [
            half_weight,
            half_weight,
            shape((count, steps, ns, part), F32),
            shape((count, steps, 1, part), F32),
        ],
        [HB] * 6,
        [VM] * 4,
        [
            pltpu.VMEM((steps, 1, channels), F32),
            pltpu.VMEM((steps, channels), BF),
            pltpu.VMEM(step_bc.shape, F32),
            pltpu.VMEM((1, channels), F32),
            pltpu.VMEM(a_log.shape, F32),
            DMA((5,)),
            DMA((2 * PIECES,)),
        ],
    )(*after([out_weight], pieces[0]), step_dt, step_input, step_bc, skip_gain, a_log)

    beside = shift(states[1], "seq", 1)
    *moved, beside, own_weight = after([*moved[::-1], beside, own_weight])
    kv = [own_piece, *moved[::-1]]
    half_shape = (heads, keep_rep, BLOCK, width)
    rows = steps * group
    *sends, kept, sent = call(
        functools.partial(attend, count, heads),
        [shape((rows, width), BF)] * 2
        + [shape((rows + state_rows(part), width), BF)] * (count - 2)
        + [shape(half_shape, BF)] * 2,
        [VM] * (2 + 2 * count),
        [VM] * (count + 2),
    )(q_near, new_near, bias, picks, *kv, *states[2:])
    order = [*range(2, count), 1]
    gathered = [shift(sends[c], "seq", c) for c in order]
    attn, mamba = call(
        functools.partial(collect, count, heads, steps, group),
        [shape((steps * count, half), BF), shape((steps, count, 1, part), F32)],
        [VM] * (4 + count),
        [VM] * 2,
        [pltpu.VMEM((heads, steps * count * group, hd), F32)],
    )(slope, base, states[0], beside, sends[0], *gathered)
    attn_other = shift(attn, "rep", 1)
    own_sum = call(
        project_own, shape((steps * count, columns), F32), [VM, VM], VM, us=0.7
    )(attn, own_weight)
    share = count // heads_count
    sums = call(
        functools.partial(project_other, heads_count, count),
        [shape((steps, share, columns), F32)] * heads_count,
        [VM, VM, VM],
        [VM] * heads_count,
        us=0.7,
    )(own_sum, attn_other, other_weight)
    sums = [sums[0]] + [shift(sums[c], "head", c) for c in range(1, heads_count)]
    got = shift(after([sent], mamba)[0], "rep", 1)
    kept = after([kept], sums[0])[0]
    operands = [kept, got, mamba] + ([shift(mamba, "rep", 1)] if split else [])
    handoff, mamba_out = call(
        functools.partial(assemble, split),
        [
            shape((1, dec_heads, keep_rep, BLOCK, width), BF),
            shape((steps, 1, channels), F32),
        ],
        [VM] * len(operands),
        [HB] * 2,
        [DMA((2 + steps * count * (2 if split else 1),))],
    )(*operands)
    sums[1:] = after(sums[1:], handoff)
    proj_out = call(
        add_up, shape((steps, share, columns), BF), [VM] * heads_count, VM, us=0.6
    )(*sums)
    return handoff, proj_out, mamba_out


def solution(mesh):
    return jax.shard_map(
        per_device,
        mesh=mesh,
        in_specs=(
            P("groups", ("head", "rep"), "seq", None),
            P("groups", None, None),
            P("groups", None),
            P(None, ("groups", "seq"), "head", None),
            P(None, ("groups", "seq"), "head", None),
            P("head", ("seq", "rep")),
            P("groups", None, ("head", "seq")),
            P(None, "head"),
            P(None, ("groups", "seq"), "head"),
            P(None, ("groups", "seq"), "head"),
            P(None, ("groups", "seq"), None, None),
            P("head"),
        ),
        out_specs=(
            P(("groups", "seq"), "head", "rep", None, None),
            P(None, ("groups", "head"), ("seq", "rep")),
            P(None, ("groups", "seq"), "head"),
        ),
        check_vma=False,
    )
```

```python
import functools

import jax
import jax.numpy as jnp
from jax import lax
from jax.experimental import pallas as pl
from jax.experimental.pallas import tpu as pltpu
from jax.sharding import PartitionSpec as P

BLOCK = 128
PIECES = 4
NEG = -1e30
BF = jnp.bfloat16
F32 = jnp.float32
VM = pl.BlockSpec(memory_space=pltpu.VMEM)
HB = pl.BlockSpec(memory_space=pltpu.HBM)
DMA = pltpu.SemaphoreType.DMA


def shift(x, axis, c):
    size = lax.axis_size(axis)
    return lax.ppermute(x, axis, [(i, i ^ c) for i in range(size)])


def across(x, c):
    count, reps = lax.axis_size("seq"), lax.axis_size("rep")
    pairs = [
        (s * reps + r, (s ^ c) * reps + (r ^ 1)) for s in range(count) for r in range(reps)
    ]
    return lax.ppermute(x, ("seq", "rep"), pairs)


def served():
    return 1 - lax.axis_index("rep")


def call(body, out_shape, in_specs, out_specs, scratch=(), us=1.0):
    return pl.pallas_call(
        body,
        out_shape=out_shape,
        in_specs=in_specs,
        out_specs=out_specs,
        scratch_shapes=list(scratch),
        cost_estimate=pl.CostEstimate(
            flops=0, bytes_accessed=int(us * 3.6e4), transcendentals=0
        ),
        compiler_params=pltpu.CompilerParams(vmem_limit_bytes=32 * 1024 * 1024),
    )


def in_hbm(x):
    return pltpu.with_memory_space_constraint(x, pltpu.HBM)


def after(arrays, *earlier):
    return lax.optimization_barrier((*arrays, *earlier))[: len(arrays)]


def run_all(copies):
    for copy in copies:
        copy.start()
    for copy in copies:
        copy.wait()


def copier(sems):
    position = iter(range(sems.shape[0]))
    return lambda src, dst: pltpu.make_async_copy(src, dst, sems.at[next(position)])


def state_rows(part):
    return 16 * pl.cdiv(part, 256)


def pack_state(piece, out_ref, first):
    ns, part = piece.shape
    for i in range(pl.cdiv(part, 256)):
        cut = piece[:, i * 256 : (i + 1) * 256]
        if cut.shape[1] < 256:
            cut = jnp.concatenate([cut, jnp.zeros((ns, 256 - cut.shape[1]), F32)], axis=1)
        out_ref[first + i * 16 : first + (i + 1) * 16, :] = cut.astype(BF)


def own_state(state_ref, c, split, part):
    me, rep = lax.axis_index("seq"), lax.axis_index("rep")
    if split:
        return state_ref.at[me ^ c, :, pl.ds(pl.multiple_of(rep * part, 128), part)]
    return state_ref.at[me ^ c]


def stage_blocks(count, kv_ref, *rest):
    outs, sems = rest[:-1], rest[-1]
    me = lax.axis_index("seq")
    copy = copier(sems)
    run_all(
        [
            copy(kv_ref.at[me ^ c, j], outs[c - 1].at[pl.ds(j * BLOCK, BLOCK)])
            for c in range(count - 1, 0, -1)
            for j in range(kv_ref.shape[1])
        ]
    )


def stage_rest(count, split, kv_ref, q_ref, new_ref, state_ref, blocks_ref, counts_ref, *rest):
    own_out, q_out, new_out, bias_out, pick_out = rest[:5]
    states = rest[5 : 5 + count]
    loaded, blocks, counts, sems, early = rest[5 + count :]
    me, rep = lax.axis_index("seq"), lax.axis_index("rep")
    heads = kv_ref.shape[1]
    copy = copier(sems)
    moves = [copy(kv_ref.at[me, j], own_out.at[pl.ds(j * BLOCK, BLOCK)]) for j in range(heads)]
    moves += [copy(q_ref, q_out), copy(new_ref, new_out)]
    copy = copier(early)
    first = [copy(blocks_ref, blocks), copy(counts_ref, counts)]
    part = loaded.shape[2]
    for c in range(count):
        if split:
            src = state_ref.at[me ^ c, :, pl.ds(pl.multiple_of(rep * part, 128), part)]
        else:
            src = state_ref.at[me ^ c]
        first.append(copy(src, loaded.at[c]))
    for move in first + moves:
        move.start()
    for move in first:
        move.wait()
    for c in range(count):
        pack_state(loaded[c], states[c], 0)
    head_first = lax.axis_index("head") * new_ref.shape[2] + served() * heads
    rows = bias_out.shape[0] // heads
    keep_rep = pick_out.shape[2]
    for j in range(heads):
        live_count = counts[me, head_first + j]
        for c in range(count):
            live = jnp.int32(0)
            for side in range(2):
                for k in range(keep_rep):
                    slot = (rep if side == 0 else 1 - rep) * keep_rep + k
                    hit = (blocks[me, slot, head_first + j] == (me ^ c)) & (slot < live_count)
                    one = jnp.where(hit, 1.0, 0.0).astype(F32)
                    pick_out[side, j, k, c] = jnp.full(pick_out.shape[4:], one, F32).astype(BF)
                    live = live | hit.astype(jnp.int32)
            dead = jnp.where(live > 0, 0.0, NEG).astype(F32)
            bias_out[j * rows : (j + 1) * rows, c * BLOCK : (c + 1) * BLOCK] = jnp.full(
                (rows, BLOCK), dead, F32
            )
    for move in moves:
        move.wait()


def dot_f32(a, b, contract):
    return lax.dot_general(a, b, (contract, ((), ())), preferred_element_type=F32)


def query_rows(q_ref, heads):
    steps, _, q_heads, _ = q_ref.shape
    own_q = q_heads // 2
    group = own_q // heads
    q_all = [q_ref[step, 0].astype(F32) for step in range(steps)]
    q_all = [jnp.where(served() == 0, q[:own_q], q[own_q:]) for q in q_all]
    return [
        jnp.concatenate([x[j * group : (j + 1) * group] for x in q_all], axis=0)
        for j in range(heads)
    ]


def block_scores(q, piece_ref, j):
    hd = piece_ref.shape[1] // 2
    keys = piece_ref[j * BLOCK : (j + 1) * BLOCK, :hd]
    return dot_f32(q.astype(BF), keys, ((1,), (1,))) * hd ** (-0.5)


def block_sums(weights, piece_ref, j):
    values = piece_ref[j * BLOCK : (j + 1) * BLOCK, piece_ref.shape[1] // 2 :]
    return dot_f32(weights, values, ((1,), (0,)))


def attend(count, heads, q_ref, new_ref, bias_ref, pick_ref, *rest):
    pieces, states = rest[:count], rest[count : 2 * count - 1]
    outs, (kept_ref, sent_ref) = rest[2 * count - 1 : 3 * count - 1], rest[3 * count - 1 :]
    queries = query_rows(q_ref, heads)
    rows, hd = queries[0].shape
    steps = q_ref.shape[0]
    group = rows // steps
    all_rows = heads * rows
    scale = hd ** (-0.5)
    scores = [
        jnp.concatenate([block_scores(q, piece, j) for piece in pieces], axis=1)
        for j, q in enumerate(queries)
    ]
    scores = jnp.concatenate(scores, axis=0)
    alive = bias_ref[...] == 0.0
    scores = jnp.where(alive, scores, NEG)
    row_step = (lax.broadcasted_iota(jnp.int32, (all_rows, 1), 0) // group) % steps
    wide_q = jnp.concatenate(queries, axis=0)
    dots, fresh_values = [], []
    top = jnp.max(scores, axis=1, keepdims=True)
    for step in range(steps):
        both = new_ref[step, 0].astype(F32)
        fresh = jnp.where(served() == 0, both[:heads], both[heads:])
        wide = jnp.concatenate(
            [jnp.broadcast_to(fresh[j : j + 1], (rows, 2 * hd)) for j in range(heads)], axis=0
        )
        dot = jnp.sum(wide_q * wide[:, :hd], axis=1, keepdims=True) * scale
        dots.append(jnp.where(row_step >= step, dot, NEG))
        fresh_values.append(wide[:, hd:])
        top = jnp.maximum(top, dots[-1])
    weights = jnp.where(alive, jnp.exp(scores - top), 0.0)
    total = jnp.sum(weights, axis=1, keepdims=True)
    weights = weights.astype(BF)
    summed = []
    for j in range(heads):
        parts = [
            block_sums(weights[j * rows : (j + 1) * rows, c * BLOCK : (c + 1) * BLOCK], piece, j)
            for c, piece in enumerate(pieces)
        ]
        summed.append(functools.reduce(jnp.add, parts))
    summed = jnp.concatenate(summed, axis=0)
    for step in range(steps):
        weight = jnp.where(row_step >= step, jnp.exp(dots[step] - top), 0.0)
        total = total + weight
        summed = summed + weight.astype(BF).astype(F32) * fresh_values[step]
    result = (summed / total).astype(BF)
    for c in range(count):
        for j in range(2):
            half = result[j * rows : (j + 1) * rows] if j < heads else jnp.zeros((rows, hd), BF)
            outs[c][:rows, j * hd : (j + 1) * hd] = half
        if c:
            outs[c][rows:, :] = states[c - 1][...]
    tile = pick_ref.shape[4]
    for side, ref in ((1, sent_ref), (0, kept_ref)):
        for j in range(heads):
            for k in range(ref.shape[1]):
                total = None
                for c in range(count):
                    piece = pieces[c][j * BLOCK : (j + 1) * BLOCK, :].reshape(-1, tile, 2 * hd)
                    term = piece * pick_ref[side, j, k, c][None]
                    total = term if total is None else total + term
                ref[j, k] = total.reshape(BLOCK, 2 * hd)


def collect(count, heads, steps, group, slope_ref, base_ref, home_ref, *rest):
    parts = [rest[0], rest[count - 1], *rest[1 : count - 1]]
    states = [home_ref, *parts[1:]]
    out_ref, mamba_ref, scratch = rest[count:]
    me = lax.axis_index("seq")
    ns, part = slope_ref.shape[2:]
    for c in range(count):
        first = states[c].shape[0] - state_rows(part)
        rows = [
            states[c][first + 16 * i : first + 16 * (i + 1), :].astype(F32)
            for i in range(pl.cdiv(part, 256))
        ]
        state = jnp.concatenate(rows, axis=1)[:, :part]
        for step in range(steps):
            mamba_ref[step, me ^ c] = base_ref[c, step] + jnp.sum(
                slope_ref[c, step] * state, axis=0, keepdims=True
            )
    for c in range(count):
        rows = parts[c][: steps * group, :].astype(F32)
        for j in range(heads):
            for step in range(steps):
                at = pl.multiple_of((step * count + (me ^ c)) * group, group)
                cut = rows[step * group : (step + 1) * group, j * 128 : (j + 1) * 128]
                scratch[j, pl.ds(at, group), :] = cut
    for j in range(heads):
        for g in range(group):
            at = (j * group + g) * 128
            tile = scratch[j, pl.ds(g, steps * count, stride=group), :]
            out_ref[:, at : at + 128] = tile.astype(BF)


def weight_half(weight_ref, out_ref, which, copy):
    half = out_ref.shape[0]
    rows = half // PIECES
    cuts = [(pl.ds(which * half + i * rows, rows), pl.ds(i * rows, rows)) for i in range(PIECES)]
    return [copy(weight_ref.at[src], out_ref.at[dst]) for src, dst in cuts]


def project_own(attn_ref, weight_ref, out_ref):
    out_ref[...] = dot_f32(attn_ref[...], weight_ref[...], ((1,), (0,)))


def pick(options, index):
    chosen = options[0]
    for i in range(1, len(options)):
        chosen = jnp.where(index == i, options[i], chosen)
    return chosen


def project_other(heads_count, count, acc_ref, attn_ref, weight_ref, *outs):
    total = acc_ref[...] + dot_f32(attn_ref[...], weight_ref[...], ((1,), (0,)))
    head = lax.axis_index("head")
    steps = total.shape[0] // count
    share = count // heads_count
    for step in range(steps):
        slices = [
            total[step * count + x * share : step * count + (x + 1) * share]
            for x in range(heads_count)
        ]
        for c in range(heads_count):
            outs[c][step] = pick(slices, head ^ c)


def add_up(*refs):
    total = refs[0][...]
    for ref in refs[1:-1]:
        total = total + ref[...]
    refs[-1][...] = total.astype(BF)


def prepare(count, split, weight_hbm, dt_hbm, x_hbm, bc_hbm, gain_hbm, log_hbm, own_ref, other_ref,
            slope_ref, base_ref, dt_ref, x_ref, bc_ref, gain_ref, log_ref, sems, weight_sems):
    copy = copier(sems)
    first = [
        copy(dt_hbm, dt_ref),
        copy(x_hbm, x_ref),
        copy(bc_hbm, bc_ref),
        copy(gain_hbm, gain_ref),
        copy(log_hbm, log_ref),
    ]
    copy, which = copier(weight_sems), served()
    weights = weight_half(weight_hbm, own_ref, which, copy)
    weights += weight_half(weight_hbm, other_ref, 1 - which, copy)
    for move in first + weights:
        move.start()
    for move in first:
        move.wait()
    me, rep = lax.axis_index("seq"), lax.axis_index("rep")
    _, steps, ns, part = slope_ref.shape
    block = part * 2 if split else part
    diagonal = lax.broadcasted_iota(jnp.int32, (ns, ns), 0) == lax.broadcasted_iota(
        jnp.int32, (ns, ns), 1
    )

    def column(row):
        return jnp.sum(jnp.where(diagonal, row, 0.0), axis=1, keepdims=True)

    drive = [column(bc_ref[step, 0, 0:1, :]) for step in range(steps)]
    read = [column(bc_ref[step, 0, 1:2, :]) for step in range(steps)]
    for c in range(count):
        first = (me ^ c) * block + (rep * part if split else 0)
        lanes = pl.ds(pl.multiple_of(first, 128), part)
        rate = -jnp.exp(log_ref[:, lanes])
        gain = gain_ref[:, lanes]
        kept = jnp.ones((ns, part), F32)
        added = jnp.zeros((ns, part), F32)
        for step in range(steps):
            dt = dt_ref[step, :, lanes]
            inputs = x_ref[step : step + 1, lanes].astype(F32)
            decay = jnp.exp(dt * rate)
            kept = kept * decay
            added = added * decay + drive[step] * (dt * inputs)
            slope_ref[c, step] = read[step] * kept
            base_ref[c, step] = (
                jnp.sum(read[step] * added, axis=0, keepdims=True) + gain * inputs
            )
    for move in weights:
        move.wait()


def assemble(split, kept_ref, got_ref, mamba_ref, *rest):
    rep = lax.axis_index("rep")
    if split:
        other_ref, handoff_ref, out_ref, sems = rest
    else:
        handoff_ref, out_ref, sems = rest
    heads = kept_ref.shape[0]
    copy = copier(sems)
    moves = [
        copy(kept_ref, handoff_ref.at[0, pl.ds((1 - rep) * heads, heads)]),
        copy(got_ref, handoff_ref.at[0, pl.ds(rep * heads, heads)]),
    ]
    steps, count, _, part = mamba_ref.shape
    for step in range(steps):
        for b in range(count):
            if split:
                for ref, side in ((mamba_ref, rep), (other_ref, 1 - rep)):
                    lanes = pl.ds(pl.multiple_of((2 * b + side) * part, 128), part)
                    moves.append(copy(ref.at[step, b], out_ref.at[step, :, lanes]))
            else:
                moves.append(copy(mamba_ref.at[step, b], out_ref.at[step, :, pl.ds(b * part, part)]))
    run_all(moves)


def per_device(
    prefill_kv,
    kept_blocks,
    kept_counts,
    queries,
    new_kv,
    out_weight,
    prefill_state,
    a_log,
    step_input,
    step_dt,
    step_bc,
    skip_gain,
):
    count = lax.axis_size("seq")
    reps = lax.axis_size("rep")
    heads_count = lax.axis_size("head")
    requests, heads, tokens, width = prefill_kv.shape
    assert requests == count and tokens == BLOCK and reps == 2 and width == 256
    assert count & (count - 1) == 0 and heads_count & (heads_count - 1) == 0
    keep = kept_blocks.shape[2]
    keep_rep = keep // reps
    steps, _, q_heads, hd = queries.shape
    dec_heads = new_kv.shape[2]
    group = q_heads // dec_heads
    _, ns, block = prefill_state.shape
    split = block % (reps * 128) == 0
    part = block // reps if split else block
    all_rows = heads * steps * group
    assert all_rows <= 128
    channels = count * block
    shape = jax.ShapeDtypeStruct
    smem = pltpu.SMEM
    blocks = jnp.swapaxes(kept_blocks, 1, 2)

    prefill_kv, prefill_state, queries, new_kv = map(in_hbm, (prefill_kv, prefill_state, queries, new_kv))
    step_dt, step_bc, a_log, out_weight = map(in_hbm, (step_dt, step_bc, a_log, out_weight))
    step_input = in_hbm(step_input.reshape(steps, channels))
    skip_gain = in_hbm(skip_gain.reshape(1, -1))
    blocks, kept_counts = in_hbm(blocks), in_hbm(kept_counts)

    columns = out_weight.shape[1]
    half = heads * group * hd
    half_weight = pltpu.VMEM((half, columns), BF)
    block_shape = shape((heads * BLOCK, width), BF)
    pieces = call(
        functools.partial(stage_blocks, count),
        [block_shape] * (count - 1),
        [HB],
        [VM] * (count - 1),
        [DMA(((count - 1) * heads,))],
    )(prefill_kv)
    moved = [across(pieces[c - 1], c) for c in range(count - 1, 0, -1)][::-1]
    own_piece, q_near, new_near, bias, picks, *states = call(
        functools.partial(stage_rest, count, split),
        [
            block_shape,
            shape(queries.shape, BF),
            shape(new_kv.shape, BF),
            shape((all_rows, count * BLOCK), F32),
            shape((reps, heads, keep_rep, count, 16, width), BF),
        ]
        + [shape((state_rows(part), width), BF)] * count,
        [HB] * 6,
        [VM] * (5 + count),
        [
            pltpu.VMEM((count, ns, part), F32),
            smem(blocks.shape, jnp.int32),
            smem(kept_counts.shape, jnp.int32),
            DMA((heads + 2,)),
            DMA((count + 2,)),
        ],
    )(*after([prefill_kv], pieces[0]), queries, new_kv, prefill_state, blocks, kept_counts)
    own_weight, other_weight, slope, base = call(
        functools.partial(prepare, count, split),
        [
            half_weight,
            half_weight,
            shape((count, steps, ns, part), F32),
            shape((count, steps, 1, part), F32),
        ],
        [HB] * 6,
        [VM] * 4,
        [
            pltpu.VMEM((steps, 1, channels), F32),
            pltpu.VMEM((steps, channels), BF),
            pltpu.VMEM(step_bc.shape, F32),
            pltpu.VMEM((1, channels), F32),
            pltpu.VMEM(a_log.shape, F32),
            DMA((5,)),
            DMA((2 * PIECES,)),
        ],
    )(*after([out_weight], pieces[0]), step_dt, step_input, step_bc, skip_gain, a_log)

    own_piece = shift(own_piece, "rep", 1)
    *moved, own_piece, own_weight = after([*moved[::-1], own_piece, own_weight])
    kv = [own_piece, *moved[::-1]]
    half_shape = (heads, keep_rep, BLOCK, width)
    rows = steps * group
    *sends, kept, sent = call(
        functools.partial(attend, count, heads),
        [shape((rows, width), BF)]
        + [shape((rows + state_rows(part), width), BF)] * (count - 1)
        + [shape(half_shape, BF)] * 2,
        [VM] * (3 + 2 * count),
        [VM] * (count + 2),
    )(q_near, new_near, bias, picks, *kv, *states[1:])
    order = [*range(2, count), 1]
    gathered = [shift(sends[c], "seq", c) for c in order]
    attn, mamba = call(
        functools.partial(collect, count, heads, steps, group),
        [shape((steps * count, half), BF), shape((steps, count, 1, part), F32)],
        [VM] * (3 + count),
        [VM] * 2,
        [pltpu.VMEM((heads, steps * count * group, hd), F32)],
    )(slope, base, states[0], sends[0], *gathered)
    attn_other = shift(attn, "rep", 1)
    own_sum = call(
        project_own, shape((steps * count, columns), F32), [VM, VM], VM, us=0.7
    )(attn, own_weight)
    share = count // heads_count
    sums = call(
        functools.partial(project_other, heads_count, count),
        [shape((steps, share, columns), F32)] * heads_count,
        [VM, VM, VM],
        [VM] * heads_count,
        us=0.7,
    )(own_sum, attn_other, other_weight)
    sums = [sums[0]] + [shift(sums[c], "head", c) for c in range(1, heads_count)]
    got = shift(after([sent], mamba)[0], "rep", 1)
    kept = after([kept], sums[0])[0]
    operands = [kept, got, mamba] + ([shift(mamba, "rep", 1)] if split else [])
    handoff, mamba_out = call(
        functools.partial(assemble, split),
        [
            shape((1, dec_heads, keep_rep, BLOCK, width), BF),
            shape((steps, 1, channels), F32),
        ],
        [VM] * len(operands),
        [HB] * 2,
        [DMA((2 + steps * count * (2 if split else 1),))],
    )(*operands)
    sums[1:] = after(sums[1:], handoff)
    proj_out = call(
        add_up, shape((steps, share, columns), BF), [VM] * heads_count, VM, us=0.6
    )(*sums)
    return handoff, proj_out, mamba_out


def solution(mesh):
    return jax.shard_map(
        per_device,
        mesh=mesh,
        in_specs=(
            P("groups", ("head", "rep"), "seq", None),
            P("groups", None, None),
            P("groups", None),
            P(None, ("groups", "seq"), "head", None),
            P(None, ("groups", "seq"), "head", None),
            P("head", ("seq", "rep")),
            P("groups", None, ("head", "seq")),
            P(None, "head"),
            P(None, ("groups", "seq"), "head"),
            P(None, ("groups", "seq"), "head"),
            P(None, ("groups", "seq"), None, None),
            P("head"),
        ),
        out_specs=(
            P(("groups", "seq"), "head", "rep", None, None),
            P(None, ("groups", "head"), ("seq", "rep")),
            P(None, ("groups", "seq"), "head"),
        ),
        check_vma=False,
    )
```

```python
import functools

import jax
import jax.numpy as jnp
from jax import lax
from jax.experimental import pallas as pl
from jax.experimental.pallas import tpu as pltpu
from jax.sharding import PartitionSpec as P

BLOCK = 128
PIECES = 4
NEG = -1e30
BF = jnp.bfloat16
F32 = jnp.float32
VM = pl.BlockSpec(memory_space=pltpu.VMEM)
HB = pl.BlockSpec(memory_space=pltpu.HBM)
DMA = pltpu.SemaphoreType.DMA


def shift(x, axis, c):
    size = lax.axis_size(axis)
    return lax.ppermute(x, axis, [(i, i ^ c) for i in range(size)])


def call(body, out_shape, in_specs, out_specs, scratch=(), us=1.0):
    return pl.pallas_call(
        body,
        out_shape=out_shape,
        in_specs=in_specs,
        out_specs=out_specs,
        scratch_shapes=list(scratch),
        cost_estimate=pl.CostEstimate(
            flops=0, bytes_accessed=int(us * 3.6e4), transcendentals=0
        ),
        compiler_params=pltpu.CompilerParams(vmem_limit_bytes=32 * 1024 * 1024),
    )


def in_hbm(x):
    return pltpu.with_memory_space_constraint(x, pltpu.HBM)


def after(arrays, *earlier):
    return lax.optimization_barrier((*arrays, *earlier))[: len(arrays)]


def run_all(copies):
    for copy in copies:
        copy.start()
    for copy in copies:
        copy.wait()


def copier(sems):
    position = iter(range(sems.shape[0]))
    return lambda src, dst: pltpu.make_async_copy(src, dst, sems.at[next(position)])


def state_rows(part):
    return 16 * pl.cdiv(part, 256)


def pack_state(piece, out_ref, first):
    ns, part = piece.shape
    for i in range(pl.cdiv(part, 256)):
        cut = piece[:, i * 256 : (i + 1) * 256]
        if cut.shape[1] < 256:
            cut = jnp.concatenate([cut, jnp.zeros((ns, 256 - cut.shape[1]), F32)], axis=1)
        out_ref[first + i * 16 : first + (i + 1) * 16, :] = cut.astype(BF)


def own_state(state_ref, c, split, part):
    me, rep = lax.axis_index("seq"), lax.axis_index("rep")
    if split:
        return state_ref.at[me ^ c, :, pl.ds(pl.multiple_of(rep * part, 128), part)]
    return state_ref.at[me ^ c]


def stage_blocks(count, kv_ref, *rest):
    outs, sems = rest[:-1], rest[-1]
    me = lax.axis_index("seq")
    copy = copier(sems)
    run_all(
        [
            copy(kv_ref.at[me ^ c, j], outs[c - 1].at[pl.ds(j * BLOCK, BLOCK)])
            for c in range(count - 1, 0, -1)
            for j in range(kv_ref.shape[1])
        ]
    )


def stage_rest(count, split, kv_ref, q_ref, new_ref, state_ref, blocks_ref, counts_ref, *rest):
    own_out, q_out, new_out, bias_out, pick_out = rest[:5]
    states = rest[5 : 5 + count]
    loaded, blocks, counts, sems, early = rest[5 + count :]
    me, rep = lax.axis_index("seq"), lax.axis_index("rep")
    heads = kv_ref.shape[1]
    copy = copier(sems)
    moves = [copy(kv_ref.at[me, j], own_out.at[pl.ds(j * BLOCK, BLOCK)]) for j in range(heads)]
    moves += [copy(q_ref, q_out), copy(new_ref, new_out)]
    copy = copier(early)
    first = [copy(blocks_ref, blocks), copy(counts_ref, counts)]
    part = loaded.shape[2]
    for c in range(count):
        if split:
            src = state_ref.at[me ^ c, :, pl.ds(pl.multiple_of(rep * part, 128), part)]
        else:
            src = state_ref.at[me ^ c]
        first.append(copy(src, loaded.at[c]))
    for move in first + moves:
        move.start()
    for move in first:
        move.wait()
    for c in range(count):
        pack_state(loaded[c], states[c], states[c].shape[0] - state_rows(part))
    head_first = lax.axis_index("head") * new_ref.shape[2] + rep * heads
    rows = bias_out.shape[0] // heads
    keep_rep = pick_out.shape[2]
    for j in range(heads):
        live_count = counts[me, head_first + j]
        for c in range(count):
            live = jnp.int32(0)
            for side in range(2):
                for k in range(keep_rep):
                    slot = (rep if side == 0 else 1 - rep) * keep_rep + k
                    hit = (blocks[me, slot, head_first + j] == (me ^ c)) & (slot < live_count)
                    one = jnp.where(hit, 1.0, 0.0).astype(F32)
                    pick_out[side, j, k, c] = jnp.full(pick_out.shape[4:], one, F32).astype(BF)
                    live = live | hit.astype(jnp.int32)
            dead = jnp.where(live > 0, 0.0, NEG).astype(F32)
            bias_out[j * rows : (j + 1) * rows, c * BLOCK : (c + 1) * BLOCK] = jnp.full(
                (rows, BLOCK), dead, F32
            )
    for move in moves:
        move.wait()


def dot_f32(a, b, contract):
    return lax.dot_general(a, b, (contract, ((), ())), preferred_element_type=F32)


def query_rows(q_ref, heads):
    rep = lax.axis_index("rep")
    steps, _, q_heads, _ = q_ref.shape
    own_q = q_heads // 2
    group = own_q // heads
    q_all = [q_ref[step, 0].astype(F32) for step in range(steps)]
    q_all = [jnp.where(rep == 0, q[:own_q], q[own_q:]) for q in q_all]
    return [
        jnp.concatenate([x[j * group : (j + 1) * group] for x in q_all], axis=0)
        for j in range(heads)
    ]


def block_scores(q, piece_ref, j):
    hd = piece_ref.shape[1] // 2
    keys = piece_ref[j * BLOCK : (j + 1) * BLOCK, :hd]
    return dot_f32(q.astype(BF), keys, ((1,), (1,))) * hd ** (-0.5)


def block_sums(weights, piece_ref, j):
    values = piece_ref[j * BLOCK : (j + 1) * BLOCK, piece_ref.shape[1] // 2 :]
    return dot_f32(weights, values, ((1,), (0,)))


def attend(count, heads, q_ref, new_ref, bias_ref, pick_ref, *rest):
    pieces, states = rest[:count], rest[count : 2 * count - 2]
    outs, (kept_ref, sent_ref) = rest[2 * count - 2 : 3 * count - 2], rest[3 * count - 2 :]
    rep = lax.axis_index("rep")
    queries = query_rows(q_ref, heads)
    rows, hd = queries[0].shape
    steps = q_ref.shape[0]
    group = rows // steps
    all_rows = heads * rows
    scale = hd ** (-0.5)
    scores = [
        jnp.concatenate([block_scores(q, piece, j) for piece in pieces], axis=1)
        for j, q in enumerate(queries)
    ]
    scores = jnp.concatenate(scores, axis=0)
    alive = bias_ref[...] == 0.0
    scores = jnp.where(alive, scores, NEG)
    row_step = (lax.broadcasted_iota(jnp.int32, (all_rows, 1), 0) // group) % steps
    wide_q = jnp.concatenate(queries, axis=0)
    dots, fresh_values = [], []
    top = jnp.max(scores, axis=1, keepdims=True)
    for step in range(steps):
        both = new_ref[step, 0].astype(F32)
        fresh = jnp.where(rep == 0, both[:heads], both[heads:])
        wide = jnp.concatenate(
            [jnp.broadcast_to(fresh[j : j + 1], (rows, 2 * hd)) for j in range(heads)], axis=0
        )
        dot = jnp.sum(wide_q * wide[:, :hd], axis=1, keepdims=True) * scale
        dots.append(jnp.where(row_step >= step, dot, NEG))
        fresh_values.append(wide[:, hd:])
        top = jnp.maximum(top, dots[-1])
    weights = jnp.where(alive, jnp.exp(scores - top), 0.0)
    total = jnp.sum(weights, axis=1, keepdims=True)
    weights = weights.astype(BF)
    summed = []
    for j in range(heads):
        parts = [
            block_sums(weights[j * rows : (j + 1) * rows, c * BLOCK : (c + 1) * BLOCK], piece, j)
            for c, piece in enumerate(pieces)
        ]
        summed.append(functools.reduce(jnp.add, parts))
    summed = jnp.concatenate(summed, axis=0)
    for step in range(steps):
        weight = jnp.where(row_step >= step, jnp.exp(dots[step] - top), 0.0)
        total = total + weight
        summed = summed + weight.astype(BF).astype(F32) * fresh_values[step]
    result = (summed / total).astype(BF)
    for c in range(count):
        for j in range(2):
            half = result[j * rows : (j + 1) * rows] if j < heads else jnp.zeros((rows, hd), BF)
            outs[c][:rows, j * hd : (j + 1) * hd] = half
        if c > 1:
            outs[c][rows:, :] = states[c - 2][...]
    tile = pick_ref.shape[4]
    for side, ref in ((1, sent_ref), (0, kept_ref)):
        for j in range(heads):
            for k in range(ref.shape[1]):
                total = None
                for c in range(count):
                    piece = pieces[c][j * BLOCK : (j + 1) * BLOCK, :].reshape(-1, tile, 2 * hd)
                    term = piece * pick_ref[side, j, k, c][None]
                    total = term if total is None else total + term
                ref[j, k] = total.reshape(BLOCK, 2 * hd)


def collect(count, heads, steps, group, slope_ref, base_ref, home_ref, beside_ref, *rest):
    parts = [rest[0], rest[count - 1], *rest[1 : count - 1]]
    states = [home_ref, beside_ref, *parts[2:]]
    out_ref, mamba_ref, scratch = rest[count:]
    me = lax.axis_index("seq")
    ns, part = slope_ref.shape[2:]
    for c in range(count):
        first = states[c].shape[0] - state_rows(part)
        rows = [
            states[c][first + 16 * i : first + 16 * (i + 1), :].astype(F32)
            for i in range(pl.cdiv(part, 256))
        ]
        state = jnp.concatenate(rows, axis=1)[:, :part]
        for step in range(steps):
            mamba_ref[step, me ^ c] = base_ref[c, step] + jnp.sum(
                slope_ref[c, step] * state, axis=0, keepdims=True
            )
    for c in range(count):
        rows = parts[c][: steps * group, :].astype(F32)
        for j in range(heads):
            for step in range(steps):
                at = pl.multiple_of((step * count + (me ^ c)) * group, group)
                cut = rows[step * group : (step + 1) * group, j * 128 : (j + 1) * 128]
                scratch[j, pl.ds(at, group), :] = cut
    for j in range(heads):
        for g in range(group):
            at = (j * group + g) * 128
            tile = scratch[j, pl.ds(g, steps * count, stride=group), :]
            out_ref[:, at : at + 128] = tile.astype(BF)


def weight_half(weight_ref, out_ref, which, copy):
    half = out_ref.shape[0]
    rows = half // PIECES
    cuts = [(pl.ds(which * half + i * rows, rows), pl.ds(i * rows, rows)) for i in range(PIECES)]
    return [copy(weight_ref.at[src], out_ref.at[dst]) for src, dst in cuts]


def project_own(attn_ref, weight_ref, out_ref):
    out_ref[...] = dot_f32(attn_ref[...], weight_ref[...], ((1,), (0,)))


def pick(options, index):
    chosen = options[0]
    for i in range(1, len(options)):
        chosen = jnp.where(index == i, options[i], chosen)
    return chosen


def project_other(heads_count, count, acc_ref, attn_ref, weight_ref, *outs):
    total = acc_ref[...] + dot_f32(attn_ref[...], weight_ref[...], ((1,), (0,)))
    head = lax.axis_index("head")
    steps = total.shape[0] // count
    share = count // heads_count
    for step in range(steps):
        slices = [
            total[step * count + x * share : step * count + (x + 1) * share]
            for x in range(heads_count)
        ]
        for c in range(heads_count):
            outs[c][step] = pick(slices, head ^ c)


def add_up(*refs):
    total = refs[0][...]
    for ref in refs[1:-1]:
        total = total + ref[...]
    refs[-1][...] = total.astype(BF)


def prepare(count, split, weight_hbm, dt_hbm, x_hbm, bc_hbm, gain_hbm, log_hbm, own_ref, other_ref,
            slope_ref, base_ref, dt_ref, x_ref, bc_ref, gain_ref, log_ref, sems, weight_sems):
    copy = copier(sems)
    first = [
        copy(dt_hbm, dt_ref),
        copy(x_hbm, x_ref),
        copy(bc_hbm, bc_ref),
        copy(gain_hbm, gain_ref),
        copy(log_hbm, log_ref),
    ]
    copy, which = copier(weight_sems), lax.axis_index("rep")
    weights = weight_half(weight_hbm, own_ref, which, copy)
    weights += weight_half(weight_hbm, other_ref, 1 - which, copy)
    for move in first + weights:
        move.start()
    for move in first:
        move.wait()
    me, rep = lax.axis_index("seq"), lax.axis_index("rep")
    _, steps, ns, part = slope_ref.shape
    block = part * 2 if split else part
    diagonal = lax.broadcasted_iota(jnp.int32, (ns, ns), 0) == lax.broadcasted_iota(
        jnp.int32, (ns, ns), 1
    )

    def column(row):
        return jnp.sum(jnp.where(diagonal, row, 0.0), axis=1, keepdims=True)

    drive = [column(bc_ref[step, 0, 0:1, :]) for step in range(steps)]
    read = [column(bc_ref[step, 0, 1:2, :]) for step in range(steps)]
    for c in range(count):
        first = (me ^ c) * block + (rep * part if split else 0)
        lanes = pl.ds(pl.multiple_of(first, 128), part)
        rate = -jnp.exp(log_ref[:, lanes])
        gain = gain_ref[:, lanes]
        kept = jnp.ones((ns, part), F32)
        added = jnp.zeros((ns, part), F32)
        for step in range(steps):
            dt = dt_ref[step, :, lanes]
            inputs = x_ref[step : step + 1, lanes].astype(F32)
            decay = jnp.exp(dt * rate)
            kept = kept * decay
            added = added * decay + drive[step] * (dt * inputs)
            slope_ref[c, step] = read[step] * kept
            base_ref[c, step] = (
                jnp.sum(read[step] * added, axis=0, keepdims=True) + gain * inputs
            )
    for move in weights:
        move.wait()


def assemble(split, kept_ref, got_ref, mamba_ref, *rest):
    rep = lax.axis_index("rep")
    if split:
        other_ref, handoff_ref, out_ref, sems = rest
    else:
        handoff_ref, out_ref, sems = rest
    heads = kept_ref.shape[0]
    copy = copier(sems)
    moves = [
        copy(kept_ref, handoff_ref.at[0, pl.ds(rep * heads, heads)]),
        copy(got_ref, handoff_ref.at[0, pl.ds((1 - rep) * heads, heads)]),
    ]
    steps, count, _, part = mamba_ref.shape
    for step in range(steps):
        for b in range(count):
            if split:
                for ref, side in ((mamba_ref, rep), (other_ref, 1 - rep)):
                    lanes = pl.ds(pl.multiple_of((2 * b + side) * part, 128), part)
                    moves.append(copy(ref.at[step, b], out_ref.at[step, :, lanes]))
            else:
                moves.append(copy(mamba_ref.at[step, b], out_ref.at[step, :, pl.ds(b * part, part)]))
    run_all(moves)


def per_device(
    prefill_kv,
    kept_blocks,
    kept_counts,
    queries,
    new_kv,
    out_weight,
    prefill_state,
    a_log,
    step_input,
    step_dt,
    step_bc,
    skip_gain,
):
    count = lax.axis_size("seq")
    reps = lax.axis_size("rep")
    heads_count = lax.axis_size("head")
    requests, heads, tokens, width = prefill_kv.shape
    assert requests == count and tokens == BLOCK and reps == 2 and width == 256
    assert count & (count - 1) == 0 and heads_count & (heads_count - 1) == 0
    keep = kept_blocks.shape[2]
    keep_rep = keep // reps
    steps, _, q_heads, hd = queries.shape
    dec_heads = new_kv.shape[2]
    group = q_heads // dec_heads
    _, ns, block = prefill_state.shape
    split = block % (reps * 128) == 0
    part = block // reps if split else block
    all_rows = heads * steps * group
    assert all_rows <= 128
    channels = count * block
    shape = jax.ShapeDtypeStruct
    smem = pltpu.SMEM
    blocks = jnp.swapaxes(kept_blocks, 1, 2)

    prefill_kv, prefill_state, queries, new_kv = map(in_hbm, (prefill_kv, prefill_state, queries, new_kv))
    step_dt, step_bc, a_log, out_weight = map(in_hbm, (step_dt, step_bc, a_log, out_weight))
    step_input = in_hbm(step_input.reshape(steps, channels))
    skip_gain = in_hbm(skip_gain.reshape(1, -1))
    blocks, kept_counts = in_hbm(blocks), in_hbm(kept_counts)

    columns = out_weight.shape[1]
    half = heads * group * hd
    half_weight = pltpu.VMEM((half, columns), BF)
    block_shape = shape((heads * BLOCK, width), BF)
    pieces = call(
        functools.partial(stage_blocks, count),
        [block_shape] * (count - 1),
        [HB],
        [VM] * (count - 1),
        [DMA(((count - 1) * heads,))],
    )(prefill_kv)
    moved = [shift(pieces[c - 1], "seq", c) for c in range(count - 1, 0, -1)][::-1]
    own_piece, q_near, new_near, bias, picks, *states = call(
        functools.partial(stage_rest, count, split),
        [
            block_shape,
            shape(queries.shape, BF),
            shape(new_kv.shape, BF),
            shape((all_rows, count * BLOCK), F32),
            shape((reps, heads, keep_rep, count, 16, width), BF),
        ]
        + [shape((state_rows(part) + (32 if c == 1 else 0), width), BF) for c in range(count)],
        [HB] * 6,
        [VM] * (5 + count),
        [
            pltpu.VMEM((count, ns, part), F32),
            smem(blocks.shape, jnp.int32),
            smem(kept_counts.shape, jnp.int32),
            DMA((heads + 2,)),
            DMA((count + 2,)),
        ],
    )(*after([prefill_kv], pieces[0]), queries, new_kv, prefill_state, blocks, kept_counts)
    own_weight, other_weight, slope, base = call(
        functools.partial(prepare, count, split),
        [
            half_weight,
            half_weight,
            shape((count, steps, ns, part), F32),
            shape((count, steps, 1, part), F32),
        ],
        [HB] * 6,
        [VM] * 4,
        [
            pltpu.VMEM((steps, 1, channels), F32),
            pltpu.VMEM((steps, channels), BF),
            pltpu.VMEM(step_bc.shape, F32),
            pltpu.VMEM((1, channels), F32),
            pltpu.VMEM(a_log.shape, F32),
            DMA((5,)),
            DMA((2 * PIECES,)),
        ],
    )(*after([out_weight], pieces[0]), step_dt, step_input, step_bc, skip_gain, a_log)

    beside = shift(after(states[1:2], own_weight)[0], "seq", 1)
    *moved, own_weight = after([*moved[::-1], own_weight])
    kv = [own_piece, *moved[::-1]]
    half_shape = (heads, keep_rep, BLOCK, width)
    rows = steps * group
    *sends, kept, sent = call(
        functools.partial(attend, count, heads),
        [shape((rows, width), BF)] * 2
        + [shape((rows + state_rows(part), width), BF)] * (count - 2)
        + [shape(half_shape, BF)] * 2,
        [VM] * (2 + 2 * count),
        [VM] * (count + 2),
    )(q_near, new_near, bias, picks, *kv, *states[2:])
    order = [*range(2, count), 1]
    gathered = [shift(sends[c], "seq", c) for c in order]
    attn, mamba = call(
        functools.partial(collect, count, heads, steps, group),
        [shape((steps * count, half), BF), shape((steps, count, 1, part), F32)],
        [VM] * (4 + count),
        [VM] * 2,
        [pltpu.VMEM((heads, steps * count * group, hd), F32)],
    )(slope, base, states[0], beside, sends[0], *gathered)
    attn_other = shift(attn, "rep", 1)
    own_sum = call(
        project_own, shape((steps * count, columns), F32), [VM, VM], VM, us=0.7
    )(attn, own_weight)
    share = count // heads_count
    sums = call(
        functools.partial(project_other, heads_count, count),
        [shape((steps, share, columns), F32)] * heads_count,
        [VM, VM, VM],
        [VM] * heads_count,
        us=0.7,
    )(own_sum, attn_other, other_weight)
    sums = [sums[0]] + [shift(sums[c], "head", c) for c in range(1, heads_count)]
    got = shift(after([sent], mamba)[0], "rep", 1)
    kept = after([kept], sums[0])[0]
    operands = [kept, got, mamba] + ([shift(mamba, "rep", 1)] if split else [])
    handoff, mamba_out = call(
        functools.partial(assemble, split),
        [
            shape((1, dec_heads, keep_rep, BLOCK, width), BF),
            shape((steps, 1, channels), F32),
        ],
        [VM] * len(operands),
        [HB] * 2,
        [DMA((2 + steps * count * (2 if split else 1),))],
    )(*operands)
    sums[1:] = after(sums[1:], handoff)
    proj_out = call(
        add_up, shape((steps, share, columns), BF), [VM] * heads_count, VM, us=0.6
    )(*sums)
    return handoff, proj_out, mamba_out


def solution(mesh):
    return jax.shard_map(
        per_device,
        mesh=mesh,
        in_specs=(
            P("groups", ("head", "rep"), "seq", None),
            P("groups", None, None),
            P("groups", None),
            P(None, ("groups", "seq"), "head", None),
            P(None, ("groups", "seq"), "head", None),
            P("head", ("seq", "rep")),
            P("groups", None, ("head", "seq")),
            P(None, "head"),
            P(None, ("groups", "seq"), "head"),
            P(None, ("groups", "seq"), "head"),
            P(None, ("groups", "seq"), None, None),
            P("head"),
        ),
        out_specs=(
            P(("groups", "seq"), "head", "rep", None, None),
            P(None, ("groups", "head"), ("seq", "rep")),
            P(None, ("groups", "seq"), "head"),
        ),
        check_vma=False,
    )
```

```python
import functools

import jax
import jax.numpy as jnp
from jax import lax
from jax.experimental import pallas as pl
from jax.experimental.pallas import tpu as pltpu
from jax.sharding import PartitionSpec as P

BLOCK = 128
PIECES = 4
NEG = -1e30
BF = jnp.bfloat16
F32 = jnp.float32
VM = pl.BlockSpec(memory_space=pltpu.VMEM)
HB = pl.BlockSpec(memory_space=pltpu.HBM)
DMA = pltpu.SemaphoreType.DMA


def shift(x, axis, c):
    size = lax.axis_size(axis)
    return lax.ppermute(x, axis, [(i, i ^ c) for i in range(size)])


def call(body, out_shape, in_specs, out_specs, scratch=(), us=1.0):
    return pl.pallas_call(
        body,
        out_shape=out_shape,
        in_specs=in_specs,
        out_specs=out_specs,
        scratch_shapes=list(scratch),
        cost_estimate=pl.CostEstimate(
            flops=0, bytes_accessed=int(us * 3.6e4), transcendentals=0
        ),
        compiler_params=pltpu.CompilerParams(vmem_limit_bytes=32 * 1024 * 1024),
    )


def in_hbm(x):
    return pltpu.with_memory_space_constraint(x, pltpu.HBM)


def after(arrays, *earlier):
    return lax.optimization_barrier((*arrays, *earlier))[: len(arrays)]


def run_all(copies):
    for copy in copies:
        copy.start()
    for copy in copies:
        copy.wait()


def copier(sems):
    position = iter(range(sems.shape[0]))
    return lambda src, dst: pltpu.make_async_copy(src, dst, sems.at[next(position)])


def state_rows(part):
    return 16 * pl.cdiv(part, 256)


def pack_state(piece, out_ref, first):
    ns, part = piece.shape
    for i in range(pl.cdiv(part, 256)):
        cut = piece[:, i * 256 : (i + 1) * 256]
        if cut.shape[1] < 256:
            cut = jnp.concatenate([cut, jnp.zeros((ns, 256 - cut.shape[1]), F32)], axis=1)
        out_ref[first + i * 16 : first + (i + 1) * 16, :] = cut.astype(BF)


def own_state(state_ref, c, split, part):
    me, rep = lax.axis_index("seq"), lax.axis_index("rep")
    if split:
        return state_ref.at[me ^ c, :, pl.ds(pl.multiple_of(rep * part, 128), part)]
    return state_ref.at[me ^ c]


def stage_blocks(count, kv_ref, *rest):
    outs, sems = rest[:-1], rest[-1]
    me = lax.axis_index("seq")
    copy = copier(sems)
    run_all(
        [
            copy(kv_ref.at[me ^ c, j], outs[c - 1].at[pl.ds(j * BLOCK, BLOCK)])
            for c in range(count - 1, 0, -1)
            for j in range(kv_ref.shape[1])
        ]
    )


def stage_rest(count, split, kv_ref, q_ref, new_ref, state_ref, blocks_ref, counts_ref, *rest):
    own_out, q_out, new_out, bias_out, pick_out = rest[:5]
    states = rest[5 : 5 + count]
    loaded, blocks, counts, sems, early = rest[5 + count :]
    me, rep = lax.axis_index("seq"), lax.axis_index("rep")
    heads = kv_ref.shape[1]
    copy = copier(sems)
    moves = [copy(kv_ref.at[me, j], own_out.at[pl.ds(j * BLOCK, BLOCK)]) for j in range(heads)]
    moves += [copy(q_ref, q_out), copy(new_ref, new_out)]
    copy = copier(early)
    first = [copy(blocks_ref, blocks), copy(counts_ref, counts)]
    part = loaded.shape[2]
    for c in range(count):
        if split:
            src = state_ref.at[me ^ c, :, pl.ds(pl.multiple_of(rep * part, 128), part)]
        else:
            src = state_ref.at[me ^ c]
        first.append(copy(src, loaded.at[c]))
    for move in first + moves:
        move.start()
    for move in first:
        move.wait()
    for c in range(count):
        pack_state(loaded[c], states[c], states[c].shape[0] - state_rows(part))
    head_first = lax.axis_index("head") * new_ref.shape[2] + rep * heads
    rows = bias_out.shape[0] // heads
    keep_rep = pick_out.shape[2]
    for j in range(heads):
        live_count = counts[me, head_first + j]
        for c in range(count):
            live = jnp.int32(0)
            for side in range(2):
                for k in range(keep_rep):
                    slot = (rep if side == 0 else 1 - rep) * keep_rep + k
                    hit = (blocks[me, slot, head_first + j] == (me ^ c)) & (slot < live_count)
                    one = jnp.where(hit, 1.0, 0.0).astype(F32)
                    pick_out[side, j, k, c] = jnp.full(pick_out.shape[4:], one, F32).astype(BF)
                    live = live | hit.astype(jnp.int32)
            dead = jnp.where(live > 0, 0.0, NEG).astype(F32)
            bias_out[j * rows : (j + 1) * rows, c * BLOCK : (c + 1) * BLOCK] = jnp.full(
                (rows, BLOCK), dead, F32
            )
    for move in moves:
        move.wait()


def dot_f32(a, b, contract):
    return lax.dot_general(a, b, (contract, ((), ())), preferred_element_type=F32)


def query_rows(q_ref, heads):
    rep = lax.axis_index("rep")
    steps, _, q_heads, _ = q_ref.shape
    own_q = q_heads // 2
    group = own_q // heads
    q_all = [q_ref[step, 0].astype(F32) for step in range(steps)]
    q_all = [jnp.where(rep == 0, q[:own_q], q[own_q:]) for q in q_all]
    return [
        jnp.concatenate([x[j * group : (j + 1) * group] for x in q_all], axis=0)
        for j in range(heads)
    ]


def block_scores(q, piece_ref, j):
    hd = piece_ref.shape[1] // 2
    keys = piece_ref[j * BLOCK : (j + 1) * BLOCK, :hd]
    return dot_f32(q.astype(BF), keys, ((1,), (1,))) * hd ** (-0.5)


def block_sums(weights, piece_ref, j):
    values = piece_ref[j * BLOCK : (j + 1) * BLOCK, piece_ref.shape[1] // 2 :]
    return dot_f32(weights, values, ((1,), (0,)))


def attend(count, heads, q_ref, new_ref, bias_ref, *rest):
    pieces, states = rest[:count], rest[count : 2 * count - 2]
    outs = rest[2 * count - 2 :]
    rep = lax.axis_index("rep")
    queries = query_rows(q_ref, heads)
    rows, hd = queries[0].shape
    steps = q_ref.shape[0]
    group = rows // steps
    all_rows = heads * rows
    scale = hd ** (-0.5)
    scores = [
        jnp.concatenate([block_scores(q, piece, j) for piece in pieces], axis=1)
        for j, q in enumerate(queries)
    ]
    scores = jnp.concatenate(scores, axis=0)
    alive = bias_ref[...] == 0.0
    scores = jnp.where(alive, scores, NEG)
    row_step = (lax.broadcasted_iota(jnp.int32, (all_rows, 1), 0) // group) % steps
    wide_q = jnp.concatenate(queries, axis=0)
    dots, fresh_values = [], []
    top = jnp.max(scores, axis=1, keepdims=True)
    for step in range(steps):
        both = new_ref[step, 0].astype(F32)
        fresh = jnp.where(rep == 0, both[:heads], both[heads:])
        wide = jnp.concatenate(
            [jnp.broadcast_to(fresh[j : j + 1], (rows, 2 * hd)) for j in range(heads)], axis=0
        )
        dot = jnp.sum(wide_q * wide[:, :hd], axis=1, keepdims=True) * scale
        dots.append(jnp.where(row_step >= step, dot, NEG))
        fresh_values.append(wide[:, hd:])
        top = jnp.maximum(top, dots[-1])
    weights = jnp.where(alive, jnp.exp(scores - top), 0.0)
    total = jnp.sum(weights, axis=1, keepdims=True)
    weights = weights.astype(BF)
    summed = []
    for j in range(heads):
        parts = [
            block_sums(weights[j * rows : (j + 1) * rows, c * BLOCK : (c + 1) * BLOCK], piece, j)
            for c, piece in enumerate(pieces)
        ]
        summed.append(functools.reduce(jnp.add, parts))
    summed = jnp.concatenate(summed, axis=0)
    for step in range(steps):
        weight = jnp.where(row_step >= step, jnp.exp(dots[step] - top), 0.0)
        total = total + weight
        summed = summed + weight.astype(BF).astype(F32) * fresh_values[step]
    result = (summed / total).astype(BF)
    for c in range(count):
        for j in range(2):
            half = result[j * rows : (j + 1) * rows] if j < heads else jnp.zeros((rows, hd), BF)
            outs[c][:rows, j * hd : (j + 1) * hd] = half
        if c > 1:
            outs[c][rows:, :] = states[c - 2][...]


def select(count, heads, pick_ref, *rest):
    pieces, (kept_ref, sent_ref) = rest[:count], rest[count:]
    width = pieces[0].shape[1]
    tile = pick_ref.shape[4]
    for side, ref in ((1, sent_ref), (0, kept_ref)):
        for j in range(heads):
            for k in range(ref.shape[1]):
                total = None
                for c in range(count):
                    piece = pieces[c][j * BLOCK : (j + 1) * BLOCK, :].reshape(-1, tile, width)
                    term = piece * pick_ref[side, j, k, c][None]
                    total = term if total is None else total + term
                ref[j, k] = total.reshape(BLOCK, width)


def collect(count, heads, steps, group, slope_ref, base_ref, home_ref, beside_ref, *rest):
    parts = [rest[0], rest[count - 1], *rest[1 : count - 1]]
    states = [home_ref, beside_ref, *parts[2:]]
    out_ref, mamba_ref, scratch = rest[count:]
    me = lax.axis_index("seq")
    ns, part = slope_ref.shape[2:]
    for c in range(count):
        first = states[c].shape[0] - state_rows(part)
        rows = [
            states[c][first + 16 * i : first + 16 * (i + 1), :].astype(F32)
            for i in range(pl.cdiv(part, 256))
        ]
        state = jnp.concatenate(rows, axis=1)[:, :part]
        for step in range(steps):
            mamba_ref[step, me ^ c] = base_ref[c, step] + jnp.sum(
                slope_ref[c, step] * state, axis=0, keepdims=True
            )
    for c in range(count):
        rows = parts[c][: steps * group, :].astype(F32)
        for j in range(heads):
            for step in range(steps):
                at = pl.multiple_of((step * count + (me ^ c)) * group, group)
                cut = rows[step * group : (step + 1) * group, j * 128 : (j + 1) * 128]
                scratch[j, pl.ds(at, group), :] = cut
    for j in range(heads):
        for g in range(group):
            at = (j * group + g) * 128
            tile = scratch[j, pl.ds(g, steps * count, stride=group), :]
            out_ref[:, at : at + 128] = tile.astype(BF)


def weight_half(weight_ref, out_ref, which, copy):
    half = out_ref.shape[0]
    rows = half // PIECES
    cuts = [(pl.ds(which * half + i * rows, rows), pl.ds(i * rows, rows)) for i in range(PIECES)]
    return [copy(weight_ref.at[src], out_ref.at[dst]) for src, dst in cuts]


def project_own(attn_ref, weight_ref, out_ref):
    out_ref[...] = dot_f32(attn_ref[...], weight_ref[...], ((1,), (0,)))


def pick(options, index):
    chosen = options[0]
    for i in range(1, len(options)):
        chosen = jnp.where(index == i, options[i], chosen)
    return chosen


def project_other(heads_count, count, acc_ref, attn_ref, weight_ref, *outs):
    total = acc_ref[...] + dot_f32(attn_ref[...], weight_ref[...], ((1,), (0,)))
    head = lax.axis_index("head")
    steps = total.shape[0] // count
    share = count // heads_count
    for step in range(steps):
        slices = [
            total[step * count + x * share : step * count + (x + 1) * share]
            for x in range(heads_count)
        ]
        for c in range(heads_count):
            outs[c][step] = pick(slices, head ^ c)


def add_up(*refs):
    total = refs[0][...]
    for ref in refs[1:-1]:
        total = total + ref[...]
    refs[-1][...] = total.astype(BF)


def prepare(count, split, weight_hbm, dt_hbm, x_hbm, bc_hbm, gain_hbm, log_hbm, own_ref, other_ref,
            slope_ref, base_ref, dt_ref, x_ref, bc_ref, gain_ref, log_ref, sems, weight_sems):
    copy = copier(sems)
    first = [
        copy(dt_hbm, dt_ref),
        copy(x_hbm, x_ref),
        copy(bc_hbm, bc_ref),
        copy(gain_hbm, gain_ref),
        copy(log_hbm, log_ref),
    ]
    copy, which = copier(weight_sems), lax.axis_index("rep")
    weights = weight_half(weight_hbm, own_ref, which, copy)
    weights += weight_half(weight_hbm, other_ref, 1 - which, copy)
    for move in first + weights:
        move.start()
    for move in first:
        move.wait()
    me, rep = lax.axis_index("seq"), lax.axis_index("rep")
    _, steps, ns, part = slope_ref.shape
    block = part * 2 if split else part
    diagonal = lax.broadcasted_iota(jnp.int32, (ns, ns), 0) == lax.broadcasted_iota(
        jnp.int32, (ns, ns), 1
    )

    def column(row):
        return jnp.sum(jnp.where(diagonal, row, 0.0), axis=1, keepdims=True)

    drive = [column(bc_ref[step, 0, 0:1, :]) for step in range(steps)]
    read = [column(bc_ref[step, 0, 1:2, :]) for step in range(steps)]
    for c in range(count):
        first = (me ^ c) * block + (rep * part if split else 0)
        lanes = pl.ds(pl.multiple_of(first, 128), part)
        rate = -jnp.exp(log_ref[:, lanes])
        gain = gain_ref[:, lanes]
        kept = jnp.ones((ns, part), F32)
        added = jnp.zeros((ns, part), F32)
        for step in range(steps):
            dt = dt_ref[step, :, lanes]
            inputs = x_ref[step : step + 1, lanes].astype(F32)
            decay = jnp.exp(dt * rate)
            kept = kept * decay
            added = added * decay + drive[step] * (dt * inputs)
            slope_ref[c, step] = read[step] * kept
            base_ref[c, step] = (
                jnp.sum(read[step] * added, axis=0, keepdims=True) + gain * inputs
            )
    for move in weights:
        move.wait()


def assemble(split, kept_ref, got_ref, mamba_ref, *rest):
    rep = lax.axis_index("rep")
    if split:
        other_ref, handoff_ref, out_ref, sems = rest
    else:
        handoff_ref, out_ref, sems = rest
    heads = kept_ref.shape[0]
    copy = copier(sems)
    moves = [
        copy(kept_ref, handoff_ref.at[0, pl.ds(rep * heads, heads)]),
        copy(got_ref, handoff_ref.at[0, pl.ds((1 - rep) * heads, heads)]),
    ]
    steps, count, _, part = mamba_ref.shape
    for step in range(steps):
        for b in range(count):
            if split:
                for ref, side in ((mamba_ref, rep), (other_ref, 1 - rep)):
                    lanes = pl.ds(pl.multiple_of((2 * b + side) * part, 128), part)
                    moves.append(copy(ref.at[step, b], out_ref.at[step, :, lanes]))
            else:
                moves.append(copy(mamba_ref.at[step, b], out_ref.at[step, :, pl.ds(b * part, part)]))
    run_all(moves)


def per_device(
    prefill_kv,
    kept_blocks,
    kept_counts,
    queries,
    new_kv,
    out_weight,
    prefill_state,
    a_log,
    step_input,
    step_dt,
    step_bc,
    skip_gain,
):
    count = lax.axis_size("seq")
    reps = lax.axis_size("rep")
    heads_count = lax.axis_size("head")
    requests, heads, tokens, width = prefill_kv.shape
    assert requests == count and tokens == BLOCK and reps == 2 and width == 256
    assert count & (count - 1) == 0 and heads_count & (heads_count - 1) == 0
    keep = kept_blocks.shape[2]
    keep_rep = keep // reps
    steps, _, q_heads, hd = queries.shape
    dec_heads = new_kv.shape[2]
    group = q_heads // dec_heads
    _, ns, block = prefill_state.shape
    split = block % (reps * 128) == 0
    part = block // reps if split else block
    all_rows = heads * steps * group
    assert all_rows <= 128
    channels = count * block
    shape = jax.ShapeDtypeStruct
    smem = pltpu.SMEM
    blocks = jnp.swapaxes(kept_blocks, 1, 2)

    prefill_kv, prefill_state, queries, new_kv = map(in_hbm, (prefill_kv, prefill_state, queries, new_kv))
    step_dt, step_bc, a_log, out_weight = map(in_hbm, (step_dt, step_bc, a_log, out_weight))
    step_input = in_hbm(step_input.reshape(steps, channels))
    skip_gain = in_hbm(skip_gain.reshape(1, -1))
    blocks, kept_counts = in_hbm(blocks), in_hbm(kept_counts)

    columns = out_weight.shape[1]
    half = heads * group * hd
    half_weight = pltpu.VMEM((half, columns), BF)
    block_shape = shape((heads * BLOCK, width), BF)
    pieces = call(
        functools.partial(stage_blocks, count),
        [block_shape] * (count - 1),
        [HB],
        [VM] * (count - 1),
        [DMA(((count - 1) * heads,))],
    )(prefill_kv)
    moved = [shift(pieces[c - 1], "seq", c) for c in range(count - 1, 0, -1)][::-1]
    own_piece, q_near, new_near, bias, picks, *states = call(
        functools.partial(stage_rest, count, split),
        [
            block_shape,
            shape(queries.shape, BF),
            shape(new_kv.shape, BF),
            shape((all_rows, count * BLOCK), F32),
            shape((reps, heads, keep_rep, count, 16, width), BF),
        ]
        + [shape((state_rows(part) + (32 if c == 1 else 0), width), BF) for c in range(count)],
        [HB] * 6,
        [VM] * (5 + count),
        [
            pltpu.VMEM((count, ns, part), F32),
            smem(blocks.shape, jnp.int32),
            smem(kept_counts.shape, jnp.int32),
            DMA((heads + 2,)),
            DMA((count + 2,)),
        ],
    )(*after([prefill_kv], pieces[0]), queries, new_kv, prefill_state, blocks, kept_counts)
    own_weight, other_weight, slope, base = call(
        functools.partial(prepare, count, split),
        [
            half_weight,
            half_weight,
            shape((count, steps, ns, part), F32),
            shape((count, steps, 1, part), F32),
        ],
        [HB] * 6,
        [VM] * 4,
        [
            pltpu.VMEM((steps, 1, channels), F32),
            pltpu.VMEM((steps, channels), BF),
            pltpu.VMEM(step_bc.shape, F32),
            pltpu.VMEM((1, channels), F32),
            pltpu.VMEM(a_log.shape, F32),
            DMA((5,)),
            DMA((2 * PIECES,)),
        ],
    )(*after([out_weight], pieces[0]), step_dt, step_input, step_bc, skip_gain, a_log)

    beside = shift(after(states[1:2], own_weight)[0], "seq", 1)
    *moved, own_weight = after([*moved[::-1], own_weight])
    kv = [own_piece, *moved[::-1]]
    half_shape = (heads, keep_rep, BLOCK, width)
    rows = steps * group
    sends = call(
        functools.partial(attend, count, heads),
        [shape((rows, width), BF)] * 2
        + [shape((rows + state_rows(part), width), BF)] * (count - 2),
        [VM] * (1 + 2 * count),
        [VM] * count,
    )(q_near, new_near, bias, *kv, *states[2:])
    kept, sent = call(
        functools.partial(select, count, heads),
        [shape(half_shape, BF)] * 2,
        [VM] * (1 + count),
        [VM] * 2,
    )(*after([picks], sends[0]), *kv)
    order = [*range(2, count), 1]
    gathered = [shift(sends[c], "seq", c) for c in order]
    attn, mamba = call(
        functools.partial(collect, count, heads, steps, group),
        [shape((steps * count, half), BF), shape((steps, count, 1, part), F32)],
        [VM] * (4 + count),
        [VM] * 2,
        [pltpu.VMEM((heads, steps * count * group, hd), F32)],
    )(slope, base, states[0], beside, sends[0], *gathered)
    attn_other = shift(attn, "rep", 1)
    own_sum = call(
        project_own, shape((steps * count, columns), F32), [VM, VM], VM, us=0.7
    )(attn, own_weight)
    share = count // heads_count
    sums = call(
        functools.partial(project_other, heads_count, count),
        [shape((steps, share, columns), F32)] * heads_count,
        [VM, VM, VM],
        [VM] * heads_count,
        us=0.7,
    )(own_sum, attn_other, other_weight)
    sums = [sums[0]] + [shift(sums[c], "head", c) for c in range(1, heads_count)]
    got = shift(after([sent], mamba)[0], "rep", 1)
    kept = after([kept], sums[0])[0]
    operands = [kept, got, mamba] + ([shift(mamba, "rep", 1)] if split else [])
    handoff, mamba_out = call(
        functools.partial(assemble, split),
        [
            shape((1, dec_heads, keep_rep, BLOCK, width), BF),
            shape((steps, 1, channels), F32),
        ],
        [VM] * len(operands),
        [HB] * 2,
        [DMA((2 + steps * count * (2 if split else 1),))],
    )(*operands)
    sums[1:] = after(sums[1:], handoff)
    proj_out = call(
        add_up, shape((steps, share, columns), BF), [VM] * heads_count, VM, us=0.6
    )(*sums)
    return handoff, proj_out, mamba_out


def solution(mesh):
    return jax.shard_map(
        per_device,
        mesh=mesh,
        in_specs=(
            P("groups", ("head", "rep"), "seq", None),
            P("groups", None, None),
            P("groups", None),
            P(None, ("groups", "seq"), "head", None),
            P(None, ("groups", "seq"), "head", None),
            P("head", ("seq", "rep")),
            P("groups", None, ("head", "seq")),
            P(None, "head"),
            P(None, ("groups", "seq"), "head"),
            P(None, ("groups", "seq"), "head"),
            P(None, ("groups", "seq"), None, None),
            P("head"),
        ),
        out_specs=(
            P(("groups", "seq"), "head", "rep", None, None),
            P(None, ("groups", "head"), ("seq", "rep")),
            P(None, ("groups", "seq"), "head"),
        ),
        check_vma=False,
    )
```

```python
import functools

import jax
import jax.numpy as jnp
from jax import lax
from jax.experimental import pallas as pl
from jax.experimental.pallas import tpu as pltpu
from jax.sharding import PartitionSpec as P

BLOCK = 128
PIECES = 4
NEG = -1e30
BF = jnp.bfloat16
F32 = jnp.float32
VM = pl.BlockSpec(memory_space=pltpu.VMEM)
HB = pl.BlockSpec(memory_space=pltpu.HBM)
DMA = pltpu.SemaphoreType.DMA


def shift(x, axis, c):
    size = lax.axis_size(axis)
    return lax.ppermute(x, axis, [(i, i ^ c) for i in range(size)])


def call(body, out_shape, in_specs, out_specs, scratch=(), us=1.0):
    return pl.pallas_call(
        body,
        out_shape=out_shape,
        in_specs=in_specs,
        out_specs=out_specs,
        scratch_shapes=list(scratch),
        cost_estimate=pl.CostEstimate(
            flops=0, bytes_accessed=int(us * 3.6e4), transcendentals=0
        ),
        compiler_params=pltpu.CompilerParams(vmem_limit_bytes=32 * 1024 * 1024),
    )


def in_hbm(x):
    return pltpu.with_memory_space_constraint(x, pltpu.HBM)


def after(arrays, *earlier):
    return lax.optimization_barrier((*arrays, *earlier))[: len(arrays)]


def run_all(copies):
    for copy in copies:
        copy.start()
    for copy in copies:
        copy.wait()


def copier(sems):
    position = iter(range(sems.shape[0]))
    return lambda src, dst: pltpu.make_async_copy(src, dst, sems.at[next(position)])


def state_rows(part):
    return 16 * pl.cdiv(part, 256)


def pack_state(piece, out_ref, first):
    ns, part = piece.shape
    for i in range(pl.cdiv(part, 256)):
        cut = piece[:, i * 256 : (i + 1) * 256]
        if cut.shape[1] < 256:
            cut = jnp.concatenate([cut, jnp.zeros((ns, 256 - cut.shape[1]), F32)], axis=1)
        out_ref[first + i * 16 : first + (i + 1) * 16, :] = cut.astype(BF)


def own_state(state_ref, c, split, part):
    me, rep = lax.axis_index("seq"), lax.axis_index("rep")
    if split:
        return state_ref.at[me ^ c, :, pl.ds(pl.multiple_of(rep * part, 128), part)]
    return state_ref.at[me ^ c]


def stage_blocks(count, kv_ref, *rest):
    outs, sems = rest[:-1], rest[-1]
    me = lax.axis_index("seq")
    copy = copier(sems)
    run_all(
        [
            copy(kv_ref.at[me ^ c, j], outs[c - 1].at[pl.ds(j * BLOCK, BLOCK)])
            for c in range(count - 1, 0, -1)
            for j in range(kv_ref.shape[1])
        ]
    )


def stage_rest(count, split, kv_ref, q_ref, new_ref, state_ref, blocks_ref, counts_ref, *rest):
    own_out, q_out, new_out, bias_out, pick_out = rest[:5]
    states = rest[5 : 5 + count]
    loaded, blocks, counts, sems, early = rest[5 + count :]
    me, rep = lax.axis_index("seq"), lax.axis_index("rep")
    heads = kv_ref.shape[1]
    copy = copier(sems)
    moves = [copy(kv_ref.at[me, j], own_out.at[pl.ds(j * BLOCK, BLOCK)]) for j in range(heads)]
    moves += [copy(q_ref, q_out), copy(new_ref, new_out)]
    copy = copier(early)
    first = [copy(blocks_ref, blocks), copy(counts_ref, counts)]
    part = loaded.shape[2]
    for c in range(count):
        if split:
            src = state_ref.at[me ^ c, :, pl.ds(pl.multiple_of(rep * part, 128), part)]
        else:
            src = state_ref.at[me ^ c]
        first.append(copy(src, loaded.at[c]))
    for move in first + moves:
        move.start()
    for move in first:
        move.wait()
    for c in range(count):
        pack_state(loaded[c], states[c], states[c].shape[0] - state_rows(part))
    head_first = lax.axis_index("head") * new_ref.shape[2] + rep * heads
    rows = bias_out.shape[0] // heads
    keep_rep = pick_out.shape[2]
    for j in range(heads):
        live_count = counts[me, head_first + j]
        for c in range(count):
            live = jnp.int32(0)
            for side in range(2):
                for k in range(keep_rep):
                    slot = (rep if side == 0 else 1 - rep) * keep_rep + k
                    hit = (blocks[me, slot, head_first + j] == (me ^ c)) & (slot < live_count)
                    one = jnp.where(hit, 1.0, 0.0).astype(F32)
                    pick_out[side, j, k, c] = jnp.full(pick_out.shape[4:], one, F32).astype(BF)
                    live = live | hit.astype(jnp.int32)
            dead = jnp.where(live > 0, 0.0, NEG).astype(F32)
            bias_out[j * rows : (j + 1) * rows, c * BLOCK : (c + 1) * BLOCK] = jnp.full(
                (rows, BLOCK), dead, F32
            )
    for move in moves:
        move.wait()


def dot_f32(a, b, contract):
    return lax.dot_general(a, b, (contract, ((), ())), preferred_element_type=F32)


def query_rows(q_ref, heads):
    rep = lax.axis_index("rep")
    steps, _, q_heads, _ = q_ref.shape
    own_q = q_heads // 2
    group = own_q // heads
    q_all = [q_ref[step, 0].astype(F32) for step in range(steps)]
    q_all = [jnp.where(rep == 0, q[:own_q], q[own_q:]) for q in q_all]
    return [
        jnp.concatenate([x[j * group : (j + 1) * group] for x in q_all], axis=0)
        for j in range(heads)
    ]


def block_scores(q, piece_ref, j):
    hd = piece_ref.shape[1] // 2
    keys = piece_ref[j * BLOCK : (j + 1) * BLOCK, :hd]
    return dot_f32(q.astype(BF), keys, ((1,), (1,))) * hd ** (-0.5)


def block_sums(weights, piece_ref, j):
    values = piece_ref[j * BLOCK : (j + 1) * BLOCK, piece_ref.shape[1] // 2 :]
    return dot_f32(weights, values, ((1,), (0,)))


def attend(count, heads, q_ref, new_ref, bias_ref, pick_ref, *rest):
    pieces = [*rest[:2], *rest[2:count][::-1]]
    states = rest[count : 2 * count - 2]
    outs, (kept_ref, sent_ref) = rest[2 * count - 2 : 3 * count - 2], rest[3 * count - 2 :]
    rep = lax.axis_index("rep")
    queries = query_rows(q_ref, heads)
    rows, hd = queries[0].shape
    steps = q_ref.shape[0]
    group = rows // steps
    all_rows = heads * rows
    scale = hd ** (-0.5)
    scores = [
        jnp.concatenate([block_scores(q, piece, j) for piece in pieces], axis=1)
        for j, q in enumerate(queries)
    ]
    scores = jnp.concatenate(scores, axis=0)
    alive = bias_ref[...] == 0.0
    scores = jnp.where(alive, scores, NEG)
    row_step = (lax.broadcasted_iota(jnp.int32, (all_rows, 1), 0) // group) % steps
    wide_q = jnp.concatenate(queries, axis=0)
    dots, fresh_values = [], []
    top = jnp.max(scores, axis=1, keepdims=True)
    for step in range(steps):
        both = new_ref[step, 0].astype(F32)
        fresh = jnp.where(rep == 0, both[:heads], both[heads:])
        wide = jnp.concatenate(
            [jnp.broadcast_to(fresh[j : j + 1], (rows, 2 * hd)) for j in range(heads)], axis=0
        )
        dot = jnp.sum(wide_q * wide[:, :hd], axis=1, keepdims=True) * scale
        dots.append(jnp.where(row_step >= step, dot, NEG))
        fresh_values.append(wide[:, hd:])
        top = jnp.maximum(top, dots[-1])
    weights = jnp.where(alive, jnp.exp(scores - top), 0.0)
    total = jnp.sum(weights, axis=1, keepdims=True)
    weights = weights.astype(BF)
    summed = []
    for j in range(heads):
        parts = [
            block_sums(weights[j * rows : (j + 1) * rows, c * BLOCK : (c + 1) * BLOCK], piece, j)
            for c, piece in enumerate(pieces)
        ]
        summed.append(functools.reduce(jnp.add, parts))
    summed = jnp.concatenate(summed, axis=0)
    for step in range(steps):
        weight = jnp.where(row_step >= step, jnp.exp(dots[step] - top), 0.0)
        total = total + weight
        summed = summed + weight.astype(BF).astype(F32) * fresh_values[step]
    result = (summed / total).astype(BF)
    for c in range(count):
        for j in range(2):
            half = result[j * rows : (j + 1) * rows] if j < heads else jnp.zeros((rows, hd), BF)
            outs[c][:rows, j * hd : (j + 1) * hd] = half
        if c > 1:
            outs[c][rows:, :] = states[c - 2][...]
    tile = pick_ref.shape[4]
    for side, ref in ((1, sent_ref), (0, kept_ref)):
        for j in range(heads):
            for k in range(ref.shape[1]):
                total = None
                for c in range(count):
                    piece = pieces[c][j * BLOCK : (j + 1) * BLOCK, :].reshape(-1, tile, 2 * hd)
                    term = piece * pick_ref[side, j, k, c][None]
                    total = term if total is None else total + term
                ref[j, k] = total.reshape(BLOCK, 2 * hd)


def collect(count, heads, steps, group, slope_ref, base_ref, home_ref, beside_ref, *rest):
    parts = [rest[0], rest[count - 1], *rest[1 : count - 1]]
    states = [home_ref, beside_ref, *parts[2:]]
    out_ref, mamba_ref, scratch = rest[count:]
    me = lax.axis_index("seq")
    ns, part = slope_ref.shape[2:]
    for c in range(count):
        first = states[c].shape[0] - state_rows(part)
        rows = [
            states[c][first + 16 * i : first + 16 * (i + 1), :].astype(F32)
            for i in range(pl.cdiv(part, 256))
        ]
        state = jnp.concatenate(rows, axis=1)[:, :part]
        for step in range(steps):
            mamba_ref[step, me ^ c] = base_ref[c, step] + jnp.sum(
                slope_ref[c, step] * state, axis=0, keepdims=True
            )
    for c in range(count):
        rows = parts[c][: steps * group, :].astype(F32)
        for j in range(heads):
            for step in range(steps):
                at = pl.multiple_of((step * count + (me ^ c)) * group, group)
                cut = rows[step * group : (step + 1) * group, j * 128 : (j + 1) * 128]
                scratch[j, pl.ds(at, group), :] = cut
    for j in range(heads):
        for g in range(group):
            at = (j * group + g) * 128
            tile = scratch[j, pl.ds(g, steps * count, stride=group), :]
            out_ref[:, at : at + 128] = tile.astype(BF)


def weight_half(weight_ref, out_ref, which, copy):
    half = out_ref.shape[0]
    rows = half // PIECES
    cuts = [(pl.ds(which * half + i * rows, rows), pl.ds(i * rows, rows)) for i in range(PIECES)]
    return [copy(weight_ref.at[src], out_ref.at[dst]) for src, dst in cuts]


def project_own(attn_ref, weight_ref, out_ref):
    out_ref[...] = dot_f32(attn_ref[...], weight_ref[...], ((1,), (0,)))


def pick(options, index):
    chosen = options[0]
    for i in range(1, len(options)):
        chosen = jnp.where(index == i, options[i], chosen)
    return chosen


def project_other(heads_count, count, acc_ref, attn_ref, weight_ref, *outs):
    total = acc_ref[...] + dot_f32(attn_ref[...], weight_ref[...], ((1,), (0,)))
    head = lax.axis_index("head")
    steps = total.shape[0] // count
    share = count // heads_count
    for step in range(steps):
        slices = [
            total[step * count + x * share : step * count + (x + 1) * share]
            for x in range(heads_count)
        ]
        for c in range(heads_count):
            outs[c][step] = pick(slices, head ^ c)


def add_up(*refs):
    total = refs[0][...]
    for ref in refs[1:-1]:
        total = total + ref[...]
    refs[-1][...] = total.astype(BF)


def prepare(count, split, weight_hbm, dt_hbm, x_hbm, bc_hbm, gain_hbm, log_hbm, own_ref, other_ref,
            slope_ref, base_ref, dt_ref, x_ref, bc_ref, gain_ref, log_ref, sems, weight_sems):
    copy = copier(sems)
    first = [
        copy(dt_hbm, dt_ref),
        copy(x_hbm, x_ref),
        copy(bc_hbm, bc_ref),
        copy(gain_hbm, gain_ref),
        copy(log_hbm, log_ref),
    ]
    copy, which = copier(weight_sems), lax.axis_index("rep")
    weights = weight_half(weight_hbm, own_ref, which, copy)
    weights += weight_half(weight_hbm, other_ref, 1 - which, copy)
    for move in first + weights:
        move.start()
    for move in first:
        move.wait()
    me, rep = lax.axis_index("seq"), lax.axis_index("rep")
    _, steps, ns, part = slope_ref.shape
    block = part * 2 if split else part
    diagonal = lax.broadcasted_iota(jnp.int32, (ns, ns), 0) == lax.broadcasted_iota(
        jnp.int32, (ns, ns), 1
    )

    def column(row):
        return jnp.sum(jnp.where(diagonal, row, 0.0), axis=1, keepdims=True)

    drive = [column(bc_ref[step, 0, 0:1, :]) for step in range(steps)]
    read = [column(bc_ref[step, 0, 1:2, :]) for step in range(steps)]
    for c in range(count):
        first = (me ^ c) * block + (rep * part if split else 0)
        lanes = pl.ds(pl.multiple_of(first, 128), part)
        rate = -jnp.exp(log_ref[:, lanes])
        gain = gain_ref[:, lanes]
        kept = jnp.ones((ns, part), F32)
        added = jnp.zeros((ns, part), F32)
        for step in range(steps):
            dt = dt_ref[step, :, lanes]
            inputs = x_ref[step : step + 1, lanes].astype(F32)
            decay = jnp.exp(dt * rate)
            kept = kept * decay
            added = added * decay + drive[step] * (dt * inputs)
            slope_ref[c, step] = read[step] * kept
            base_ref[c, step] = (
                jnp.sum(read[step] * added, axis=0, keepdims=True) + gain * inputs
            )
    for move in weights:
        move.wait()


def assemble(split, kept_ref, got_ref, mamba_ref, *rest):
    rep = lax.axis_index("rep")
    if split:
        other_ref, handoff_ref, out_ref, sems = rest
    else:
        handoff_ref, out_ref, sems = rest
    heads = kept_ref.shape[0]
    copy = copier(sems)
    moves = [
        copy(kept_ref, handoff_ref.at[0, pl.ds(rep * heads, heads)]),
        copy(got_ref, handoff_ref.at[0, pl.ds((1 - rep) * heads, heads)]),
    ]
    steps, count, _, part = mamba_ref.shape
    for step in range(steps):
        for b in range(count):
            if split:
                for ref, side in ((mamba_ref, rep), (other_ref, 1 - rep)):
                    lanes = pl.ds(pl.multiple_of((2 * b + side) * part, 128), part)
                    moves.append(copy(ref.at[step, b], out_ref.at[step, :, lanes]))
            else:
                moves.append(copy(mamba_ref.at[step, b], out_ref.at[step, :, pl.ds(b * part, part)]))
    run_all(moves)


def per_device(
    prefill_kv,
    kept_blocks,
    kept_counts,
    queries,
    new_kv,
    out_weight,
    prefill_state,
    a_log,
    step_input,
    step_dt,
    step_bc,
    skip_gain,
):
    count = lax.axis_size("seq")
    reps = lax.axis_size("rep")
    heads_count = lax.axis_size("head")
    requests, heads, tokens, width = prefill_kv.shape
    assert requests == count and tokens == BLOCK and reps == 2 and width == 256
    assert count & (count - 1) == 0 and heads_count & (heads_count - 1) == 0
    keep = kept_blocks.shape[2]
    keep_rep = keep // reps
    steps, _, q_heads, hd = queries.shape
    dec_heads = new_kv.shape[2]
    group = q_heads // dec_heads
    _, ns, block = prefill_state.shape
    split = block % (reps * 128) == 0
    part = block // reps if split else block
    all_rows = heads * steps * group
    assert all_rows <= 128
    channels = count * block
    shape = jax.ShapeDtypeStruct
    smem = pltpu.SMEM
    blocks = jnp.swapaxes(kept_blocks, 1, 2)

    prefill_kv, prefill_state, queries, new_kv = map(in_hbm, (prefill_kv, prefill_state, queries, new_kv))
    step_dt, step_bc, a_log, out_weight = map(in_hbm, (step_dt, step_bc, a_log, out_weight))
    step_input = in_hbm(step_input.reshape(steps, channels))
    skip_gain = in_hbm(skip_gain.reshape(1, -1))
    blocks, kept_counts = in_hbm(blocks), in_hbm(kept_counts)

    columns = out_weight.shape[1]
    half = heads * group * hd
    half_weight = pltpu.VMEM((half, columns), BF)
    block_shape = shape((heads * BLOCK, width), BF)
    pieces = call(
        functools.partial(stage_blocks, count),
        [block_shape] * (count - 1),
        [HB],
        [VM] * (count - 1),
        [DMA(((count - 1) * heads,))],
    )(prefill_kv)
    moved = [shift(pieces[c - 1], "seq", c) for c in range(count - 1, 0, -1)][::-1]
    own_piece, q_near, new_near, bias, picks, *states = call(
        functools.partial(stage_rest, count, split),
        [
            block_shape,
            shape(queries.shape, BF),
            shape(new_kv.shape, BF),
            shape((all_rows, count * BLOCK), F32),
            shape((reps, heads, keep_rep, count, 16, width), BF),
        ]
        + [shape((state_rows(part) + (32 if c == 1 else 0), width), BF) for c in range(count)],
        [HB] * 6,
        [VM] * (5 + count),
        [
            pltpu.VMEM((count, ns, part), F32),
            smem(blocks.shape, jnp.int32),
            smem(kept_counts.shape, jnp.int32),
            DMA((heads + 2,)),
            DMA((count + 2,)),
        ],
    )(*after([prefill_kv], pieces[0]), queries, new_kv, prefill_state, blocks, kept_counts)
    own_weight, other_weight, slope, base = call(
        functools.partial(prepare, count, split),
        [
            half_weight,
            half_weight,
            shape((count, steps, ns, part), F32),
            shape((count, steps, 1, part), F32),
        ],
        [HB] * 6,
        [VM] * 4,
        [
            pltpu.VMEM((steps, 1, channels), F32),
            pltpu.VMEM((steps, channels), BF),
            pltpu.VMEM(step_bc.shape, F32),
            pltpu.VMEM((1, channels), F32),
            pltpu.VMEM(a_log.shape, F32),
            DMA((5,)),
            DMA((2 * PIECES,)),
        ],
    )(*after([out_weight], pieces[0]), step_dt, step_input, step_bc, skip_gain, a_log)

    beside = shift(after(states[1:2], own_weight)[0], "seq", 1)
    *moved, own_weight = after([*moved, own_weight])
    kv = [own_piece, moved[0], *moved[:0:-1]]
    half_shape = (heads, keep_rep, BLOCK, width)
    rows = steps * group
    *sends, kept, sent = call(
        functools.partial(attend, count, heads),
        [shape((rows, width), BF)] * 2
        + [shape((rows + state_rows(part), width), BF)] * (count - 2)
        + [shape(half_shape, BF)] * 2,
        [VM] * (2 + 2 * count),
        [VM] * (count + 2),
    )(q_near, new_near, bias, picks, *kv, *states[2:])
    order = [*range(2, count), 1]
    gathered = [shift(sends[c], "seq", c) for c in order]
    attn, mamba = call(
        functools.partial(collect, count, heads, steps, group),
        [shape((steps * count, half), BF), shape((steps, count, 1, part), F32)],
        [VM] * (4 + count),
        [VM] * 2,
        [pltpu.VMEM((heads, steps * count * group, hd), F32)],
    )(slope, base, states[0], beside, sends[0], *gathered)
    attn_other = shift(attn, "rep", 1)
    own_sum = call(
        project_own, shape((steps * count, columns), F32), [VM, VM], VM, us=0.7
    )(attn, own_weight)
    share = count // heads_count
    sums = call(
        functools.partial(project_other, heads_count, count),
        [shape((steps, share, columns), F32)] * heads_count,
        [VM, VM, VM],
        [VM] * heads_count,
        us=0.7,
    )(own_sum, attn_other, other_weight)
    sums = [sums[0]] + [shift(sums[c], "head", c) for c in range(1, heads_count)]
    got = shift(after([sent], mamba)[0], "rep", 1)
    kept = after([kept], sums[0])[0]
    operands = [kept, got, mamba] + ([shift(mamba, "rep", 1)] if split else [])
    handoff, mamba_out = call(
        functools.partial(assemble, split),
        [
            shape((1, dec_heads, keep_rep, BLOCK, width), BF),
            shape((steps, 1, channels), F32),
        ],
        [VM] * len(operands),
        [HB] * 2,
        [DMA((2 + steps * count * (2 if split else 1),))],
    )(*operands)
    sums[1:] = after(sums[1:], handoff)
    proj_out = call(
        add_up, shape((steps, share, columns), BF), [VM] * heads_count, VM, us=0.6
    )(*sums)
    return handoff, proj_out, mamba_out


def solution(mesh):
    return jax.shard_map(
        per_device,
        mesh=mesh,
        in_specs=(
            P("groups", ("head", "rep"), "seq", None),
            P("groups", None, None),
            P("groups", None),
            P(None, ("groups", "seq"), "head", None),
            P(None, ("groups", "seq"), "head", None),
            P("head", ("seq", "rep")),
            P("groups", None, ("head", "seq")),
            P(None, "head"),
            P(None, ("groups", "seq"), "head"),
            P(None, ("groups", "seq"), "head"),
            P(None, ("groups", "seq"), None, None),
            P("head"),
        ),
        out_specs=(
            P(("groups", "seq"), "head", "rep", None, None),
            P(None, ("groups", "head"), ("seq", "rep")),
            P(None, ("groups", "seq"), "head"),
        ),
        check_vma=False,
    )
```

```python
import functools

import jax
import jax.numpy as jnp
from jax import lax
from jax.experimental import pallas as pl
from jax.experimental.pallas import tpu as pltpu
from jax.sharding import PartitionSpec as P

BLOCK = 128
PIECES = 4
NEG = -1e30
BF = jnp.bfloat16
F32 = jnp.float32
VM = pl.BlockSpec(memory_space=pltpu.VMEM)
HB = pl.BlockSpec(memory_space=pltpu.HBM)
DMA = pltpu.SemaphoreType.DMA


def shift(x, axis, c):
    size = lax.axis_size(axis)
    return lax.ppermute(x, axis, [(i, i ^ c) for i in range(size)])


def call(body, out_shape, in_specs, out_specs, scratch=(), us=1.0):
    return pl.pallas_call(
        body,
        out_shape=out_shape,
        in_specs=in_specs,
        out_specs=out_specs,
        scratch_shapes=list(scratch),
        cost_estimate=pl.CostEstimate(
            flops=0, bytes_accessed=int(us * 3.6e4), transcendentals=0
        ),
        compiler_params=pltpu.CompilerParams(vmem_limit_bytes=32 * 1024 * 1024),
    )


def in_hbm(x):
    return pltpu.with_memory_space_constraint(x, pltpu.HBM)


def after(arrays, *earlier):
    return lax.optimization_barrier((*arrays, *earlier))[: len(arrays)]


def run_all(copies):
    for copy in copies:
        copy.start()
    for copy in copies:
        copy.wait()


def copier(sems):
    position = iter(range(sems.shape[0]))
    return lambda src, dst: pltpu.make_async_copy(src, dst, sems.at[next(position)])


def state_rows(part):
    return 16 * pl.cdiv(part, 256)


def pack_state(piece, out_ref, first):
    ns, part = piece.shape
    for i in range(pl.cdiv(part, 256)):
        cut = piece[:, i * 256 : (i + 1) * 256]
        if cut.shape[1] < 256:
            cut = jnp.concatenate([cut, jnp.zeros((ns, 256 - cut.shape[1]), F32)], axis=1)
        out_ref[first + i * 16 : first + (i + 1) * 16, :] = cut.astype(BF)


def own_state(state_ref, c, split, part):
    me, rep = lax.axis_index("seq"), lax.axis_index("rep")
    if split:
        return state_ref.at[me ^ c, :, pl.ds(pl.multiple_of(rep * part, 128), part)]
    return state_ref.at[me ^ c]


def stage_blocks(partners, kv_ref, *rest):
    outs, sems = rest[:-1], rest[-1]
    me = lax.axis_index("seq")
    copy = copier(sems)
    run_all(
        [
            copy(kv_ref.at[me ^ c, j], outs[i].at[pl.ds(j * BLOCK, BLOCK)])
            for i, c in enumerate(partners)
            for j in range(kv_ref.shape[1])
        ]
    )


def stage_rest(count, split, kv_ref, q_ref, new_ref, state_ref, blocks_ref, counts_ref, *rest):
    own_out, q_out, new_out, bias_out, pick_out = rest[:5]
    states = rest[5 : 5 + count]
    loaded, blocks, counts, sems, early = rest[5 + count :]
    me, rep = lax.axis_index("seq"), lax.axis_index("rep")
    heads = kv_ref.shape[1]
    copy = copier(sems)
    moves = [copy(kv_ref.at[me, j], own_out.at[pl.ds(j * BLOCK, BLOCK)]) for j in range(heads)]
    moves += [copy(q_ref, q_out), copy(new_ref, new_out)]
    copy = copier(early)
    first = [copy(blocks_ref, blocks), copy(counts_ref, counts)]
    part = loaded.shape[2]
    for c in range(count):
        if split:
            src = state_ref.at[me ^ c, :, pl.ds(pl.multiple_of(rep * part, 128), part)]
        else:
            src = state_ref.at[me ^ c]
        first.append(copy(src, loaded.at[c]))
    for move in first + moves:
        move.start()
    for move in first:
        move.wait()
    for c in range(count):
        pack_state(loaded[c], states[c], states[c].shape[0] - state_rows(part))
    head_first = lax.axis_index("head") * new_ref.shape[2] + rep * heads
    rows = bias_out.shape[0] // heads
    keep_rep = pick_out.shape[2]
    for j in range(heads):
        live_count = counts[me, head_first + j]
        for c in range(count):
            live = jnp.int32(0)
            for side in range(2):
                for k in range(keep_rep):
                    slot = (rep if side == 0 else 1 - rep) * keep_rep + k
                    hit = (blocks[me, slot, head_first + j] == (me ^ c)) & (slot < live_count)
                    one = jnp.where(hit, 1.0, 0.0).astype(F32)
                    pick_out[side, j, k, c] = jnp.full(pick_out.shape[4:], one, F32).astype(BF)
                    live = live | hit.astype(jnp.int32)
            dead = jnp.where(live > 0, 0.0, NEG).astype(F32)
            bias_out[j * rows : (j + 1) * rows, c * BLOCK : (c + 1) * BLOCK] = jnp.full(
                (rows, BLOCK), dead, F32
            )
    for move in moves:
        move.wait()


def dot_f32(a, b, contract):
    return lax.dot_general(a, b, (contract, ((), ())), preferred_element_type=F32)


def query_rows(q_ref, heads):
    rep = lax.axis_index("rep")
    steps, _, q_heads, _ = q_ref.shape
    own_q = q_heads // 2
    group = own_q // heads
    q_all = [q_ref[step, 0].astype(F32) for step in range(steps)]
    q_all = [jnp.where(rep == 0, q[:own_q], q[own_q:]) for q in q_all]
    return [
        jnp.concatenate([x[j * group : (j + 1) * group] for x in q_all], axis=0)
        for j in range(heads)
    ]


def block_scores(q, piece_ref, j):
    hd = piece_ref.shape[1] // 2
    keys = piece_ref[j * BLOCK : (j + 1) * BLOCK, :hd]
    return dot_f32(q.astype(BF), keys, ((1,), (1,))) * hd ** (-0.5)


def block_sums(weights, piece_ref, j):
    values = piece_ref[j * BLOCK : (j + 1) * BLOCK, piece_ref.shape[1] // 2 :]
    return dot_f32(weights, values, ((1,), (0,)))


def attend(count, heads, q_ref, new_ref, bias_ref, pick_ref, *rest):
    pieces, states = rest[:count], rest[count : 2 * count - 2]
    outs, (kept_ref, sent_ref) = rest[2 * count - 2 : 3 * count - 2], rest[3 * count - 2 :]
    rep = lax.axis_index("rep")
    queries = query_rows(q_ref, heads)
    rows, hd = queries[0].shape
    steps = q_ref.shape[0]
    group = rows // steps
    all_rows = heads * rows
    scale = hd ** (-0.5)
    scores = [
        jnp.concatenate([block_scores(q, piece, j) for piece in pieces], axis=1)
        for j, q in enumerate(queries)
    ]
    scores = jnp.concatenate(scores, axis=0)
    alive = bias_ref[...] == 0.0
    scores = jnp.where(alive, scores, NEG)
    row_step = (lax.broadcasted_iota(jnp.int32, (all_rows, 1), 0) // group) % steps
    wide_q = jnp.concatenate(queries, axis=0)
    dots, fresh_values = [], []
    top = jnp.max(scores, axis=1, keepdims=True)
    for step in range(steps):
        both = new_ref[step, 0].astype(F32)
        fresh = jnp.where(rep == 0, both[:heads], both[heads:])
        wide = jnp.concatenate(
            [jnp.broadcast_to(fresh[j : j + 1], (rows, 2 * hd)) for j in range(heads)], axis=0
        )
        dot = jnp.sum(wide_q * wide[:, :hd], axis=1, keepdims=True) * scale
        dots.append(jnp.where(row_step >= step, dot, NEG))
        fresh_values.append(wide[:, hd:])
        top = jnp.maximum(top, dots[-1])
    weights = jnp.where(alive, jnp.exp(scores - top), 0.0)
    total = jnp.sum(weights, axis=1, keepdims=True)
    weights = weights.astype(BF)
    summed = []
    for j in range(heads):
        parts = [
            block_sums(weights[j * rows : (j + 1) * rows, c * BLOCK : (c + 1) * BLOCK], piece, j)
            for c, piece in enumerate(pieces)
        ]
        summed.append(functools.reduce(jnp.add, parts))
    summed = jnp.concatenate(summed, axis=0)
    for step in range(steps):
        weight = jnp.where(row_step >= step, jnp.exp(dots[step] - top), 0.0)
        total = total + weight
        summed = summed + weight.astype(BF).astype(F32) * fresh_values[step]
    result = (summed / total).astype(BF)
    for c in range(count):
        for j in range(2):
            half = result[j * rows : (j + 1) * rows] if j < heads else jnp.zeros((rows, hd), BF)
            outs[c][:rows, j * hd : (j + 1) * hd] = half
        if c > 1:
            outs[c][rows:, :] = states[c - 2][...]
    tile = pick_ref.shape[4]
    for side, ref in ((1, sent_ref), (0, kept_ref)):
        for j in range(heads):
            for k in range(ref.shape[1]):
                total = None
                for c in range(count):
                    piece = pieces[c][j * BLOCK : (j + 1) * BLOCK, :].reshape(-1, tile, 2 * hd)
                    term = piece * pick_ref[side, j, k, c][None]
                    total = term if total is None else total + term
                ref[j, k] = total.reshape(BLOCK, 2 * hd)


def collect(count, heads, steps, group, slope_ref, base_ref, home_ref, beside_ref, *rest):
    parts = [rest[0], rest[count - 1], *rest[1 : count - 1]]
    states = [home_ref, beside_ref, *parts[2:]]
    out_ref, mamba_ref, scratch = rest[count:]
    me = lax.axis_index("seq")
    ns, part = slope_ref.shape[2:]
    for c in range(count):
        first = states[c].shape[0] - state_rows(part)
        rows = [
            states[c][first + 16 * i : first + 16 * (i + 1), :].astype(F32)
            for i in range(pl.cdiv(part, 256))
        ]
        state = jnp.concatenate(rows, axis=1)[:, :part]
        for step in range(steps):
            mamba_ref[step, me ^ c] = base_ref[c, step] + jnp.sum(
                slope_ref[c, step] * state, axis=0, keepdims=True
            )
    for c in range(count):
        rows = parts[c][: steps * group, :].astype(F32)
        for j in range(heads):
            for step in range(steps):
                at = pl.multiple_of((step * count + (me ^ c)) * group, group)
                cut = rows[step * group : (step + 1) * group, j * 128 : (j + 1) * 128]
                scratch[j, pl.ds(at, group), :] = cut
    for j in range(heads):
        for g in range(group):
            at = (j * group + g) * 128
            tile = scratch[j, pl.ds(g, steps * count, stride=group), :]
            out_ref[:, at : at + 128] = tile.astype(BF)


def weight_half(weight_ref, out_ref, which, copy):
    half = out_ref.shape[0]
    rows = half // PIECES
    cuts = [(pl.ds(which * half + i * rows, rows), pl.ds(i * rows, rows)) for i in range(PIECES)]
    return [copy(weight_ref.at[src], out_ref.at[dst]) for src, dst in cuts]


def project_own(attn_ref, weight_ref, out_ref):
    out_ref[...] = dot_f32(attn_ref[...], weight_ref[...], ((1,), (0,)))


def pick(options, index):
    chosen = options[0]
    for i in range(1, len(options)):
        chosen = jnp.where(index == i, options[i], chosen)
    return chosen


def project_other(heads_count, count, acc_ref, attn_ref, weight_ref, *outs):
    total = acc_ref[...] + dot_f32(attn_ref[...], weight_ref[...], ((1,), (0,)))
    head = lax.axis_index("head")
    steps = total.shape[0] // count
    share = count // heads_count
    for step in range(steps):
        slices = [
            total[step * count + x * share : step * count + (x + 1) * share]
            for x in range(heads_count)
        ]
        for c in range(heads_count):
            outs[c][step] = pick(slices, head ^ c)


def add_up(*refs):
    total = refs[0][...]
    for ref in refs[1:-1]:
        total = total + ref[...]
    refs[-1][...] = total.astype(BF)


def prepare(count, split, weight_hbm, dt_hbm, x_hbm, bc_hbm, gain_hbm, log_hbm, own_ref, other_ref,
            slope_ref, base_ref, dt_ref, x_ref, bc_ref, gain_ref, log_ref, sems, weight_sems):
    copy = copier(sems)
    first = [
        copy(dt_hbm, dt_ref),
        copy(x_hbm, x_ref),
        copy(bc_hbm, bc_ref),
        copy(gain_hbm, gain_ref),
        copy(log_hbm, log_ref),
    ]
    copy, which = copier(weight_sems), lax.axis_index("rep")
    weights = weight_half(weight_hbm, own_ref, which, copy)
    weights += weight_half(weight_hbm, other_ref, 1 - which, copy)
    for move in first + weights:
        move.start()
    for move in first:
        move.wait()
    me, rep = lax.axis_index("seq"), lax.axis_index("rep")
    _, steps, ns, part = slope_ref.shape
    block = part * 2 if split else part
    diagonal = lax.broadcasted_iota(jnp.int32, (ns, ns), 0) == lax.broadcasted_iota(
        jnp.int32, (ns, ns), 1
    )

    def column(row):
        return jnp.sum(jnp.where(diagonal, row, 0.0), axis=1, keepdims=True)

    drive = [column(bc_ref[step, 0, 0:1, :]) for step in range(steps)]
    read = [column(bc_ref[step, 0, 1:2, :]) for step in range(steps)]
    for c in range(count):
        first = (me ^ c) * block + (rep * part if split else 0)
        lanes = pl.ds(pl.multiple_of(first, 128), part)
        rate = -jnp.exp(log_ref[:, lanes])
        gain = gain_ref[:, lanes]
        kept = jnp.ones((ns, part), F32)
        added = jnp.zeros((ns, part), F32)
        for step in range(steps):
            dt = dt_ref[step, :, lanes]
            inputs = x_ref[step : step + 1, lanes].astype(F32)
            decay = jnp.exp(dt * rate)
            kept = kept * decay
            added = added * decay + drive[step] * (dt * inputs)
            slope_ref[c, step] = read[step] * kept
            base_ref[c, step] = (
                jnp.sum(read[step] * added, axis=0, keepdims=True) + gain * inputs
            )
    for move in weights:
        move.wait()


def assemble(split, kept_ref, got_ref, mamba_ref, *rest):
    rep = lax.axis_index("rep")
    if split:
        other_ref, handoff_ref, out_ref, sems = rest
    else:
        handoff_ref, out_ref, sems = rest
    heads = kept_ref.shape[0]
    copy = copier(sems)
    moves = [
        copy(kept_ref, handoff_ref.at[0, pl.ds(rep * heads, heads)]),
        copy(got_ref, handoff_ref.at[0, pl.ds((1 - rep) * heads, heads)]),
    ]
    steps, count, _, part = mamba_ref.shape
    for step in range(steps):
        for b in range(count):
            if split:
                for ref, side in ((mamba_ref, rep), (other_ref, 1 - rep)):
                    lanes = pl.ds(pl.multiple_of((2 * b + side) * part, 128), part)
                    moves.append(copy(ref.at[step, b], out_ref.at[step, :, lanes]))
            else:
                moves.append(copy(mamba_ref.at[step, b], out_ref.at[step, :, pl.ds(b * part, part)]))
    run_all(moves)


def per_device(
    prefill_kv,
    kept_blocks,
    kept_counts,
    queries,
    new_kv,
    out_weight,
    prefill_state,
    a_log,
    step_input,
    step_dt,
    step_bc,
    skip_gain,
):
    count = lax.axis_size("seq")
    reps = lax.axis_size("rep")
    heads_count = lax.axis_size("head")
    requests, heads, tokens, width = prefill_kv.shape
    assert requests == count and tokens == BLOCK and reps == 2 and width == 256
    assert count & (count - 1) == 0 and heads_count & (heads_count - 1) == 0
    keep = kept_blocks.shape[2]
    keep_rep = keep // reps
    steps, _, q_heads, hd = queries.shape
    dec_heads = new_kv.shape[2]
    group = q_heads // dec_heads
    _, ns, block = prefill_state.shape
    split = block % (reps * 128) == 0
    part = block // reps if split else block
    all_rows = heads * steps * group
    assert all_rows <= 128
    channels = count * block
    shape = jax.ShapeDtypeStruct
    smem = pltpu.SMEM
    blocks = jnp.swapaxes(kept_blocks, 1, 2)

    prefill_kv, prefill_state, queries, new_kv = map(in_hbm, (prefill_kv, prefill_state, queries, new_kv))
    step_dt, step_bc, a_log, out_weight = map(in_hbm, (step_dt, step_bc, a_log, out_weight))
    step_input = in_hbm(step_input.reshape(steps, channels))
    skip_gain = in_hbm(skip_gain.reshape(1, -1))
    blocks, kept_counts = in_hbm(blocks), in_hbm(kept_counts)

    columns = out_weight.shape[1]
    half = heads * group * hd
    half_weight = pltpu.VMEM((half, columns), BF)
    block_shape = shape((heads * BLOCK, width), BF)
    pieces = {}
    for partners in ([count - 1], range(count - 2, 0, -1)):
        staged = call(
            functools.partial(stage_blocks, partners),
            [block_shape] * len(partners),
            [HB],
            [VM] * len(partners),
            [DMA((len(partners) * heads,))],
        )(prefill_kv)
        pieces.update(zip(partners, staged))
    pieces = [pieces[c] for c in range(1, count)]
    moved = [shift(pieces[c - 1], "seq", c) for c in range(count - 1, 0, -1)][::-1]
    own_piece, q_near, new_near, bias, picks, *states = call(
        functools.partial(stage_rest, count, split),
        [
            block_shape,
            shape(queries.shape, BF),
            shape(new_kv.shape, BF),
            shape((all_rows, count * BLOCK), F32),
            shape((reps, heads, keep_rep, count, 16, width), BF),
        ]
        + [shape((state_rows(part) + (32 if c == 1 else 0), width), BF) for c in range(count)],
        [HB] * 6,
        [VM] * (5 + count),
        [
            pltpu.VMEM((count, ns, part), F32),
            smem(blocks.shape, jnp.int32),
            smem(kept_counts.shape, jnp.int32),
            DMA((heads + 2,)),
            DMA((count + 2,)),
        ],
    )(*after([prefill_kv], pieces[0]), queries, new_kv, prefill_state, blocks, kept_counts)
    own_weight, other_weight, slope, base = call(
        functools.partial(prepare, count, split),
        [
            half_weight,
            half_weight,
            shape((count, steps, ns, part), F32),
            shape((count, steps, 1, part), F32),
        ],
        [HB] * 6,
        [VM] * 4,
        [
            pltpu.VMEM((steps, 1, channels), F32),
            pltpu.VMEM((steps, channels), BF),
            pltpu.VMEM(step_bc.shape, F32),
            pltpu.VMEM((1, channels), F32),
            pltpu.VMEM(a_log.shape, F32),
            DMA((5,)),
            DMA((2 * PIECES,)),
        ],
    )(*after([out_weight], pieces[0]), step_dt, step_input, step_bc, skip_gain, a_log)

    beside = shift(after(states[1:2], own_weight)[0], "seq", 1)
    *moved, own_weight = after([*moved[::-1], own_weight])
    kv = [own_piece, *moved[::-1]]
    half_shape = (heads, keep_rep, BLOCK, width)
    rows = steps * group
    *sends, kept, sent = call(
        functools.partial(attend, count, heads),
        [shape((rows, width), BF)] * 2
        + [shape((rows + state_rows(part), width), BF)] * (count - 2)
        + [shape(half_shape, BF)] * 2,
        [VM] * (2 + 2 * count),
        [VM] * (count + 2),
    )(q_near, new_near, bias, picks, *kv, *states[2:])
    order = [*range(2, count), 1]
    gathered = [shift(sends[c], "seq", c) for c in order]
    attn, mamba = call(
        functools.partial(collect, count, heads, steps, group),
        [shape((steps * count, half), BF), shape((steps, count, 1, part), F32)],
        [VM] * (4 + count),
        [VM] * 2,
        [pltpu.VMEM((heads, steps * count * group, hd), F32)],
    )(slope, base, states[0], beside, sends[0], *gathered)
    attn_other = shift(attn, "rep", 1)
    own_sum = call(
        project_own, shape((steps * count, columns), F32), [VM, VM], VM, us=0.7
    )(attn, own_weight)
    share = count // heads_count
    sums = call(
        functools.partial(project_other, heads_count, count),
        [shape((steps, share, columns), F32)] * heads_count,
        [VM, VM, VM],
        [VM] * heads_count,
        us=0.7,
    )(own_sum, attn_other, other_weight)
    sums = [sums[0]] + [shift(sums[c], "head", c) for c in range(1, heads_count)]
    got = shift(after([sent], mamba)[0], "rep", 1)
    kept = after([kept], sums[0])[0]
    operands = [kept, got, mamba] + ([shift(mamba, "rep", 1)] if split else [])
    handoff, mamba_out = call(
        functools.partial(assemble, split),
        [
            shape((1, dec_heads, keep_rep, BLOCK, width), BF),
            shape((steps, 1, channels), F32),
        ],
        [VM] * len(operands),
        [HB] * 2,
        [DMA((2 + steps * count * (2 if split else 1),))],
    )(*operands)
    sums[1:] = after(sums[1:], handoff)
    proj_out = call(
        add_up, shape((steps, share, columns), BF), [VM] * heads_count, VM, us=0.6
    )(*sums)
    return handoff, proj_out, mamba_out


def solution(mesh):
    return jax.shard_map(
        per_device,
        mesh=mesh,
        in_specs=(
            P("groups", ("head", "rep"), "seq", None),
            P("groups", None, None),
            P("groups", None),
            P(None, ("groups", "seq"), "head", None),
            P(None, ("groups", "seq"), "head", None),
            P("head", ("seq", "rep")),
            P("groups", None, ("head", "seq")),
            P(None, "head"),
            P(None, ("groups", "seq"), "head"),
            P(None, ("groups", "seq"), "head"),
            P(None, ("groups", "seq"), None, None),
            P("head"),
        ),
        out_specs=(
            P(("groups", "seq"), "head", "rep", None, None),
            P(None, ("groups", "head"), ("seq", "rep")),
            P(None, ("groups", "seq"), "head"),
        ),
        check_vma=False,
    )
```

```python
import functools

import jax
import jax.numpy as jnp
from jax import lax
from jax.experimental import pallas as pl
from jax.experimental.pallas import tpu as pltpu
from jax.sharding import PartitionSpec as P

BLOCK = 128
PIECES = 4
NEG = -1e30
BF = jnp.bfloat16
F32 = jnp.float32
VM = pl.BlockSpec(memory_space=pltpu.VMEM)
HB = pl.BlockSpec(memory_space=pltpu.HBM)
DMA = pltpu.SemaphoreType.DMA


def shift(x, axis, c):
    size = lax.axis_size(axis)
    return lax.ppermute(x, axis, [(i, i ^ c) for i in range(size)])


def call(body, out_shape, in_specs, out_specs, scratch=(), us=1.0):
    return pl.pallas_call(
        body,
        out_shape=out_shape,
        in_specs=in_specs,
        out_specs=out_specs,
        scratch_shapes=list(scratch),
        cost_estimate=pl.CostEstimate(
            flops=0, bytes_accessed=int(us * 3.6e4), transcendentals=0
        ),
        compiler_params=pltpu.CompilerParams(vmem_limit_bytes=32 * 1024 * 1024),
    )


def in_hbm(x):
    return pltpu.with_memory_space_constraint(x, pltpu.HBM)


def after(arrays, *earlier):
    return lax.optimization_barrier((*arrays, *earlier))[: len(arrays)]


def run_all(copies):
    for copy in copies:
        copy.start()
    for copy in copies:
        copy.wait()


def copier(sems):
    position = iter(range(sems.shape[0]))
    return lambda src, dst: pltpu.make_async_copy(src, dst, sems.at[next(position)])


def state_rows(part):
    return 16 * pl.cdiv(part, 256)


def pack_state(piece, out_ref, first):
    ns, part = piece.shape
    for i in range(pl.cdiv(part, 256)):
        cut = piece[:, i * 256 : (i + 1) * 256]
        if cut.shape[1] < 256:
            cut = jnp.concatenate([cut, jnp.zeros((ns, 256 - cut.shape[1]), F32)], axis=1)
        out_ref[first + i * 16 : first + (i + 1) * 16, :] = cut.astype(BF)


def own_state(state_ref, c, split, part):
    me, rep = lax.axis_index("seq"), lax.axis_index("rep")
    if split:
        return state_ref.at[me ^ c, :, pl.ds(pl.multiple_of(rep * part, 128), part)]
    return state_ref.at[me ^ c]


def stage_blocks(partners, kv_ref, *rest):
    outs, sems = rest[:-1], rest[-1]
    me = lax.axis_index("seq")
    copy = copier(sems)
    run_all(
        [
            copy(kv_ref.at[me ^ c, j], outs[i].at[pl.ds(j * BLOCK, BLOCK)])
            for i, c in enumerate(partners)
            for j in range(kv_ref.shape[1])
        ]
    )


def stage_rest(count, split, kv_ref, q_ref, new_ref, state_ref, blocks_ref, counts_ref, *rest):
    own_out, q_out, new_out, bias_out, pick_out = rest[:5]
    states = rest[5 : 5 + count]
    loaded, blocks, counts, sems, early = rest[5 + count :]
    me, rep = lax.axis_index("seq"), lax.axis_index("rep")
    heads = kv_ref.shape[1]
    copy = copier(sems)
    moves = [copy(kv_ref.at[me, j], own_out.at[pl.ds(j * BLOCK, BLOCK)]) for j in range(heads)]
    moves += [copy(q_ref, q_out), copy(new_ref, new_out)]
    copy = copier(early)
    first = [copy(blocks_ref, blocks), copy(counts_ref, counts)]
    part = loaded.shape[2]
    for c in range(count):
        if split:
            src = state_ref.at[me ^ c, :, pl.ds(pl.multiple_of(rep * part, 128), part)]
        else:
            src = state_ref.at[me ^ c]
        first.append(copy(src, loaded.at[c]))
    for move in first + moves:
        move.start()
    for move in first:
        move.wait()
    for c in range(count):
        pack_state(loaded[c], states[c], states[c].shape[0] - state_rows(part))
    head_first = lax.axis_index("head") * new_ref.shape[2] + rep * heads
    rows = bias_out.shape[0] // heads
    keep_rep = pick_out.shape[2]
    for j in range(heads):
        live_count = counts[me, head_first + j]
        for c in range(count):
            live = jnp.int32(0)
            for side in range(2):
                for k in range(keep_rep):
                    slot = (rep if side == 0 else 1 - rep) * keep_rep + k
                    hit = (blocks[me, slot, head_first + j] == (me ^ c)) & (slot < live_count)
                    one = jnp.where(hit, 1.0, 0.0).astype(F32)
                    pick_out[side, j, k, c] = jnp.full(pick_out.shape[4:], one, F32).astype(BF)
                    live = live | hit.astype(jnp.int32)
            dead = jnp.where(live > 0, 0.0, NEG).astype(F32)
            bias_out[j * rows : (j + 1) * rows, c * BLOCK : (c + 1) * BLOCK] = jnp.full(
                (rows, BLOCK), dead, F32
            )
    for move in moves:
        move.wait()


def dot_f32(a, b, contract):
    return lax.dot_general(a, b, (contract, ((), ())), preferred_element_type=F32)


def query_rows(q_ref, heads):
    rep = lax.axis_index("rep")
    steps, _, q_heads, _ = q_ref.shape
    own_q = q_heads // 2
    group = own_q // heads
    q_all = [q_ref[step, 0].astype(F32) for step in range(steps)]
    q_all = [jnp.where(rep == 0, q[:own_q], q[own_q:]) for q in q_all]
    return [
        jnp.concatenate([x[j * group : (j + 1) * group] for x in q_all], axis=0)
        for j in range(heads)
    ]


def block_scores(q, piece_ref, j):
    hd = piece_ref.shape[1] // 2
    keys = piece_ref[j * BLOCK : (j + 1) * BLOCK, :hd]
    return dot_f32(q.astype(BF), keys, ((1,), (1,))) * hd ** (-0.5)


def block_sums(weights, piece_ref, j):
    values = piece_ref[j * BLOCK : (j + 1) * BLOCK, piece_ref.shape[1] // 2 :]
    return dot_f32(weights, values, ((1,), (0,)))


def attend(count, heads, q_ref, new_ref, bias_ref, pick_ref, *rest):
    pieces, states = rest[:count], rest[count : 2 * count - 2]
    outs, (kept_ref, sent_ref) = rest[2 * count - 2 : 3 * count - 2], rest[3 * count - 2 :]
    rep = lax.axis_index("rep")
    queries = query_rows(q_ref, heads)
    rows, hd = queries[0].shape
    steps = q_ref.shape[0]
    group = rows // steps
    all_rows = heads * rows
    scale = hd ** (-0.5)
    scores = [
        jnp.concatenate([block_scores(q, piece, j) for piece in pieces], axis=1)
        for j, q in enumerate(queries)
    ]
    scores = jnp.concatenate(scores, axis=0)
    alive = bias_ref[...] == 0.0
    scores = jnp.where(alive, scores, NEG)
    row_step = (lax.broadcasted_iota(jnp.int32, (all_rows, 1), 0) // group) % steps
    wide_q = jnp.concatenate(queries, axis=0)
    dots, fresh_values = [], []
    top = jnp.max(scores, axis=1, keepdims=True)
    for step in range(steps):
        both = new_ref[step, 0].astype(F32)
        fresh = jnp.where(rep == 0, both[:heads], both[heads:])
        wide = jnp.concatenate(
            [jnp.broadcast_to(fresh[j : j + 1], (rows, 2 * hd)) for j in range(heads)], axis=0
        )
        dot = jnp.sum(wide_q * wide[:, :hd], axis=1, keepdims=True) * scale
        dots.append(jnp.where(row_step >= step, dot, NEG))
        fresh_values.append(wide[:, hd:])
        top = jnp.maximum(top, dots[-1])
    weights = jnp.where(alive, jnp.exp(scores - top), 0.0)
    total = jnp.sum(weights, axis=1, keepdims=True)
    weights = weights.astype(BF)
    summed = []
    for j in range(heads):
        parts = [
            block_sums(weights[j * rows : (j + 1) * rows, c * BLOCK : (c + 1) * BLOCK], piece, j)
            for c, piece in enumerate(pieces)
        ]
        summed.append(functools.reduce(jnp.add, parts))
    summed = jnp.concatenate(summed, axis=0)
    for step in range(steps):
        weight = jnp.where(row_step >= step, jnp.exp(dots[step] - top), 0.0)
        total = total + weight
        summed = summed + weight.astype(BF).astype(F32) * fresh_values[step]
    result = (summed / total).astype(BF)
    for c in range(count):
        for j in range(2):
            half = result[j * rows : (j + 1) * rows] if j < heads else jnp.zeros((rows, hd), BF)
            outs[c][:rows, j * hd : (j + 1) * hd] = half
        if c > 1:
            outs[c][rows:, :] = states[c - 2][...]
    tile = pick_ref.shape[4]
    for side, ref in ((1, sent_ref), (0, kept_ref)):
        for j in range(heads):
            for k in range(ref.shape[1]):
                total = None
                for c in range(count):
                    piece = pieces[c][j * BLOCK : (j + 1) * BLOCK, :].reshape(-1, tile, 2 * hd)
                    term = piece * pick_ref[side, j, k, c][None]
                    total = term if total is None else total + term
                ref[j, k] = total.reshape(BLOCK, 2 * hd)


def collect(count, heads, steps, group, slope_ref, base_ref, home_ref, beside_ref, *rest):
    parts = [rest[0], rest[count - 1], *rest[1 : count - 1]]
    states = [home_ref, beside_ref, *parts[2:]]
    out_ref, mamba_ref, scratch = rest[count:]
    me = lax.axis_index("seq")
    ns, part = slope_ref.shape[2:]
    for c in range(count):
        first = states[c].shape[0] - state_rows(part)
        rows = [
            states[c][first + 16 * i : first + 16 * (i + 1), :].astype(F32)
            for i in range(pl.cdiv(part, 256))
        ]
        state = jnp.concatenate(rows, axis=1)[:, :part]
        for step in range(steps):
            mamba_ref[step, me ^ c] = base_ref[c, step] + jnp.sum(
                slope_ref[c, step] * state, axis=0, keepdims=True
            )
    for c in range(count):
        rows = parts[c][: steps * group, :].astype(F32)
        for j in range(heads):
            for step in range(steps):
                at = pl.multiple_of((step * count + (me ^ c)) * group, group)
                cut = rows[step * group : (step + 1) * group, j * 128 : (j + 1) * 128]
                scratch[j, pl.ds(at, group), :] = cut
    for j in range(heads):
        for g in range(group):
            at = (j * group + g) * 128
            tile = scratch[j, pl.ds(g, steps * count, stride=group), :]
            out_ref[:, at : at + 128] = tile.astype(BF)


def weight_half(weight_ref, out_ref, which, copy):
    half = out_ref.shape[0]
    rows = half // PIECES
    cuts = [(pl.ds(which * half + i * rows, rows), pl.ds(i * rows, rows)) for i in range(PIECES)]
    return [copy(weight_ref.at[src], out_ref.at[dst]) for src, dst in cuts]


def project_own(attn_ref, weight_ref, out_ref):
    out_ref[...] = dot_f32(attn_ref[...], weight_ref[...], ((1,), (0,)))


def pick(options, index):
    chosen = options[0]
    for i in range(1, len(options)):
        chosen = jnp.where(index == i, options[i], chosen)
    return chosen


def project_other(heads_count, count, acc_ref, attn_ref, weight_ref, *outs):
    total = acc_ref[...] + dot_f32(attn_ref[...], weight_ref[...], ((1,), (0,)))
    head = lax.axis_index("head")
    steps = total.shape[0] // count
    share = count // heads_count
    for step in range(steps):
        slices = [
            total[step * count + x * share : step * count + (x + 1) * share]
            for x in range(heads_count)
        ]
        for c in range(heads_count):
            outs[c][step] = pick(slices, head ^ c)


def add_up(*refs):
    total = refs[0][...]
    for ref in refs[1:-1]:
        total = total + ref[...]
    refs[-1][...] = total.astype(BF)


def prepare(count, split, weight_hbm, dt_hbm, x_hbm, bc_hbm, gain_hbm, log_hbm, own_ref, other_ref,
            slope_ref, base_ref, dt_ref, x_ref, bc_ref, gain_ref, log_ref, sems, weight_sems):
    copy = copier(sems)
    first = [
        copy(dt_hbm, dt_ref),
        copy(x_hbm, x_ref),
        copy(bc_hbm, bc_ref),
        copy(gain_hbm, gain_ref),
        copy(log_hbm, log_ref),
    ]
    copy, which = copier(weight_sems), lax.axis_index("rep")
    weights = weight_half(weight_hbm, own_ref, which, copy)
    weights += weight_half(weight_hbm, other_ref, 1 - which, copy)
    for move in first + weights:
        move.start()
    for move in first:
        move.wait()
    me, rep = lax.axis_index("seq"), lax.axis_index("rep")
    _, steps, ns, part = slope_ref.shape
    block = part * 2 if split else part
    diagonal = lax.broadcasted_iota(jnp.int32, (ns, ns), 0) == lax.broadcasted_iota(
        jnp.int32, (ns, ns), 1
    )

    def column(row):
        return jnp.sum(jnp.where(diagonal, row, 0.0), axis=1, keepdims=True)

    drive = [column(bc_ref[step, 0, 0:1, :]) for step in range(steps)]
    read = [column(bc_ref[step, 0, 1:2, :]) for step in range(steps)]
    for c in range(count):
        first = (me ^ c) * block + (rep * part if split else 0)
        lanes = pl.ds(pl.multiple_of(first, 128), part)
        rate = -jnp.exp(log_ref[:, lanes])
        gain = gain_ref[:, lanes]
        kept = jnp.ones((ns, part), F32)
        added = jnp.zeros((ns, part), F32)
        for step in range(steps):
            dt = dt_ref[step, :, lanes]
            inputs = x_ref[step : step + 1, lanes].astype(F32)
            decay = jnp.exp(dt * rate)
            kept = kept * decay
            added = added * decay + drive[step] * (dt * inputs)
            slope_ref[c, step] = read[step] * kept
            base_ref[c, step] = (
                jnp.sum(read[step] * added, axis=0, keepdims=True) + gain * inputs
            )
    for move in weights:
        move.wait()


def assemble(split, kept_ref, got_ref, mamba_ref, *rest):
    rep = lax.axis_index("rep")
    if split:
        other_ref, handoff_ref, out_ref, sems = rest
    else:
        handoff_ref, out_ref, sems = rest
    heads = kept_ref.shape[0]
    copy = copier(sems)
    moves = [
        copy(kept_ref, handoff_ref.at[0, pl.ds(rep * heads, heads)]),
        copy(got_ref, handoff_ref.at[0, pl.ds((1 - rep) * heads, heads)]),
    ]
    steps, count, _, part = mamba_ref.shape
    for step in range(steps):
        for b in range(count):
            if split:
                for ref, side in ((mamba_ref, rep), (other_ref, 1 - rep)):
                    lanes = pl.ds(pl.multiple_of((2 * b + side) * part, 128), part)
                    moves.append(copy(ref.at[step, b], out_ref.at[step, :, lanes]))
            else:
                moves.append(copy(mamba_ref.at[step, b], out_ref.at[step, :, pl.ds(b * part, part)]))
    run_all(moves)


def per_device(
    prefill_kv,
    kept_blocks,
    kept_counts,
    queries,
    new_kv,
    out_weight,
    prefill_state,
    a_log,
    step_input,
    step_dt,
    step_bc,
    skip_gain,
):
    count = lax.axis_size("seq")
    reps = lax.axis_size("rep")
    heads_count = lax.axis_size("head")
    requests, heads, tokens, width = prefill_kv.shape
    assert requests == count and tokens == BLOCK and reps == 2 and width == 256
    assert count & (count - 1) == 0 and heads_count & (heads_count - 1) == 0
    keep = kept_blocks.shape[2]
    keep_rep = keep // reps
    steps, _, q_heads, hd = queries.shape
    dec_heads = new_kv.shape[2]
    group = q_heads // dec_heads
    _, ns, block = prefill_state.shape
    split = block % (reps * 128) == 0
    part = block // reps if split else block
    all_rows = heads * steps * group
    assert all_rows <= 128
    channels = count * block
    shape = jax.ShapeDtypeStruct
    smem = pltpu.SMEM
    blocks = jnp.swapaxes(kept_blocks, 1, 2)

    prefill_kv, prefill_state, queries, new_kv = map(in_hbm, (prefill_kv, prefill_state, queries, new_kv))
    step_dt, step_bc, a_log, out_weight = map(in_hbm, (step_dt, step_bc, a_log, out_weight))
    step_input = in_hbm(step_input.reshape(steps, channels))
    skip_gain = in_hbm(skip_gain.reshape(1, -1))
    blocks, kept_counts = in_hbm(blocks), in_hbm(kept_counts)

    columns = out_weight.shape[1]
    half = heads * group * hd
    half_weight = pltpu.VMEM((half, columns), BF)
    block_shape = shape((heads * BLOCK, width), BF)
    pieces = {}
    for partners in ([count - 1], range(count - 2, 0, -1)):
        staged = call(
            functools.partial(stage_blocks, partners),
            [block_shape] * len(partners),
            [HB],
            [VM] * len(partners),
            [DMA((len(partners) * heads,))],
        )(prefill_kv)
        pieces.update(zip(partners, staged))
    pieces = [pieces[c] for c in range(1, count)]
    moved = [shift(pieces[c - 1], "seq", c) for c in range(count - 1, 1, -1)][::-1]
    own_piece, q_near, new_near, bias, picks, *states = call(
        functools.partial(stage_rest, count, split),
        [
            block_shape,
            shape(queries.shape, BF),
            shape(new_kv.shape, BF),
            shape((all_rows, count * BLOCK), F32),
            shape((reps, heads, keep_rep, count, 16, width), BF),
        ]
        + [shape((state_rows(part) + (32 if c == 1 else 0), width), BF) for c in range(count)],
        [HB] * 6,
        [VM] * (5 + count),
        [
            pltpu.VMEM((count, ns, part), F32),
            smem(blocks.shape, jnp.int32),
            smem(kept_counts.shape, jnp.int32),
            DMA((heads + 2,)),
            DMA((count + 2,)),
        ],
    )(*after([prefill_kv], pieces[0]), queries, new_kv, prefill_state, blocks, kept_counts)
    own_weight, other_weight, slope, base = call(
        functools.partial(prepare, count, split),
        [
            half_weight,
            half_weight,
            shape((count, steps, ns, part), F32),
            shape((count, steps, 1, part), F32),
        ],
        [HB] * 6,
        [VM] * 4,
        [
            pltpu.VMEM((steps, 1, channels), F32),
            pltpu.VMEM((steps, channels), BF),
            pltpu.VMEM(step_bc.shape, F32),
            pltpu.VMEM((1, channels), F32),
            pltpu.VMEM(a_log.shape, F32),
            DMA((5,)),
            DMA((2 * PIECES,)),
        ],
    )(*after([out_weight], pieces[0]), step_dt, step_input, step_bc, skip_gain, a_log)

    moved = [shift(after(pieces[:1], own_weight)[0], "seq", 1), *moved]
    beside = shift(after(states[1:2], own_weight)[0], "seq", 1)
    *moved, own_weight = after([*moved[::-1], own_weight])
    kv = [own_piece, *moved[::-1]]
    half_shape = (heads, keep_rep, BLOCK, width)
    rows = steps * group
    *sends, kept, sent = call(
        functools.partial(attend, count, heads),
        [shape((rows, width), BF)] * 2
        + [shape((rows + state_rows(part), width), BF)] * (count - 2)
        + [shape(half_shape, BF)] * 2,
        [VM] * (2 + 2 * count),
        [VM] * (count + 2),
    )(q_near, new_near, bias, picks, *kv, *states[2:])
    order = [*range(2, count), 1]
    gathered = [shift(sends[c], "seq", c) for c in order]
    attn, mamba = call(
        functools.partial(collect, count, heads, steps, group),
        [shape((steps * count, half), BF), shape((steps, count, 1, part), F32)],
        [VM] * (4 + count),
        [VM] * 2,
        [pltpu.VMEM((heads, steps * count * group, hd), F32)],
    )(slope, base, states[0], beside, sends[0], *gathered)
    attn_other = shift(attn, "rep", 1)
    own_sum = call(
        project_own, shape((steps * count, columns), F32), [VM, VM], VM, us=0.7
    )(attn, own_weight)
    share = count // heads_count
    sums = call(
        functools.partial(project_other, heads_count, count),
        [shape((steps, share, columns), F32)] * heads_count,
        [VM, VM, VM],
        [VM] * heads_count,
        us=0.7,
    )(own_sum, attn_other, other_weight)
    sums = [sums[0]] + [shift(sums[c], "head", c) for c in range(1, heads_count)]
    got = shift(after([sent], mamba)[0], "rep", 1)
    kept = after([kept], sums[0])[0]
    operands = [kept, got, mamba] + ([shift(mamba, "rep", 1)] if split else [])
    handoff, mamba_out = call(
        functools.partial(assemble, split),
        [
            shape((1, dec_heads, keep_rep, BLOCK, width), BF),
            shape((steps, 1, channels), F32),
        ],
        [VM] * len(operands),
        [HB] * 2,
        [DMA((2 + steps * count * (2 if split else 1),))],
    )(*operands)
    sums[1:] = after(sums[1:], handoff)
    proj_out = call(
        add_up, shape((steps, share, columns), BF), [VM] * heads_count, VM, us=0.6
    )(*sums)
    return handoff, proj_out, mamba_out


def solution(mesh):
    return jax.shard_map(
        per_device,
        mesh=mesh,
        in_specs=(
            P("groups", ("head", "rep"), "seq", None),
            P("groups", None, None),
            P("groups", None),
            P(None, ("groups", "seq"), "head", None),
            P(None, ("groups", "seq"), "head", None),
            P("head", ("seq", "rep")),
            P("groups", None, ("head", "seq")),
            P(None, "head"),
            P(None, ("groups", "seq"), "head"),
            P(None, ("groups", "seq"), "head"),
            P(None, ("groups", "seq"), None, None),
            P("head"),
        ),
        out_specs=(
            P(("groups", "seq"), "head", "rep", None, None),
            P(None, ("groups", "head"), ("seq", "rep")),
            P(None, ("groups", "seq"), "head"),
        ),
        check_vma=False,
    )
```

```python
import functools

import jax
import jax.numpy as jnp
from jax import lax
from jax.experimental import pallas as pl
from jax.experimental.pallas import tpu as pltpu
from jax.sharding import PartitionSpec as P

BLOCK = 128
PIECES = 4
NEG = -1e30
BF = jnp.bfloat16
F32 = jnp.float32
VM = pl.BlockSpec(memory_space=pltpu.VMEM)
HB = pl.BlockSpec(memory_space=pltpu.HBM)
DMA = pltpu.SemaphoreType.DMA


def shift(x, axis, c):
    size = lax.axis_size(axis)
    return lax.ppermute(x, axis, [(i, i ^ c) for i in range(size)])


def call(body, out_shape, in_specs, out_specs, scratch=(), us=1.0):
    return pl.pallas_call(
        body,
        out_shape=out_shape,
        in_specs=in_specs,
        out_specs=out_specs,
        scratch_shapes=list(scratch),
        cost_estimate=pl.CostEstimate(
            flops=0, bytes_accessed=int(us * 3.6e4), transcendentals=0
        ),
        compiler_params=pltpu.CompilerParams(vmem_limit_bytes=32 * 1024 * 1024),
    )


def in_hbm(x):
    return pltpu.with_memory_space_constraint(x, pltpu.HBM)


def after(arrays, *earlier):
    return lax.optimization_barrier((*arrays, *earlier))[: len(arrays)]


def run_all(copies):
    for copy in copies:
        copy.start()
    for copy in copies:
        copy.wait()


def copier(sems):
    position = iter(range(sems.shape[0]))
    return lambda src, dst: pltpu.make_async_copy(src, dst, sems.at[next(position)])


def state_rows(part):
    return 16 * pl.cdiv(part, 256)


def pack_state(piece, out_ref, first):
    ns, part = piece.shape
    for i in range(pl.cdiv(part, 256)):
        cut = piece[:, i * 256 : (i + 1) * 256]
        if cut.shape[1] < 256:
            cut = jnp.concatenate([cut, jnp.zeros((ns, 256 - cut.shape[1]), F32)], axis=1)
        out_ref[first + i * 16 : first + (i + 1) * 16, :] = cut.astype(BF)


def own_state(state_ref, c, split, part):
    me, rep = lax.axis_index("seq"), lax.axis_index("rep")
    if split:
        return state_ref.at[me ^ c, :, pl.ds(pl.multiple_of(rep * part, 128), part)]
    return state_ref.at[me ^ c]


def stage_blocks(partners, kv_ref, *rest):
    outs, sems = rest[:-1], rest[-1]
    me = lax.axis_index("seq")
    copy = copier(sems)
    run_all(
        [
            copy(kv_ref.at[me ^ c, j], outs[i].at[pl.ds(j * BLOCK, BLOCK)])
            for i, c in enumerate(partners)
            for j in range(kv_ref.shape[1])
        ]
    )


def stage_rest(count, split, kv_ref, q_ref, new_ref, state_ref, blocks_ref, counts_ref, *rest):
    own_out, q_out, new_out, bias_out, pick_out = rest[:5]
    states = rest[5 : 5 + count]
    loaded, blocks, counts, sems, early = rest[5 + count :]
    me, rep = lax.axis_index("seq"), lax.axis_index("rep")
    heads = kv_ref.shape[1]
    copy = copier(sems)
    moves = [copy(kv_ref.at[me, j], own_out.at[pl.ds(j * BLOCK, BLOCK)]) for j in range(heads)]
    moves += [copy(q_ref, q_out), copy(new_ref, new_out)]
    copy = copier(early)
    first = [copy(blocks_ref, blocks), copy(counts_ref, counts)]
    part = loaded.shape[2]
    for c in range(count):
        if split:
            src = state_ref.at[me ^ c, :, pl.ds(pl.multiple_of(rep * part, 128), part)]
        else:
            src = state_ref.at[me ^ c]
        first.append(copy(src, loaded.at[c]))
    for move in first + moves:
        move.start()
    for move in first:
        move.wait()
    for c in range(count):
        pack_state(loaded[c], states[c], states[c].shape[0] - state_rows(part))
    head_first = lax.axis_index("head") * new_ref.shape[2] + rep * heads
    rows = bias_out.shape[0] // heads
    keep_rep = pick_out.shape[2]
    for j in range(heads):
        live_count = counts[me, head_first + j]
        for c in range(count):
            live = jnp.int32(0)
            for side in range(2):
                for k in range(keep_rep):
                    slot = (rep if side == 0 else 1 - rep) * keep_rep + k
                    hit = (blocks[me, slot, head_first + j] == (me ^ c)) & (slot < live_count)
                    one = jnp.where(hit, 1.0, 0.0).astype(F32)
                    pick_out[side, j, k, c] = jnp.full(pick_out.shape[4:], one, F32).astype(BF)
                    live = live | hit.astype(jnp.int32)
            dead = jnp.where(live > 0, 0.0, NEG).astype(F32)
            bias_out[j * rows : (j + 1) * rows, c * BLOCK : (c + 1) * BLOCK] = jnp.full(
                (rows, BLOCK), dead, F32
            )
    for move in moves:
        move.wait()


def dot_f32(a, b, contract):
    return lax.dot_general(a, b, (contract, ((), ())), preferred_element_type=F32)


def query_rows(q_ref, heads):
    rep = lax.axis_index("rep")
    steps, _, q_heads, _ = q_ref.shape
    own_q = q_heads // 2
    group = own_q // heads
    q_all = [q_ref[step, 0].astype(F32) for step in range(steps)]
    q_all = [jnp.where(rep == 0, q[:own_q], q[own_q:]) for q in q_all]
    return [
        jnp.concatenate([x[j * group : (j + 1) * group] for x in q_all], axis=0)
        for j in range(heads)
    ]


def block_scores(q, piece_ref, j):
    hd = piece_ref.shape[1] // 2
    keys = piece_ref[j * BLOCK : (j + 1) * BLOCK, :hd]
    return dot_f32(q.astype(BF), keys, ((1,), (1,))) * hd ** (-0.5)


def block_sums(weights, piece_ref, j):
    values = piece_ref[j * BLOCK : (j + 1) * BLOCK, piece_ref.shape[1] // 2 :]
    return dot_f32(weights, values, ((1,), (0,)))


def attend(count, heads, q_ref, new_ref, bias_ref, pick_ref, *rest):
    pieces, states = rest[:count], rest[count : 2 * count - 2]
    outs, (kept_ref, sent_ref) = rest[2 * count - 2 : 3 * count - 2], rest[3 * count - 2 :]
    rep = lax.axis_index("rep")
    queries = query_rows(q_ref, heads)
    rows, hd = queries[0].shape
    steps = q_ref.shape[0]
    group = rows // steps
    all_rows = heads * rows
    scale = hd ** (-0.5)
    scores = [
        jnp.concatenate([block_scores(q, piece, j) for piece in pieces], axis=1)
        for j, q in enumerate(queries)
    ]
    scores = jnp.concatenate(scores, axis=0)
    alive = bias_ref[...] == 0.0
    scores = jnp.where(alive, scores, NEG)
    row_step = (lax.broadcasted_iota(jnp.int32, (all_rows, 1), 0) // group) % steps
    wide_q = jnp.concatenate(queries, axis=0)
    dots, fresh_values = [], []
    top = jnp.max(scores, axis=1, keepdims=True)
    for step in range(steps):
        both = new_ref[step, 0].astype(F32)
        fresh = jnp.where(rep == 0, both[:heads], both[heads:])
        wide = jnp.concatenate(
            [jnp.broadcast_to(fresh[j : j + 1], (rows, 2 * hd)) for j in range(heads)], axis=0
        )
        dot = jnp.sum(wide_q * wide[:, :hd], axis=1, keepdims=True) * scale
        dots.append(jnp.where(row_step >= step, dot, NEG))
        fresh_values.append(wide[:, hd:])
        top = jnp.maximum(top, dots[-1])
    weights = jnp.where(alive, jnp.exp(scores - top), 0.0)
    total = jnp.sum(weights, axis=1, keepdims=True)
    weights = weights.astype(BF)
    summed = []
    for j in range(heads):
        parts = [
            block_sums(weights[j * rows : (j + 1) * rows, c * BLOCK : (c + 1) * BLOCK], piece, j)
            for c, piece in enumerate(pieces)
        ]
        summed.append(functools.reduce(jnp.add, parts))
    summed = jnp.concatenate(summed, axis=0)
    for step in range(steps):
        weight = jnp.where(row_step >= step, jnp.exp(dots[step] - top), 0.0)
        total = total + weight
        summed = summed + weight.astype(BF).astype(F32) * fresh_values[step]
    result = (summed / total).astype(BF)
    for c in range(count):
        for j in range(2):
            half = result[j * rows : (j + 1) * rows] if j < heads else jnp.zeros((rows, hd), BF)
            outs[c][:rows, j * hd : (j + 1) * hd] = half
        if c > 1:
            outs[c][rows:, :] = states[c - 2][...]
    tile = pick_ref.shape[4]
    for side, ref in ((1, sent_ref), (0, kept_ref)):
        for j in range(heads):
            for k in range(ref.shape[1]):
                total = None
                for c in range(count):
                    piece = pieces[c][j * BLOCK : (j + 1) * BLOCK, :].reshape(-1, tile, 2 * hd)
                    term = piece * pick_ref[side, j, k, c][None]
                    total = term if total is None else total + term
                ref[j, k] = total.reshape(BLOCK, 2 * hd)


def collect(count, heads, steps, group, slope_ref, base_ref, home_ref, beside_ref, *rest):
    parts = [rest[0], rest[count - 1], *rest[1 : count - 1]]
    states = [home_ref, beside_ref, *parts[2:]]
    out_ref, mamba_ref, scratch = rest[count:]
    me = lax.axis_index("seq")
    ns, part = slope_ref.shape[2:]
    for c in range(count):
        first = states[c].shape[0] - state_rows(part)
        rows = [
            states[c][first + 16 * i : first + 16 * (i + 1), :].astype(F32)
            for i in range(pl.cdiv(part, 256))
        ]
        state = jnp.concatenate(rows, axis=1)[:, :part]
        for step in range(steps):
            mamba_ref[step, me ^ c] = base_ref[c, step] + jnp.sum(
                slope_ref[c, step] * state, axis=0, keepdims=True
            )
    for c in range(count):
        rows = parts[c][: steps * group, :].astype(F32)
        for j in range(heads):
            for step in range(steps):
                at = pl.multiple_of((step * count + (me ^ c)) * group, group)
                cut = rows[step * group : (step + 1) * group, j * 128 : (j + 1) * 128]
                scratch[j, pl.ds(at, group), :] = cut
    for j in range(heads):
        for g in range(group):
            at = (j * group + g) * 128
            tile = scratch[j, pl.ds(g, steps * count, stride=group), :]
            out_ref[:, at : at + 128] = tile.astype(BF)


def weight_half(weight_ref, out_ref, which, copy):
    half = out_ref.shape[0]
    rows = half // PIECES
    cuts = [(pl.ds(which * half + i * rows, rows), pl.ds(i * rows, rows)) for i in range(PIECES)]
    return [copy(weight_ref.at[src], out_ref.at[dst]) for src, dst in cuts]


def project_own(attn_ref, weight_ref, out_ref):
    out_ref[...] = dot_f32(attn_ref[...], weight_ref[...], ((1,), (0,)))


def pick(options, index):
    chosen = options[0]
    for i in range(1, len(options)):
        chosen = jnp.where(index == i, options[i], chosen)
    return chosen


def project_other(heads_count, count, acc_ref, attn_ref, weight_ref, *outs):
    total = acc_ref[...] + dot_f32(attn_ref[...], weight_ref[...], ((1,), (0,)))
    head = lax.axis_index("head")
    steps = total.shape[0] // count
    share = count // heads_count
    for step in range(steps):
        slices = [
            total[step * count + x * share : step * count + (x + 1) * share]
            for x in range(heads_count)
        ]
        for c in range(heads_count):
            outs[c][step] = pick(slices, head ^ c)


def add_up(*refs):
    total = refs[0][...]
    for ref in refs[1:-1]:
        total = total + ref[...]
    refs[-1][...] = total.astype(BF)


def prepare(count, split, weight_hbm, dt_hbm, x_hbm, bc_hbm, gain_hbm, log_hbm, own_ref, other_ref,
            slope_ref, base_ref, dt_ref, x_ref, bc_ref, gain_ref, log_ref, sems, weight_sems):
    copy = copier(sems)
    first = [
        copy(dt_hbm, dt_ref),
        copy(x_hbm, x_ref),
        copy(bc_hbm, bc_ref),
        copy(gain_hbm, gain_ref),
        copy(log_hbm, log_ref),
    ]
    copy, which = copier(weight_sems), lax.axis_index("rep")
    weights = weight_half(weight_hbm, own_ref, which, copy)
    weights += weight_half(weight_hbm, other_ref, 1 - which, copy)
    for move in first + weights:
        move.start()
    for move in first:
        move.wait()
    me, rep = lax.axis_index("seq"), lax.axis_index("rep")
    _, steps, ns, part = slope_ref.shape
    block = part * 2 if split else part
    diagonal = lax.broadcasted_iota(jnp.int32, (ns, ns), 0) == lax.broadcasted_iota(
        jnp.int32, (ns, ns), 1
    )

    def column(row):
        return jnp.sum(jnp.where(diagonal, row, 0.0), axis=1, keepdims=True)

    drive = [column(bc_ref[step, 0, 0:1, :]) for step in range(steps)]
    read = [column(bc_ref[step, 0, 1:2, :]) for step in range(steps)]
    for c in range(count):
        first = (me ^ c) * block + (rep * part if split else 0)
        lanes = pl.ds(pl.multiple_of(first, 128), part)
        rate = -jnp.exp(log_ref[:, lanes])
        gain = gain_ref[:, lanes]
        kept = jnp.ones((ns, part), F32)
        added = jnp.zeros((ns, part), F32)
        for step in range(steps):
            dt = dt_ref[step, :, lanes]
            inputs = x_ref[step : step + 1, lanes].astype(F32)
            decay = jnp.exp(dt * rate)
            kept = kept * decay
            added = added * decay + drive[step] * (dt * inputs)
            slope_ref[c, step] = read[step] * kept
            base_ref[c, step] = (
                jnp.sum(read[step] * added, axis=0, keepdims=True) + gain * inputs
            )
    for move in weights:
        move.wait()


def assemble(split, kept_ref, got_ref, mamba_ref, *rest):
    rep = lax.axis_index("rep")
    if split:
        other_ref, handoff_ref, out_ref, sems = rest
    else:
        handoff_ref, out_ref, sems = rest
    heads = kept_ref.shape[0]
    copy = copier(sems)
    moves = [
        copy(kept_ref, handoff_ref.at[0, pl.ds(rep * heads, heads)]),
        copy(got_ref, handoff_ref.at[0, pl.ds((1 - rep) * heads, heads)]),
    ]
    steps, count, _, part = mamba_ref.shape
    for step in range(steps):
        for b in range(count):
            if split:
                for ref, side in ((mamba_ref, rep), (other_ref, 1 - rep)):
                    lanes = pl.ds(pl.multiple_of((2 * b + side) * part, 128), part)
                    moves.append(copy(ref.at[step, b], out_ref.at[step, :, lanes]))
            else:
                moves.append(copy(mamba_ref.at[step, b], out_ref.at[step, :, pl.ds(b * part, part)]))
    run_all(moves)


def per_device(
    prefill_kv,
    kept_blocks,
    kept_counts,
    queries,
    new_kv,
    out_weight,
    prefill_state,
    a_log,
    step_input,
    step_dt,
    step_bc,
    skip_gain,
):
    count = lax.axis_size("seq")
    reps = lax.axis_size("rep")
    heads_count = lax.axis_size("head")
    requests, heads, tokens, width = prefill_kv.shape
    assert requests == count and tokens == BLOCK and reps == 2 and width == 256
    assert count & (count - 1) == 0 and heads_count & (heads_count - 1) == 0
    keep = kept_blocks.shape[2]
    keep_rep = keep // reps
    steps, _, q_heads, hd = queries.shape
    dec_heads = new_kv.shape[2]
    group = q_heads // dec_heads
    _, ns, block = prefill_state.shape
    split = block % (reps * 128) == 0
    part = block // reps if split else block
    all_rows = heads * steps * group
    assert all_rows <= 128
    channels = count * block
    shape = jax.ShapeDtypeStruct
    smem = pltpu.SMEM
    blocks = jnp.swapaxes(kept_blocks, 1, 2)

    prefill_kv, prefill_state, queries, new_kv = map(in_hbm, (prefill_kv, prefill_state, queries, new_kv))
    step_dt, step_bc, a_log, out_weight = map(in_hbm, (step_dt, step_bc, a_log, out_weight))
    step_input = in_hbm(step_input.reshape(steps, channels))
    skip_gain = in_hbm(skip_gain.reshape(1, -1))
    blocks, kept_counts = in_hbm(blocks), in_hbm(kept_counts)

    columns = out_weight.shape[1]
    half = heads * group * hd
    half_weight = pltpu.VMEM((half, columns), BF)
    block_shape = shape((heads * BLOCK, width), BF)
    pieces = {}
    for partners in ([count - 1], range(count - 2, 0, -1)):
        staged = call(
            functools.partial(stage_blocks, partners),
            [block_shape] * len(partners),
            [HB],
            [VM] * len(partners),
            [DMA((len(partners) * heads,))],
        )(prefill_kv)
        pieces.update(zip(partners, staged))
    pieces = [pieces[c] for c in range(1, count)]
    moved = [shift(pieces[c - 1], "seq", c) for c in range(count - 1, 1, -1)][::-1]
    own_piece, q_near, new_near, bias, picks, *states = call(
        functools.partial(stage_rest, count, split),
        [
            block_shape,
            shape(queries.shape, BF),
            shape(new_kv.shape, BF),
            shape((all_rows, count * BLOCK), F32),
            shape((reps, heads, keep_rep, count, 16, width), BF),
        ]
        + [shape((state_rows(part) + (32 if c == 1 else 0), width), BF) for c in range(count)],
        [HB] * 6,
        [VM] * (5 + count),
        [
            pltpu.VMEM((count, ns, part), F32),
            smem(blocks.shape, jnp.int32),
            smem(kept_counts.shape, jnp.int32),
            DMA((heads + 2,)),
            DMA((count + 2,)),
        ],
    )(*after([prefill_kv], pieces[0]), queries, new_kv, prefill_state, blocks, kept_counts)
    own_weight, other_weight, slope, base = call(
        functools.partial(prepare, count, split),
        [
            half_weight,
            half_weight,
            shape((count, steps, ns, part), F32),
            shape((count, steps, 1, part), F32),
        ],
        [HB] * 6,
        [VM] * 4,
        [
            pltpu.VMEM((steps, 1, channels), F32),
            pltpu.VMEM((steps, channels), BF),
            pltpu.VMEM(step_bc.shape, F32),
            pltpu.VMEM((1, channels), F32),
            pltpu.VMEM(a_log.shape, F32),
            DMA((5,)),
            DMA((2 * PIECES,)),
        ],
    )(*after([out_weight], pieces[0]), step_dt, step_input, step_bc, skip_gain, a_log)

    moved = [shift(after(pieces[:1], own_piece)[0], "seq", 1), *moved]
    beside = shift(after(states[1:2], own_weight)[0], "seq", 1)
    *moved, own_weight = after([*moved[::-1], own_weight])
    kv = [own_piece, *moved[::-1]]
    half_shape = (heads, keep_rep, BLOCK, width)
    rows = steps * group
    *sends, kept, sent = call(
        functools.partial(attend, count, heads),
        [shape((rows, width), BF)] * 2
        + [shape((rows + state_rows(part), width), BF)] * (count - 2)
        + [shape(half_shape, BF)] * 2,
        [VM] * (2 + 2 * count),
        [VM] * (count + 2),
    )(q_near, new_near, bias, picks, *kv, *states[2:])
    order = [*range(2, count), 1]
    gathered = [shift(sends[c], "seq", c) for c in order]
    attn, mamba = call(
        functools.partial(collect, count, heads, steps, group),
        [shape((steps * count, half), BF), shape((steps, count, 1, part), F32)],
        [VM] * (4 + count),
        [VM] * 2,
        [pltpu.VMEM((heads, steps * count * group, hd), F32)],
    )(slope, base, states[0], beside, sends[0], *gathered)
    attn_other = shift(attn, "rep", 1)
    own_sum = call(
        project_own, shape((steps * count, columns), F32), [VM, VM], VM, us=0.7
    )(attn, own_weight)
    share = count // heads_count
    sums = call(
        functools.partial(project_other, heads_count, count),
        [shape((steps, share, columns), F32)] * heads_count,
        [VM, VM, VM],
        [VM] * heads_count,
        us=0.7,
    )(own_sum, attn_other, other_weight)
    sums = [sums[0]] + [shift(sums[c], "head", c) for c in range(1, heads_count)]
    got = shift(after([sent], mamba)[0], "rep", 1)
    kept = after([kept], sums[0])[0]
    operands = [kept, got, mamba] + ([shift(mamba, "rep", 1)] if split else [])
    handoff, mamba_out = call(
        functools.partial(assemble, split),
        [
            shape((1, dec_heads, keep_rep, BLOCK, width), BF),
            shape((steps, 1, channels), F32),
        ],
        [VM] * len(operands),
        [HB] * 2,
        [DMA((2 + steps * count * (2 if split else 1),))],
    )(*operands)
    sums[1:] = after(sums[1:], handoff)
    proj_out = call(
        add_up, shape((steps, share, columns), BF), [VM] * heads_count, VM, us=0.6
    )(*sums)
    return handoff, proj_out, mamba_out


def solution(mesh):
    return jax.shard_map(
        per_device,
        mesh=mesh,
        in_specs=(
            P("groups", ("head", "rep"), "seq", None),
            P("groups", None, None),
            P("groups", None),
            P(None, ("groups", "seq"), "head", None),
            P(None, ("groups", "seq"), "head", None),
            P("head", ("seq", "rep")),
            P("groups", None, ("head", "seq")),
            P(None, "head"),
            P(None, ("groups", "seq"), "head"),
            P(None, ("groups", "seq"), "head"),
            P(None, ("groups", "seq"), None, None),
            P("head"),
        ),
        out_specs=(
            P(("groups", "seq"), "head", "rep", None, None),
            P(None, ("groups", "head"), ("seq", "rep")),
            P(None, ("groups", "seq"), "head"),
        ),
        check_vma=False,
    )
```

```python
import functools

import jax
import jax.numpy as jnp
from jax import lax
from jax.experimental import pallas as pl
from jax.experimental.pallas import tpu as pltpu
from jax.sharding import PartitionSpec as P

BLOCK = 128
PIECES = 4
NEG = -1e30
BF = jnp.bfloat16
F32 = jnp.float32
VM = pl.BlockSpec(memory_space=pltpu.VMEM)
HB = pl.BlockSpec(memory_space=pltpu.HBM)
DMA = pltpu.SemaphoreType.DMA


def shift(x, axis, c):
    size = lax.axis_size(axis)
    return lax.ppermute(x, axis, [(i, i ^ c) for i in range(size)])


def call(body, out_shape, in_specs, out_specs, scratch=(), us=1.0):
    return pl.pallas_call(
        body,
        out_shape=out_shape,
        in_specs=in_specs,
        out_specs=out_specs,
        scratch_shapes=list(scratch),
        cost_estimate=pl.CostEstimate(
            flops=0, bytes_accessed=int(us * 3.6e4), transcendentals=0
        ),
        compiler_params=pltpu.CompilerParams(vmem_limit_bytes=32 * 1024 * 1024),
    )


def in_hbm(x):
    return pltpu.with_memory_space_constraint(x, pltpu.HBM)


def after(arrays, *earlier):
    return lax.optimization_barrier((*arrays, *earlier))[: len(arrays)]


def run_all(copies):
    for copy in copies:
        copy.start()
    for copy in copies:
        copy.wait()


def copier(sems):
    position = iter(range(sems.shape[0]))
    return lambda src, dst: pltpu.make_async_copy(src, dst, sems.at[next(position)])


def state_rows(part):
    return 16 * pl.cdiv(part, 256)


def pack_state(piece, out_ref, first):
    ns, part = piece.shape
    for i in range(pl.cdiv(part, 256)):
        cut = piece[:, i * 256 : (i + 1) * 256]
        if cut.shape[1] < 256:
            cut = jnp.concatenate([cut, jnp.zeros((ns, 256 - cut.shape[1]), F32)], axis=1)
        out_ref[first + i * 16 : first + (i + 1) * 16, :] = cut.astype(BF)


def own_state(state_ref, c, split, part):
    me, rep = lax.axis_index("seq"), lax.axis_index("rep")
    if split:
        return state_ref.at[me ^ c, :, pl.ds(pl.multiple_of(rep * part, 128), part)]
    return state_ref.at[me ^ c]


def stage_blocks(partners, kv_ref, *rest):
    outs, sems = rest[:-1], rest[-1]
    me = lax.axis_index("seq")
    copy = copier(sems)
    run_all(
        [
            copy(kv_ref.at[me ^ c, j], outs[i].at[pl.ds(j * BLOCK, BLOCK)])
            for i, c in enumerate(partners)
            for j in range(kv_ref.shape[1])
        ]
    )


def stage_rest(count, split, kv_ref, q_ref, new_ref, state_ref, blocks_ref, counts_ref, *rest):
    own_out, q_out, new_out, bias_out, pick_out = rest[:5]
    states = rest[5 : 5 + count]
    loaded, blocks, counts, sems, early = rest[5 + count :]
    me, rep = lax.axis_index("seq"), lax.axis_index("rep")
    heads = kv_ref.shape[1]
    copy = copier(sems)
    moves = [copy(kv_ref.at[me, j], own_out.at[pl.ds(j * BLOCK, BLOCK)]) for j in range(heads)]
    moves += [copy(q_ref, q_out), copy(new_ref, new_out)]
    copy = copier(early)
    first = [copy(blocks_ref, blocks), copy(counts_ref, counts)]
    part = loaded.shape[2]
    for c in range(count):
        if split:
            src = state_ref.at[me ^ c, :, pl.ds(pl.multiple_of(rep * part, 128), part)]
        else:
            src = state_ref.at[me ^ c]
        first.append(copy(src, loaded.at[c]))
    for move in first + moves:
        move.start()
    for move in first:
        move.wait()
    for c in range(count):
        pack_state(loaded[c], states[c], states[c].shape[0] - state_rows(part))
    head_first = lax.axis_index("head") * new_ref.shape[2] + rep * heads
    rows = bias_out.shape[0] // heads
    keep_rep = pick_out.shape[2]
    for j in range(heads):
        live_count = counts[me, head_first + j]
        for c in range(count):
            live = jnp.int32(0)
            for side in range(2):
                for k in range(keep_rep):
                    slot = (rep if side == 0 else 1 - rep) * keep_rep + k
                    hit = (blocks[me, slot, head_first + j] == (me ^ c)) & (slot < live_count)
                    one = jnp.where(hit, 1.0, 0.0).astype(F32)
                    pick_out[side, j, k, c] = jnp.full(pick_out.shape[4:], one, F32).astype(BF)
                    live = live | hit.astype(jnp.int32)
            dead = jnp.where(live > 0, 0.0, NEG).astype(F32)
            bias_out[j * rows : (j + 1) * rows, c * BLOCK : (c + 1) * BLOCK] = jnp.full(
                (rows, BLOCK), dead, F32
            )
    for move in moves:
        move.wait()


def dot_f32(a, b, contract):
    return lax.dot_general(a, b, (contract, ((), ())), preferred_element_type=F32)


def query_rows(q_ref, heads):
    rep = lax.axis_index("rep")
    steps, _, q_heads, _ = q_ref.shape
    own_q = q_heads // 2
    group = own_q // heads
    q_all = [q_ref[step, 0].astype(F32) for step in range(steps)]
    q_all = [jnp.where(rep == 0, q[:own_q], q[own_q:]) for q in q_all]
    return [
        jnp.concatenate([x[j * group : (j + 1) * group] for x in q_all], axis=0)
        for j in range(heads)
    ]


def block_scores(q, piece_ref, j):
    hd = piece_ref.shape[1] // 2
    keys = piece_ref[j * BLOCK : (j + 1) * BLOCK, :hd]
    return dot_f32(q.astype(BF), keys, ((1,), (1,))) * hd ** (-0.5)


def block_sums(weights, piece_ref, j):
    values = piece_ref[j * BLOCK : (j + 1) * BLOCK, piece_ref.shape[1] // 2 :]
    return dot_f32(weights, values, ((1,), (0,)))


def attend(count, heads, q_ref, new_ref, bias_ref, pick_ref, *rest):
    pieces, states = rest[:count], rest[count : 2 * count - 2]
    outs, (kept_ref, sent_ref) = rest[2 * count - 2 : 3 * count - 2], rest[3 * count - 2 :]
    rep = lax.axis_index("rep")
    queries = query_rows(q_ref, heads)
    rows, hd = queries[0].shape
    steps = q_ref.shape[0]
    group = rows // steps
    all_rows = heads * rows
    scale = hd ** (-0.5)
    scores = [
        jnp.concatenate([block_scores(q, piece, j) for piece in pieces], axis=1)
        for j, q in enumerate(queries)
    ]
    scores = jnp.concatenate(scores, axis=0)
    alive = bias_ref[...] == 0.0
    scores = jnp.where(alive, scores, NEG)
    row_step = (lax.broadcasted_iota(jnp.int32, (all_rows, 1), 0) // group) % steps
    wide_q = jnp.concatenate(queries, axis=0)
    dots, fresh_values = [], []
    top = jnp.max(scores, axis=1, keepdims=True)
    for step in range(steps):
        both = new_ref[step, 0].astype(F32)
        fresh = jnp.where(rep == 0, both[:heads], both[heads:])
        wide = jnp.concatenate(
            [jnp.broadcast_to(fresh[j : j + 1], (rows, 2 * hd)) for j in range(heads)], axis=0
        )
        dot = jnp.sum(wide_q * wide[:, :hd], axis=1, keepdims=True) * scale
        dots.append(jnp.where(row_step >= step, dot, NEG))
        fresh_values.append(wide[:, hd:])
        top = jnp.maximum(top, dots[-1])
    weights = jnp.where(alive, jnp.exp(scores - top), 0.0)
    total = jnp.sum(weights, axis=1, keepdims=True)
    weights = weights.astype(BF)
    summed = []
    for j in range(heads):
        parts = [
            block_sums(weights[j * rows : (j + 1) * rows, c * BLOCK : (c + 1) * BLOCK], piece, j)
            for c, piece in enumerate(pieces)
        ]
        summed.append(functools.reduce(jnp.add, parts))
    summed = jnp.concatenate(summed, axis=0)
    for step in range(steps):
        weight = jnp.where(row_step >= step, jnp.exp(dots[step] - top), 0.0)
        total = total + weight
        summed = summed + weight.astype(BF).astype(F32) * fresh_values[step]
    result = (summed / total).astype(BF)
    for c in range(count):
        for j in range(2):
            half = result[j * rows : (j + 1) * rows] if j < heads else jnp.zeros((rows, hd), BF)
            outs[c][:rows, j * hd : (j + 1) * hd] = half
        if c > 1:
            outs[c][rows:, :] = states[c - 2][...]
    tile = pick_ref.shape[4]
    for side, ref in ((1, sent_ref), (0, kept_ref)):
        for j in range(heads):
            for k in range(ref.shape[1]):
                total = None
                for c in range(count):
                    piece = pieces[c][j * BLOCK : (j + 1) * BLOCK, :].reshape(-1, tile, 2 * hd)
                    term = piece * pick_ref[side, j, k, c][None]
                    total = term if total is None else total + term
                ref[j, k] = total.reshape(BLOCK, 2 * hd)


def collect(count, heads, steps, group, slope_ref, base_ref, home_ref, beside_ref, *rest):
    parts = [rest[0], rest[count - 1], *rest[1 : count - 1]]
    states = [home_ref, beside_ref, *parts[2:]]
    out_ref, mamba_ref, scratch = rest[count:]
    me = lax.axis_index("seq")
    ns, part = slope_ref.shape[2:]
    for c in range(count):
        first = states[c].shape[0] - state_rows(part)
        rows = [
            states[c][first + 16 * i : first + 16 * (i + 1), :].astype(F32)
            for i in range(pl.cdiv(part, 256))
        ]
        state = jnp.concatenate(rows, axis=1)[:, :part]
        for step in range(steps):
            mamba_ref[step, me ^ c] = base_ref[c, step] + jnp.sum(
                slope_ref[c, step] * state, axis=0, keepdims=True
            )
    for c in range(count):
        rows = parts[c][: steps * group, :].astype(F32)
        for j in range(heads):
            for step in range(steps):
                at = pl.multiple_of((step * count + (me ^ c)) * group, group)
                cut = rows[step * group : (step + 1) * group, j * 128 : (j + 1) * 128]
                scratch[j, pl.ds(at, group), :] = cut
    for j in range(heads):
        for g in range(group):
            at = (j * group + g) * 128
            tile = scratch[j, pl.ds(g, steps * count, stride=group), :]
            out_ref[:, at : at + 128] = tile.astype(BF)


def weight_half(weight_ref, out_ref, which, copy):
    half = out_ref.shape[0]
    rows = half // PIECES
    cuts = [(pl.ds(which * half + i * rows, rows), pl.ds(i * rows, rows)) for i in range(PIECES)]
    return [copy(weight_ref.at[src], out_ref.at[dst]) for src, dst in cuts]


def project_own(attn_ref, weight_ref, out_ref):
    out_ref[...] = dot_f32(attn_ref[...], weight_ref[...], ((1,), (0,)))


def pick(options, index):
    chosen = options[0]
    for i in range(1, len(options)):
        chosen = jnp.where(index == i, options[i], chosen)
    return chosen


def project_other(heads_count, count, acc_ref, attn_ref, weight_ref, *outs):
    total = acc_ref[...] + dot_f32(attn_ref[...], weight_ref[...], ((1,), (0,)))
    head = lax.axis_index("head")
    steps = total.shape[0] // count
    share = count // heads_count
    for step in range(steps):
        slices = [
            total[step * count + x * share : step * count + (x + 1) * share]
            for x in range(heads_count)
        ]
        for c in range(heads_count):
            outs[c][step] = pick(slices, head ^ c)


def add_up(*refs):
    total = refs[0][...]
    for ref in refs[1:-1]:
        total = total + ref[...]
    refs[-1][...] = total.astype(BF)


def prepare(count, split, weight_hbm, dt_hbm, x_hbm, bc_hbm, gain_hbm, log_hbm, own_ref, other_ref,
            slope_ref, base_ref, dt_ref, x_ref, bc_ref, gain_ref, log_ref, sems, weight_sems):
    copy = copier(sems)
    first = [
        copy(dt_hbm, dt_ref),
        copy(x_hbm, x_ref),
        copy(bc_hbm, bc_ref),
        copy(gain_hbm, gain_ref),
        copy(log_hbm, log_ref),
    ]
    copy, which = copier(weight_sems), lax.axis_index("rep")
    weights = weight_half(weight_hbm, own_ref, which, copy)
    weights += weight_half(weight_hbm, other_ref, 1 - which, copy)
    for move in first + weights:
        move.start()
    for move in first:
        move.wait()
    me, rep = lax.axis_index("seq"), lax.axis_index("rep")
    _, steps, ns, part = slope_ref.shape
    block = part * 2 if split else part
    diagonal = lax.broadcasted_iota(jnp.int32, (ns, ns), 0) == lax.broadcasted_iota(
        jnp.int32, (ns, ns), 1
    )

    def column(row):
        return jnp.sum(jnp.where(diagonal, row, 0.0), axis=1, keepdims=True)

    drive = [column(bc_ref[step, 0, 0:1, :]) for step in range(steps)]
    read = [column(bc_ref[step, 0, 1:2, :]) for step in range(steps)]
    for c in range(count):
        first = (me ^ c) * block + (rep * part if split else 0)
        lanes = pl.ds(pl.multiple_of(first, 128), part)
        rate = -jnp.exp(log_ref[:, lanes])
        gain = gain_ref[:, lanes]
        kept = jnp.ones((ns, part), F32)
        added = jnp.zeros((ns, part), F32)
        for step in range(steps):
            dt = dt_ref[step, :, lanes]
            inputs = x_ref[step : step + 1, lanes].astype(F32)
            decay = jnp.exp(dt * rate)
            kept = kept * decay
            added = added * decay + drive[step] * (dt * inputs)
            slope_ref[c, step] = read[step] * kept
            base_ref[c, step] = (
                jnp.sum(read[step] * added, axis=0, keepdims=True) + gain * inputs
            )
    for move in weights:
        move.wait()


def assemble(split, kept_ref, got_ref, mamba_ref, *rest):
    rep = lax.axis_index("rep")
    if split:
        other_ref, handoff_ref, out_ref, sems = rest
    else:
        handoff_ref, out_ref, sems = rest
    heads = kept_ref.shape[0]
    copy = copier(sems)
    moves = [
        copy(kept_ref, handoff_ref.at[0, pl.ds(rep * heads, heads)]),
        copy(got_ref, handoff_ref.at[0, pl.ds((1 - rep) * heads, heads)]),
    ]
    steps, count, _, part = mamba_ref.shape
    for step in range(steps):
        for b in range(count):
            if split:
                for ref, side in ((mamba_ref, rep), (other_ref, 1 - rep)):
                    lanes = pl.ds(pl.multiple_of((2 * b + side) * part, 128), part)
                    moves.append(copy(ref.at[step, b], out_ref.at[step, :, lanes]))
            else:
                moves.append(copy(mamba_ref.at[step, b], out_ref.at[step, :, pl.ds(b * part, part)]))
    run_all(moves)


def per_device(
    prefill_kv,
    kept_blocks,
    kept_counts,
    queries,
    new_kv,
    out_weight,
    prefill_state,
    a_log,
    step_input,
    step_dt,
    step_bc,
    skip_gain,
):
    count = lax.axis_size("seq")
    reps = lax.axis_size("rep")
    heads_count = lax.axis_size("head")
    requests, heads, tokens, width = prefill_kv.shape
    assert requests == count and tokens == BLOCK and reps == 2 and width == 256
    assert count & (count - 1) == 0 and heads_count & (heads_count - 1) == 0
    keep = kept_blocks.shape[2]
    keep_rep = keep // reps
    steps, _, q_heads, hd = queries.shape
    dec_heads = new_kv.shape[2]
    group = q_heads // dec_heads
    _, ns, block = prefill_state.shape
    split = block % (reps * 128) == 0
    part = block // reps if split else block
    all_rows = heads * steps * group
    assert all_rows <= 128
    channels = count * block
    shape = jax.ShapeDtypeStruct
    smem = pltpu.SMEM
    blocks = jnp.swapaxes(kept_blocks, 1, 2)

    prefill_kv, prefill_state, queries, new_kv = map(in_hbm, (prefill_kv, prefill_state, queries, new_kv))
    step_dt, step_bc, a_log, out_weight = map(in_hbm, (step_dt, step_bc, a_log, out_weight))
    step_input = in_hbm(step_input.reshape(steps, channels))
    skip_gain = in_hbm(skip_gain.reshape(1, -1))
    blocks, kept_counts = in_hbm(blocks), in_hbm(kept_counts)

    columns = out_weight.shape[1]
    half = heads * group * hd
    half_weight = pltpu.VMEM((half, columns), BF)
    block_shape = shape((heads * BLOCK, width), BF)
    pieces = {}
    for partners in ([count - 1], range(count - 2, 0, -1)):
        staged = call(
            functools.partial(stage_blocks, partners),
            [block_shape] * len(partners),
            [HB],
            [VM] * len(partners),
            [DMA((len(partners) * heads,))],
        )(prefill_kv)
        pieces.update(zip(partners, staged))
    pieces = [pieces[c] for c in range(1, count)]
    moved = [shift(pieces[c - 1], "seq", c) for c in range(count - 1, 1, -1)][::-1]
    own_piece, q_near, new_near, bias, picks, *states = call(
        functools.partial(stage_rest, count, split),
        [
            block_shape,
            shape(queries.shape, BF),
            shape(new_kv.shape, BF),
            shape((all_rows, count * BLOCK), F32),
            shape((reps, heads, keep_rep, count, 16, width), BF),
        ]
        + [shape((state_rows(part) + (32 if c == 1 else 0), width), BF) for c in range(count)],
        [HB] * 6,
        [VM] * (5 + count),
        [
            pltpu.VMEM((count, ns, part), F32),
            smem(blocks.shape, jnp.int32),
            smem(kept_counts.shape, jnp.int32),
            DMA((heads + 2,)),
            DMA((count + 2,)),
        ],
    )(*after([prefill_kv], pieces[0]), queries, new_kv, prefill_state, blocks, kept_counts)
    own_weight, other_weight, slope, base = call(
        functools.partial(prepare, count, split),
        [
            half_weight,
            half_weight,
            shape((count, steps, ns, part), F32),
            shape((count, steps, 1, part), F32),
        ],
        [HB] * 6,
        [VM] * 4,
        [
            pltpu.VMEM((steps, 1, channels), F32),
            pltpu.VMEM((steps, channels), BF),
            pltpu.VMEM(step_bc.shape, F32),
            pltpu.VMEM((1, channels), F32),
            pltpu.VMEM(a_log.shape, F32),
            DMA((5,)),
            DMA((2 * PIECES,)),
        ],
    )(*after([out_weight], pieces[0]), step_dt, step_input, step_bc, skip_gain, a_log)

    moved = [shift(after(pieces[:1], own_piece)[0], "seq", 1), *moved]
    beside = shift(after(states[1:2], own_weight)[0], "seq", 1)
    *moved, own_weight = after([*moved[::-1], own_weight])
    kv = [own_piece, *moved[::-1]]
    half_shape = (heads, keep_rep, BLOCK, width)
    rows = steps * group
    *sends, kept, sent = call(
        functools.partial(attend, count, heads),
        [shape((rows, width), BF)] * 2
        + [shape((rows + state_rows(part), width), BF)] * (count - 2)
        + [shape(half_shape, BF)] * 2,
        [VM] * (2 + 2 * count),
        [VM] * (count + 2),
    )(q_near, new_near, bias, picks, *kv, *states[2:])
    order = [*range(2, count), 1]
    gathered = [shift(sends[c], "seq", c) for c in order]
    attn, mamba = call(
        functools.partial(collect, count, heads, steps, group),
        [shape((steps * count, half), BF), shape((steps, count, 1, part), F32)],
        [VM] * (4 + count),
        [VM] * 2,
        [pltpu.VMEM((heads, (steps * count + 1) * group, hd), F32)],
    )(slope, base, states[0], beside, sends[0], *gathered)
    attn_other = shift(attn, "rep", 1)
    own_sum = call(
        project_own, shape((steps * count, columns), F32), [VM, VM], VM, us=0.7
    )(attn, own_weight)
    share = count // heads_count
    sums = call(
        functools.partial(project_other, heads_count, count),
        [shape((steps, share, columns), F32)] * heads_count,
        [VM, VM, VM],
        [VM] * heads_count,
        us=0.7,
    )(own_sum, attn_other, other_weight)
    sums = [sums[0]] + [shift(sums[c], "head", c) for c in range(1, heads_count)]
    got = shift(after([sent], mamba)[0], "rep", 1)
    kept = after([kept], sums[0])[0]
    operands = [kept, got, mamba] + ([shift(mamba, "rep", 1)] if split else [])
    handoff, mamba_out = call(
        functools.partial(assemble, split),
        [
            shape((1, dec_heads, keep_rep, BLOCK, width), BF),
            shape((steps, 1, channels), F32),
        ],
        [VM] * len(operands),
        [HB] * 2,
        [DMA((2 + steps * count * (2 if split else 1),))],
    )(*operands)
    sums[1:] = after(sums[1:], handoff)
    proj_out = call(
        add_up, shape((steps, share, columns), BF), [VM] * heads_count, VM, us=0.6
    )(*sums)
    return handoff, proj_out, mamba_out


def solution(mesh):
    return jax.shard_map(
        per_device,
        mesh=mesh,
        in_specs=(
            P("groups", ("head", "rep"), "seq", None),
            P("groups", None, None),
            P("groups", None),
            P(None, ("groups", "seq"), "head", None),
            P(None, ("groups", "seq"), "head", None),
            P("head", ("seq", "rep")),
            P("groups", None, ("head", "seq")),
            P(None, "head"),
            P(None, ("groups", "seq"), "head"),
            P(None, ("groups", "seq"), "head"),
            P(None, ("groups", "seq"), None, None),
            P("head"),
        ),
        out_specs=(
            P(("groups", "seq"), "head", "rep", None, None),
            P(None, ("groups", "head"), ("seq", "rep")),
            P(None, ("groups", "seq"), "head"),
        ),
        check_vma=False,
    )
```

```python
import functools

import jax
import jax.numpy as jnp
from jax import lax
from jax.experimental import pallas as pl
from jax.experimental.pallas import tpu as pltpu
from jax.sharding import PartitionSpec as P

BLOCK = 128
PIECES = 4
NEG = -1e30
BF = jnp.bfloat16
F32 = jnp.float32
VM = pl.BlockSpec(memory_space=pltpu.VMEM)
HB = pl.BlockSpec(memory_space=pltpu.HBM)
DMA = pltpu.SemaphoreType.DMA


def shift(x, axis, c):
    size = lax.axis_size(axis)
    return lax.ppermute(x, axis, [(i, i ^ c) for i in range(size)])


def call(body, out_shape, in_specs, out_specs, scratch=(), us=1.0):
    return pl.pallas_call(
        body,
        out_shape=out_shape,
        in_specs=in_specs,
        out_specs=out_specs,
        scratch_shapes=list(scratch),
        cost_estimate=pl.CostEstimate(
            flops=0, bytes_accessed=int(us * 3.6e4), transcendentals=0
        ),
        compiler_params=pltpu.CompilerParams(vmem_limit_bytes=32 * 1024 * 1024),
    )


def in_hbm(x):
    return pltpu.with_memory_space_constraint(x, pltpu.HBM)


def after(arrays, *earlier):
    return lax.optimization_barrier((*arrays, *earlier))[: len(arrays)]


def run_all(copies):
    for copy in copies:
        copy.start()
    for copy in copies:
        copy.wait()


def copier(sems):
    position = iter(range(sems.shape[0]))
    return lambda src, dst: pltpu.make_async_copy(src, dst, sems.at[next(position)])


def state_rows(part):
    return 16 * pl.cdiv(part, 256)


def pack_state(piece, out_ref, first):
    ns, part = piece.shape
    for i in range(pl.cdiv(part, 256)):
        cut = piece[:, i * 256 : (i + 1) * 256]
        if cut.shape[1] < 256:
            cut = jnp.concatenate([cut, jnp.zeros((ns, 256 - cut.shape[1]), F32)], axis=1)
        out_ref[first + i * 16 : first + (i + 1) * 16, :] = cut.astype(BF)


def own_state(state_ref, c, split, part):
    me, rep = lax.axis_index("seq"), lax.axis_index("rep")
    if split:
        return state_ref.at[me ^ c, :, pl.ds(pl.multiple_of(rep * part, 128), part)]
    return state_ref.at[me ^ c]


def stage_blocks(partners, kv_ref, *rest):
    outs, sems = rest[:-1], rest[-1]
    me = lax.axis_index("seq")
    copy = copier(sems)
    run_all(
        [
            copy(kv_ref.at[me ^ c, j], outs[i].at[pl.ds(j * BLOCK, BLOCK)])
            for i, c in enumerate(partners)
            for j in range(kv_ref.shape[1])
        ]
    )


def stage_rest(count, split, kv_ref, q_ref, new_ref, state_ref, blocks_ref, counts_ref, *rest):
    own_out, q_out, new_out, bias_out, pick_out = rest[:5]
    states = rest[5 : 5 + count]
    loaded, blocks, counts, sems, early = rest[5 + count :]
    me, rep = lax.axis_index("seq"), lax.axis_index("rep")
    heads = kv_ref.shape[1]
    copy = copier(sems)
    moves = [copy(kv_ref.at[me, j], own_out.at[pl.ds(j * BLOCK, BLOCK)]) for j in range(heads)]
    moves += [copy(q_ref, q_out), copy(new_ref, new_out)]
    copy = copier(early)
    first = [copy(blocks_ref, blocks), copy(counts_ref, counts)]
    part = loaded.shape[2]
    for c in range(count):
        if split:
            src = state_ref.at[me ^ c, :, pl.ds(pl.multiple_of(rep * part, 128), part)]
        else:
            src = state_ref.at[me ^ c]
        first.append(copy(src, loaded.at[c]))
    for move in first + moves:
        move.start()
    for move in first:
        move.wait()
    for c in range(count):
        pack_state(loaded[c], states[c], states[c].shape[0] - state_rows(part))
    head_first = lax.axis_index("head") * new_ref.shape[2] + rep * heads
    rows = bias_out.shape[0] // heads
    keep_rep = pick_out.shape[2]
    for j in range(heads):
        live_count = counts[me, head_first + j]
        for c in range(count):
            live = jnp.int32(0)
            for side in range(2):
                for k in range(keep_rep):
                    slot = (rep if side == 0 else 1 - rep) * keep_rep + k
                    hit = (blocks[me, slot, head_first + j] == (me ^ c)) & (slot < live_count)
                    one = jnp.where(hit, 1.0, 0.0).astype(F32)
                    pick_out[side, j, k, c] = jnp.full(pick_out.shape[4:], one, F32).astype(BF)
                    live = live | hit.astype(jnp.int32)
            dead = jnp.where(live > 0, 0.0, NEG).astype(F32)
            bias_out[j * rows : (j + 1) * rows, c * BLOCK : (c + 1) * BLOCK] = jnp.full(
                (rows, BLOCK), dead, F32
            )
    for move in moves:
        move.wait()


def dot_f32(a, b, contract):
    return lax.dot_general(a, b, (contract, ((), ())), preferred_element_type=F32)


def query_rows(q_ref, heads):
    rep = lax.axis_index("rep")
    steps, _, q_heads, _ = q_ref.shape
    own_q = q_heads // 2
    group = own_q // heads
    q_all = [q_ref[step, 0].astype(F32) for step in range(steps)]
    q_all = [jnp.where(rep == 0, q[:own_q], q[own_q:]) for q in q_all]
    return [
        jnp.concatenate([x[j * group : (j + 1) * group] for x in q_all], axis=0)
        for j in range(heads)
    ]


def block_scores(q, piece_ref, j):
    hd = piece_ref.shape[1] // 2
    keys = piece_ref[j * BLOCK : (j + 1) * BLOCK, :hd]
    return dot_f32(q.astype(BF), keys, ((1,), (1,))) * hd ** (-0.5)


def block_sums(weights, piece_ref, j):
    values = piece_ref[j * BLOCK : (j + 1) * BLOCK, piece_ref.shape[1] // 2 :]
    return dot_f32(weights, values, ((1,), (0,)))


def attend(count, heads, q_ref, new_ref, bias_ref, pick_ref, *rest):
    pieces, states = rest[:count], rest[count : 2 * count - 2]
    outs, (kept_ref, sent_ref) = rest[2 * count - 2 : 3 * count - 2], rest[3 * count - 2 :]
    rep = lax.axis_index("rep")
    queries = query_rows(q_ref, heads)
    rows, hd = queries[0].shape
    steps = q_ref.shape[0]
    group = rows // steps
    all_rows = heads * rows
    scale = hd ** (-0.5)
    scores = [
        jnp.concatenate([block_scores(q, piece, j) for piece in pieces], axis=1)
        for j, q in enumerate(queries)
    ]
    scores = jnp.concatenate(scores, axis=0)
    alive = bias_ref[...] == 0.0
    scores = jnp.where(alive, scores, NEG)
    row_step = (lax.broadcasted_iota(jnp.int32, (all_rows, 1), 0) // group) % steps
    wide_q = jnp.concatenate(queries, axis=0)
    dots, fresh_values = [], []
    top = jnp.max(scores, axis=1, keepdims=True)
    for step in range(steps):
        both = new_ref[step, 0].astype(F32)
        fresh = jnp.where(rep == 0, both[:heads], both[heads:])
        wide = jnp.concatenate(
            [jnp.broadcast_to(fresh[j : j + 1], (rows, 2 * hd)) for j in range(heads)], axis=0
        )
        dot = jnp.sum(wide_q * wide[:, :hd], axis=1, keepdims=True) * scale
        dots.append(jnp.where(row_step >= step, dot, NEG))
        fresh_values.append(wide[:, hd:])
        top = jnp.maximum(top, dots[-1])
    weights = jnp.where(alive, jnp.exp(scores - top), 0.0)
    total = jnp.sum(weights, axis=1, keepdims=True)
    weights = weights.astype(BF)
    summed = []
    for j in range(heads):
        parts = [
            block_sums(weights[j * rows : (j + 1) * rows, c * BLOCK : (c + 1) * BLOCK], piece, j)
            for c, piece in enumerate(pieces)
        ]
        summed.append(functools.reduce(jnp.add, parts))
    summed = jnp.concatenate(summed, axis=0)
    for step in range(steps):
        weight = jnp.where(row_step >= step, jnp.exp(dots[step] - top), 0.0)
        total = total + weight
        summed = summed + weight.astype(BF).astype(F32) * fresh_values[step]
    result = (summed / total).astype(BF)
    for c in range(count):
        for j in range(2):
            half = result[j * rows : (j + 1) * rows] if j < heads else jnp.zeros((rows, hd), BF)
            outs[c][:rows, j * hd : (j + 1) * hd] = half
        if c > 1:
            outs[c][rows:, :] = states[c - 2][...]
    tile = pick_ref.shape[4]
    for side, ref in ((1, sent_ref), (0, kept_ref)):
        for j in range(heads):
            for k in range(ref.shape[1]):
                total = None
                for c in range(count):
                    piece = pieces[c][j * BLOCK : (j + 1) * BLOCK, :].reshape(-1, tile, 2 * hd)
                    term = piece * pick_ref[side, j, k, c][None]
                    total = term if total is None else total + term
                ref[j, k] = total.reshape(BLOCK, 2 * hd)


def collect(count, heads, steps, group, slope_ref, base_ref, home_ref, beside_ref, *rest):
    parts = [rest[0], rest[count - 1], *rest[1 : count - 1]]
    states = [home_ref, beside_ref, *parts[2:]]
    out_ref, mamba_ref, scratch = rest[count:]
    me = lax.axis_index("seq")
    ns, part = slope_ref.shape[2:]
    for c in range(count):
        first = states[c].shape[0] - state_rows(part)
        rows = [
            states[c][first + 16 * i : first + 16 * (i + 1), :].astype(F32)
            for i in range(pl.cdiv(part, 256))
        ]
        state = jnp.concatenate(rows, axis=1)[:, :part]
        for step in range(steps):
            mamba_ref[step, me ^ c] = base_ref[c, step] + jnp.sum(
                slope_ref[c, step] * state, axis=0, keepdims=True
            )
    for c in range(count):
        rows = parts[c][: steps * group, :].astype(F32)
        for j in range(heads):
            for step in range(steps):
                at = pl.multiple_of((step * count + (me ^ c)) * group, group)
                cut = rows[step * group : (step + 1) * group, j * 128 : (j + 1) * 128]
                scratch[j, pl.ds(at, group), :] = cut
    for j in range(heads):
        for g in range(group):
            at = (j * group + g) * 128
            tile = scratch[j, pl.ds(g, steps * count, stride=group), :]
            out_ref[:, at : at + 128] = tile.astype(BF)


def weight_half(weight_ref, out_ref, which, copy):
    half = out_ref.shape[0]
    rows = half // PIECES
    cuts = [(pl.ds(which * half + i * rows, rows), pl.ds(i * rows, rows)) for i in range(PIECES)]
    return [copy(weight_ref.at[src], out_ref.at[dst]) for src, dst in cuts]


def project_own(attn_ref, weight_ref, out_ref):
    out_ref[...] = dot_f32(attn_ref[...], weight_ref[...], ((1,), (0,)))


def pick(options, index):
    chosen = options[0]
    for i in range(1, len(options)):
        chosen = jnp.where(index == i, options[i], chosen)
    return chosen


def project_other(heads_count, count, acc_ref, attn_ref, weight_ref, *outs):
    total = acc_ref[...] + dot_f32(attn_ref[...], weight_ref[...], ((1,), (0,)))
    head = lax.axis_index("head")
    steps = total.shape[0] // count
    share = count // heads_count
    for step in range(steps):
        slices = [
            total[step * count + x * share : step * count + (x + 1) * share]
            for x in range(heads_count)
        ]
        for c in range(heads_count):
            outs[c][step] = pick(slices, head ^ c)


def add_up(*refs):
    total = refs[0][...]
    for ref in refs[1:-1]:
        total = total + ref[...]
    refs[-1][...] = total.astype(BF)


def prepare(count, split, weight_hbm, dt_hbm, x_hbm, bc_hbm, gain_hbm, log_hbm, own_ref, other_ref,
            slope_ref, base_ref, dt_ref, x_ref, bc_ref, gain_ref, log_ref, sems, weight_sems):
    copy = copier(sems)
    first = [
        copy(dt_hbm, dt_ref),
        copy(x_hbm, x_ref),
        copy(bc_hbm, bc_ref),
        copy(gain_hbm, gain_ref),
        copy(log_hbm, log_ref),
    ]
    copy, which = copier(weight_sems), lax.axis_index("rep")
    weights = weight_half(weight_hbm, own_ref, which, copy)
    weights += weight_half(weight_hbm, other_ref, 1 - which, copy)
    for move in first + weights:
        move.start()
    for move in first:
        move.wait()
    me, rep = lax.axis_index("seq"), lax.axis_index("rep")
    _, steps, ns, part = slope_ref.shape
    block = part * 2 if split else part
    diagonal = lax.broadcasted_iota(jnp.int32, (ns, ns), 0) == lax.broadcasted_iota(
        jnp.int32, (ns, ns), 1
    )

    def column(row):
        return jnp.sum(jnp.where(diagonal, row, 0.0), axis=1, keepdims=True)

    drive = [column(bc_ref[step, 0, 0:1, :]) for step in range(steps)]
    read = [column(bc_ref[step, 0, 1:2, :]) for step in range(steps)]
    for c in range(count):
        first = (me ^ c) * block + (rep * part if split else 0)
        lanes = pl.ds(pl.multiple_of(first, 128), part)
        rate = -jnp.exp(log_ref[:, lanes])
        gain = gain_ref[:, lanes]
        kept = jnp.ones((ns, part), F32)
        added = jnp.zeros((ns, part), F32)
        for step in range(steps):
            dt = dt_ref[step, :, lanes]
            inputs = x_ref[step : step + 1, lanes].astype(F32)
            decay = jnp.exp(dt * rate)
            kept = kept * decay
            added = added * decay + drive[step] * (dt * inputs)
            slope_ref[c, step] = read[step] * kept
            base_ref[c, step] = (
                jnp.sum(read[step] * added, axis=0, keepdims=True) + gain * inputs
            )
    for move in weights:
        move.wait()


def assemble(split, kept_ref, got_ref, mamba_ref, *rest):
    rep = lax.axis_index("rep")
    if split:
        other_ref, handoff_ref, out_ref, sems = rest
    else:
        handoff_ref, out_ref, sems = rest
    heads = kept_ref.shape[0]
    copy = copier(sems)
    moves = [
        copy(kept_ref, handoff_ref.at[0, pl.ds(rep * heads, heads)]),
        copy(got_ref, handoff_ref.at[0, pl.ds((1 - rep) * heads, heads)]),
    ]
    steps, count, _, part = mamba_ref.shape
    for step in range(steps):
        for b in range(count):
            if split:
                for ref, side in ((mamba_ref, rep), (other_ref, 1 - rep)):
                    lanes = pl.ds(pl.multiple_of((2 * b + side) * part, 128), part)
                    moves.append(copy(ref.at[step, b], out_ref.at[step, :, lanes]))
            else:
                moves.append(copy(mamba_ref.at[step, b], out_ref.at[step, :, pl.ds(b * part, part)]))
    run_all(moves)


def per_device(
    prefill_kv,
    kept_blocks,
    kept_counts,
    queries,
    new_kv,
    out_weight,
    prefill_state,
    a_log,
    step_input,
    step_dt,
    step_bc,
    skip_gain,
):
    count = lax.axis_size("seq")
    reps = lax.axis_size("rep")
    heads_count = lax.axis_size("head")
    requests, heads, tokens, width = prefill_kv.shape
    assert requests == count and tokens == BLOCK and reps == 2 and width == 256
    assert count & (count - 1) == 0 and heads_count & (heads_count - 1) == 0
    keep = kept_blocks.shape[2]
    keep_rep = keep // reps
    steps, _, q_heads, hd = queries.shape
    dec_heads = new_kv.shape[2]
    group = q_heads // dec_heads
    _, ns, block = prefill_state.shape
    split = block % (reps * 128) == 0
    part = block // reps if split else block
    all_rows = heads * steps * group
    assert all_rows <= 128
    channels = count * block
    shape = jax.ShapeDtypeStruct
    smem = pltpu.SMEM
    blocks = jnp.swapaxes(kept_blocks, 1, 2)

    prefill_kv, prefill_state, queries, new_kv = map(in_hbm, (prefill_kv, prefill_state, queries, new_kv))
    step_dt, step_bc, a_log, out_weight = map(in_hbm, (step_dt, step_bc, a_log, out_weight))
    step_input = in_hbm(step_input.reshape(steps, channels))
    skip_gain = in_hbm(skip_gain.reshape(1, -1))
    blocks, kept_counts = in_hbm(blocks), in_hbm(kept_counts)

    columns = out_weight.shape[1]
    half = heads * group * hd
    half_weight = pltpu.VMEM((half, columns), BF)
    block_shape = shape((heads * BLOCK, width), BF)
    pieces = {}
    for partners in ([count - 1], range(count - 2, 0, -1)):
        staged = call(
            functools.partial(stage_blocks, partners),
            [block_shape] * len(partners),
            [HB],
            [VM] * len(partners),
            [DMA((len(partners) * heads,))],
        )(prefill_kv)
        pieces.update(zip(partners, staged))
    pieces = [pieces[c] for c in range(1, count)]
    moved = [shift(pieces[c - 1], "seq", c) for c in range(count - 1, 1, -1)][::-1]
    own_piece, q_near, new_near, bias, picks, *states = call(
        functools.partial(stage_rest, count, split),
        [
            block_shape,
            shape(queries.shape, BF),
            shape(new_kv.shape, BF),
            shape((all_rows, count * BLOCK), F32),
            shape((reps, heads, keep_rep, count, 16, width), BF),
        ]
        + [shape((state_rows(part) + (32 if c == 1 else 0), width), BF) for c in range(count)],
        [HB] * 6,
        [VM] * (5 + count),
        [
            pltpu.VMEM((count, ns, part), F32),
            smem(blocks.shape, jnp.int32),
            smem(kept_counts.shape, jnp.int32),
            DMA((heads + 2,)),
            DMA((count + 2,)),
        ],
    )(*after([prefill_kv], pieces[0]), queries, new_kv, prefill_state, blocks, kept_counts)
    own_weight, other_weight, slope, base = call(
        functools.partial(prepare, count, split),
        [
            half_weight,
            half_weight,
            shape((count, steps, ns, part), F32),
            shape((count, steps, 1, part), F32),
        ],
        [HB] * 6,
        [VM] * 4,
        [
            pltpu.VMEM((steps, 1, channels), F32),
            pltpu.VMEM((steps, channels), BF),
            pltpu.VMEM(step_bc.shape, F32),
            pltpu.VMEM((1, channels), F32),
            pltpu.VMEM(a_log.shape, F32),
            DMA((5,)),
            DMA((2 * PIECES,)),
        ],
    )(*after([out_weight], pieces[0]), step_dt, step_input, step_bc, skip_gain, a_log)

    moved = [shift(after(pieces[:1], own_piece)[0], "seq", 1), *moved]
    beside = shift(after(states[1:2], own_weight)[0], "seq", 1)
    *moved, own_weight = after([*moved[::-1], own_weight])
    kv = [own_piece, *moved[::-1]]
    half_shape = (heads, keep_rep, BLOCK, width)
    rows = steps * group
    *sends, kept, sent = call(
        functools.partial(attend, count, heads),
        [shape((rows, width), BF)] * 2
        + [shape((rows + state_rows(part), width), BF)] * (count - 2)
        + [shape(half_shape, BF)] * 2,
        [VM] * (2 + 2 * count),
        [VM] * (count + 2),
    )(q_near, new_near, bias, picks, *kv, *states[2:])
    order = [*range(2, count), 1]
    gathered = [shift(sends[c], "seq", c) for c in order]
    attn, mamba = call(
        functools.partial(collect, count, heads, steps, group),
        [shape((steps * count, half), BF), shape((steps, count, 1, part), F32)],
        [VM] * (4 + count),
        [VM] * 2,
        [pltpu.VMEM((heads, (steps * count + 1) * group, hd), F32)],
    )(slope, base, states[0], beside, sends[0], *gathered)
    attn_other = shift(attn, "rep", 1)
    own_sum = call(
        project_own, shape((steps * count, columns), F32), [VM, VM], VM, us=0.7
    )(attn, own_weight)
    share = count // heads_count
    sums = call(
        functools.partial(project_other, heads_count, count),
        [shape((steps, share, columns), F32)] * heads_count,
        [VM, VM, VM],
        [VM] * heads_count,
        us=0.7,
    )(own_sum, attn_other, other_weight)
    sums = [sums[0]] + [shift(sums[c], "head", c) for c in range(1, heads_count)]
    got = shift(after([sent], mamba)[0], "rep", 1)
    mamba = after([mamba], own_sum)[0]
    kept = after([kept], sums[0])[0]
    operands = [kept, got, mamba] + ([shift(mamba, "rep", 1)] if split else [])
    handoff, mamba_out = call(
        functools.partial(assemble, split),
        [
            shape((1, dec_heads, keep_rep, BLOCK, width), BF),
            shape((steps, 1, channels), F32),
        ],
        [VM] * len(operands),
        [HB] * 2,
        [DMA((2 + steps * count * (2 if split else 1),))],
    )(*operands)
    sums[1:] = after(sums[1:], handoff)
    proj_out = call(
        add_up, shape((steps, share, columns), BF), [VM] * heads_count, VM, us=0.6
    )(*sums)
    return handoff, proj_out, mamba_out


def solution(mesh):
    return jax.shard_map(
        per_device,
        mesh=mesh,
        in_specs=(
            P("groups", ("head", "rep"), "seq", None),
            P("groups", None, None),
            P("groups", None),
            P(None, ("groups", "seq"), "head", None),
            P(None, ("groups", "seq"), "head", None),
            P("head", ("seq", "rep")),
            P("groups", None, ("head", "seq")),
            P(None, "head"),
            P(None, ("groups", "seq"), "head"),
            P(None, ("groups", "seq"), "head"),
            P(None, ("groups", "seq"), None, None),
            P("head"),
        ),
        out_specs=(
            P(("groups", "seq"), "head", "rep", None, None),
            P(None, ("groups", "head"), ("seq", "rep")),
            P(None, ("groups", "seq"), "head"),
        ),
        check_vma=False,
    )
```
